32 devices in a mesh: az: 8 (over z, y), rad: 4 (over x, core).
Axes of the slice: x: 2, y: 2, z: 4, core: 2. Of those that a mesh axis runs over, the one named last changes fastest.
Arguments:
- material_id: int32 [8, 2048], P('rad', 'az'), may hold values from 0 to 7
- thickness: float32 [8, 2048], P('rad', 'az'), may hold values from 0.7 to 1.4
- sigma_table: float32 [8], replicated, may hold values from 0.01 to 0.03
- nu_table: float32 [8], replicated, may hold values from 0.5 to 2
- angular_frequency: float32 [1], replicated, may hold values from 0.5 to 2
Outputs:
- merged_map: float32 [2, 1040, 4160], P(None, 'rad', 'az')
The draws below stay inside these ranges and needn't reach their ends.
All inputs are finite; a program needn't handle non-finite values.
Results may differ from the reference program's by a relative error of at most 0.0003.
Values sent between devices are 32-bit elements; how exact they have to be, the bound alone decides.
No kernel may reach another device: no remote copies, remote signals or barrier semaphores. Data moves between devices by JAX's collectives and lax.ppermute only.
A program may use at most 128 MiB of HBM per device.

```python
import math
import jax
import jax.numpy as jnp
import numpy as np
from jax import lax

ARC_CELLS = 256
DEPTH_CELLS = 2
SHEET_NODES = 16
MATERIALS = 8
OUTER_NODES = 260
PAIR_NODES = 520
RADIAL_CELLS = 8
AZIMUTH_CELLS = 2048
N_AZ = 8
N_RAD = 4


def place_ends(array, key, least, largest):
    longest = array.shape.index(max(array.shape))
    spots = []
    for shift in (0, 1):
        where = [jax.random.randint(jax.random.fold_in(key, axis), (), 0, length) for axis, length in enumerate(array.shape)]
        where[longest] = (where[longest] + shift) % array.shape[longest]
        spots.append(tuple(where))
    return array.at[spots[0]].set(least).at[spots[1]].set(largest)


def shard_levels(stream_key, dims, split, smallest, largest):
    def one(dim, parts):
        heights = jax.random.uniform(jax.random.fold_in(jax.random.fold_in(stream_key, 6), dim), (parts,), jnp.float32, smallest / len(split), largest / len(split))
        return jnp.repeat(jnp.exp(heights), dims[dim] // parts).reshape((-1,) + (1,) * (len(dims) - dim - 1))

    factor_of = one(*split[0])
    for cut in split[1:]:
        factor_of = factor_of * one(*cut)
    return factor_of


def setup_inputs(seed: int = 0) -> dict:
    arg_keys = jax.random.split(jax.random.key(seed), 6)
    return {
        "material_id": place_ends(jax.random.randint(arg_keys[0], (RADIAL_CELLS, AZIMUTH_CELLS), 0, MATERIALS), jax.random.fold_in(arg_keys[0], 1), 0, MATERIALS - 1).astype(jnp.int32),
        "thickness": jnp.clip(jnp.exp(math.log(1.4) - 0.6931472 * jax.random.uniform(arg_keys[1], (RADIAL_CELLS, AZIMUTH_CELLS), jnp.float32) ** shard_levels(arg_keys[1], (RADIAL_CELLS, AZIMUTH_CELLS), ((0, 4), (1, 8)), -0.2, 0.2)), 0.7, 1.4),
        "sigma_table": jnp.clip(jnp.exp(jax.random.uniform(arg_keys[2], (MATERIALS,), jnp.float32, math.log(0.01), math.log(0.03))), 0.01, 0.03),
        "nu_table": jnp.clip(jnp.exp(jax.random.uniform(arg_keys[3], (MATERIALS,), jnp.float32, math.log(0.5), math.log(2.0))), 0.5, 2.0),
        "angular_frequency": jnp.clip(jnp.exp(jax.random.uniform(arg_keys[4], (1,), jnp.float32, math.log(0.5), math.log(2.0))), 0.5, 2.0),
    }


def matmul(left_factor, right_factor):
    return jnp.dot(left_factor, right_factor, precision=lax.Precision.HIGHEST)

def complex_times(left_value, right_value):
    return jnp.stack([left_value[0] * right_value[0] - left_value[1] * right_value[1], left_value[0] * right_value[1] + left_value[1] * right_value[0]])

def complex_divide(numerator, denominator):
    magnitude = denominator[0] * denominator[0] + denominator[1] * denominator[1]
    return jnp.stack([(numerator[0] * denominator[0] + numerator[1] * denominator[1]) / magnitude, (numerator[1] * denominator[0] - numerator[0] * denominator[1]) / magnitude])

def harmonic(left_value, right_value):
    return complex_divide(2.0 * complex_times(left_value, right_value), left_value + right_value)

def cell_inputs(material_id, thickness, sigma_table, nu_table, angular_frequency):
    levels = jnp.arange(sigma_table.shape[0], dtype=jnp.int32)
    onehot = (material_id[None] == levels[:, None, None]).astype(jnp.float32)
    sigma_cell = jnp.sum(onehot * sigma_table[:, None, None], axis=0)
    base_value = jnp.sum(onehot * nu_table[:, None, None], axis=0)
    angular = angular_frequency[0]
    skin_ratio = angular * sigma_cell * thickness * thickness
    return (skin_ratio, base_value)

def lamination(skin_ratio, base_value):
    zero_field = jnp.zeros_like(skin_ratio)
    unit_value = jnp.stack([zero_field + 1.0, zero_field])
    factors = []
    carries = []
    for sheet_node in range(SHEET_NODES):
        if sheet_node < SHEET_NODES - 1:
            pivot_value = jnp.stack([zero_field + 2.0, skin_ratio])
        else:
            pivot_value = jnp.stack([zero_field + 1.0, 0.5 * skin_ratio])
        if sheet_node == 0:
            source = unit_value
        else:
            pivot_value = pivot_value + factors[-1]
            source = carries[-1]
        inverse = complex_divide(unit_value, pivot_value)
        factors.append(-inverse)
        carries.append(complex_times(source, inverse))
    sheet_field = carries[-1]
    total_field = sheet_field
    for sheet_node in range(SHEET_NODES - 2, -1, -1):
        sheet_field = carries[sheet_node] - complex_times(factors[sheet_node], sheet_field)
        total_field = total_field + sheet_field
    average = total_field / SHEET_NODES
    return complex_divide(jnp.stack([base_value, zero_field]), average)

def tile_faces(own_cells, left_rim, right_rim, below_rim, above_rim, center_radius, face_radius):
    depth_count = own_cells.shape[1]
    arc_inner = harmonic(own_cells[:, :, :-1], own_cells[:, :, 1:]) / center_radius[:, None]
    left_edge = harmonic(left_rim, own_cells[:, :, 0]) / center_radius
    right_edge = harmonic(own_cells[:, :, -1], right_rim) / center_radius
    west_faces = jnp.concatenate([2.0 * left_edge[:, :, None], arc_inner], axis=2)
    east_faces = jnp.concatenate([arc_inner, 2.0 * right_edge[:, :, None]], axis=2)
    column = jnp.concatenate([below_rim[:, None, :], own_cells, above_rim[:, None, :]], axis=1)
    radial = harmonic(column[:, :-1], column[:, 1:]) * face_radius[:, None]
    south_faces = jnp.concatenate([2.0 * radial[:, :1], radial[:, 1:depth_count]], axis=1)
    north_faces = jnp.concatenate([radial[:, 1:depth_count], 2.0 * radial[:, depth_count:]], axis=1)
    return (west_faces, east_faces, south_faces, north_faces)

def complex_inverse(matrix):
    lower_factor = jnp.linalg.cholesky(matrix[0])
    coupling = jax.scipy.linalg.cho_solve((lower_factor, True), matrix[1])
    coupled = matrix[0] + matmul(matrix[1], coupling)
    second_factor = jnp.linalg.cholesky(coupled)
    identity = jnp.eye(matrix.shape[1], dtype=matrix.dtype)
    inverse_re = jax.scipy.linalg.cho_solve((second_factor, True), identity)
    inverse_im = -matmul(coupling, inverse_re)
    return jnp.stack([inverse_re, inverse_im])

def complex_solve(matrix, right_side):
    lower_factor = jnp.linalg.cholesky(matrix[0])
    coupling = jax.scipy.linalg.cho_solve((lower_factor, True), matrix[1])
    shifted = jax.scipy.linalg.cho_solve((lower_factor, True), right_side[1])
    coupled = matrix[0] + matmul(matrix[1], coupling)
    second_factor = jnp.linalg.cholesky(coupled)
    solved_re = jax.scipy.linalg.cho_solve((second_factor, True), right_side[0] + matmul(matrix[1], shifted))
    solved_im = shifted - matmul(coupling, solved_re)
    return jnp.stack([solved_re, solved_im])

def boundary_cells(depth_count, arc_count):
    return np.concatenate([np.arange(arc_count), (depth_count - 1) * arc_count + np.arange(arc_count), np.arange(depth_count) * arc_count, np.arange(depth_count) * arc_count + arc_count - 1]).astype(np.int32)

def node_orders(depth_count, arc_count):
    sides = 2 * arc_count + np.arange(2 * depth_count)
    order_alpha = np.concatenate([np.arange(arc_count), sides, arc_count + np.arange(arc_count)]).astype(np.int32)
    order_beta = np.concatenate([arc_count + np.arange(arc_count), sides, np.arange(arc_count)]).astype(np.int32)
    return (order_alpha, order_beta)

def permute(local_map, node_order):
    return jnp.take(jnp.take(local_map, node_order, axis=1), node_order, axis=2)

def tile_map(west_faces, east_faces, south_faces, north_faces):
    depth_count = west_faces.shape[1]
    arc_count = west_faces.shape[2]
    cell_count = depth_count * arc_count
    diagonal = (west_faces + east_faces + south_faces + north_faces).reshape(2, cell_count)
    along_arc = jnp.concatenate([east_faces[:, :, :-1], jnp.zeros_like(east_faces[:, :, :1])], axis=2)
    along_arc = along_arc.reshape(2, cell_count)[:, :-1]
    along_radius = north_faces[:, :-1, :].reshape(2, cell_count - arc_count)
    matrices = []
    for component in range(2):
        matrices.append(jnp.diag(diagonal[component]) - jnp.diag(along_arc[component], 1) - jnp.diag(along_arc[component], -1) - jnp.diag(along_radius[component], arc_count) - jnp.diag(along_radius[component], -arc_count))
    inverse = complex_inverse(jnp.stack(matrices))
    cell_index = boundary_cells(depth_count, arc_count)
    picked = inverse[:, cell_index][:, :, cell_index]
    edge_gains = jnp.concatenate([south_faces[:, 0, :], north_faces[:, -1, :], west_faces[:, :, 0], east_faces[:, :, -1]], axis=1)
    scaled = complex_times(complex_times(edge_gains[:, :, None], picked), edge_gains[:, None, :])
    return jnp.stack([jnp.diag(edge_gains[0]), jnp.diag(edge_gains[1])]) - scaled

def merge_half(own_perm, partner_se, partner_ss, is_alpha):
    arc_count = partner_ss.shape[1]
    outer_count = own_perm.shape[1] - arc_count
    own_ee = own_perm[:, :outer_count, :outer_count]
    own_es = own_perm[:, :outer_count, outer_count:]
    own_se = own_perm[:, outer_count:, :outer_count]
    own_ss = own_perm[:, outer_count:, outer_count:]
    total_ss = own_ss + partner_ss
    first_block = jnp.where(is_alpha, own_se, partner_se)
    second_block = jnp.where(is_alpha, partner_se, own_se)
    right_side = jnp.concatenate([first_block, second_block], axis=2)
    solved = complex_solve(total_ss, right_side)
    product_re = matmul(own_es[0], solved[0]) - matmul(own_es[1], solved[1])
    product_im = matmul(own_es[0], solved[1]) + matmul(own_es[1], solved[0])
    empty_block = jnp.zeros_like(own_ee)
    placed = jnp.where(is_alpha, jnp.concatenate([own_ee, empty_block], axis=2), jnp.concatenate([empty_block, own_ee], axis=2))
    return placed - jnp.stack([product_re, product_im])

def reference(material_id, thickness, sigma_table, nu_table, angular_frequency):
    skin_ratio, base_value = cell_inputs(material_id, thickness, sigma_table, nu_table, angular_frequency)
    reluctivity = lamination(skin_ratio, base_value)
    center_all = 1.0 + (jnp.arange(RADIAL_CELLS, dtype=jnp.float32) + 0.5) / RADIAL_CELLS
    face_all = 1.0 + jnp.arange(RADIAL_CELLS + 1, dtype=jnp.float32) / RADIAL_CELLS
    order_alpha, order_beta = node_orders(DEPTH_CELLS, ARC_CELLS)
    zero_index = jnp.zeros((), jnp.int32)

    def one_tile(cycle_tile, sector_tile):
        first_row = (cycle_tile * DEPTH_CELLS).astype(jnp.int32)
        first_col = (sector_tile * ARC_CELLS).astype(jnp.int32)
        own_cells = lax.dynamic_slice(reluctivity, (zero_index, first_row, first_col), (2, DEPTH_CELLS, ARC_CELLS))
        left_col = ((first_col - 1) % AZIMUTH_CELLS).astype(jnp.int32)
        right_col = ((first_col + ARC_CELLS) % AZIMUTH_CELLS).astype(jnp.int32)
        left_rim = lax.dynamic_slice(reluctivity, (zero_index, first_row, left_col), (2, DEPTH_CELLS, 1))[:, :, 0]
        right_rim = lax.dynamic_slice(reluctivity, (zero_index, first_row, right_col), (2, DEPTH_CELLS, 1))[:, :, 0]
        below_row = jnp.maximum(first_row - 1, 0).astype(jnp.int32)
        above_row = jnp.minimum(first_row + DEPTH_CELLS, RADIAL_CELLS - 1).astype(jnp.int32)
        below_slab = lax.dynamic_slice(reluctivity, (zero_index, below_row, first_col), (2, 1, ARC_CELLS))[:, 0, :]
        above_slab = lax.dynamic_slice(reluctivity, (zero_index, above_row, first_col), (2, 1, ARC_CELLS))[:, 0, :]
        below_rim = jnp.where(cycle_tile == 0, own_cells[:, 0, :], below_slab)
        above_rim = jnp.where(cycle_tile == N_RAD - 1, own_cells[:, -1, :], above_slab)
        center_radius = lax.dynamic_slice(center_all, (first_row,), (DEPTH_CELLS,))
        face_radius = lax.dynamic_slice(face_all, (first_row,), (DEPTH_CELLS + 1,))
        face_set = tile_faces(own_cells, left_rim, right_rim, below_rim, above_rim, center_radius, face_radius)
        return tile_map(face_set[0], face_set[1], face_set[2], face_set[3])

    def one_pair(pair_index):
        cycle_pair = pair_index // N_AZ
        sector = pair_index % N_AZ
        alpha_map = permute(one_tile(2 * cycle_pair, sector), order_alpha)
        beta_map = permute(one_tile(2 * cycle_pair + 1, sector), order_beta)
        alpha_rows = merge_half(alpha_map, beta_map[:, OUTER_NODES:, :OUTER_NODES], beta_map[:, OUTER_NODES:, OUTER_NODES:], True)
        beta_rows = merge_half(beta_map, alpha_map[:, OUTER_NODES:, :OUTER_NODES], alpha_map[:, OUTER_NODES:, OUTER_NODES:], False)
        return jnp.concatenate([alpha_rows, beta_rows], axis=1)
    blocks = lax.map(one_pair, jnp.arange(N_RAD // 2 * N_AZ, dtype=jnp.int32))
    blocks = blocks.reshape(N_RAD // 2, N_AZ, 2, PAIR_NODES, PAIR_NODES)
    return jnp.transpose(blocks, (2, 0, 3, 1, 4)).reshape(2, N_RAD // 2 * PAIR_NODES, N_AZ * PAIR_NODES)
```

```python
import jax
import jax.numpy as jnp
from jax import lax
from jax.experimental import pallas as pl
from jax.experimental.pallas import tpu as pltpu
from jax.sharding import PartitionSpec as P

SHEET_NODES = 16
LANES = 128
GROUPS = 4


def lane_roll(value, shift):
    return pltpu.roll(value, shift % value.shape[1], 1)


def sub_roll(value, shift):
    return pltpu.roll(value, shift % value.shape[0], 0)


def lane_take(value, index):
    return jnp.take_along_axis(value, index, axis=1, mode="promise_in_bounds")


def iota(dim):
    return lax.broadcasted_iota(jnp.int32, (8, LANES), dim)


class Cx:
    def __init__(self, re, im):
        self.re, self.im = re, im

    def __add__(self, other):
        return Cx(self.re + other.re, self.im + other.im)

    def __sub__(self, other):
        return Cx(self.re - other.re, self.im - other.im)

    def __neg__(self):
        return Cx(-self.re, -self.im)

    def __mul__(self, other):
        if not isinstance(other, Cx):
            return Cx(self.re * other, self.im * other)
        return Cx(
            self.re * other.re - self.im * other.im, self.re * other.im + self.im * other.re
        )

    def inverse(self):
        scale = 1.0 / (self.re * self.re + self.im * self.im)
        return Cx(self.re * scale, -self.im * scale)

    def root(self):
        size = jnp.sqrt(self.re * self.re + self.im * self.im)
        re = jnp.sqrt(0.5 * (size + self.re))
        return Cx(re, 0.5 * self.im / re)

    def map(self, function):
        return Cx(function(self.re), function(self.im))

    def row(self, index):
        return self.map(lambda part: jnp.broadcast_to(part[index : index + 1], (8, LANES)))

    def lanes(self, shift):
        return self.map(lambda part: lane_roll(part, shift))

    def subs(self, shift):
        return self.map(lambda part: sub_roll(part, shift))


def pick(mask, first, second):
    if not isinstance(second, Cx):
        return first.map(lambda part: jnp.where(mask, part, second))
    return Cx(jnp.where(mask, first.re, second.re), jnp.where(mask, first.im, second.im))


def total(terms):
    terms = list(terms)
    while len(terms) > 1:
        terms = [
            terms[i] + terms[i + 1] if i + 1 < len(terms) else terms[i]
            for i in range(0, len(terms), 2)
        ]
    return terms[0]


def harmonic(left, right):
    return (left * right) * (left + right).inverse() * 2.0


def lamination(skin, base):
    above = Cx(jnp.ones_like(skin), jnp.zeros_like(skin))
    field = Cx(jnp.ones_like(skin), 0.5 * skin)
    summed = above
    for _ in range(SHEET_NODES - 1):
        summed = summed + field
        below = Cx(
            2.0 * field.re - skin * field.im - above.re,
            2.0 * field.im + skin * field.re - above.im,
        )
        above, field = field, below
    return field * summed.inverse() * (base * SHEET_NODES)


def factor(entry):
    work = {(r, c): entry(r, c) for r in range(4) for c in range(r + 1)}
    lower, pivots = {}, []
    for k in range(4):
        inverse = work[k, k].inverse()
        pivots.append(inverse)
        for r in range(k + 1, 4):
            lower[r, k] = work[r, k] * inverse
        for r in range(k + 1, 4):
            for c in range(k + 1, r + 1):
                work[r, c] = work[r, c] - lower[r, k] * work[c, k]
    return lower, pivots


def solve(lower, pivots, right):
    half = []
    for r in range(4):
        value = right[r]
        for c in range(r):
            value = value - lower[r, c] * half[c]
        half.append(value)
    out = [None] * 4
    for r in range(3, -1, -1):
        value = half[r] * pivots[r]
        for c in range(r + 1, 4):
            value = value - lower[c, r] * out[c]
        out[r] = value
    return out


def seeds(lower, pivots):
    column = iota(0) & 3
    unit = {}
    for r in range(4):
        for c in range(r - 1, -1, -1):
            value = -lower[r, c]
            for k in range(c + 1, r):
                value = value - lower[r, k] * unit[k, c]
            unit[r, c] = value
    roots = [pivot.root() for pivot in pivots]
    out = []
    for r in range(4):
        value = pick(column == r, roots[r], 0.0)
        for k in range(r + 1, 4):
            value = pick(column == k, roots[k] * unit[k, r], value)
        out.append(value)
    return out


def evens(tiles):
    lane = iota(1)
    index = (2 * lane) & (LANES - 1)

    def one(offset):
        return Cx(
            *(
                jnp.where(
                    lane < LANES // 2,
                    lane_take(first, index + offset),
                    lane_take(second, index + offset),
                )
                for first, second in ((tiles[0].re, tiles[1].re), (tiles[0].im, tiles[1].im))
            )
        )

    return one(0), one(1)


def natural(even, odd):
    lane = iota(1)
    out = []
    for half in range(2):
        index = half * (LANES // 2) + (lane >> 1)
        out.append(
            Cx(
                *(
                    jnp.where((lane & 1) == 0, lane_take(first, index), lane_take(second, index))
                    for first, second in ((even.re, odd.re), (even.im, odd.im))
                )
            )
        )
    return out


def split(value):
    high = value.map(lambda part: part.astype(jnp.bfloat16).astype(jnp.float32))
    return high, value - high


def contract(left, right):
    return lax.dot_general(
        left.astype(jnp.bfloat16),
        right.astype(jnp.bfloat16),
        (((0,), (0,)), ((), ())),
        preferred_element_type=jnp.float32,
    )


def strip(main, side, is_alpha, first_cycle, radial_count):
    lane, sub = iota(1), iota(0)
    lower4 = sub < 4
    column = sub & 3

    cells = lamination(main[0], main[1])
    rims = lamination(side[0], side[1])
    tiles = [cells.map(lambda part: part[:, :LANES]), cells.map(lambda part: part[:, LANES:])]
    cycle = (first_cycle + sub - 1).astype(jnp.float32)
    center = 1.0 + (cycle + 0.5) / radial_count
    face = 1.0 + cycle / radial_count
    per_center = 1.0 / center
    first_lane, last_lane = lane == 0, lane == LANES - 1

    ahead = [tile.lanes(1) for tile in tiles]
    west = [
        harmonic(pick(first_lane, rims.lanes(1), ahead[0]), tiles[0]) * per_center,
        harmonic(pick(first_lane, ahead[0], ahead[1]), tiles[1]) * per_center,
    ]
    wall = harmonic(tiles[1], rims.lanes(-1)) * per_center * 2.0
    back = [tile.lanes(-1) for tile in west]
    east = [pick(last_lane, back[1], back[0]), pick(last_lane, wall, back[1])]
    west[0] = pick(first_lane, west[0] * 2.0, west[0])
    south, north = [], []
    for tile in tiles:
        radial = harmonic(tile.subs(1), tile) * face
        radial = pick((sub == 1) | (sub == 5), radial * 2.0, radial)
        south.append(radial)
        north.append(radial.subs(-1))
    diagonal = [west[h] + east[h] + south[h] + north[h] for h in range(2)]
    gain_in = [south[h].row(1) for h in range(2)]
    gain_out = [north[h].row(4) for h in range(2)]

    diag_e, diag_o = evens(diagonal)
    east_e, east_o = evens(east)
    up_e, up_o = evens(north)
    left_e = pick(last_lane, east_o, 0.0)
    left_e = (east_o - left_e).lanes(1)

    def entry_e(r, c):
        if r == c:
            return diag_e.row(r + 1)
        return -up_e.row(r)

    lower_e, pivots_e = {}, []
    work = diag_e.row(1)
    for r in range(4):
        pivots_e.append(work.inverse())
        if r < 3:
            coupling = up_e.row(r + 1)
            lower_e[r + 1, r] = -(coupling * pivots_e[r])
            work = diag_e.row(r + 2) + lower_e[r + 1, r] * coupling
    zero = jnp.zeros((8, LANES), jnp.float32)
    nothing = Cx(zero, zero)
    half = []
    for r in range(4):
        value = Cx(jnp.where(column == r, 1.0, zero), zero)
        if r:
            value = value - lower_e[r, r - 1] * half[r - 1]
        half.append(value)
    inverse_e = [None] * 4
    for r in range(3, -1, -1):
        value = half[r] * pivots_e[r]
        if r < 3:
            value = value - lower_e[r + 1, r] * inverse_e[r + 1]
        inverse_e[r] = value
    for r in range(4):
        for c in range(r - 1):
            lower_e[r, c] = nothing
    seeds_e = seeds(lower_e, pivots_e)
    sides_e = pick(lower4, left_e.subs(-1), east_e.subs(3))
    reach_e = [inverse_e[r] * sides_e for r in range(4)]
    matrix, pair = [], []
    for r in range(4):
        to_left = (left_e.row(r + 1) * reach_e[r]).lanes(-1)
        to_right = east_e.row(r + 1) * reach_e[r]
        pair.append(pick(lower4, to_right, to_left))
        change = pick(lower4, to_left, to_right)
        base = pick(column == r, diag_o.row(r + 1), 0.0)
        if r < 3:
            base = pick(column == r + 1, -up_o.row(r + 1), base)
        if r > 0:
            base = pick(column == r - 1, -up_o.row(r), base)
        matrix.append(base - change - change.subs(4))

    for level in range(1, 8):
        step = 1 << (level - 1)
        stay = ((lane + 1) & (2 * step - 1)) == 0
        reach = solve(*factor(lambda r, c: matrix[r].row(c)), pair)
        next_matrix, next_pair = [], []
        for r in range(4):
            to_left = total(pair[k].row(r) * reach[k] for k in range(4)).lanes(-step)
            to_right = total(pair[k].row(4 + r) * reach[k] for k in range(4)).lanes(step)
            change = pick(lower4, to_left, to_right)
            change = change + change.subs(4)
            next_matrix.append(pick(stay, matrix[r] - change, matrix[r]))
            next_pair.append(pick(stay, pick(lower4, to_right, to_left), pair[r]))
        matrix, pair = next_matrix, next_pair

    lower, pivots = factor(lambda r, c: matrix[r].row(c))
    reach = solve(lower, pivots, pair)
    reach_rows = [[reach[r].row(k) for k in range(8)] for r in range(4)]
    seed = seeds(lower, pivots)

    def level_of(group):
        return jnp.where(lower4, 2 * group - 1, 2 * group)

    own_level = jnp.ones((8, LANES), jnp.int32)
    for level in range(2, 9):
        own_level = own_level + (((lane + 1) & ((1 << (level - 1)) - 1)) == 0).astype(jnp.int32)

    odd = {}
    for group in range(1, GROUPS + 1):
        rows = [pick(own_level == level_of(group), seed[r], 0.0) for r in range(4)]
        for level in range(min(2 * group - 1, 7), 0, -1):
            step = 1 << (level - 1)
            here = own_level == level
            before = [row.lanes(step) for row in rows]
            after = [row.lanes(-step) for row in rows]
            fresh = []
            for r in range(4):
                terms = [reach_rows[r][k] * before[k] for k in range(4)]
                terms += [reach_rows[r][4 + k] * after[k] for k in range(4)]
                fresh.append(rows[r] + pick(here, total(terms), 0.0))
            rows = fresh
        odd[group] = rows

    reach_e_rows = [[reach_e[r].row(k) for k in range(8)] for r in range(4)]
    even = {0: [pick(first_lane & lower4, seeds_e[r], 0.0) for r in range(4)]}
    odd[0] = [nothing] * 4
    for group in range(1, GROUPS + 1):
        before = [row.lanes(1) for row in odd[group]]
        even[group] = []
        for r in range(4):
            terms = [reach_e_rows[r][k] * before[k] for k in range(4)]
            terms += [reach_e_rows[r][4 + k] * odd[group][k] for k in range(4)]
            even[group].append(total(terms))

    def corners(lefts, rights):
        return pick(
            lane == 0,
            lefts[0],
            pick(
                lane == 1,
                lefts[1].lanes(1),
                pick(lane == 2, rights[0].lanes(3), pick(lane == 3, rights[1].lanes(4), 0.0)),
            ),
        )

    gains_left = [west[0].row(r + 1) for r in range(4)]
    gains_right = [east[1].row(r + 1) for r in range(4)]
    gain_corner = [
        corners(gains_left[2 * t : 2 * t + 2], gains_right[2 * t : 2 * t + 2]) for t in range(2)
    ]
    inner, outer, corner = {}, {}, {}
    for group in range(GROUPS + 1):
        if group:
            low = natural(even[group][0], odd[group][0])
            high = natural(even[group][3], odd[group][3])
        else:
            low, high = [even[0][0], nothing], [even[0][3], nothing]
        inner[group] = [low[h] * gain_in[h] for h in range(2)]
        outer[group] = [high[h] * gain_out[h] for h in range(2)]
        corner[group] = [
            corners(even[group][2 * t : 2 * t + 2], odd[group][2 * t : 2 * t + 2]) * gain_corner[t]
            for t in range(2)
        ]

    left_parts, right_parts = [], []
    for group in range(GROUPS + 1):
        if group in (0, GROUPS):
            low, high = inner[group], outer[group]
        else:
            near = lane < (2 << level_of(group))
            low = [pick(near, inner[group][0], 0.0), nothing]
            high = [pick(near, outer[group][0], 0.0), nothing]
        side_a, side_b = corner[group]
        own = [pick(is_alpha, low[h], high[h]) for h in range(2)]
        own.append(pick(is_alpha, side_a, side_b))
        moved = [high[0].lanes(4), high[1].lanes(4)]
        every = [
            low[0],
            low[1],
            pick(lower_lanes(lane, 4), side_a, moved[0]),
            pick(lower_lanes(lane, 4), moved[0], moved[1]),
            pick(lower_lanes(lane, 4), moved[1], pick(lane < 8, side_b.lanes(4), 0.0)),
        ]
        left_parts.append([split(value) for value in own])
        right_parts.append([split(value) for value in every])

    def wide(parts, which, name, sign=1.0):
        rows = []
        for group in parts:
            pieces = [getattr(value[which], name) for value in group]
            rows.append(jnp.concatenate(pieces, axis=1) * sign)
        return rows

    fill = [jnp.zeros((8, 3 * LANES), jnp.float32)] * 2
    left = (
        wide(left_parts, 0, "re")
        + wide(left_parts, 0, "re")
        + wide(left_parts, 1, "re")
        + wide(left_parts, 0, "im")
        + wide(left_parts, 0, "im")
        + wide(left_parts, 1, "im")
        + fill
    )
    fill = [jnp.zeros((8, 5 * LANES), jnp.float32)] * 2
    right_re = (
        wide(right_parts, 0, "re")
        + wide(right_parts, 1, "re")
        + wide(right_parts, 0, "re")
        + wide(right_parts, 0, "im", -1.0)
        + wide(right_parts, 1, "im", -1.0)
        + wide(right_parts, 0, "im", -1.0)
        + fill
    )
    right_im = (
        wide(right_parts, 0, "im")
        + wide(right_parts, 1, "im")
        + wide(right_parts, 0, "im")
        + wide(right_parts, 0, "re")
        + wide(right_parts, 1, "re")
        + wide(right_parts, 0, "re")
        + fill
    )
    left = jnp.concatenate(left, axis=0)
    top = Cx(
        contract(left, jnp.concatenate(right_re, axis=0)),
        contract(left, jnp.concatenate(right_im, axis=0)),
    )

    masks = []
    for level in range(1, 7):
        for tile in range(max((1 << (6 - level)) // 2, 1)):
            masks.append((level, (lane >> (level + 1)) == 2 * tile + (sub >> 2)))

    def spread(value):
        out = []
        for level, mask in masks:
            out.append(jnp.where(mask, value[level], 0.0))
        return jnp.concatenate(out, axis=0)

    def both(values, half):
        levels = {}
        for group in range(1, GROUPS):
            value = values[group][half]
            if half == 0:
                value = pick(lane < (2 << level_of(group)), nothing, value)
            turned = value.subs(4)
            levels[2 * group - 1] = split(pick(lower4, value, turned))
            levels[2 * group] = split(pick(lower4, turned, value))
        return {
            (which, name): spread(
                {level: getattr(pair[which], name) for level, pair in levels.items()}
            )
            for which in range(2)
            for name in ("re", "im")
        }

    even_d = [inverse_e[0].row(0), inverse_e[0].row(3), inverse_e[3].row(3)]
    even_d = [natural(value, nothing) for value in even_d]
    local = []
    for half in range(2):
        low, high = both(inner, half), both(outer, half)
        own = {key: jnp.where(is_alpha, low[key], high[key]) for key in low}
        every = {key: jnp.concatenate([low[key], high[key]], axis=1) for key in low}
        hr, hi, lr, li = (0, "re"), (0, "im"), (1, "re"), (1, "im")
        left = jnp.concatenate([own[key] for key in (hr, hi, hr, hi, lr, li)], axis=0)
        right_re = jnp.concatenate(
            [every[hr], -every[hi], every[lr], -every[li], every[hr], -every[hi]], axis=0
        )
        right_im = jnp.concatenate([every[key] for key in (hi, hr, li, lr, hi, hr)], axis=0)
        product = Cx(contract(left, right_re), contract(left, right_im))
        g_in, g_out = gain_in[half], gain_out[half]
        solo = (lane & 1) == 0
        if half == 0:
            solo = solo & (lane > 0)
        cross = even_d[1][half] * g_in * g_out
        on_in = pick(is_alpha, even_d[0][half] * g_in * g_in, cross)
        on_out = pick(is_alpha, cross, even_d[2][half] * g_out * g_out)
        on_in = pick(solo, on_in, 0.0) - pick(is_alpha, g_in, nothing)
        on_out = pick(solo, on_out, 0.0) - pick(is_alpha, nothing, g_out)
        local.append((product, on_in, on_out))
    edge = pick((lane == sub) & lower4, pick(is_alpha, gain_corner[0], gain_corner[1]), 0.0)
    return top, local, edge


def lower_lanes(lane, count):
    return lane < count


def finish(top, local, edge, is_alpha, store):
    lane, sub = iota(1), iota(0)
    for part, name in enumerate(("re", "im")):
        full = getattr(top, name)
        edge_part = getattr(edge, name)
        for half in range(2):
            product = getattr(local[half][0], name)
            on_in = getattr(local[half][1], name)
            on_out = getattr(local[half][2], name)
            for row in range(0, LANES, 8):
                here = lane == sub + row
                low = product[row : row + 8, :LANES] + jnp.where(here, on_in, 0.0)
                high = product[row : row + 8, LANES:] + jnp.where(here, on_out, 0.0)
                high = lane_roll(high, 4)
                at = half * LANES + row
                out = [full[at : at + 8, t * LANES : (t + 1) * LANES] for t in range(5)]
                out[half] = out[half] + low
                out[2 + half] = out[2 + half] + jnp.where(lane < 4, 0.0, high)
                out[3 + half] = out[3 + half] + jnp.where(lane < 4, high, 0.0)
                store(part, at, 8, [-value for value in out])
        at = 2 * LANES
        out = [full[at : at + 8, t * LANES : (t + 1) * LANES] for t in range(5)]
        out[2] = out[2] - jnp.where(is_alpha, edge_part, 0.0)
        out[4] = out[4] - jnp.where(is_alpha, 0.0, lane_roll(edge_part, 4))
        store(part, at, 4, [-value for value in out])


def gather_rows(own, sides, partner, near, far, is_alpha, is_first, is_last, main, side):
    lane = lax.broadcasted_iota(jnp.int32, (2, LANES), 1)
    for field in range(2):
        at = 2 * field
        mine, other = own[at : at + 2, :], partner[at : at + 2, :]
        alpha = jnp.where(is_alpha, mine, other)
        beta = jnp.where(is_alpha, other, mine)
        below = jnp.where(is_alpha, near[at + 1 : at + 2, :], far[at + 1 : at + 2, :])
        above = jnp.where(is_alpha, far[at : at + 1, :], near[at : at + 1, :])
        main[field, 0:1, :] = jnp.where(is_first, alpha[0:1], below)
        main[field, 1:3, :] = alpha
        main[field, 3:5, :] = beta
        main[field, 5:6, :] = jnp.where(is_last, beta[1:2], above)
        main[field, 6:8, :] = beta
        left_own, right_own = sides[at : at + 2, LANES:], sides[4 + at : 6 + at, :LANES]
        left_other = partner[4 + at : 6 + at, LANES:]
        right_other = partner[8 + at : 10 + at, :LANES]
        ends_own = jnp.where(lane == LANES - 1, left_own, jnp.where(lane == 0, right_own, 1.0))
        ends_other = jnp.where(
            lane == LANES - 1, left_other, jnp.where(lane == 0, right_other, 1.0)
        )
        ends_alpha = jnp.where(is_alpha, ends_own, ends_other)
        ends_beta = jnp.where(is_alpha, ends_other, ends_own)
        side[field, 0:1, :] = ends_alpha[0:1]
        side[field, 1:3, :] = ends_alpha
        side[field, 3:5, :] = ends_beta
        side[field, 5:7, :] = ends_beta
        side[field, 7:8, :] = ends_beta[0:1]


def merge_kernel(cycles, depth, own, sides, partner, near, far, out, main, side):
    index = lax.axis_index("rad")
    is_alpha = index % 2 == 0
    is_first = index // 2 == 0
    is_last = index // 2 == cycles // 2 - 1
    gather_rows(own, sides, partner, near, far, is_alpha, is_first, is_last, main, side)
    top, local, edge = strip(
        (main[0], main[1]),
        (side[0], side[1]),
        is_alpha,
        (index // 2) * (2 * depth),
        cycles * depth,
    )

    def store(part, row, count, tiles):
        for number, tile in enumerate(tiles):
            width = min(LANES, out.shape[2] - number * LANES)
            out[part, row : row + count, number * LANES : number * LANES + width] = tile[
                :count, :width
            ]

    finish(top, local, edge, is_alpha, store)


def cell_inputs(material_id, thickness, sigma_table, nu_table, angular_frequency):
    levels = jnp.arange(sigma_table.shape[0], dtype=jnp.int32)
    onehot = (material_id[None] == levels[:, None, None]).astype(jnp.float32)
    sigma_cell = jnp.sum(onehot * sigma_table[:, None, None], axis=0)
    base_value = jnp.sum(onehot * nu_table[:, None, None], axis=0)
    angular = angular_frequency[0]
    skin_ratio = angular * sigma_cell * thickness * thickness
    return (skin_ratio, base_value)


def per_device(material_id, thickness, sigma_table, nu_table, angular_frequency):
    depth, arc = thickness.shape
    cells = jnp.concatenate(
        cell_inputs(material_id, thickness, sigma_table, nu_table, angular_frequency), axis=0
    )
    cycles, blocks = lax.axis_size("rad"), lax.axis_size("az")
    left = lax.ppermute(cells, "az", [(i, (i + 1) % blocks) for i in range(blocks)])
    right = lax.ppermute(cells, "az", [((i + 1) % blocks, i) for i in range(blocks)])
    near, far = [], []
    for low in range(1, cycles - 1, 2):
        near += [(low, low + 1), (low + 1, low)]
    for low in range(0, cycles - 2, 2):
        far += [(low + 2, low), (low + 1, low + 3)]
    near = lax.ppermute(cells, "rad", near)
    far = lax.ppermute(cells, "rad", far)
    swap = [(i, i ^ 1) for i in range(cycles)]
    partner = lax.ppermute(jnp.concatenate([cells, left, right], axis=0), "rad", swap)
    outer_nodes = arc + 2 * depth
    return pl.pallas_call(
        lambda *refs: merge_kernel(cycles, depth, *refs),
        out_shape=jax.ShapeDtypeStruct((2, outer_nodes, 2 * outer_nodes), jnp.float32),
        in_specs=[pl.BlockSpec(memory_space=pltpu.VMEM)] * 5,
        out_specs=pl.BlockSpec(memory_space=pltpu.VMEM),
        scratch_shapes=[
            pltpu.VMEM((2, 8, arc), jnp.float32),
            pltpu.VMEM((2, 8, LANES), jnp.float32),
        ],
        compiler_params=pltpu.CompilerParams(vmem_limit_bytes=48 * 1024 * 1024),
        name="pair_map",
    )(cells, jnp.concatenate([left, right], axis=0), partner, near, far)


def solution(mesh):
    placed = (P("rad", "az"), P("rad", "az"), P(), P(), P())
    return jax.shard_map(
        per_device, mesh=mesh, in_specs=placed, out_specs=P(None, "rad", "az"), check_vma=False
    )
```

```python
import jax
import jax.numpy as jnp
from jax import lax
from jax.experimental import pallas as pl
from jax.experimental.pallas import tpu as pltpu
from jax.sharding import PartitionSpec as P

SHEET_NODES = 16
LANES = 128
GROUPS = 4


def lane_roll(value, shift):
    return pltpu.roll(value, shift % value.shape[1], 1)


def sub_roll(value, shift):
    return pltpu.roll(value, shift % value.shape[0], 0)


def lane_take(value, index):
    return jnp.take_along_axis(value, index, axis=1, mode="promise_in_bounds")


def iota(dim):
    return lax.broadcasted_iota(jnp.int32, (8, LANES), dim)


class Cx:
    def __init__(self, re, im):
        self.re, self.im = re, im

    def __add__(self, other):
        return Cx(self.re + other.re, self.im + other.im)

    def __sub__(self, other):
        return Cx(self.re - other.re, self.im - other.im)

    def __neg__(self):
        return Cx(-self.re, -self.im)

    def __mul__(self, other):
        if not isinstance(other, Cx):
            return Cx(self.re * other, self.im * other)
        return Cx(
            self.re * other.re - self.im * other.im, self.re * other.im + self.im * other.re
        )

    def inverse(self):
        scale = 1.0 / (self.re * self.re + self.im * self.im)
        return Cx(self.re * scale, -self.im * scale)

    def root(self):
        size = jnp.sqrt(self.re * self.re + self.im * self.im)
        re = jnp.sqrt(0.5 * (size + self.re))
        return Cx(re, 0.5 * self.im / re)

    def map(self, function):
        return Cx(function(self.re), function(self.im))

    def row(self, index):
        return self.map(lambda part: jnp.broadcast_to(part[index : index + 1], (8, LANES)))

    def lanes(self, shift):
        return self.map(lambda part: lane_roll(part, shift))

    def subs(self, shift):
        return self.map(lambda part: sub_roll(part, shift))


def pick(mask, first, second):
    if not isinstance(second, Cx):
        return first.map(lambda part: jnp.where(mask, part, second))
    return Cx(jnp.where(mask, first.re, second.re), jnp.where(mask, first.im, second.im))


def total(terms):
    terms = list(terms)
    while len(terms) > 1:
        terms = [
            terms[i] + terms[i + 1] if i + 1 < len(terms) else terms[i]
            for i in range(0, len(terms), 2)
        ]
    return terms[0]


def harmonic(left, right):
    return (left * right) * (left + right).inverse() * 2.0


def lamination(skin, base):
    above = Cx(jnp.ones_like(skin), jnp.zeros_like(skin))
    field = Cx(jnp.ones_like(skin), 0.5 * skin)
    summed = above
    for _ in range(SHEET_NODES - 1):
        summed = summed + field
        below = Cx(
            2.0 * field.re - skin * field.im - above.re,
            2.0 * field.im + skin * field.re - above.im,
        )
        above, field = field, below
    return field * summed.inverse() * (base * SHEET_NODES)


def factor(entry):
    work = {(r, c): entry(r, c) for r in range(4) for c in range(r + 1)}
    lower, pivots = {}, []
    for k in range(4):
        inverse = work[k, k].inverse()
        pivots.append(inverse)
        for r in range(k + 1, 4):
            lower[r, k] = work[r, k] * inverse
        for r in range(k + 1, 4):
            for c in range(k + 1, r + 1):
                work[r, c] = work[r, c] - lower[r, k] * work[c, k]
    return lower, pivots


def solve(lower, pivots, right):
    half = []
    for r in range(4):
        value = right[r]
        for c in range(r):
            value = value - lower[r, c] * half[c]
        half.append(value)
    out = [None] * 4
    for r in range(3, -1, -1):
        value = half[r] * pivots[r]
        for c in range(r + 1, 4):
            value = value - lower[c, r] * out[c]
        out[r] = value
    return out


def seeds(lower, pivots):
    column = iota(0) & 3
    unit = {}
    for r in range(4):
        for c in range(r - 1, -1, -1):
            value = -lower[r, c]
            for k in range(c + 1, r):
                value = value - lower[r, k] * unit[k, c]
            unit[r, c] = value
    roots = [pivot.root() for pivot in pivots]
    out = []
    for r in range(4):
        value = pick(column == r, roots[r], 0.0)
        for k in range(r + 1, 4):
            value = pick(column == k, roots[k] * unit[k, r], value)
        out.append(value)
    return out


def evens(tiles):
    lane = iota(1)
    index = (2 * lane) & (LANES - 1)

    def one(offset):
        return Cx(
            *(
                jnp.where(
                    lane < LANES // 2,
                    lane_take(first, index + offset),
                    lane_take(second, index + offset),
                )
                for first, second in ((tiles[0].re, tiles[1].re), (tiles[0].im, tiles[1].im))
            )
        )

    return one(0), one(1)


def natural(even, odd):
    lane = iota(1)
    out = []
    for half in range(2):
        index = half * (LANES // 2) + (lane >> 1)
        out.append(
            Cx(
                *(
                    jnp.where((lane & 1) == 0, lane_take(first, index), lane_take(second, index))
                    for first, second in ((even.re, odd.re), (even.im, odd.im))
                )
            )
        )
    return out


def split(value):
    high = value.map(lambda part: part.astype(jnp.bfloat16).astype(jnp.float32))
    return high, value - high


def contract(left, right):
    return lax.dot_general(
        left.astype(jnp.bfloat16),
        right.astype(jnp.bfloat16),
        (((0,), (0,)), ((), ())),
        preferred_element_type=jnp.float32,
    )


def strip(main, side, is_alpha, first_cycle, radial_count):
    lane, sub = iota(1), iota(0)
    lower4 = sub < 4
    column = sub & 3

    cells = lamination(main[0], main[1])
    rims = lamination(side[0], side[1])
    tiles = [cells.map(lambda part: part[:, :LANES]), cells.map(lambda part: part[:, LANES:])]
    cycle = (first_cycle + sub - 1).astype(jnp.float32)
    center = 1.0 + (cycle + 0.5) / radial_count
    face = 1.0 + cycle / radial_count
    per_center = 1.0 / center
    first_lane, last_lane = lane == 0, lane == LANES - 1

    ahead = [tile.lanes(1) for tile in tiles]
    west = [
        harmonic(pick(first_lane, rims.lanes(1), ahead[0]), tiles[0]) * per_center,
        harmonic(pick(first_lane, ahead[0], ahead[1]), tiles[1]) * per_center,
    ]
    wall = harmonic(tiles[1], rims.lanes(-1)) * per_center * 2.0
    back = [tile.lanes(-1) for tile in west]
    east = [pick(last_lane, back[1], back[0]), pick(last_lane, wall, back[1])]
    west[0] = pick(first_lane, west[0] * 2.0, west[0])
    south, north = [], []
    for tile in tiles:
        radial = harmonic(tile.subs(1), tile) * face
        radial = pick((sub == 1) | (sub == 5), radial * 2.0, radial)
        south.append(radial)
        north.append(radial.subs(-1))
    diagonal = [west[h] + east[h] + south[h] + north[h] for h in range(2)]
    gain_in = [south[h].row(1) for h in range(2)]
    gain_out = [north[h].row(4) for h in range(2)]

    diag_e, diag_o = evens(diagonal)
    east_e, east_o = evens(east)
    up_e, up_o = evens(north)
    left_e = pick(last_lane, east_o, 0.0)
    left_e = (east_o - left_e).lanes(1)

    def entry_e(r, c):
        if r == c:
            return diag_e.row(r + 1)
        return -up_e.row(r)

    lower_e, pivots_e = {}, []
    work = diag_e.row(1)
    for r in range(4):
        pivots_e.append(work.inverse())
        if r < 3:
            coupling = up_e.row(r + 1)
            lower_e[r + 1, r] = -(coupling * pivots_e[r])
            work = diag_e.row(r + 2) + lower_e[r + 1, r] * coupling
    zero = jnp.zeros((8, LANES), jnp.float32)
    nothing = Cx(zero, zero)
    half = []
    for r in range(4):
        value = Cx(jnp.where(column == r, 1.0, zero), zero)
        if r:
            value = value - lower_e[r, r - 1] * half[r - 1]
        half.append(value)
    inverse_e = [None] * 4
    for r in range(3, -1, -1):
        value = half[r] * pivots_e[r]
        if r < 3:
            value = value - lower_e[r + 1, r] * inverse_e[r + 1]
        inverse_e[r] = value
    for r in range(4):
        for c in range(r - 1):
            lower_e[r, c] = nothing
    seeds_e = seeds(lower_e, pivots_e)
    sides_e = pick(lower4, left_e.subs(-1), east_e.subs(3))
    reach_e = [inverse_e[r] * sides_e for r in range(4)]
    matrix, pair = [], []
    for r in range(4):
        to_left = (left_e.row(r + 1) * reach_e[r]).lanes(-1)
        to_right = east_e.row(r + 1) * reach_e[r]
        pair.append(pick(lower4, to_right, to_left))
        change = pick(lower4, to_left, to_right)
        base = pick(column == r, diag_o.row(r + 1), 0.0)
        if r < 3:
            base = pick(column == r + 1, -up_o.row(r + 1), base)
        if r > 0:
            base = pick(column == r - 1, -up_o.row(r), base)
        matrix.append(base - change - change.subs(4))

    for level in range(1, 8):
        step = 1 << (level - 1)
        stay = ((lane + 1) & (2 * step - 1)) == 0
        reach = solve(*factor(lambda r, c: matrix[r].row(c)), pair)
        next_matrix, next_pair = [], []
        for r in range(4):
            to_left = total(pair[k].row(r) * reach[k] for k in range(4)).lanes(-step)
            to_right = total(pair[k].row(4 + r) * reach[k] for k in range(4)).lanes(step)
            change = pick(lower4, to_left, to_right)
            change = change + change.subs(4)
            next_matrix.append(pick(stay, matrix[r] - change, matrix[r]))
            next_pair.append(pick(stay, pick(lower4, to_right, to_left), pair[r]))
        matrix, pair = next_matrix, next_pair

    lower, pivots = factor(lambda r, c: matrix[r].row(c))
    reach = solve(lower, pivots, pair)
    reach_rows = [[reach[r].row(k) for k in range(8)] for r in range(4)]
    seed = seeds(lower, pivots)

    def level_of(group):
        return jnp.where(lower4, 2 * group - 1, 2 * group)

    own_level = jnp.ones((8, LANES), jnp.int32)
    for level in range(2, 9):
        own_level = own_level + (((lane + 1) & ((1 << (level - 1)) - 1)) == 0).astype(jnp.int32)

    odd = {}
    for group in range(1, GROUPS + 1):
        rows = [pick(own_level == level_of(group), seed[r], 0.0) for r in range(4)]
        for level in range(min(2 * group - 1, 7), 0, -1):
            step = 1 << (level - 1)
            here = own_level == level
            before = [row.lanes(step) for row in rows]
            after = [row.lanes(-step) for row in rows]
            fresh = []
            for r in range(4):
                terms = [reach_rows[r][k] * before[k] for k in range(4)]
                terms += [reach_rows[r][4 + k] * after[k] for k in range(4)]
                fresh.append(rows[r] + pick(here, total(terms), 0.0))
            rows = fresh
        odd[group] = rows

    reach_e_rows = [[reach_e[r].row(k) for k in range(8)] for r in range(4)]
    even = {0: [pick(first_lane & lower4, seeds_e[r], 0.0) for r in range(4)]}
    odd[0] = [nothing] * 4
    for group in range(1, GROUPS + 1):
        before = [row.lanes(1) for row in odd[group]]
        even[group] = []
        for r in range(4):
            terms = [reach_e_rows[r][k] * before[k] for k in range(4)]
            terms += [reach_e_rows[r][4 + k] * odd[group][k] for k in range(4)]
            even[group].append(total(terms))

    def corners(lefts, rights):
        return pick(
            lane == 0,
            lefts[0],
            pick(
                lane == 1,
                lefts[1].lanes(1),
                pick(lane == 2, rights[0].lanes(3), pick(lane == 3, rights[1].lanes(4), 0.0)),
            ),
        )

    gains_left = [west[0].row(r + 1) for r in range(4)]
    gains_right = [east[1].row(r + 1) for r in range(4)]
    gain_corner = [
        corners(gains_left[2 * t : 2 * t + 2], gains_right[2 * t : 2 * t + 2]) for t in range(2)
    ]
    inner, outer, corner = {}, {}, {}
    for group in range(GROUPS + 1):
        if group:
            low = natural(even[group][0], odd[group][0])
            high = natural(even[group][3], odd[group][3])
        else:
            low, high = [even[0][0], nothing], [even[0][3], nothing]
        inner[group] = [low[h] * gain_in[h] for h in range(2)]
        outer[group] = [high[h] * gain_out[h] for h in range(2)]
        corner[group] = [
            corners(even[group][2 * t : 2 * t + 2], odd[group][2 * t : 2 * t + 2]) * gain_corner[t]
            for t in range(2)
        ]

    left_parts, right_parts = [], []
    for group in range(GROUPS + 1):
        if group in (0, GROUPS):
            low, high = inner[group], outer[group]
        else:
            near = lane < (2 << level_of(group))
            low = [pick(near, inner[group][0], 0.0), nothing]
            high = [pick(near, outer[group][0], 0.0), nothing]
        side_a, side_b = corner[group]
        own = [pick(is_alpha, low[h], high[h]) for h in range(2)]
        own.append(pick(is_alpha, side_a, side_b))
        moved = [high[0].lanes(4), high[1].lanes(4)]
        every = [
            low[0],
            low[1],
            pick(lower_lanes(lane, 4), side_a, moved[0]),
            pick(lower_lanes(lane, 4), moved[0], moved[1]),
            pick(lower_lanes(lane, 4), moved[1], pick(lane < 8, side_b.lanes(4), 0.0)),
        ]
        left_parts.append([split(value) for value in own])
        right_parts.append([split(value) for value in every])

    def wide(parts, which, name, sign=1.0):
        rows = []
        for group in parts:
            pieces = [getattr(value[which], name) for value in group]
            rows.append(jnp.concatenate(pieces, axis=1) * sign)
        return rows

    fill = [jnp.zeros((8, 3 * LANES), jnp.float32)] * 2
    left = (
        wide(left_parts, 0, "re")
        + wide(left_parts, 0, "re")
        + wide(left_parts, 1, "re")
        + wide(left_parts, 0, "im")
        + wide(left_parts, 0, "im")
        + wide(left_parts, 1, "im")
        + fill
    )
    fill = [jnp.zeros((8, 5 * LANES), jnp.float32)] * 2
    right_re = (
        wide(right_parts, 0, "re")
        + wide(right_parts, 1, "re")
        + wide(right_parts, 0, "re")
        + wide(right_parts, 0, "im", -1.0)
        + wide(right_parts, 1, "im", -1.0)
        + wide(right_parts, 0, "im", -1.0)
        + fill
    )
    right_im = (
        wide(right_parts, 0, "im")
        + wide(right_parts, 1, "im")
        + wide(right_parts, 0, "im")
        + wide(right_parts, 0, "re")
        + wide(right_parts, 1, "re")
        + wide(right_parts, 0, "re")
        + fill
    )
    left = jnp.concatenate(left, axis=0)
    top = Cx(
        contract(left, jnp.concatenate(right_re, axis=0)),
        contract(left, jnp.concatenate(right_im, axis=0)),
    )

    masks = []
    for level in range(1, 7):
        for tile in range(max((1 << (6 - level)) // 2, 1)):
            masks.append((level, (lane >> (level + 1)) == 2 * tile + (sub >> 2)))

    def spread(value):
        out = []
        for level, mask in masks:
            out.append(jnp.where(mask, value[level], 0.0))
        return jnp.concatenate(out, axis=0)

    def both(values, half):
        levels = {}
        for group in range(1, GROUPS):
            value = values[group][half]
            if half == 0:
                value = pick(lane < (2 << level_of(group)), nothing, value)
            turned = value.subs(4)
            levels[2 * group - 1] = split(pick(lower4, value, turned))
            levels[2 * group] = split(pick(lower4, turned, value))
        return {
            (which, name): spread(
                {level: getattr(pair[which], name) for level, pair in levels.items()}
            )
            for which in range(2)
            for name in ("re", "im")
        }

    even_d = [inverse_e[0].row(0), inverse_e[0].row(3), inverse_e[3].row(3)]
    even_d = [natural(value, nothing) for value in even_d]
    local = []
    for half in range(2):
        low, high = both(inner, half), both(outer, half)
        own = {key: jnp.where(is_alpha, low[key], high[key]) for key in low}
        every = {key: jnp.concatenate([low[key], high[key]], axis=1) for key in low}
        hr, hi, lr, li = (0, "re"), (0, "im"), (1, "re"), (1, "im")
        left = jnp.concatenate([own[key] for key in (hr, hi, hr, hi, lr, li)], axis=0)
        right_re = jnp.concatenate(
            [every[hr], -every[hi], every[lr], -every[li], every[hr], -every[hi]], axis=0
        )
        right_im = jnp.concatenate([every[key] for key in (hi, hr, li, lr, hi, hr)], axis=0)
        product = Cx(contract(left, right_re), contract(left, right_im))
        g_in, g_out = gain_in[half], gain_out[half]
        solo = (lane & 1) == 0
        if half == 0:
            solo = solo & (lane > 0)
        cross = even_d[1][half] * g_in * g_out
        on_in = pick(is_alpha, even_d[0][half] * g_in * g_in, cross)
        on_out = pick(is_alpha, cross, even_d[2][half] * g_out * g_out)
        on_in = pick(solo, on_in, 0.0) - pick(is_alpha, g_in, nothing)
        on_out = pick(solo, on_out, 0.0) - pick(is_alpha, nothing, g_out)
        local.append((product, on_in, on_out))
    edge = pick((lane == sub) & lower4, pick(is_alpha, gain_corner[0], gain_corner[1]), 0.0)
    return top, local, edge


def lower_lanes(lane, count):
    return lane < count


def finish(top, local, edge, is_alpha, store):
    lane, sub = iota(1), iota(0)
    for part, name in enumerate(("re", "im")):
        full = getattr(top, name)
        edge_part = getattr(edge, name)
        for half in range(2):
            product = getattr(local[half][0], name)
            on_in = getattr(local[half][1], name)
            on_out = getattr(local[half][2], name)
            for row in range(0, LANES, 8):
                here = lane == sub + row
                low = product[row : row + 8, :LANES] + jnp.where(here, on_in, 0.0)
                high = product[row : row + 8, LANES:] + jnp.where(here, on_out, 0.0)
                high = lane_roll(high, 4)
                at = half * LANES + row
                out = [full[at : at + 8, t * LANES : (t + 1) * LANES] for t in range(5)]
                out[half] = out[half] + low
                out[2 + half] = out[2 + half] + jnp.where(lane < 4, 0.0, high)
                out[3 + half] = out[3 + half] + jnp.where(lane < 4, high, 0.0)
                store(part, at, 8, [-value for value in out])
        at = 2 * LANES
        out = [full[at : at + 8, t * LANES : (t + 1) * LANES] for t in range(5)]
        out[2] = out[2] - jnp.where(is_alpha, edge_part, 0.0)
        out[4] = out[4] - jnp.where(is_alpha, 0.0, lane_roll(edge_part, 4))
        store(part, at, 4, [-value for value in out])


def gather_rows(own, partner, is_alpha, is_even, is_first, is_last, main, side):
    lane = lax.broadcasted_iota(jnp.int32, (2, LANES), 1)
    for field in range(2):
        at = 2 * field
        mine, other = own[at : at + 2, :], partner[at : at + 2, :]
        alpha = jnp.where(is_alpha, mine, other)
        beta = jnp.where(is_alpha, other, mine)
        near, far = own[12 + at : 14 + at, :], partner[12 + at : 14 + at, :]
        main[field, 0:1, :] = jnp.where(is_first, alpha[0:1], jnp.where(is_alpha, near, far)[1:2])
        main[field, 1:3, :] = alpha
        main[field, 3:5, :] = beta
        main[field, 5:6, :] = jnp.where(is_last, beta[1:2], jnp.where(is_alpha, far, near)[0:1])
        main[field, 6:8, :] = beta
        ends = []
        for tiles in (own, partner):
            long, short = tiles[4 + at : 6 + at, :], tiles[8 + at : 10 + at, :]
            left = jnp.where(is_even, long, short)[:, LANES:]
            right = jnp.where(is_even, short, long)[:, :LANES]
            ends.append(jnp.where(lane == LANES - 1, left, jnp.where(lane == 0, right, 1.0)))
        ends_alpha = jnp.where(is_alpha, ends[0], ends[1])
        ends_beta = jnp.where(is_alpha, ends[1], ends[0])
        side[field, 0:1, :] = ends_alpha[0:1]
        side[field, 1:3, :] = ends_alpha
        side[field, 3:5, :] = ends_beta
        side[field, 5:7, :] = ends_beta
        side[field, 7:8, :] = ends_beta[0:1]


def merge_kernel(cycles, depth, own, partner, out, main, side):
    index = lax.axis_index("rad")
    is_even = lax.axis_index("az") % 2 == 0
    is_alpha = index % 2 == 0
    is_first = index // 2 == 0
    is_last = index // 2 == cycles // 2 - 1
    gather_rows(own, partner, is_alpha, is_even, is_first, is_last, main, side)
    top, local, edge = strip(
        (main[0], main[1]),
        (side[0], side[1]),
        is_alpha,
        (index // 2) * (2 * depth),
        cycles * depth,
    )

    def store(part, row, count, tiles):
        for number, tile in enumerate(tiles):
            width = min(LANES, out.shape[2] - number * LANES)
            out[part, row : row + count, number * LANES : number * LANES + width] = tile[
                :count, :width
            ]

    finish(top, local, edge, is_alpha, store)


def cell_kernel(*refs):
    sources, (out_ref,), targets, sems = refs[:5], refs[5:6], refs[6:11], refs[11]
    copies = [
        pltpu.make_async_copy(source, target, sems.at[number])
        for number, (source, target) in enumerate(zip(sources, targets))
    ]
    for copy in copies:
        copy.start()
    for copy in copies:
        copy.wait()
    material_ref, sheet_ref, sigma_ref, nu_ref, angular_ref = targets
    material, sheet = material_ref[...], sheet_ref[...]
    sigma, base = jnp.zeros_like(sheet), jnp.zeros_like(sheet)
    for level in range(sigma_ref.shape[0]):
        sigma = jnp.where(material == level, sigma_ref[level], sigma)
        base = jnp.where(material == level, nu_ref[level], base)
    out_ref[:2, :] = angular_ref[0] * sigma * sheet * sheet
    out_ref[2:, :] = base


def cell_inputs(*arguments):
    spaces = (pltpu.VMEM, pltpu.VMEM, pltpu.SMEM, pltpu.SMEM, pltpu.SMEM)
    return pl.pallas_call(
        cell_kernel,
        out_shape=jax.ShapeDtypeStruct((4, arguments[1].shape[1]), jnp.float32),
        in_specs=[pl.BlockSpec(memory_space=pltpu.HBM)] * 5,
        out_specs=pl.BlockSpec(memory_space=pltpu.VMEM),
        scratch_shapes=[
            space(value.shape, value.dtype) for space, value in zip(spaces, arguments)
        ]
        + [pltpu.SemaphoreType.DMA((5,))],
        compiler_params=pltpu.CompilerParams(vmem_limit_bytes=63 * 1024 * 1024),
        name="cells",
    )(*arguments)


def swapped(cells, axis, first):
    count = lax.axis_size(axis)
    route = []
    for low in range(first, count, 2):
        high = (low + 1) % count
        if high or axis == "az":
            route += [(low, high), (high, low)]
    return lax.ppermute(cells, axis, route)


def per_device(material_id, thickness, sigma_table, nu_table, angular_frequency):
    depth, arc = thickness.shape
    cells = cell_inputs(material_id, thickness, sigma_table, nu_table, angular_frequency)
    cycles = lax.axis_size("rad")
    near = swapped(cells, "rad", 1)
    short = swapped(cells, "az", 0)
    long = swapped(cells, "az", 1)
    known = jnp.concatenate([cells, long, short, near], axis=0)
    outer_nodes = arc + 2 * depth
    return pl.pallas_call(
        lambda *refs: merge_kernel(cycles, depth, *refs),
        out_shape=jax.ShapeDtypeStruct((2, outer_nodes, 2 * outer_nodes), jnp.float32),
        in_specs=[pl.BlockSpec(memory_space=pltpu.VMEM)] * 2,
        out_specs=pl.BlockSpec(memory_space=pltpu.VMEM),
        scratch_shapes=[
            pltpu.VMEM((2, 8, arc), jnp.float32),
            pltpu.VMEM((2, 8, LANES), jnp.float32),
        ],
        compiler_params=pltpu.CompilerParams(vmem_limit_bytes=48 * 1024 * 1024),
        name="pair_map",
    )(known, swapped(known, "rad", 0))


def solution(mesh):
    placed = (P("rad", "az"), P("rad", "az"), P(), P(), P())
    return jax.shard_map(
        per_device, mesh=mesh, in_specs=placed, out_specs=P(None, "rad", "az"), check_vma=False
    )
```

```python
import jax
import jax.numpy as jnp
from jax import lax
from jax.experimental import pallas as pl
from jax.experimental.pallas import tpu as pltpu
from jax.sharding import PartitionSpec as P

SHEET_NODES = 16
LANES = 128
GROUPS = 4


def lane_roll(value, shift):
    return pltpu.roll(value, shift % value.shape[1], 1)


def sub_roll(value, shift):
    return pltpu.roll(value, shift % value.shape[0], 0)


def lane_take(value, index):
    return jnp.take_along_axis(value, index, axis=1, mode="promise_in_bounds")


def iota(dim):
    return lax.broadcasted_iota(jnp.int32, (8, LANES), dim)


class Cx:
    def __init__(self, re, im):
        self.re, self.im = re, im

    def __add__(self, other):
        return Cx(self.re + other.re, self.im + other.im)

    def __sub__(self, other):
        return Cx(self.re - other.re, self.im - other.im)

    def __neg__(self):
        return Cx(-self.re, -self.im)

    def __mul__(self, other):
        if not isinstance(other, Cx):
            return Cx(self.re * other, self.im * other)
        return Cx(
            self.re * other.re - self.im * other.im, self.re * other.im + self.im * other.re
        )

    def inverse(self):
        scale = 1.0 / (self.re * self.re + self.im * self.im)
        return Cx(self.re * scale, -self.im * scale)

    def root(self):
        size = jnp.sqrt(self.re * self.re + self.im * self.im)
        re = jnp.sqrt(0.5 * (size + self.re))
        return Cx(re, 0.5 * self.im / re)

    def map(self, function):
        return Cx(function(self.re), function(self.im))

    def row(self, index):
        return self.map(lambda part: jnp.broadcast_to(part[index : index + 1], (8, LANES)))

    def lanes(self, shift):
        return self.map(lambda part: lane_roll(part, shift))

    def subs(self, shift):
        return self.map(lambda part: sub_roll(part, shift))


def pick(mask, first, second):
    if not isinstance(second, Cx):
        return first.map(lambda part: jnp.where(mask, part, second))
    return Cx(jnp.where(mask, first.re, second.re), jnp.where(mask, first.im, second.im))


def total(terms):
    terms = list(terms)
    while len(terms) > 1:
        terms = [
            terms[i] + terms[i + 1] if i + 1 < len(terms) else terms[i]
            for i in range(0, len(terms), 2)
        ]
    return terms[0]


def harmonic(left, right):
    return (left * right) * (left + right).inverse() * 2.0


def lamination(skin, base):
    above = Cx(jnp.ones_like(skin), jnp.zeros_like(skin))
    field = Cx(jnp.ones_like(skin), 0.5 * skin)
    summed = above
    for _ in range(SHEET_NODES - 1):
        summed = summed + field
        below = Cx(
            2.0 * field.re - skin * field.im - above.re,
            2.0 * field.im + skin * field.re - above.im,
        )
        above, field = field, below
    return field * summed.inverse() * (base * SHEET_NODES)


def factor(entry):
    work = {(r, c): entry(r, c) for r in range(4) for c in range(r + 1)}
    lower, pivots = {}, []
    for k in range(4):
        inverse = work[k, k].inverse()
        pivots.append(inverse)
        for r in range(k + 1, 4):
            lower[r, k] = work[r, k] * inverse
        for r in range(k + 1, 4):
            for c in range(k + 1, r + 1):
                work[r, c] = work[r, c] - lower[r, k] * work[c, k]
    return lower, pivots


def solve(lower, pivots, right):
    half = []
    for r in range(4):
        value = right[r]
        for c in range(r):
            value = value - lower[r, c] * half[c]
        half.append(value)
    out = [None] * 4
    for r in range(3, -1, -1):
        value = half[r] * pivots[r]
        for c in range(r + 1, 4):
            value = value - lower[c, r] * out[c]
        out[r] = value
    return out


def seeds(lower, pivots):
    column = iota(0) & 3
    unit = {}
    for r in range(4):
        for c in range(r - 1, -1, -1):
            value = -lower[r, c]
            for k in range(c + 1, r):
                value = value - lower[r, k] * unit[k, c]
            unit[r, c] = value
    roots = [pivot.root() for pivot in pivots]
    out = []
    for r in range(4):
        value = pick(column == r, roots[r], 0.0)
        for k in range(r + 1, 4):
            value = pick(column == k, roots[k] * unit[k, r], value)
        out.append(value)
    return out


def evens(tiles):
    lane = iota(1)
    index = (2 * lane) & (LANES - 1)

    def one(offset):
        return Cx(
            *(
                jnp.where(
                    lane < LANES // 2,
                    lane_take(first, index + offset),
                    lane_take(second, index + offset),
                )
                for first, second in ((tiles[0].re, tiles[1].re), (tiles[0].im, tiles[1].im))
            )
        )

    return one(0), one(1)


def natural(even, odd):
    lane = iota(1)
    out = []
    for half in range(2):
        index = half * (LANES // 2) + (lane >> 1)
        out.append(
            Cx(
                *(
                    jnp.where((lane & 1) == 0, lane_take(first, index), lane_take(second, index))
                    for first, second in ((even.re, odd.re), (even.im, odd.im))
                )
            )
        )
    return out


def split(value):
    high = value.map(lambda part: part.astype(jnp.bfloat16).astype(jnp.float32))
    return high, value - high


def contract(left, right):
    return lax.dot_general(
        left.astype(jnp.bfloat16),
        right.astype(jnp.bfloat16),
        (((0,), (0,)), ((), ())),
        preferred_element_type=jnp.float32,
    )


def strip(main, side, is_alpha, first_cycle, radial_count):
    lane, sub = iota(1), iota(0)
    lower4 = sub < 4
    column = sub & 3

    cells = lamination(main[0], main[1])
    rims = lamination(side[0], side[1])
    tiles = [cells.map(lambda part: part[:, :LANES]), cells.map(lambda part: part[:, LANES:])]
    cycle = (first_cycle + sub - 1).astype(jnp.float32)
    center = 1.0 + (cycle + 0.5) / radial_count
    face = 1.0 + cycle / radial_count
    per_center = 1.0 / center
    first_lane, last_lane = lane == 0, lane == LANES - 1

    ahead = [tile.lanes(1) for tile in tiles]
    west = [
        harmonic(pick(first_lane, rims.lanes(1), ahead[0]), tiles[0]) * per_center,
        harmonic(pick(first_lane, ahead[0], ahead[1]), tiles[1]) * per_center,
    ]
    wall = harmonic(tiles[1], rims.lanes(-1)) * per_center * 2.0
    back = [tile.lanes(-1) for tile in west]
    east = [pick(last_lane, back[1], back[0]), pick(last_lane, wall, back[1])]
    west[0] = pick(first_lane, west[0] * 2.0, west[0])
    south, north = [], []
    for tile in tiles:
        radial = harmonic(tile.subs(1), tile) * face
        radial = pick((sub == 1) | (sub == 5), radial * 2.0, radial)
        south.append(radial)
        north.append(radial.subs(-1))
    diagonal = [west[h] + east[h] + south[h] + north[h] for h in range(2)]
    gain_in = [south[h].row(1) for h in range(2)]
    gain_out = [north[h].row(4) for h in range(2)]

    diag_e, diag_o = evens(diagonal)
    east_e, east_o = evens(east)
    up_e, up_o = evens(north)
    left_e = pick(last_lane, east_o, 0.0)
    left_e = (east_o - left_e).lanes(1)

    def entry_e(r, c):
        if r == c:
            return diag_e.row(r + 1)
        return -up_e.row(r)

    lower_e, pivots_e = {}, []
    work = diag_e.row(1)
    for r in range(4):
        pivots_e.append(work.inverse())
        if r < 3:
            coupling = up_e.row(r + 1)
            lower_e[r + 1, r] = -(coupling * pivots_e[r])
            work = diag_e.row(r + 2) + lower_e[r + 1, r] * coupling
    zero = jnp.zeros((8, LANES), jnp.float32)
    nothing = Cx(zero, zero)
    half = []
    for r in range(4):
        value = Cx(jnp.where(column == r, 1.0, zero), zero)
        if r:
            value = value - lower_e[r, r - 1] * half[r - 1]
        half.append(value)
    inverse_e = [None] * 4
    for r in range(3, -1, -1):
        value = half[r] * pivots_e[r]
        if r < 3:
            value = value - lower_e[r + 1, r] * inverse_e[r + 1]
        inverse_e[r] = value
    for r in range(4):
        for c in range(r - 1):
            lower_e[r, c] = nothing
    seeds_e = seeds(lower_e, pivots_e)
    sides_e = pick(lower4, left_e.subs(-1), east_e.subs(3))
    reach_e = [inverse_e[r] * sides_e for r in range(4)]
    matrix, pair = [], []
    for r in range(4):
        to_left = (left_e.row(r + 1) * reach_e[r]).lanes(-1)
        to_right = east_e.row(r + 1) * reach_e[r]
        pair.append(pick(lower4, to_right, to_left))
        change = pick(lower4, to_left, to_right)
        base = pick(column == r, diag_o.row(r + 1), 0.0)
        if r < 3:
            base = pick(column == r + 1, -up_o.row(r + 1), base)
        if r > 0:
            base = pick(column == r - 1, -up_o.row(r), base)
        matrix.append(base - change - change.subs(4))

    for level in range(1, 8):
        step = 1 << (level - 1)
        stay = ((lane + 1) & (2 * step - 1)) == 0
        reach = solve(*factor(lambda r, c: matrix[r].row(c)), pair)
        next_matrix, next_pair = [], []
        for r in range(4):
            to_left = total(pair[k].row(r) * reach[k] for k in range(4)).lanes(-step)
            to_right = total(pair[k].row(4 + r) * reach[k] for k in range(4)).lanes(step)
            change = pick(lower4, to_left, to_right)
            change = change + change.subs(4)
            next_matrix.append(pick(stay, matrix[r] - change, matrix[r]))
            next_pair.append(pick(stay, pick(lower4, to_right, to_left), pair[r]))
        matrix, pair = next_matrix, next_pair

    lower, pivots = factor(lambda r, c: matrix[r].row(c))
    reach = solve(lower, pivots, pair)
    reach_rows = [[reach[r].row(k) for k in range(8)] for r in range(4)]
    seed = seeds(lower, pivots)

    def level_of(group):
        return jnp.where(lower4, 2 * group - 1, 2 * group)

    own_level = jnp.ones((8, LANES), jnp.int32)
    for level in range(2, 9):
        own_level = own_level + (((lane + 1) & ((1 << (level - 1)) - 1)) == 0).astype(jnp.int32)

    odd = {}
    for group in range(1, GROUPS + 1):
        rows = [pick(own_level == level_of(group), seed[r], 0.0) for r in range(4)]
        for level in range(min(2 * group - 1, 7), 0, -1):
            step = 1 << (level - 1)
            here = own_level == level
            before = [row.lanes(step) for row in rows]
            after = [row.lanes(-step) for row in rows]
            fresh = []
            for r in range(4):
                terms = [reach_rows[r][k] * before[k] for k in range(4)]
                terms += [reach_rows[r][4 + k] * after[k] for k in range(4)]
                fresh.append(rows[r] + pick(here, total(terms), 0.0))
            rows = fresh
        odd[group] = rows

    reach_e_rows = [[reach_e[r].row(k) for k in range(8)] for r in range(4)]
    even = {0: [pick(first_lane & lower4, seeds_e[r], 0.0) for r in range(4)]}
    odd[0] = [nothing] * 4
    for group in range(1, GROUPS + 1):
        before = [row.lanes(1) for row in odd[group]]
        even[group] = []
        for r in range(4):
            terms = [reach_e_rows[r][k] * before[k] for k in range(4)]
            terms += [reach_e_rows[r][4 + k] * odd[group][k] for k in range(4)]
            even[group].append(total(terms))

    def corners(lefts, rights):
        return pick(
            lane == 0,
            lefts[0],
            pick(
                lane == 1,
                lefts[1].lanes(1),
                pick(lane == 2, rights[0].lanes(3), pick(lane == 3, rights[1].lanes(4), 0.0)),
            ),
        )

    gains_left = [west[0].row(r + 1) for r in range(4)]
    gains_right = [east[1].row(r + 1) for r in range(4)]
    gain_corner = [
        corners(gains_left[2 * t : 2 * t + 2], gains_right[2 * t : 2 * t + 2]) for t in range(2)
    ]
    inner, outer, corner = {}, {}, {}
    for group in range(GROUPS + 1):
        if group:
            low = natural(even[group][0], odd[group][0])
            high = natural(even[group][3], odd[group][3])
        else:
            low, high = [even[0][0], nothing], [even[0][3], nothing]
        inner[group] = [low[h] * gain_in[h] for h in range(2)]
        outer[group] = [high[h] * gain_out[h] for h in range(2)]
        corner[group] = [
            corners(even[group][2 * t : 2 * t + 2], odd[group][2 * t : 2 * t + 2]) * gain_corner[t]
            for t in range(2)
        ]

    left_parts, right_parts = [], []
    for group in range(GROUPS + 1):
        if group in (0, GROUPS):
            low, high = inner[group], outer[group]
        else:
            near = lane < (2 << level_of(group))
            low = [pick(near, inner[group][0], 0.0), nothing]
            high = [pick(near, outer[group][0], 0.0), nothing]
        side_a, side_b = corner[group]
        own = [pick(is_alpha, low[h], high[h]) for h in range(2)]
        own.append(pick(is_alpha, side_a, side_b))
        moved = [high[0].lanes(4), high[1].lanes(4)]
        every = [
            low[0],
            low[1],
            pick(lower_lanes(lane, 4), side_a, moved[0]),
            pick(lower_lanes(lane, 4), moved[0], moved[1]),
            pick(lower_lanes(lane, 4), moved[1], pick(lane < 8, side_b.lanes(4), 0.0)),
        ]
        left_parts.append([split(value) for value in own])
        right_parts.append([split(value) for value in every])

    def wide(parts, which, name, sign=1.0):
        rows = []
        for group in parts:
            pieces = [getattr(value[which], name) for value in group]
            rows.append(jnp.concatenate(pieces, axis=1) * sign)
        return rows

    fill = [jnp.zeros((8, 3 * LANES), jnp.float32)] * 2
    left = (
        wide(left_parts, 0, "re")
        + wide(left_parts, 0, "re")
        + wide(left_parts, 1, "re")
        + wide(left_parts, 0, "im")
        + wide(left_parts, 0, "im")
        + wide(left_parts, 1, "im")
        + fill
    )
    fill = [jnp.zeros((8, 5 * LANES), jnp.float32)] * 2
    right_re = (
        wide(right_parts, 0, "re")
        + wide(right_parts, 1, "re")
        + wide(right_parts, 0, "re")
        + wide(right_parts, 0, "im", -1.0)
        + wide(right_parts, 1, "im", -1.0)
        + wide(right_parts, 0, "im", -1.0)
        + fill
    )
    right_im = (
        wide(right_parts, 0, "im")
        + wide(right_parts, 1, "im")
        + wide(right_parts, 0, "im")
        + wide(right_parts, 0, "re")
        + wide(right_parts, 1, "re")
        + wide(right_parts, 0, "re")
        + fill
    )
    left = jnp.concatenate(left, axis=0)
    top = Cx(
        contract(left, jnp.concatenate(right_re, axis=0)),
        contract(left, jnp.concatenate(right_im, axis=0)),
    )

    masks = []
    for level in range(1, 7):
        for tile in range(max((1 << (6 - level)) // 2, 1)):
            masks.append((level, (lane >> (level + 1)) == 2 * tile + (sub >> 2)))

    def spread(value):
        out = []
        for level, mask in masks:
            out.append(jnp.where(mask, value[level], 0.0))
        return jnp.concatenate(out, axis=0)

    def both(values, half):
        levels = {}
        for group in range(1, GROUPS):
            value = values[group][half]
            if half == 0:
                value = pick(lane < (2 << level_of(group)), nothing, value)
            turned = value.subs(4)
            levels[2 * group - 1] = split(pick(lower4, value, turned))
            levels[2 * group] = split(pick(lower4, turned, value))
        return {
            (which, name): spread(
                {level: getattr(pair[which], name) for level, pair in levels.items()}
            )
            for which in range(2)
            for name in ("re", "im")
        }

    even_d = [inverse_e[0].row(0), inverse_e[0].row(3), inverse_e[3].row(3)]
    even_d = [natural(value, nothing) for value in even_d]
    local = []
    for half in range(2):
        low, high = both(inner, half), both(outer, half)
        own = {key: jnp.where(is_alpha, low[key], high[key]) for key in low}
        every = {key: jnp.concatenate([low[key], high[key]], axis=1) for key in low}
        hr, hi, lr, li = (0, "re"), (0, "im"), (1, "re"), (1, "im")
        left = jnp.concatenate([own[key] for key in (hr, hi, hr, hi, lr, li)], axis=0)
        right_re = jnp.concatenate(
            [every[hr], -every[hi], every[lr], -every[li], every[hr], -every[hi]], axis=0
        )
        right_im = jnp.concatenate([every[key] for key in (hi, hr, li, lr, hi, hr)], axis=0)
        product = Cx(contract(left, right_re), contract(left, right_im))
        g_in, g_out = gain_in[half], gain_out[half]
        solo = (lane & 1) == 0
        if half == 0:
            solo = solo & (lane > 0)
        cross = even_d[1][half] * g_in * g_out
        on_in = pick(is_alpha, even_d[0][half] * g_in * g_in, cross)
        on_out = pick(is_alpha, cross, even_d[2][half] * g_out * g_out)
        on_in = pick(solo, on_in, 0.0) - pick(is_alpha, g_in, nothing)
        on_out = pick(solo, on_out, 0.0) - pick(is_alpha, nothing, g_out)
        local.append((product, on_in, on_out))
    edge = pick((lane == sub) & lower4, pick(is_alpha, gain_corner[0], gain_corner[1]), 0.0)
    return top, local, edge


def lower_lanes(lane, count):
    return lane < count


def finish(top, local, edge, is_alpha, store):
    lane, sub = iota(1), iota(0)
    for part, name in enumerate(("re", "im")):
        full = getattr(top, name)
        edge_part = getattr(edge, name)
        for half in range(2):
            product = getattr(local[half][0], name)
            on_in = getattr(local[half][1], name)
            on_out = getattr(local[half][2], name)
            for row in range(0, LANES, 8):
                here = lane == sub + row
                low = product[row : row + 8, :LANES] + jnp.where(here, on_in, 0.0)
                high = product[row : row + 8, LANES:] + jnp.where(here, on_out, 0.0)
                high = lane_roll(high, 4)
                at = half * LANES + row
                out = [full[at : at + 8, t * LANES : (t + 1) * LANES] for t in range(5)]
                out[half] = out[half] + low
                out[2 + half] = out[2 + half] + jnp.where(lane < 4, 0.0, high)
                out[3 + half] = out[3 + half] + jnp.where(lane < 4, high, 0.0)
                store(part, at, 8, [-value for value in out])
        at = 2 * LANES
        out = [full[at : at + 8, t * LANES : (t + 1) * LANES] for t in range(5)]
        out[2] = out[2] - jnp.where(is_alpha, edge_part, 0.0)
        out[4] = out[4] - jnp.where(is_alpha, 0.0, lane_roll(edge_part, 4))
        store(part, at, 4, [-value for value in out])


def gather_rows(known, block, pair, is_first, is_last, main, side):
    blocks, cycles = known.shape[:2]
    lane = lax.broadcasted_iota(jnp.int32, (2, LANES), 1)
    low, high = 2 * pair, 2 * pair + 1
    under, over = jnp.maximum(low - 1, 0), jnp.minimum(high + 1, cycles - 1)
    before, after = (block + blocks - 1) % blocks, (block + 1) % blocks
    for field in range(2):
        rows = slice(2 * field, 2 * field + 2)
        alpha, beta = known[block, low, rows, :], known[block, high, rows, :]
        below, above = known[block, under, rows, :], known[block, over, rows, :]
        main[field, 0:1, :] = jnp.where(is_first, alpha[0:1], below[1:2])
        main[field, 1:3, :] = alpha
        main[field, 3:5, :] = beta
        main[field, 5:6, :] = jnp.where(is_last, beta[1:2], above[0:1])
        main[field, 6:8, :] = beta
        ends = []
        for cycle in (low, high):
            left = known[before, cycle, rows, LANES:]
            right = known[after, cycle, rows, :LANES]
            ends.append(jnp.where(lane == LANES - 1, left, jnp.where(lane == 0, right, 1.0)))
        side[field, 0:1, :] = ends[0][0:1]
        side[field, 1:3, :] = ends[0]
        side[field, 3:5, :] = ends[1]
        side[field, 5:7, :] = ends[1]
        side[field, 7:8, :] = ends[1][0:1]


def merge_kernel(cycles, depth, known, out, main, side):
    index = lax.axis_index("rad")
    is_alpha = index % 2 == 0
    is_first = index // 2 == 0
    is_last = index // 2 == cycles // 2 - 1
    gather_rows(known, lax.axis_index("az"), index // 2, is_first, is_last, main, side)
    top, local, edge = strip(
        (main[0], main[1]),
        (side[0], side[1]),
        is_alpha,
        (index // 2) * (2 * depth),
        cycles * depth,
    )

    def store(part, row, count, tiles):
        for number, tile in enumerate(tiles):
            width = min(LANES, out.shape[2] - number * LANES)
            out[part, row : row + count, number * LANES : number * LANES + width] = tile[
                :count, :width
            ]

    finish(top, local, edge, is_alpha, store)


def cell_kernel(*refs):
    sources, (out_ref,), targets, sems = refs[:5], refs[5:6], refs[6:11], refs[11]
    copies = [
        pltpu.make_async_copy(source, target, sems.at[number])
        for number, (source, target) in enumerate(zip(sources, targets))
    ]
    for copy in copies:
        copy.start()
    for copy in copies:
        copy.wait()
    material_ref, sheet_ref, sigma_ref, nu_ref, angular_ref = targets
    material, sheet = material_ref[...], sheet_ref[...]
    sigma, base = jnp.zeros_like(sheet), jnp.zeros_like(sheet)
    for level in range(sigma_ref.shape[0]):
        sigma = jnp.where(material == level, sigma_ref[level], sigma)
        base = jnp.where(material == level, nu_ref[level], base)
    out_ref[:2, :] = angular_ref[0] * sigma * sheet * sheet
    out_ref[2:, :] = base


def cell_inputs(*arguments):
    spaces = (pltpu.VMEM, pltpu.VMEM, pltpu.SMEM, pltpu.SMEM, pltpu.SMEM)
    return pl.pallas_call(
        cell_kernel,
        out_shape=jax.ShapeDtypeStruct((4, arguments[1].shape[1]), jnp.float32),
        in_specs=[pl.BlockSpec(memory_space=pltpu.HBM)] * 5,
        out_specs=pl.BlockSpec(memory_space=pltpu.VMEM),
        scratch_shapes=[
            space(value.shape, value.dtype) for space, value in zip(spaces, arguments)
        ]
        + [pltpu.SemaphoreType.DMA((5,))],
        compiler_params=pltpu.CompilerParams(vmem_limit_bytes=63 * 1024 * 1024),
        name="cells",
    )(*arguments)


def per_device(material_id, thickness, sigma_table, nu_table, angular_frequency):
    depth, arc = thickness.shape
    cells = cell_inputs(material_id, thickness, sigma_table, nu_table, angular_frequency)
    cycles = lax.axis_size("rad")
    known = lax.all_gather(cells, ("az", "rad"))
    known = known.reshape((lax.axis_size("az"), cycles) + cells.shape)
    outer_nodes = arc + 2 * depth
    return pl.pallas_call(
        lambda *refs: merge_kernel(cycles, depth, *refs),
        out_shape=jax.ShapeDtypeStruct((2, outer_nodes, 2 * outer_nodes), jnp.float32),
        in_specs=[pl.BlockSpec(memory_space=pltpu.VMEM)],
        out_specs=pl.BlockSpec(memory_space=pltpu.VMEM),
        scratch_shapes=[
            pltpu.VMEM((2, 8, arc), jnp.float32),
            pltpu.VMEM((2, 8, LANES), jnp.float32),
        ],
        compiler_params=pltpu.CompilerParams(vmem_limit_bytes=48 * 1024 * 1024),
        name="pair_map",
    )(known)


def solution(mesh):
    placed = (P("rad", "az"), P("rad", "az"), P(), P(), P())
    return jax.shard_map(
        per_device, mesh=mesh, in_specs=placed, out_specs=P(None, "rad", "az"), check_vma=False
    )
```

```python
import jax
import jax.numpy as jnp
from jax import lax
from jax.experimental import pallas as pl
from jax.experimental.pallas import tpu as pltpu
from jax.sharding import PartitionSpec as P

SHEET_NODES = 16
LANES = 128
GROUPS = 4


def lane_roll(value, shift):
    return pltpu.roll(value, shift % value.shape[1], 1)


def sub_roll(value, shift):
    return pltpu.roll(value, shift % value.shape[0], 0)


def lane_take(value, index):
    return jnp.take_along_axis(value, index, axis=1, mode="promise_in_bounds")


def iota(dim):
    return lax.broadcasted_iota(jnp.int32, (8, LANES), dim)


class Cx:
    def __init__(self, re, im):
        self.re, self.im = re, im

    def __add__(self, other):
        return Cx(self.re + other.re, self.im + other.im)

    def __sub__(self, other):
        return Cx(self.re - other.re, self.im - other.im)

    def __neg__(self):
        return Cx(-self.re, -self.im)

    def __mul__(self, other):
        if not isinstance(other, Cx):
            return Cx(self.re * other, self.im * other)
        return Cx(
            self.re * other.re - self.im * other.im, self.re * other.im + self.im * other.re
        )

    def inverse(self):
        scale = 1.0 / (self.re * self.re + self.im * self.im)
        return Cx(self.re * scale, -self.im * scale)

    def root(self):
        size = jnp.sqrt(self.re * self.re + self.im * self.im)
        re = jnp.sqrt(0.5 * (size + self.re))
        return Cx(re, 0.5 * self.im / re)

    def map(self, function):
        return Cx(function(self.re), function(self.im))

    def row(self, index):
        return self.map(lambda part: jnp.broadcast_to(part[index : index + 1], (8, LANES)))

    def lanes(self, shift):
        return self.map(lambda part: lane_roll(part, shift))

    def subs(self, shift):
        return self.map(lambda part: sub_roll(part, shift))


def pick(mask, first, second):
    if not isinstance(second, Cx):
        return first.map(lambda part: jnp.where(mask, part, second))
    return Cx(jnp.where(mask, first.re, second.re), jnp.where(mask, first.im, second.im))


def total(terms):
    terms = list(terms)
    while len(terms) > 1:
        terms = [
            terms[i] + terms[i + 1] if i + 1 < len(terms) else terms[i]
            for i in range(0, len(terms), 2)
        ]
    return terms[0]


def harmonic(left, right):
    return (left * right) * (left + right).inverse() * 2.0


def lamination(skin, base):
    above = Cx(jnp.ones_like(skin), jnp.zeros_like(skin))
    field = Cx(jnp.ones_like(skin), 0.5 * skin)
    summed = above
    for _ in range(SHEET_NODES - 1):
        summed = summed + field
        below = Cx(
            2.0 * field.re - skin * field.im - above.re,
            2.0 * field.im + skin * field.re - above.im,
        )
        above, field = field, below
    return field * summed.inverse() * (base * SHEET_NODES)


def factor(entry):
    work = {(r, c): entry(r, c) for r in range(4) for c in range(r + 1)}
    lower, pivots = {}, []
    for k in range(4):
        inverse = work[k, k].inverse()
        pivots.append(inverse)
        for r in range(k + 1, 4):
            lower[r, k] = work[r, k] * inverse
        for r in range(k + 1, 4):
            for c in range(k + 1, r + 1):
                work[r, c] = work[r, c] - lower[r, k] * work[c, k]
    return lower, pivots


def solve(lower, pivots, right):
    half = []
    for r in range(4):
        value = right[r]
        for c in range(r):
            value = value - lower[r, c] * half[c]
        half.append(value)
    out = [None] * 4
    for r in range(3, -1, -1):
        value = half[r] * pivots[r]
        for c in range(r + 1, 4):
            value = value - lower[c, r] * out[c]
        out[r] = value
    return out


def seeds(lower, pivots):
    column = iota(0) & 3
    unit = {}
    for r in range(4):
        for c in range(r - 1, -1, -1):
            value = -lower[r, c]
            for k in range(c + 1, r):
                value = value - lower[r, k] * unit[k, c]
            unit[r, c] = value
    roots = [pivot.root() for pivot in pivots]
    out = []
    for r in range(4):
        value = pick(column == r, roots[r], 0.0)
        for k in range(r + 1, 4):
            value = pick(column == k, roots[k] * unit[k, r], value)
        out.append(value)
    return out


def evens(tiles):
    lane = iota(1)
    index = (2 * lane) & (LANES - 1)

    def one(offset):
        return Cx(
            *(
                jnp.where(
                    lane < LANES // 2,
                    lane_take(first, index + offset),
                    lane_take(second, index + offset),
                )
                for first, second in ((tiles[0].re, tiles[1].re), (tiles[0].im, tiles[1].im))
            )
        )

    return one(0), one(1)


def natural(even, odd):
    lane = iota(1)
    out = []
    for half in range(2):
        index = half * (LANES // 2) + (lane >> 1)
        out.append(
            Cx(
                *(
                    jnp.where((lane & 1) == 0, lane_take(first, index), lane_take(second, index))
                    for first, second in ((even.re, odd.re), (even.im, odd.im))
                )
            )
        )
    return out


def split(value):
    high = value.map(lambda part: part.astype(jnp.bfloat16).astype(jnp.float32))
    return high, value - high


def contract(left, right):
    return lax.dot_general(
        left.astype(jnp.bfloat16),
        right.astype(jnp.bfloat16),
        (((0,), (0,)), ((), ())),
        preferred_element_type=jnp.float32,
    )


def strip(main, side, is_alpha, first_cycle, radial_count):
    lane, sub = iota(1), iota(0)
    lower4 = sub < 4
    column = sub & 3

    cells = lamination(main[0], main[1])
    rims = lamination(side[0], side[1])
    tiles = [cells.map(lambda part: part[:, :LANES]), cells.map(lambda part: part[:, LANES:])]
    cycle = (first_cycle + sub - 1).astype(jnp.float32)
    center = 1.0 + (cycle + 0.5) / radial_count
    face = 1.0 + cycle / radial_count
    per_center = 1.0 / center
    first_lane, last_lane = lane == 0, lane == LANES - 1

    ahead = [tile.lanes(1) for tile in tiles]
    west = [
        harmonic(pick(first_lane, rims.lanes(1), ahead[0]), tiles[0]) * per_center,
        harmonic(pick(first_lane, ahead[0], ahead[1]), tiles[1]) * per_center,
    ]
    wall = harmonic(tiles[1], rims.lanes(-1)) * per_center * 2.0
    back = [tile.lanes(-1) for tile in west]
    east = [pick(last_lane, back[1], back[0]), pick(last_lane, wall, back[1])]
    west[0] = pick(first_lane, west[0] * 2.0, west[0])
    south, north = [], []
    for tile in tiles:
        radial = harmonic(tile.subs(1), tile) * face
        radial = pick((sub == 1) | (sub == 5), radial * 2.0, radial)
        south.append(radial)
        north.append(radial.subs(-1))
    diagonal = [west[h] + east[h] + south[h] + north[h] for h in range(2)]
    gain_in = [south[h].row(1) for h in range(2)]
    gain_out = [north[h].row(4) for h in range(2)]

    diag_e, diag_o = evens(diagonal)
    east_e, east_o = evens(east)
    up_e, up_o = evens(north)
    left_e = pick(last_lane, east_o, 0.0)
    left_e = (east_o - left_e).lanes(1)

    def entry_e(r, c):
        if r == c:
            return diag_e.row(r + 1)
        return -up_e.row(r)

    lower_e, pivots_e = {}, []
    work = diag_e.row(1)
    for r in range(4):
        pivots_e.append(work.inverse())
        if r < 3:
            coupling = up_e.row(r + 1)
            lower_e[r + 1, r] = -(coupling * pivots_e[r])
            work = diag_e.row(r + 2) + lower_e[r + 1, r] * coupling
    zero = jnp.zeros((8, LANES), jnp.float32)
    nothing = Cx(zero, zero)
    half = []
    for r in range(4):
        value = Cx(jnp.where(column == r, 1.0, zero), zero)
        if r:
            value = value - lower_e[r, r - 1] * half[r - 1]
        half.append(value)
    inverse_e = [None] * 4
    for r in range(3, -1, -1):
        value = half[r] * pivots_e[r]
        if r < 3:
            value = value - lower_e[r + 1, r] * inverse_e[r + 1]
        inverse_e[r] = value
    for r in range(4):
        for c in range(r - 1):
            lower_e[r, c] = nothing
    seeds_e = seeds(lower_e, pivots_e)
    sides_e = pick(lower4, left_e.subs(-1), east_e.subs(3))
    reach_e = [inverse_e[r] * sides_e for r in range(4)]
    matrix, pair = [], []
    for r in range(4):
        to_left = (left_e.row(r + 1) * reach_e[r]).lanes(-1)
        to_right = east_e.row(r + 1) * reach_e[r]
        pair.append(pick(lower4, to_right, to_left))
        change = pick(lower4, to_left, to_right)
        base = pick(column == r, diag_o.row(r + 1), 0.0)
        if r < 3:
            base = pick(column == r + 1, -up_o.row(r + 1), base)
        if r > 0:
            base = pick(column == r - 1, -up_o.row(r), base)
        matrix.append(base - change - change.subs(4))

    for level in range(1, 8):
        step = 1 << (level - 1)
        stay = ((lane + 1) & (2 * step - 1)) == 0
        reach = solve(*factor(lambda r, c: matrix[r].row(c)), pair)
        next_matrix, next_pair = [], []
        for r in range(4):
            to_left = total(pair[k].row(r) * reach[k] for k in range(4)).lanes(-step)
            to_right = total(pair[k].row(4 + r) * reach[k] for k in range(4)).lanes(step)
            change = pick(lower4, to_left, to_right)
            change = change + change.subs(4)
            next_matrix.append(pick(stay, matrix[r] - change, matrix[r]))
            next_pair.append(pick(stay, pick(lower4, to_right, to_left), pair[r]))
        matrix, pair = next_matrix, next_pair

    lower, pivots = factor(lambda r, c: matrix[r].row(c))
    reach = solve(lower, pivots, pair)
    reach_rows = [[reach[r].row(k) for k in range(8)] for r in range(4)]
    seed = seeds(lower, pivots)

    def level_of(group):
        return jnp.where(lower4, 2 * group - 1, 2 * group)

    own_level = jnp.ones((8, LANES), jnp.int32)
    for level in range(2, 9):
        own_level = own_level + (((lane + 1) & ((1 << (level - 1)) - 1)) == 0).astype(jnp.int32)

    odd = {}
    for group in range(1, GROUPS + 1):
        rows = [pick(own_level == level_of(group), seed[r], 0.0) for r in range(4)]
        for level in range(min(2 * group - 1, 7), 0, -1):
            step = 1 << (level - 1)
            here = own_level == level
            before = [row.lanes(step) for row in rows]
            after = [row.lanes(-step) for row in rows]
            fresh = []
            for r in range(4):
                terms = [reach_rows[r][k] * before[k] for k in range(4)]
                terms += [reach_rows[r][4 + k] * after[k] for k in range(4)]
                fresh.append(rows[r] + pick(here, total(terms), 0.0))
            rows = fresh
        odd[group] = rows

    reach_e_rows = [[reach_e[r].row(k) for k in range(8)] for r in range(4)]
    even = {0: [pick(first_lane & lower4, seeds_e[r], 0.0) for r in range(4)]}
    odd[0] = [nothing] * 4
    for group in range(1, GROUPS + 1):
        before = [row.lanes(1) for row in odd[group]]
        even[group] = []
        for r in range(4):
            terms = [reach_e_rows[r][k] * before[k] for k in range(4)]
            terms += [reach_e_rows[r][4 + k] * odd[group][k] for k in range(4)]
            even[group].append(total(terms))

    def corners(lefts, rights):
        return pick(
            lane == 0,
            lefts[0],
            pick(
                lane == 1,
                lefts[1].lanes(1),
                pick(lane == 2, rights[0].lanes(3), pick(lane == 3, rights[1].lanes(4), 0.0)),
            ),
        )

    gains_left = [west[0].row(r + 1) for r in range(4)]
    gains_right = [east[1].row(r + 1) for r in range(4)]
    gain_corner = [
        corners(gains_left[2 * t : 2 * t + 2], gains_right[2 * t : 2 * t + 2]) for t in range(2)
    ]
    inner, outer, corner = {}, {}, {}
    for group in range(GROUPS + 1):
        if group:
            low = natural(even[group][0], odd[group][0])
            high = natural(even[group][3], odd[group][3])
        else:
            low, high = [even[0][0], nothing], [even[0][3], nothing]
        inner[group] = [low[h] * gain_in[h] for h in range(2)]
        outer[group] = [high[h] * gain_out[h] for h in range(2)]
        corner[group] = [
            corners(even[group][2 * t : 2 * t + 2], odd[group][2 * t : 2 * t + 2]) * gain_corner[t]
            for t in range(2)
        ]

    left_parts, right_parts = [], []
    for group in range(GROUPS + 1):
        if group in (0, GROUPS):
            low, high = inner[group], outer[group]
        else:
            near = lane < (2 << level_of(group))
            low = [pick(near, inner[group][0], 0.0), nothing]
            high = [pick(near, outer[group][0], 0.0), nothing]
        side_a, side_b = corner[group]
        own = [pick(is_alpha, low[h], high[h]) for h in range(2)]
        own.append(pick(is_alpha, side_a, side_b))
        moved = [high[0].lanes(4), high[1].lanes(4)]
        every = [
            low[0],
            low[1],
            pick(lower_lanes(lane, 4), side_a, moved[0]),
            pick(lower_lanes(lane, 4), moved[0], moved[1]),
            pick(lower_lanes(lane, 4), moved[1], pick(lane < 8, side_b.lanes(4), 0.0)),
        ]
        left_parts.append([split(value) for value in own])
        right_parts.append([split(value) for value in every])

    def wide(parts, which, name, sign=1.0):
        rows = []
        for group in parts:
            pieces = [getattr(value[which], name) for value in group]
            rows.append(jnp.concatenate(pieces, axis=1) * sign)
        return rows

    fill = [jnp.zeros((8, 3 * LANES), jnp.float32)] * 2
    left = (
        wide(left_parts, 0, "re")
        + wide(left_parts, 0, "re")
        + wide(left_parts, 1, "re")
        + wide(left_parts, 0, "im")
        + wide(left_parts, 0, "im")
        + wide(left_parts, 1, "im")
        + fill
    )
    fill = [jnp.zeros((8, 5 * LANES), jnp.float32)] * 2
    right_re = (
        wide(right_parts, 0, "re")
        + wide(right_parts, 1, "re")
        + wide(right_parts, 0, "re")
        + wide(right_parts, 0, "im", -1.0)
        + wide(right_parts, 1, "im", -1.0)
        + wide(right_parts, 0, "im", -1.0)
        + fill
    )
    right_im = (
        wide(right_parts, 0, "im")
        + wide(right_parts, 1, "im")
        + wide(right_parts, 0, "im")
        + wide(right_parts, 0, "re")
        + wide(right_parts, 1, "re")
        + wide(right_parts, 0, "re")
        + fill
    )
    left = jnp.concatenate(left, axis=0)
    top = Cx(
        contract(left, jnp.concatenate(right_re, axis=0)),
        contract(left, jnp.concatenate(right_im, axis=0)),
    )

    masks = []
    for level in range(1, 7):
        for tile in range(max((1 << (6 - level)) // 2, 1)):
            masks.append((level, (lane >> (level + 1)) == 2 * tile + (sub >> 2)))

    def spread(value):
        out = []
        for level, mask in masks:
            out.append(jnp.where(mask, value[level], 0.0))
        return jnp.concatenate(out, axis=0)

    def both(values, half):
        levels = {}
        for group in range(1, GROUPS):
            value = values[group][half]
            if half == 0:
                value = pick(lane < (2 << level_of(group)), nothing, value)
            turned = value.subs(4)
            levels[2 * group - 1] = split(pick(lower4, value, turned))
            levels[2 * group] = split(pick(lower4, turned, value))
        return {
            (which, name): spread(
                {level: getattr(pair[which], name) for level, pair in levels.items()}
            )
            for which in range(2)
            for name in ("re", "im")
        }

    even_d = [inverse_e[0].row(0), inverse_e[0].row(3), inverse_e[3].row(3)]
    even_d = [natural(value, nothing) for value in even_d]
    local = []
    for half in range(2):
        low, high = both(inner, half), both(outer, half)
        own = {key: jnp.where(is_alpha, low[key], high[key]) for key in low}
        every = {key: jnp.concatenate([low[key], high[key]], axis=1) for key in low}
        hr, hi, lr, li = (0, "re"), (0, "im"), (1, "re"), (1, "im")
        left = jnp.concatenate([own[key] for key in (hr, hi, hr, hi, lr, li)], axis=0)
        right_re = jnp.concatenate(
            [every[hr], -every[hi], every[lr], -every[li], every[hr], -every[hi]], axis=0
        )
        right_im = jnp.concatenate([every[key] for key in (hi, hr, li, lr, hi, hr)], axis=0)
        product = Cx(contract(left, right_re), contract(left, right_im))
        g_in, g_out = gain_in[half], gain_out[half]
        solo = (lane & 1) == 0
        if half == 0:
            solo = solo & (lane > 0)
        cross = even_d[1][half] * g_in * g_out
        on_in = pick(is_alpha, even_d[0][half] * g_in * g_in, cross)
        on_out = pick(is_alpha, cross, even_d[2][half] * g_out * g_out)
        on_in = pick(solo, on_in, 0.0) - pick(is_alpha, g_in, nothing)
        on_out = pick(solo, on_out, 0.0) - pick(is_alpha, nothing, g_out)
        local.append((product, on_in, on_out))
    edge = pick((lane == sub) & lower4, pick(is_alpha, gain_corner[0], gain_corner[1]), 0.0)
    return top, local, edge


def lower_lanes(lane, count):
    return lane < count


def finish(top, local, edge, is_alpha, store):
    lane, sub = iota(1), iota(0)
    for part, name in enumerate(("re", "im")):
        full = getattr(top, name)
        edge_part = getattr(edge, name)
        for half in range(2):
            product = getattr(local[half][0], name)
            on_in = getattr(local[half][1], name)
            on_out = getattr(local[half][2], name)
            for row in range(0, LANES, 8):
                here = lane == sub + row
                low = product[row : row + 8, :LANES] + jnp.where(here, on_in, 0.0)
                high = product[row : row + 8, LANES:] + jnp.where(here, on_out, 0.0)
                high = lane_roll(high, 4)
                at = half * LANES + row
                out = [full[at : at + 8, t * LANES : (t + 1) * LANES] for t in range(5)]
                out[half] = out[half] + low
                out[2 + half] = out[2 + half] + jnp.where(lane < 4, 0.0, high)
                out[3 + half] = out[3 + half] + jnp.where(lane < 4, high, 0.0)
                store(part, at, 8, [-value for value in out])
        at = 2 * LANES
        out = [full[at : at + 8, t * LANES : (t + 1) * LANES] for t in range(5)]
        out[2] = out[2] - jnp.where(is_alpha, edge_part, 0.0)
        out[4] = out[4] - jnp.where(is_alpha, 0.0, lane_roll(edge_part, 4))
        store(part, at, 4, [-value for value in out])


def gather_rows(angular, own, other, is_alpha, is_even, is_first, is_last, main, side):
    lane = lax.broadcasted_iota(jnp.int32, (2, LANES), 1)
    for field in range(2):
        scale = angular if field == 0 else 1.0
        rows = slice(2 * field, 2 * field + 2)
        (mine, near, short, long), (theirs, far, short_x, long_x) = (
            [ref[rows, :] * scale for ref in refs] for refs in (own, other)
        )
        alpha, beta = jnp.where(is_alpha, mine, theirs), jnp.where(is_alpha, theirs, mine)
        main[field, 0:1, :] = jnp.where(is_first, alpha[0:1], jnp.where(is_alpha, near, far)[1:2])
        main[field, 1:3, :] = alpha
        main[field, 3:5, :] = beta
        main[field, 5:6, :] = jnp.where(is_last, beta[1:2], jnp.where(is_alpha, far, near)[0:1])
        main[field, 6:8, :] = beta
        ends = []
        for longs, shorts in ((long, short), (long_x, short_x)):
            left = jnp.where(is_even, longs, shorts)[:, LANES:]
            right = jnp.where(is_even, shorts, longs)[:, :LANES]
            ends.append(jnp.where(lane == LANES - 1, left, jnp.where(lane == 0, right, 1.0)))
        ends_alpha = jnp.where(is_alpha, ends[0], ends[1])
        ends_beta = jnp.where(is_alpha, ends[1], ends[0])
        side[field, 0:1, :] = ends_alpha[0:1]
        side[field, 1:3, :] = ends_alpha
        side[field, 3:5, :] = ends_beta
        side[field, 5:7, :] = ends_beta
        side[field, 7:8, :] = ends_beta[0:1]


def merge_kernel(cycles, depth, angular, *refs):
    own, other, (out, main, side) = refs[:4], refs[4:8], refs[8:]
    index = lax.axis_index("rad")
    is_even = lax.axis_index("az") % 2 == 0
    is_alpha = index % 2 == 0
    is_first = index // 2 == 0
    is_last = index // 2 == cycles // 2 - 1
    gather_rows(angular[0], own, other, is_alpha, is_even, is_first, is_last, main, side)
    top, local, edge = strip(
        (main[0], main[1]),
        (side[0], side[1]),
        is_alpha,
        (index // 2) * (2 * depth),
        cycles * depth,
    )

    def store(part, row, count, tiles):
        for number, tile in enumerate(tiles):
            width = min(LANES, out.shape[2] - number * LANES)
            out[part, row : row + count, number * LANES : number * LANES + width] = tile[
                :count, :width
            ]

    finish(top, local, edge, is_alpha, store)


def cell_kernel(*refs):
    sources, (out_ref,), targets, sems = refs[:4], refs[4:5], refs[5:9], refs[9]
    copies = [
        pltpu.make_async_copy(source, target, sems.at[number])
        for number, (source, target) in enumerate(zip(sources, targets))
    ]
    for copy in copies:
        copy.start()
    for copy in copies:
        copy.wait()
    material_ref, sheet_ref, sigma_ref, nu_ref = targets
    material, sheet = material_ref[...], sheet_ref[...]
    sigma, base = jnp.zeros_like(sheet), jnp.zeros_like(sheet)
    for level in range(sigma_ref.shape[0]):
        sigma = jnp.where(material == level, sigma_ref[level], sigma)
        base = jnp.where(material == level, nu_ref[level], base)
    out_ref[:2, :] = sigma * sheet * sheet
    out_ref[2:, :] = base


def cell_inputs(*arguments):
    spaces = (pltpu.VMEM, pltpu.VMEM, pltpu.SMEM, pltpu.SMEM)
    return pl.pallas_call(
        cell_kernel,
        out_shape=jax.ShapeDtypeStruct((4, arguments[1].shape[1]), jnp.float32),
        in_specs=[pl.BlockSpec(memory_space=pl.ANY)] * 4,
        out_specs=pl.BlockSpec(memory_space=pltpu.VMEM),
        scratch_shapes=[
            space(value.shape, value.dtype) for space, value in zip(spaces, arguments)
        ]
        + [pltpu.SemaphoreType.DMA((4,))],
        compiler_params=pltpu.CompilerParams(vmem_limit_bytes=40 * 1024 * 1024),
        name="cells",
    )(*arguments)


def swapped(cells, axis, first):
    count = lax.axis_size(axis)
    route = []
    for low in range(first, count, 2):
        high = (low + 1) % count
        route += [(low, high), (high, low)]
    return lax.ppermute(cells, axis, route)


def per_device(material_id, thickness, sigma_table, nu_table, angular_frequency):
    depth, arc = thickness.shape
    cells = cell_inputs(material_id, thickness, sigma_table, nu_table)
    cycles = lax.axis_size("rad")
    long, short = swapped(cells, "az", 1), swapped(cells, "az", 0)
    own = [cells, swapped(cells, "rad", 1), short, long]
    other = [swapped(part, "rad", 0) for part in own]
    outer_nodes = arc + 2 * depth
    return pl.pallas_call(
        lambda *refs: merge_kernel(cycles, depth, *refs),
        out_shape=jax.ShapeDtypeStruct((2, outer_nodes, 2 * outer_nodes), jnp.float32),
        in_specs=[pl.BlockSpec(memory_space=pltpu.SMEM)]
        + [pl.BlockSpec(memory_space=pltpu.VMEM)] * 8,
        out_specs=pl.BlockSpec(memory_space=pltpu.VMEM),
        scratch_shapes=[
            pltpu.VMEM((2, 8, arc), jnp.float32),
            pltpu.VMEM((2, 8, LANES), jnp.float32),
        ],
        compiler_params=pltpu.CompilerParams(vmem_limit_bytes=48 * 1024 * 1024),
        name="pair_map",
    )(angular_frequency, *own, *other)


def solution(mesh):
    placed = (P("rad", "az"), P("rad", "az"), P(), P(), P())
    return jax.shard_map(
        per_device, mesh=mesh, in_specs=placed, out_specs=P(None, "rad", "az"), check_vma=False
    )
```

```python
import jax
import jax.numpy as jnp
from jax import lax
from jax.experimental import pallas as pl
from jax.experimental.pallas import tpu as pltpu
from jax.sharding import PartitionSpec as P

SHEET_NODES = 16
LANES = 128
GROUPS = 4


def lane_roll(value, shift):
    return pltpu.roll(value, shift % value.shape[1], 1)


def sub_roll(value, shift):
    return pltpu.roll(value, shift % value.shape[0], 0)


def lane_take(value, index):
    return jnp.take_along_axis(value, index, axis=1, mode="promise_in_bounds")


def iota(dim):
    return lax.broadcasted_iota(jnp.int32, (8, LANES), dim)


class Cx:
    def __init__(self, re, im):
        self.re, self.im = re, im

    def __add__(self, other):
        return Cx(self.re + other.re, self.im + other.im)

    def __sub__(self, other):
        return Cx(self.re - other.re, self.im - other.im)

    def __neg__(self):
        return Cx(-self.re, -self.im)

    def __mul__(self, other):
        if not isinstance(other, Cx):
            return Cx(self.re * other, self.im * other)
        return Cx(
            self.re * other.re - self.im * other.im, self.re * other.im + self.im * other.re
        )

    def inverse(self):
        scale = 1.0 / (self.re * self.re + self.im * self.im)
        return Cx(self.re * scale, -self.im * scale)

    def root(self):
        size = jnp.sqrt(self.re * self.re + self.im * self.im)
        re = jnp.sqrt(0.5 * (size + self.re))
        return Cx(re, 0.5 * self.im / re)

    def map(self, function):
        return Cx(function(self.re), function(self.im))

    def row(self, index):
        return self.map(lambda part: jnp.broadcast_to(part[index : index + 1], (8, LANES)))

    def lanes(self, shift):
        return self.map(lambda part: lane_roll(part, shift))

    def subs(self, shift):
        return self.map(lambda part: sub_roll(part, shift))


def pick(mask, first, second):
    if not isinstance(second, Cx):
        return first.map(lambda part: jnp.where(mask, part, second))
    return Cx(jnp.where(mask, first.re, second.re), jnp.where(mask, first.im, second.im))


def total(terms):
    terms = list(terms)
    while len(terms) > 1:
        terms = [
            terms[i] + terms[i + 1] if i + 1 < len(terms) else terms[i]
            for i in range(0, len(terms), 2)
        ]
    return terms[0]


def harmonic(left, right):
    return (left * right) * (left + right).inverse() * 2.0


def lamination(skin, base):
    above = Cx(jnp.ones_like(skin), jnp.zeros_like(skin))
    field = Cx(jnp.ones_like(skin), 0.5 * skin)
    summed = above
    for _ in range(SHEET_NODES - 1):
        summed = summed + field
        below = Cx(
            2.0 * field.re - skin * field.im - above.re,
            2.0 * field.im + skin * field.re - above.im,
        )
        above, field = field, below
    return field * summed.inverse() * (base * SHEET_NODES)


def factor(entry):
    work = {(r, c): entry(r, c) for r in range(4) for c in range(r + 1)}
    lower, pivots = {}, []
    for k in range(4):
        inverse = work[k, k].inverse()
        pivots.append(inverse)
        for r in range(k + 1, 4):
            lower[r, k] = work[r, k] * inverse
        for r in range(k + 1, 4):
            for c in range(k + 1, r + 1):
                work[r, c] = work[r, c] - lower[r, k] * work[c, k]
    return lower, pivots


def solve(lower, pivots, right):
    half = []
    for r in range(4):
        value = right[r]
        for c in range(r):
            value = value - lower[r, c] * half[c]
        half.append(value)
    out = [None] * 4
    for r in range(3, -1, -1):
        value = half[r] * pivots[r]
        for c in range(r + 1, 4):
            value = value - lower[c, r] * out[c]
        out[r] = value
    return out


def seeds(lower, pivots):
    column = iota(0) & 3
    unit = {}
    for r in range(4):
        for c in range(r - 1, -1, -1):
            value = -lower[r, c]
            for k in range(c + 1, r):
                value = value - lower[r, k] * unit[k, c]
            unit[r, c] = value
    roots = [pivot.root() for pivot in pivots]
    out = []
    for r in range(4):
        value = pick(column == r, roots[r], 0.0)
        for k in range(r + 1, 4):
            value = pick(column == k, roots[k] * unit[k, r], value)
        out.append(value)
    return out


def evens(tiles):
    lane = iota(1)
    index = (2 * lane) & (LANES - 1)

    def one(offset):
        return Cx(
            *(
                jnp.where(
                    lane < LANES // 2,
                    lane_take(first, index + offset),
                    lane_take(second, index + offset),
                )
                for first, second in ((tiles[0].re, tiles[1].re), (tiles[0].im, tiles[1].im))
            )
        )

    return one(0), one(1)


def natural(even, odd):
    lane = iota(1)
    out = []
    for half in range(2):
        index = half * (LANES // 2) + (lane >> 1)
        out.append(
            Cx(
                *(
                    jnp.where((lane & 1) == 0, lane_take(first, index), lane_take(second, index))
                    for first, second in ((even.re, odd.re), (even.im, odd.im))
                )
            )
        )
    return out


def split(value):
    high = value.map(lambda part: part.astype(jnp.bfloat16).astype(jnp.float32))
    return high, value - high


def contract(left, right):
    return lax.dot_general(
        left.astype(jnp.bfloat16),
        right.astype(jnp.bfloat16),
        (((0,), (0,)), ((), ())),
        preferred_element_type=jnp.float32,
    )


def strip(main, side, is_alpha, first_cycle, radial_count):
    lane, sub = iota(1), iota(0)
    lower4 = sub < 4
    column = sub & 3

    cells = lamination(main[0], main[1])
    rims = lamination(side[0], side[1])
    tiles = [cells.map(lambda part: part[:, :LANES]), cells.map(lambda part: part[:, LANES:])]
    cycle = (first_cycle + sub - 1).astype(jnp.float32)
    center = 1.0 + (cycle + 0.5) / radial_count
    face = 1.0 + cycle / radial_count
    per_center = 1.0 / center
    first_lane, last_lane = lane == 0, lane == LANES - 1

    ahead = [tile.lanes(1) for tile in tiles]
    west = [
        harmonic(pick(first_lane, rims.lanes(1), ahead[0]), tiles[0]) * per_center,
        harmonic(pick(first_lane, ahead[0], ahead[1]), tiles[1]) * per_center,
    ]
    wall = harmonic(tiles[1], rims.lanes(-1)) * per_center * 2.0
    back = [tile.lanes(-1) for tile in west]
    east = [pick(last_lane, back[1], back[0]), pick(last_lane, wall, back[1])]
    west[0] = pick(first_lane, west[0] * 2.0, west[0])
    south, north = [], []
    for tile in tiles:
        radial = harmonic(tile.subs(1), tile) * face
        radial = pick((sub == 1) | (sub == 5), radial * 2.0, radial)
        south.append(radial)
        north.append(radial.subs(-1))
    diagonal = [west[h] + east[h] + south[h] + north[h] for h in range(2)]
    gain_in = [south[h].row(1) for h in range(2)]
    gain_out = [north[h].row(4) for h in range(2)]

    diag_e, diag_o = evens(diagonal)
    east_e, east_o = evens(east)
    up_e, up_o = evens(north)
    left_e = pick(last_lane, east_o, 0.0)
    left_e = (east_o - left_e).lanes(1)

    def entry_e(r, c):
        if r == c:
            return diag_e.row(r + 1)
        return -up_e.row(r)

    lower_e, pivots_e = {}, []
    work = diag_e.row(1)
    for r in range(4):
        pivots_e.append(work.inverse())
        if r < 3:
            coupling = up_e.row(r + 1)
            lower_e[r + 1, r] = -(coupling * pivots_e[r])
            work = diag_e.row(r + 2) + lower_e[r + 1, r] * coupling
    zero = jnp.zeros((8, LANES), jnp.float32)
    nothing = Cx(zero, zero)
    half = []
    for r in range(4):
        value = Cx(jnp.where(column == r, 1.0, zero), zero)
        if r:
            value = value - lower_e[r, r - 1] * half[r - 1]
        half.append(value)
    inverse_e = [None] * 4
    for r in range(3, -1, -1):
        value = half[r] * pivots_e[r]
        if r < 3:
            value = value - lower_e[r + 1, r] * inverse_e[r + 1]
        inverse_e[r] = value
    for r in range(4):
        for c in range(r - 1):
            lower_e[r, c] = nothing
    seeds_e = seeds(lower_e, pivots_e)
    sides_e = pick(lower4, left_e.subs(-1), east_e.subs(3))
    reach_e = [inverse_e[r] * sides_e for r in range(4)]
    matrix, pair = [], []
    for r in range(4):
        to_left = (left_e.row(r + 1) * reach_e[r]).lanes(-1)
        to_right = east_e.row(r + 1) * reach_e[r]
        pair.append(pick(lower4, to_right, to_left))
        change = pick(lower4, to_left, to_right)
        base = pick(column == r, diag_o.row(r + 1), 0.0)
        if r < 3:
            base = pick(column == r + 1, -up_o.row(r + 1), base)
        if r > 0:
            base = pick(column == r - 1, -up_o.row(r), base)
        matrix.append(base - change - change.subs(4))

    for level in range(1, 8):
        step = 1 << (level - 1)
        stay = ((lane + 1) & (2 * step - 1)) == 0
        reach = solve(*factor(lambda r, c: matrix[r].row(c)), pair)
        next_matrix, next_pair = [], []
        for r in range(4):
            to_left = total(pair[k].row(r) * reach[k] for k in range(4)).lanes(-step)
            to_right = total(pair[k].row(4 + r) * reach[k] for k in range(4)).lanes(step)
            change = pick(lower4, to_left, to_right)
            change = change + change.subs(4)
            next_matrix.append(pick(stay, matrix[r] - change, matrix[r]))
            next_pair.append(pick(stay, pick(lower4, to_right, to_left), pair[r]))
        matrix, pair = next_matrix, next_pair

    lower, pivots = factor(lambda r, c: matrix[r].row(c))
    reach = solve(lower, pivots, pair)
    reach_rows = [[reach[r].row(k) for k in range(8)] for r in range(4)]
    seed = seeds(lower, pivots)

    def level_of(group):
        return jnp.where(lower4, 2 * group - 1, 2 * group)

    own_level = jnp.ones((8, LANES), jnp.int32)
    for level in range(2, 9):
        own_level = own_level + (((lane + 1) & ((1 << (level - 1)) - 1)) == 0).astype(jnp.int32)

    odd = {}
    for group in range(1, GROUPS + 1):
        rows = [pick(own_level == level_of(group), seed[r], 0.0) for r in range(4)]
        for level in range(min(2 * group - 1, 7), 0, -1):
            step = 1 << (level - 1)
            here = own_level == level
            before = [row.lanes(step) for row in rows]
            after = [row.lanes(-step) for row in rows]
            fresh = []
            for r in range(4):
                terms = [reach_rows[r][k] * before[k] for k in range(4)]
                terms += [reach_rows[r][4 + k] * after[k] for k in range(4)]
                fresh.append(rows[r] + pick(here, total(terms), 0.0))
            rows = fresh
        odd[group] = rows

    reach_e_rows = [[reach_e[r].row(k) for k in range(8)] for r in range(4)]
    even = {0: [pick(first_lane & lower4, seeds_e[r], 0.0) for r in range(4)]}
    odd[0] = [nothing] * 4
    for group in range(1, GROUPS + 1):
        before = [row.lanes(1) for row in odd[group]]
        even[group] = []
        for r in range(4):
            terms = [reach_e_rows[r][k] * before[k] for k in range(4)]
            terms += [reach_e_rows[r][4 + k] * odd[group][k] for k in range(4)]
            even[group].append(total(terms))

    def corners(lefts, rights):
        return pick(
            lane == 0,
            lefts[0],
            pick(
                lane == 1,
                lefts[1].lanes(1),
                pick(lane == 2, rights[0].lanes(3), pick(lane == 3, rights[1].lanes(4), 0.0)),
            ),
        )

    gains_left = [west[0].row(r + 1) for r in range(4)]
    gains_right = [east[1].row(r + 1) for r in range(4)]
    gain_corner = [
        corners(gains_left[2 * t : 2 * t + 2], gains_right[2 * t : 2 * t + 2]) for t in range(2)
    ]
    inner, outer, corner = {}, {}, {}
    for group in range(GROUPS + 1):
        if group:
            low = natural(even[group][0], odd[group][0])
            high = natural(even[group][3], odd[group][3])
        else:
            low, high = [even[0][0], nothing], [even[0][3], nothing]
        inner[group] = [low[h] * gain_in[h] for h in range(2)]
        outer[group] = [high[h] * gain_out[h] for h in range(2)]
        corner[group] = [
            corners(even[group][2 * t : 2 * t + 2], odd[group][2 * t : 2 * t + 2]) * gain_corner[t]
            for t in range(2)
        ]

    left_parts, right_parts = [], []
    for group in range(GROUPS + 1):
        if group in (0, GROUPS):
            low, high = inner[group], outer[group]
        else:
            near = lane < (2 << level_of(group))
            low = [pick(near, inner[group][0], 0.0), nothing]
            high = [pick(near, outer[group][0], 0.0), nothing]
        side_a, side_b = corner[group]
        own = [pick(is_alpha, low[h], high[h]) for h in range(2)]
        own.append(pick(is_alpha, side_a, side_b))
        moved = [high[0].lanes(4), high[1].lanes(4)]
        every = [
            low[0],
            low[1],
            pick(lower_lanes(lane, 4), side_a, moved[0]),
            pick(lower_lanes(lane, 4), moved[0], moved[1]),
            pick(lower_lanes(lane, 4), moved[1], pick(lane < 8, side_b.lanes(4), 0.0)),
        ]
        left_parts.append([split(value) for value in own])
        right_parts.append([split(value) for value in every])

    def wide(parts, which, name, sign=1.0):
        rows = []
        for group in parts:
            pieces = [getattr(value[which], name) for value in group]
            rows.append(jnp.concatenate(pieces, axis=1) * sign)
        return rows

    fill = [jnp.zeros((8, 3 * LANES), jnp.float32)] * 2
    left = (
        wide(left_parts, 0, "re")
        + wide(left_parts, 0, "re")
        + wide(left_parts, 1, "re")
        + wide(left_parts, 0, "im")
        + wide(left_parts, 0, "im")
        + wide(left_parts, 1, "im")
        + fill
    )
    fill = [jnp.zeros((8, 5 * LANES), jnp.float32)] * 2
    right_re = (
        wide(right_parts, 0, "re")
        + wide(right_parts, 1, "re")
        + wide(right_parts, 0, "re")
        + wide(right_parts, 0, "im", -1.0)
        + wide(right_parts, 1, "im", -1.0)
        + wide(right_parts, 0, "im", -1.0)
        + fill
    )
    right_im = (
        wide(right_parts, 0, "im")
        + wide(right_parts, 1, "im")
        + wide(right_parts, 0, "im")
        + wide(right_parts, 0, "re")
        + wide(right_parts, 1, "re")
        + wide(right_parts, 0, "re")
        + fill
    )
    left = jnp.concatenate(left, axis=0)
    top = Cx(
        contract(left, jnp.concatenate(right_re, axis=0)),
        contract(left, jnp.concatenate(right_im, axis=0)),
    )

    masks = []
    for level in range(1, 7):
        for tile in range(max((1 << (6 - level)) // 2, 1)):
            masks.append((level, (lane >> (level + 1)) == 2 * tile + (sub >> 2)))

    def spread(value):
        out = []
        for level, mask in masks:
            out.append(jnp.where(mask, value[level], 0.0))
        return jnp.concatenate(out, axis=0)

    def both(values, half):
        levels = {}
        for group in range(1, GROUPS):
            value = values[group][half]
            if half == 0:
                value = pick(lane < (2 << level_of(group)), nothing, value)
            turned = value.subs(4)
            levels[2 * group - 1] = split(pick(lower4, value, turned))
            levels[2 * group] = split(pick(lower4, turned, value))
        return {
            (which, name): spread(
                {level: getattr(pair[which], name) for level, pair in levels.items()}
            )
            for which in range(2)
            for name in ("re", "im")
        }

    even_d = [inverse_e[0].row(0), inverse_e[0].row(3), inverse_e[3].row(3)]
    even_d = [natural(value, nothing) for value in even_d]
    local = []
    for half in range(2):
        low, high = both(inner, half), both(outer, half)
        own = {key: jnp.where(is_alpha, low[key], high[key]) for key in low}
        every = {key: jnp.concatenate([low[key], high[key]], axis=1) for key in low}
        hr, hi, lr, li = (0, "re"), (0, "im"), (1, "re"), (1, "im")
        left = jnp.concatenate([own[key] for key in (hr, hi, hr, hi, lr, li)], axis=0)
        right_re = jnp.concatenate(
            [every[hr], -every[hi], every[lr], -every[li], every[hr], -every[hi]], axis=0
        )
        right_im = jnp.concatenate([every[key] for key in (hi, hr, li, lr, hi, hr)], axis=0)
        product = Cx(contract(left, right_re), contract(left, right_im))
        g_in, g_out = gain_in[half], gain_out[half]
        solo = (lane & 1) == 0
        if half == 0:
            solo = solo & (lane > 0)
        cross = even_d[1][half] * g_in * g_out
        on_in = pick(is_alpha, even_d[0][half] * g_in * g_in, cross)
        on_out = pick(is_alpha, cross, even_d[2][half] * g_out * g_out)
        on_in = pick(solo, on_in, 0.0) - pick(is_alpha, g_in, nothing)
        on_out = pick(solo, on_out, 0.0) - pick(is_alpha, nothing, g_out)
        local.append((product, on_in, on_out))
    edge = pick((lane == sub) & lower4, pick(is_alpha, gain_corner[0], gain_corner[1]), 0.0)
    return top, local, edge


def lower_lanes(lane, count):
    return lane < count


def finish(top, local, edge, is_alpha, store):
    lane, sub = iota(1), iota(0)
    for part, name in enumerate(("re", "im")):
        full = getattr(top, name)
        edge_part = getattr(edge, name)
        for half in range(2):
            product = getattr(local[half][0], name)
            on_in = getattr(local[half][1], name)
            on_out = getattr(local[half][2], name)
            for row in range(0, LANES, 8):
                here = lane == sub + row
                low = product[row : row + 8, :LANES] + jnp.where(here, on_in, 0.0)
                high = product[row : row + 8, LANES:] + jnp.where(here, on_out, 0.0)
                high = lane_roll(high, 4)
                at = half * LANES + row
                out = [full[at : at + 8, t * LANES : (t + 1) * LANES] for t in range(5)]
                out[half] = out[half] + low
                out[2 + half] = out[2 + half] + jnp.where(lane < 4, 0.0, high)
                out[3 + half] = out[3 + half] + jnp.where(lane < 4, high, 0.0)
                store(part, at, 8, [-value for value in out])
        at = 2 * LANES
        out = [full[at : at + 8, t * LANES : (t + 1) * LANES] for t in range(5)]
        out[2] = out[2] - jnp.where(is_alpha, edge_part, 0.0)
        out[4] = out[4] - jnp.where(is_alpha, 0.0, lane_roll(edge_part, 4))
        store(part, at, 4, [-value for value in out])


def cell_data(ref, angular):
    value = ref[...]
    levels = value[:2].astype(jnp.int32)
    lookups = []
    for row in (4, 5):
        table = jnp.broadcast_to(value[row : row + 1, :LANES], (8, LANES))
        halves = []
        for half in range(2):
            index = levels[:, half * LANES : (half + 1) * LANES]
            index = jnp.concatenate([index] * 4, axis=0)
            halves.append(lane_take(table, index)[:2])
        lookups.append(jnp.concatenate(halves, axis=1))
    sheet = value[2:4]
    return angular * lookups[0] * sheet * sheet, lookups[1]


def gather_rows(angular, own, other, is_alpha, is_even, is_first, is_last, main, side):
    lane = lax.broadcasted_iota(jnp.int32, (2, LANES), 1)
    own, other = [[cell_data(ref, angular) for ref in refs] for refs in (own, other)]
    for field in range(2):
        (mine, near, long, short), (theirs, far, long_x, short_x) = (
            [data[field] for data in part] for part in (own, other)
        )
        alpha, beta = jnp.where(is_alpha, mine, theirs), jnp.where(is_alpha, theirs, mine)
        main[field, 0:1, :] = jnp.where(is_first, alpha[0:1], jnp.where(is_alpha, near, far)[1:2])
        main[field, 1:3, :] = alpha
        main[field, 3:5, :] = beta
        main[field, 5:6, :] = jnp.where(is_last, beta[1:2], jnp.where(is_alpha, far, near)[0:1])
        main[field, 6:8, :] = beta
        ends = []
        for longs, shorts in ((long, short), (long_x, short_x)):
            left = jnp.where(is_even, longs, shorts)[:, LANES:]
            right = jnp.where(is_even, shorts, longs)[:, :LANES]
            ends.append(jnp.where(lane == LANES - 1, left, jnp.where(lane == 0, right, 1.0)))
        ends_alpha = jnp.where(is_alpha, ends[0], ends[1])
        ends_beta = jnp.where(is_alpha, ends[1], ends[0])
        side[field, 0:1, :] = ends_alpha[0:1]
        side[field, 1:3, :] = ends_alpha
        side[field, 3:5, :] = ends_beta
        side[field, 5:7, :] = ends_beta
        side[field, 7:8, :] = ends_beta[0:1]


def merge_kernel(cycles, depth, angular, *refs):
    own, other, (out, main, side) = refs[:4], refs[4:8], refs[8:]
    index = lax.axis_index("rad")
    is_even = lax.axis_index("az") % 2 == 0
    is_alpha = index % 2 == 0
    is_first = index // 2 == 0
    is_last = index // 2 == cycles // 2 - 1
    gather_rows(angular[0], own, other, is_alpha, is_even, is_first, is_last, main, side)
    top, local, edge = strip(
        (main[0], main[1]),
        (side[0], side[1]),
        is_alpha,
        (index // 2) * (2 * depth),
        cycles * depth,
    )

    def store(part, row, count, tiles):
        for number, tile in enumerate(tiles):
            width = min(LANES, out.shape[2] - number * LANES)
            out[part, row : row + count, number * LANES : number * LANES + width] = tile[
                :count, :width
            ]

    finish(top, local, edge, is_alpha, store)


def pack_kernel(*refs):
    sources, (out_ref,), targets, sems = refs[:4], refs[4:5], refs[5:9], refs[9]
    copies = [
        pltpu.make_async_copy(source, target, sems.at[number])
        for number, (source, target) in enumerate(zip(sources, targets))
    ]
    for copy in copies:
        copy.start()
    for copy in copies:
        copy.wait()
    material_ref, sheet_ref, sigma_ref, nu_ref = targets
    out_ref[:2, :] = material_ref[...].astype(jnp.float32)
    out_ref[2:4, :] = sheet_ref[...]
    for row, ref in ((4, sigma_ref), (5, nu_ref)):
        out_ref[row : row + 1, : ref.shape[0]] = ref[...].reshape(1, ref.shape[0])


def packed(*arguments):
    held = [pltpu.with_memory_space_constraint(value, pltpu.HBM) for value in arguments]
    return pl.pallas_call(
        pack_kernel,
        out_shape=jax.ShapeDtypeStruct((8, arguments[1].shape[1]), jnp.float32),
        in_specs=[pl.BlockSpec(memory_space=pltpu.HBM)] * 4,
        out_specs=pl.BlockSpec(memory_space=pltpu.VMEM),
        scratch_shapes=[pltpu.VMEM(value.shape, value.dtype) for value in arguments]
        + [pltpu.SemaphoreType.DMA((4,))],
        name="cells",
    )(*held)


def swapped(cells, axis, first):
    count = lax.axis_size(axis)
    route = []
    for low in range(first, count, 2):
        high = (low + 1) % count
        route += [(low, high), (high, low)]
    return lax.ppermute(cells, axis, route)


def per_device(material_id, thickness, sigma_table, nu_table, angular_frequency):
    depth, arc = thickness.shape
    cells = packed(material_id, thickness, sigma_table, nu_table)
    cycles = lax.axis_size("rad")
    own = [cells, swapped(cells, "rad", 1), swapped(cells, "az", 1), swapped(cells, "az", 0)]
    other = [swapped(part, "rad", 0) for part in own]
    outer_nodes = arc + 2 * depth
    return pl.pallas_call(
        lambda *refs: merge_kernel(cycles, depth, *refs),
        out_shape=jax.ShapeDtypeStruct((2, outer_nodes, 2 * outer_nodes), jnp.float32),
        in_specs=[pl.BlockSpec(memory_space=pltpu.SMEM)]
        + [pl.BlockSpec(memory_space=pltpu.VMEM)] * 8,
        out_specs=pl.BlockSpec(memory_space=pltpu.VMEM),
        scratch_shapes=[
            pltpu.VMEM((2, 8, arc), jnp.float32),
            pltpu.VMEM((2, 8, LANES), jnp.float32),
        ],
        compiler_params=pltpu.CompilerParams(vmem_limit_bytes=48 * 1024 * 1024),
        name="pair_map",
    )(angular_frequency, *own, *other)


def solution(mesh):
    placed = (P("rad", "az"), P("rad", "az"), P(), P(), P())
    return jax.shard_map(
        per_device, mesh=mesh, in_specs=placed, out_specs=P(None, "rad", "az"), check_vma=False
    )
```

```python
import jax
import jax.numpy as jnp
from jax import lax
from jax.experimental import pallas as pl
from jax.experimental.pallas import tpu as pltpu
from jax.sharding import PartitionSpec as P

SHEET_NODES = 16
LANES = 128
GROUPS = 4


def lane_roll(value, shift):
    return pltpu.roll(value, shift % value.shape[1], 1)


def sub_roll(value, shift):
    return pltpu.roll(value, shift % value.shape[0], 0)


def lane_take(value, index):
    return jnp.take_along_axis(value, index, axis=1, mode="promise_in_bounds")


def sub_take(value, index):
    return jnp.take_along_axis(value, index, axis=0, mode="promise_in_bounds")


def iota(dim):
    return lax.broadcasted_iota(jnp.int32, (8, LANES), dim)


class Cx:
    def __init__(self, re, im):
        self.re, self.im = re, im

    def __add__(self, other):
        return Cx(self.re + other.re, self.im + other.im)

    def __sub__(self, other):
        return Cx(self.re - other.re, self.im - other.im)

    def __neg__(self):
        return Cx(-self.re, -self.im)

    def __mul__(self, other):
        if not isinstance(other, Cx):
            return Cx(self.re * other, self.im * other)
        return Cx(
            self.re * other.re - self.im * other.im, self.re * other.im + self.im * other.re
        )

    def inverse(self):
        scale = 1.0 / (self.re * self.re + self.im * self.im)
        return Cx(self.re * scale, -self.im * scale)

    def root(self):
        size = jnp.sqrt(self.re * self.re + self.im * self.im)
        re = jnp.sqrt(0.5 * (size + self.re))
        return Cx(re, 0.5 * self.im / re)

    def map(self, function):
        return Cx(function(self.re), function(self.im))

    def row(self, index):
        return self.map(lambda part: jnp.broadcast_to(part[index : index + 1], (8, LANES)))

    def lanes(self, shift):
        return self.map(lambda part: lane_roll(part, shift))

    def subs(self, shift):
        return self.map(lambda part: sub_roll(part, shift))


def pick(mask, first, second):
    if not isinstance(second, Cx):
        return first.map(lambda part: jnp.where(mask, part, second))
    return Cx(jnp.where(mask, first.re, second.re), jnp.where(mask, first.im, second.im))


def total(terms):
    terms = list(terms)
    while len(terms) > 1:
        terms = [
            terms[i] + terms[i + 1] if i + 1 < len(terms) else terms[i]
            for i in range(0, len(terms), 2)
        ]
    return terms[0]


def harmonic(left, right):
    return (left * right) * (left + right).inverse() * 2.0


def lamination(skin, base):
    above = Cx(jnp.ones_like(skin), jnp.zeros_like(skin))
    field = Cx(jnp.ones_like(skin), 0.5 * skin)
    summed = above
    for _ in range(SHEET_NODES - 1):
        summed = summed + field
        below = Cx(
            2.0 * field.re - skin * field.im - above.re,
            2.0 * field.im + skin * field.re - above.im,
        )
        above, field = field, below
    return field * summed.inverse() * (base * SHEET_NODES)


def factor(entry):
    work = {(r, c): entry(r, c) for r in range(4) for c in range(r + 1)}
    lower, pivots = {}, []
    for k in range(4):
        inverse = work[k, k].inverse()
        pivots.append(inverse)
        for r in range(k + 1, 4):
            lower[r, k] = work[r, k] * inverse
        for r in range(k + 1, 4):
            for c in range(k + 1, r + 1):
                work[r, c] = work[r, c] - lower[r, k] * work[c, k]
    return lower, pivots


def solve(lower, pivots, right):
    half = []
    for r in range(4):
        value = right[r]
        for c in range(r):
            value = value - lower[r, c] * half[c]
        half.append(value)
    out = [None] * 4
    for r in range(3, -1, -1):
        value = half[r] * pivots[r]
        for c in range(r + 1, 4):
            value = value - lower[c, r] * out[c]
        out[r] = value
    return out


def seeds(lower, pivots):
    column = iota(0) & 3
    unit = {}
    for r in range(4):
        for c in range(r - 1, -1, -1):
            value = -lower[r, c]
            for k in range(c + 1, r):
                value = value - lower[r, k] * unit[k, c]
            unit[r, c] = value
    roots = [pivot.root() for pivot in pivots]
    out = []
    for r in range(4):
        value = pick(column == r, roots[r], 0.0)
        for k in range(r + 1, 4):
            value = pick(column == k, roots[k] * unit[k, r], value)
        out.append(value)
    return out


def evens(tiles):
    lane = iota(1)
    index = (2 * lane) & (LANES - 1)

    def one(offset):
        return Cx(
            *(
                jnp.where(
                    lane < LANES // 2,
                    lane_take(first, index + offset),
                    lane_take(second, index + offset),
                )
                for first, second in ((tiles[0].re, tiles[1].re), (tiles[0].im, tiles[1].im))
            )
        )

    return one(0), one(1)


def natural(even, odd):
    lane = iota(1)
    out = []
    for half in range(2):
        index = half * (LANES // 2) + (lane >> 1)
        out.append(
            Cx(
                *(
                    jnp.where((lane & 1) == 0, lane_take(first, index), lane_take(second, index))
                    for first, second in ((even.re, odd.re), (even.im, odd.im))
                )
            )
        )
    return out


def split(value):
    high = value.map(lambda part: part.astype(jnp.bfloat16).astype(jnp.float32))
    return high, value - high


def contract(left, right):
    return lax.dot_general(
        left.astype(jnp.bfloat16),
        right.astype(jnp.bfloat16),
        (((0,), (0,)), ((), ())),
        preferred_element_type=jnp.float32,
    )


def strip(main, side, is_alpha, first_cycle, radial_count):
    lane, sub = iota(1), iota(0)
    lower4 = sub < 4
    column = sub & 3

    cells = lamination(main[0], main[1])
    rims = lamination(side[0], side[1])
    tiles = [cells.map(lambda part: part[:, :LANES]), cells.map(lambda part: part[:, LANES:])]
    cycle = (first_cycle + sub - 1).astype(jnp.float32)
    center = 1.0 + (cycle + 0.5) / radial_count
    face = 1.0 + cycle / radial_count
    per_center = 1.0 / center
    first_lane, last_lane = lane == 0, lane == LANES - 1

    ahead = [tile.lanes(1) for tile in tiles]
    west = [
        harmonic(pick(first_lane, rims.lanes(1), ahead[0]), tiles[0]) * per_center,
        harmonic(pick(first_lane, ahead[0], ahead[1]), tiles[1]) * per_center,
    ]
    wall = harmonic(tiles[1], rims.lanes(-1)) * per_center * 2.0
    back = [tile.lanes(-1) for tile in west]
    east = [pick(last_lane, back[1], back[0]), pick(last_lane, wall, back[1])]
    west[0] = pick(first_lane, west[0] * 2.0, west[0])
    south, north = [], []
    for tile in tiles:
        radial = harmonic(tile.subs(1), tile) * face
        radial = pick((sub == 1) | (sub == 5), radial * 2.0, radial)
        south.append(radial)
        north.append(radial.subs(-1))
    diagonal = [west[h] + east[h] + south[h] + north[h] for h in range(2)]
    gain_in = [south[h].row(1) for h in range(2)]
    gain_out = [north[h].row(4) for h in range(2)]

    diag_e, diag_o = evens(diagonal)
    east_e, east_o = evens(east)
    up_e, up_o = evens(north)
    left_e = pick(last_lane, east_o, 0.0)
    left_e = (east_o - left_e).lanes(1)

    def entry_e(r, c):
        if r == c:
            return diag_e.row(r + 1)
        return -up_e.row(r)

    lower_e, pivots_e = {}, []
    work = diag_e.row(1)
    for r in range(4):
        pivots_e.append(work.inverse())
        if r < 3:
            coupling = up_e.row(r + 1)
            lower_e[r + 1, r] = -(coupling * pivots_e[r])
            work = diag_e.row(r + 2) + lower_e[r + 1, r] * coupling
    zero = jnp.zeros((8, LANES), jnp.float32)
    nothing = Cx(zero, zero)
    half = []
    for r in range(4):
        value = Cx(jnp.where(column == r, 1.0, zero), zero)
        if r:
            value = value - lower_e[r, r - 1] * half[r - 1]
        half.append(value)
    inverse_e = [None] * 4
    for r in range(3, -1, -1):
        value = half[r] * pivots_e[r]
        if r < 3:
            value = value - lower_e[r + 1, r] * inverse_e[r + 1]
        inverse_e[r] = value
    for r in range(4):
        for c in range(r - 1):
            lower_e[r, c] = nothing
    seeds_e = seeds(lower_e, pivots_e)
    sides_e = pick(lower4, left_e.subs(-1), east_e.subs(3))
    reach_e = [inverse_e[r] * sides_e for r in range(4)]
    matrix, pair = [], []
    for r in range(4):
        to_left = (left_e.row(r + 1) * reach_e[r]).lanes(-1)
        to_right = east_e.row(r + 1) * reach_e[r]
        pair.append(pick(lower4, to_right, to_left))
        change = pick(lower4, to_left, to_right)
        base = pick(column == r, diag_o.row(r + 1), 0.0)
        if r < 3:
            base = pick(column == r + 1, -up_o.row(r + 1), base)
        if r > 0:
            base = pick(column == r - 1, -up_o.row(r), base)
        matrix.append(base - change - change.subs(4))

    for level in range(1, 8):
        step = 1 << (level - 1)
        stay = ((lane + 1) & (2 * step - 1)) == 0
        reach = solve(*factor(lambda r, c: matrix[r].row(c)), pair)
        next_matrix, next_pair = [], []
        for r in range(4):
            to_left = total(pair[k].row(r) * reach[k] for k in range(4)).lanes(-step)
            to_right = total(pair[k].row(4 + r) * reach[k] for k in range(4)).lanes(step)
            change = pick(lower4, to_left, to_right)
            change = change + change.subs(4)
            next_matrix.append(pick(stay, matrix[r] - change, matrix[r]))
            next_pair.append(pick(stay, pick(lower4, to_right, to_left), pair[r]))
        matrix, pair = next_matrix, next_pair

    lower, pivots = factor(lambda r, c: matrix[r].row(c))
    reach = solve(lower, pivots, pair)
    reach_rows = [[reach[r].row(k) for k in range(8)] for r in range(4)]
    seed = seeds(lower, pivots)

    def level_of(group):
        return jnp.where(lower4, 2 * group - 1, 2 * group)

    own_level = jnp.ones((8, LANES), jnp.int32)
    for level in range(2, 9):
        own_level = own_level + (((lane + 1) & ((1 << (level - 1)) - 1)) == 0).astype(jnp.int32)

    odd = {}
    for group in range(1, GROUPS + 1):
        rows = [pick(own_level == level_of(group), seed[r], 0.0) for r in range(4)]
        for level in range(min(2 * group - 1, 7), 0, -1):
            step = 1 << (level - 1)
            here = own_level == level
            before = [row.lanes(step) for row in rows]
            after = [row.lanes(-step) for row in rows]
            fresh = []
            for r in range(4):
                terms = [reach_rows[r][k] * before[k] for k in range(4)]
                terms += [reach_rows[r][4 + k] * after[k] for k in range(4)]
                fresh.append(rows[r] + pick(here, total(terms), 0.0))
            rows = fresh
        odd[group] = rows

    reach_e_rows = [[reach_e[r].row(k) for k in range(8)] for r in range(4)]
    even = {0: [pick(first_lane & lower4, seeds_e[r], 0.0) for r in range(4)]}
    odd[0] = [nothing] * 4
    for group in range(1, GROUPS + 1):
        before = [row.lanes(1) for row in odd[group]]
        even[group] = []
        for r in range(4):
            terms = [reach_e_rows[r][k] * before[k] for k in range(4)]
            terms += [reach_e_rows[r][4 + k] * odd[group][k] for k in range(4)]
            even[group].append(total(terms))

    def corners(lefts, rights):
        return pick(
            lane == 0,
            lefts[0],
            pick(
                lane == 1,
                lefts[1].lanes(1),
                pick(lane == 2, rights[0].lanes(3), pick(lane == 3, rights[1].lanes(4), 0.0)),
            ),
        )

    gains_left = [west[0].row(r + 1) for r in range(4)]
    gains_right = [east[1].row(r + 1) for r in range(4)]
    gain_corner = [
        corners(gains_left[2 * t : 2 * t + 2], gains_right[2 * t : 2 * t + 2]) for t in range(2)
    ]
    inner, outer, corner = {}, {}, {}
    for group in range(GROUPS + 1):
        if group:
            low = natural(even[group][0], odd[group][0])
            high = natural(even[group][3], odd[group][3])
        else:
            low, high = [even[0][0], nothing], [even[0][3], nothing]
        inner[group] = [low[h] * gain_in[h] for h in range(2)]
        outer[group] = [high[h] * gain_out[h] for h in range(2)]
        corner[group] = [
            corners(even[group][2 * t : 2 * t + 2], odd[group][2 * t : 2 * t + 2]) * gain_corner[t]
            for t in range(2)
        ]

    left_parts, right_parts = [], []
    for group in range(GROUPS + 1):
        if group in (0, GROUPS):
            low, high = inner[group], outer[group]
        else:
            near = lane < (2 << level_of(group))
            low = [pick(near, inner[group][0], 0.0), nothing]
            high = [pick(near, outer[group][0], 0.0), nothing]
        side_a, side_b = corner[group]
        own = [pick(is_alpha, low[h], high[h]) for h in range(2)]
        own.append(pick(is_alpha, side_a, side_b))
        moved = [high[0].lanes(4), high[1].lanes(4)]
        every = [
            low[0],
            low[1],
            pick(lower_lanes(lane, 4), side_a, moved[0]),
            pick(lower_lanes(lane, 4), moved[0], moved[1]),
            pick(lower_lanes(lane, 4), moved[1], pick(lane < 8, side_b.lanes(4), 0.0)),
        ]
        left_parts.append([split(value) for value in own])
        right_parts.append([split(value) for value in every])

    def wide(parts, which, name, sign=1.0):
        rows = []
        for group in parts:
            pieces = [getattr(value[which], name) for value in group]
            rows.append(jnp.concatenate(pieces, axis=1) * sign)
        return rows

    fill = [jnp.zeros((8, 3 * LANES), jnp.float32)] * 2
    left = (
        wide(left_parts, 0, "re")
        + wide(left_parts, 0, "re")
        + wide(left_parts, 1, "re")
        + wide(left_parts, 0, "im")
        + wide(left_parts, 0, "im")
        + wide(left_parts, 1, "im")
        + fill
    )
    fill = [jnp.zeros((8, 5 * LANES), jnp.float32)] * 2
    right_re = (
        wide(right_parts, 0, "re")
        + wide(right_parts, 1, "re")
        + wide(right_parts, 0, "re")
        + wide(right_parts, 0, "im", -1.0)
        + wide(right_parts, 1, "im", -1.0)
        + wide(right_parts, 0, "im", -1.0)
        + fill
    )
    right_im = (
        wide(right_parts, 0, "im")
        + wide(right_parts, 1, "im")
        + wide(right_parts, 0, "im")
        + wide(right_parts, 0, "re")
        + wide(right_parts, 1, "re")
        + wide(right_parts, 0, "re")
        + fill
    )
    left = jnp.concatenate(left, axis=0)
    top = Cx(
        contract(left, jnp.concatenate(right_re, axis=0)),
        contract(left, jnp.concatenate(right_im, axis=0)),
    )

    masks = []
    for level in range(1, 7):
        for tile in range(max((1 << (6 - level)) // 2, 1)):
            masks.append((level, (lane >> (level + 1)) == 2 * tile + (sub >> 2)))

    def spread(value):
        out = []
        for level, mask in masks:
            out.append(jnp.where(mask, value[level], 0.0))
        return jnp.concatenate(out, axis=0)

    def both(values, half):
        levels = {}
        for group in range(1, GROUPS):
            value = values[group][half]
            if half == 0:
                value = pick(lane < (2 << level_of(group)), nothing, value)
            turned = value.subs(4)
            levels[2 * group - 1] = split(pick(lower4, value, turned))
            levels[2 * group] = split(pick(lower4, turned, value))
        return {
            (which, name): spread(
                {level: getattr(pair[which], name) for level, pair in levels.items()}
            )
            for which in range(2)
            for name in ("re", "im")
        }

    even_d = [inverse_e[0].row(0), inverse_e[0].row(3), inverse_e[3].row(3)]
    even_d = [natural(value, nothing) for value in even_d]
    local = []
    for half in range(2):
        low, high = both(inner, half), both(outer, half)
        own = {key: jnp.where(is_alpha, low[key], high[key]) for key in low}
        every = {key: jnp.concatenate([low[key], high[key]], axis=1) for key in low}
        hr, hi, lr, li = (0, "re"), (0, "im"), (1, "re"), (1, "im")
        left = jnp.concatenate([own[key] for key in (hr, hi, hr, hi, lr, li)], axis=0)
        right_re = jnp.concatenate(
            [every[hr], -every[hi], every[lr], -every[li], every[hr], -every[hi]], axis=0
        )
        right_im = jnp.concatenate([every[key] for key in (hi, hr, li, lr, hi, hr)], axis=0)
        product = Cx(contract(left, right_re), contract(left, right_im))
        g_in, g_out = gain_in[half], gain_out[half]
        solo = (lane & 1) == 0
        if half == 0:
            solo = solo & (lane > 0)
        cross = even_d[1][half] * g_in * g_out
        on_in = pick(is_alpha, even_d[0][half] * g_in * g_in, cross)
        on_out = pick(is_alpha, cross, even_d[2][half] * g_out * g_out)
        on_in = pick(solo, on_in, 0.0) - pick(is_alpha, g_in, nothing)
        on_out = pick(solo, on_out, 0.0) - pick(is_alpha, nothing, g_out)
        local.append((product, on_in, on_out))
    edge = pick((lane == sub) & lower4, pick(is_alpha, gain_corner[0], gain_corner[1]), 0.0)
    return top, local, edge


def lower_lanes(lane, count):
    return lane < count


def finish(top, local, edge, is_alpha, store):
    lane, sub = iota(1), iota(0)
    full = [top.re, top.im]
    for half in range(2):
        for row in range(0, LANES, 8):
            here = lane == sub + row
            at = half * LANES + row
            both = []
            for part, name in enumerate(("re", "im")):
                product, on_in, on_out = [getattr(value, name) for value in local[half]]
                low = product[row : row + 8, :LANES] + jnp.where(here, on_in, 0.0)
                high = product[row : row + 8, LANES:] + jnp.where(here, on_out, 0.0)
                high = lane_roll(high, 4)
                out = [full[part][at : at + 8, t * LANES : (t + 1) * LANES] for t in range(5)]
                out[half] = out[half] + low
                out[2 + half] = out[2 + half] + jnp.where(lane < 4, 0.0, high)
                out[3 + half] = out[3 + half] + jnp.where(lane < 4, high, 0.0)
                both.append([-value for value in out])
            store(at, 8, both)
    at = 2 * LANES
    both = []
    for part, name in enumerate(("re", "im")):
        edge_part = getattr(edge, name)
        out = [full[part][at : at + 8, t * LANES : (t + 1) * LANES] for t in range(5)]
        out[2] = out[2] - jnp.where(is_alpha, edge_part, 0.0)
        out[4] = out[4] - jnp.where(is_alpha, 0.0, lane_roll(edge_part, 4))
        both.append([-value for value in out])
    store(at, 4, both)


def interleaved(first, second, half):
    sub = iota(0)
    index = 4 * half + (sub >> 1)
    return jnp.where((sub & 1) == 0, sub_take(first, index), sub_take(second, index))


def cell_data(ref, angular):
    value = ref[...]
    levels = value[:2].astype(jnp.int32)
    lookups = []
    for row in (4, 5):
        table = jnp.broadcast_to(value[row : row + 1, :LANES], (8, LANES))
        halves = []
        for half in range(2):
            index = levels[:, half * LANES : (half + 1) * LANES]
            index = jnp.concatenate([index] * 4, axis=0)
            halves.append(lane_take(table, index)[:2])
        lookups.append(jnp.concatenate(halves, axis=1))
    sheet = value[2:4]
    return angular * lookups[0] * sheet * sheet, lookups[1]


def gather_rows(angular, own, other, is_alpha, is_even, is_first, is_last, main, side):
    lane = lax.broadcasted_iota(jnp.int32, (2, LANES), 1)
    own, other = [[cell_data(ref, angular) for ref in refs] for refs in (own, other)]
    for field in range(2):
        (mine, near, long, short), (theirs, far, long_x, short_x) = (
            [data[field] for data in part] for part in (own, other)
        )
        alpha, beta = jnp.where(is_alpha, mine, theirs), jnp.where(is_alpha, theirs, mine)
        main[field, 0:1, :] = jnp.where(is_first, alpha[0:1], jnp.where(is_alpha, near, far)[1:2])
        main[field, 1:3, :] = alpha
        main[field, 3:5, :] = beta
        main[field, 5:6, :] = jnp.where(is_last, beta[1:2], jnp.where(is_alpha, far, near)[0:1])
        main[field, 6:8, :] = beta
        ends = []
        for longs, shorts in ((long, short), (long_x, short_x)):
            left = jnp.where(is_even, longs, shorts)[:, LANES:]
            right = jnp.where(is_even, shorts, longs)[:, :LANES]
            ends.append(jnp.where(lane == LANES - 1, left, jnp.where(lane == 0, right, 1.0)))
        ends_alpha = jnp.where(is_alpha, ends[0], ends[1])
        ends_beta = jnp.where(is_alpha, ends[1], ends[0])
        side[field, 0:1, :] = ends_alpha[0:1]
        side[field, 1:3, :] = ends_alpha
        side[field, 3:5, :] = ends_beta
        side[field, 5:7, :] = ends_beta
        side[field, 7:8, :] = ends_beta[0:1]


def merge_kernel(cycles, depth, angular, *refs):
    own, other, (out, main, side) = refs[:4], refs[4:8], refs[8:]
    index = lax.axis_index("rad")
    is_even = lax.axis_index("az") % 2 == 0
    is_alpha = index % 2 == 0
    is_first = index // 2 == 0
    is_last = index // 2 == cycles // 2 - 1
    gather_rows(angular[0], own, other, is_alpha, is_even, is_first, is_last, main, side)
    top, local, edge = strip(
        (main[0], main[1]),
        (side[0], side[1]),
        is_alpha,
        (index // 2) * (2 * depth),
        cycles * depth,
    )

    def store(row, count, both):
        for number, (real, imag) in enumerate(zip(*both)):
            at = number * LANES
            width = min(LANES, out.shape[2] - at)
            for half in range(count // 4):
                tile = interleaved(real, imag, half)
                first = row + 4 * half
                out[first : first + 4, :, at : at + width] = tile.reshape(4, 2, LANES)[
                    :, :, :width
                ]

    finish(top, local, edge, is_alpha, store)


def pack_kernel(*refs):
    sources, (out_ref,), targets, sems = refs[:4], refs[4:5], refs[5:9], refs[9]
    copies = [
        pltpu.make_async_copy(source, target, sems.at[number])
        for number, (source, target) in enumerate(zip(sources, targets))
    ]
    for copy in copies:
        copy.start()
    for copy in copies:
        copy.wait()
    material_ref, sheet_ref, sigma_ref, nu_ref = targets
    out_ref[:2, :] = material_ref[...].astype(jnp.float32)
    out_ref[2:4, :] = sheet_ref[...]
    for row, ref in ((4, sigma_ref), (5, nu_ref)):
        out_ref[row : row + 1, : ref.shape[0]] = ref[...].reshape(1, ref.shape[0])


def packed(*arguments):
    held = [pltpu.with_memory_space_constraint(value, pltpu.HBM) for value in arguments]
    return pl.pallas_call(
        pack_kernel,
        out_shape=jax.ShapeDtypeStruct((8, arguments[1].shape[1]), jnp.float32),
        in_specs=[pl.BlockSpec(memory_space=pltpu.HBM)] * 4,
        out_specs=pl.BlockSpec(memory_space=pltpu.VMEM),
        scratch_shapes=[pltpu.VMEM(value.shape, value.dtype) for value in arguments]
        + [pltpu.SemaphoreType.DMA((4,))],
        compiler_params=pltpu.CompilerParams(vmem_limit_bytes=4 * 1024 * 1024),
        name="cells",
    )(*held)


def swapped(cells, axis, first):
    count = lax.axis_size(axis)
    route = []
    for low in range(first, count, 2):
        high = (low + 1) % count
        route += [(low, high), (high, low)]
    return lax.ppermute(cells, axis, route)


def per_device(material_id, thickness, sigma_table, nu_table, angular_frequency):
    depth, arc = thickness.shape
    cells = packed(material_id, thickness, sigma_table, nu_table)
    cycles = lax.axis_size("rad")
    own = [cells, swapped(cells, "rad", 1), swapped(cells, "az", 1), swapped(cells, "az", 0)]
    other = [swapped(part, "rad", 0) for part in own]
    outer_nodes = arc + 2 * depth
    out = pl.pallas_call(
        lambda *refs: merge_kernel(cycles, depth, *refs),
        out_shape=jax.ShapeDtypeStruct((outer_nodes, 2, 2 * outer_nodes), jnp.float32),
        in_specs=[pl.BlockSpec(memory_space=pltpu.SMEM)]
        + [pl.BlockSpec(memory_space=pltpu.VMEM)] * 8,
        out_specs=pl.BlockSpec(memory_space=pltpu.VMEM),
        scratch_shapes=[
            pltpu.VMEM((2, 8, arc), jnp.float32),
            pltpu.VMEM((2, 8, LANES), jnp.float32),
        ],
        compiler_params=pltpu.CompilerParams(vmem_limit_bytes=48 * 1024 * 1024),
        name="pair_map",
    )(angular_frequency, *own, *other)
    return jnp.transpose(out, (1, 0, 2))


def solution(mesh):
    placed = (P("rad", "az"), P("rad", "az"), P(), P(), P())
    return jax.shard_map(
        per_device, mesh=mesh, in_specs=placed, out_specs=P(None, "rad", "az"), check_vma=False
    )
```

```python
import jax
import jax.numpy as jnp
from jax import lax
from jax.experimental import pallas as pl
from jax.experimental.pallas import tpu as pltpu
from jax.sharding import PartitionSpec as P

SHEET_NODES = 16
LANES = 128
GROUPS = 4


def lane_roll(value, shift):
    return pltpu.roll(value, shift % value.shape[1], 1)


def sub_roll(value, shift):
    return pltpu.roll(value, shift % value.shape[0], 0)


def lane_take(value, index):
    return jnp.take_along_axis(value, index, axis=1, mode="promise_in_bounds")


def sub_take(value, index):
    return jnp.take_along_axis(value, index, axis=0, mode="promise_in_bounds")


def iota(dim):
    return lax.broadcasted_iota(jnp.int32, (8, LANES), dim)


class Cx:
    def __init__(self, re, im):
        self.re, self.im = re, im

    def __add__(self, other):
        return Cx(self.re + other.re, self.im + other.im)

    def __sub__(self, other):
        return Cx(self.re - other.re, self.im - other.im)

    def __neg__(self):
        return Cx(-self.re, -self.im)

    def __mul__(self, other):
        if not isinstance(other, Cx):
            return Cx(self.re * other, self.im * other)
        return Cx(
            self.re * other.re - self.im * other.im, self.re * other.im + self.im * other.re
        )

    def inverse(self):
        scale = 1.0 / (self.re * self.re + self.im * self.im)
        return Cx(self.re * scale, -self.im * scale)

    def root(self):
        size = jnp.sqrt(self.re * self.re + self.im * self.im)
        re = jnp.sqrt(0.5 * (size + self.re))
        return Cx(re, 0.5 * self.im / re)

    def map(self, function):
        return Cx(function(self.re), function(self.im))

    def row(self, index):
        return self.map(lambda part: jnp.broadcast_to(part[index : index + 1], (8, LANES)))

    def lanes(self, shift):
        return self.map(lambda part: lane_roll(part, shift))

    def subs(self, shift):
        return self.map(lambda part: sub_roll(part, shift))


def pick(mask, first, second):
    if not isinstance(second, Cx):
        return first.map(lambda part: jnp.where(mask, part, second))
    return Cx(jnp.where(mask, first.re, second.re), jnp.where(mask, first.im, second.im))


def total(terms):
    terms = list(terms)
    while len(terms) > 1:
        terms = [
            terms[i] + terms[i + 1] if i + 1 < len(terms) else terms[i]
            for i in range(0, len(terms), 2)
        ]
    return terms[0]


def harmonic(left, right):
    return (left * right) * (left + right).inverse() * 2.0


def lamination(skin, base):
    above = Cx(jnp.ones_like(skin), jnp.zeros_like(skin))
    field = Cx(jnp.ones_like(skin), 0.5 * skin)
    summed = above
    for _ in range(SHEET_NODES - 1):
        summed = summed + field
        below = Cx(
            2.0 * field.re - skin * field.im - above.re,
            2.0 * field.im + skin * field.re - above.im,
        )
        above, field = field, below
    return field * summed.inverse() * (base * SHEET_NODES)


def factor(entry):
    work = {(r, c): entry(r, c) for r in range(4) for c in range(r + 1)}
    lower, pivots = {}, []
    for k in range(4):
        inverse = work[k, k].inverse()
        pivots.append(inverse)
        for r in range(k + 1, 4):
            lower[r, k] = work[r, k] * inverse
        for r in range(k + 1, 4):
            for c in range(k + 1, r + 1):
                work[r, c] = work[r, c] - lower[r, k] * work[c, k]
    return lower, pivots


def solve(lower, pivots, right):
    half = []
    for r in range(4):
        value = right[r]
        for c in range(r):
            value = value - lower[r, c] * half[c]
        half.append(value)
    out = [None] * 4
    for r in range(3, -1, -1):
        value = half[r] * pivots[r]
        for c in range(r + 1, 4):
            value = value - lower[c, r] * out[c]
        out[r] = value
    return out


def seeds(lower, pivots):
    column = iota(0) & 3
    unit = {}
    for r in range(4):
        for c in range(r - 1, -1, -1):
            value = -lower[r, c]
            for k in range(c + 1, r):
                value = value - lower[r, k] * unit[k, c]
            unit[r, c] = value
    roots = [pivot.root() for pivot in pivots]
    out = []
    for r in range(4):
        value = pick(column == r, roots[r], 0.0)
        for k in range(r + 1, 4):
            value = pick(column == k, roots[k] * unit[k, r], value)
        out.append(value)
    return out


def evens(tiles):
    lane = iota(1)
    index = (2 * lane) & (LANES - 1)

    def one(offset):
        return Cx(
            *(
                jnp.where(
                    lane < LANES // 2,
                    lane_take(first, index + offset),
                    lane_take(second, index + offset),
                )
                for first, second in ((tiles[0].re, tiles[1].re), (tiles[0].im, tiles[1].im))
            )
        )

    return one(0), one(1)


def natural(even, odd):
    lane = iota(1)
    out = []
    for half in range(2):
        index = half * (LANES // 2) + (lane >> 1)
        out.append(
            Cx(
                *(
                    jnp.where((lane & 1) == 0, lane_take(first, index), lane_take(second, index))
                    for first, second in ((even.re, odd.re), (even.im, odd.im))
                )
            )
        )
    return out


def split(value):
    high = value.map(lambda part: part.astype(jnp.bfloat16).astype(jnp.float32))
    return high, value - high


def contract(left, right):
    return lax.dot_general(
        left.astype(jnp.bfloat16),
        right.astype(jnp.bfloat16),
        (((0,), (0,)), ((), ())),
        preferred_element_type=jnp.float32,
    )


def strip(main, side, is_alpha, first_cycle, radial_count):
    lane, sub = iota(1), iota(0)
    lower4 = sub < 4
    column = sub & 3

    cells = lamination(main[0], main[1])
    rims = lamination(side[0], side[1])
    tiles = [cells.map(lambda part: part[:, :LANES]), cells.map(lambda part: part[:, LANES:])]
    cycle = (first_cycle + sub - 1).astype(jnp.float32)
    center = 1.0 + (cycle + 0.5) / radial_count
    face = 1.0 + cycle / radial_count
    per_center = 1.0 / center
    first_lane, last_lane = lane == 0, lane == LANES - 1

    ahead = [tile.lanes(1) for tile in tiles]
    west = [
        harmonic(pick(first_lane, rims.lanes(1), ahead[0]), tiles[0]) * per_center,
        harmonic(pick(first_lane, ahead[0], ahead[1]), tiles[1]) * per_center,
    ]
    wall = harmonic(tiles[1], rims.lanes(-1)) * per_center * 2.0
    back = [tile.lanes(-1) for tile in west]
    east = [pick(last_lane, back[1], back[0]), pick(last_lane, wall, back[1])]
    west[0] = pick(first_lane, west[0] * 2.0, west[0])
    south, north = [], []
    for tile in tiles:
        radial = harmonic(tile.subs(1), tile) * face
        radial = pick((sub == 1) | (sub == 5), radial * 2.0, radial)
        south.append(radial)
        north.append(radial.subs(-1))
    diagonal = [west[h] + east[h] + south[h] + north[h] for h in range(2)]
    gain_in = [south[h].row(1) for h in range(2)]
    gain_out = [north[h].row(4) for h in range(2)]

    diag_e, diag_o = evens(diagonal)
    east_e, east_o = evens(east)
    up_e, up_o = evens(north)
    left_e = pick(last_lane, east_o, 0.0)
    left_e = (east_o - left_e).lanes(1)

    def entry_e(r, c):
        if r == c:
            return diag_e.row(r + 1)
        return -up_e.row(r)

    lower_e, pivots_e = {}, []
    work = diag_e.row(1)
    for r in range(4):
        pivots_e.append(work.inverse())
        if r < 3:
            coupling = up_e.row(r + 1)
            lower_e[r + 1, r] = -(coupling * pivots_e[r])
            work = diag_e.row(r + 2) + lower_e[r + 1, r] * coupling
    zero = jnp.zeros((8, LANES), jnp.float32)
    nothing = Cx(zero, zero)
    half = []
    for r in range(4):
        value = Cx(jnp.where(column == r, 1.0, zero), zero)
        if r:
            value = value - lower_e[r, r - 1] * half[r - 1]
        half.append(value)
    inverse_e = [None] * 4
    for r in range(3, -1, -1):
        value = half[r] * pivots_e[r]
        if r < 3:
            value = value - lower_e[r + 1, r] * inverse_e[r + 1]
        inverse_e[r] = value
    for r in range(4):
        for c in range(r - 1):
            lower_e[r, c] = nothing
    seeds_e = seeds(lower_e, pivots_e)
    sides_e = pick(lower4, left_e.subs(-1), east_e.subs(3))
    reach_e = [inverse_e[r] * sides_e for r in range(4)]
    matrix, pair = [], []
    for r in range(4):
        to_left = (left_e.row(r + 1) * reach_e[r]).lanes(-1)
        to_right = east_e.row(r + 1) * reach_e[r]
        pair.append(pick(lower4, to_right, to_left))
        change = pick(lower4, to_left, to_right)
        base = pick(column == r, diag_o.row(r + 1), 0.0)
        if r < 3:
            base = pick(column == r + 1, -up_o.row(r + 1), base)
        if r > 0:
            base = pick(column == r - 1, -up_o.row(r), base)
        matrix.append(base - change - change.subs(4))

    for level in range(1, 8):
        step = 1 << (level - 1)
        stay = ((lane + 1) & (2 * step - 1)) == 0
        reach = solve(*factor(lambda r, c: matrix[r].row(c)), pair)
        next_matrix, next_pair = [], []
        for r in range(4):
            to_left = total(pair[k].row(r) * reach[k] for k in range(4)).lanes(-step)
            to_right = total(pair[k].row(4 + r) * reach[k] for k in range(4)).lanes(step)
            change = pick(lower4, to_left, to_right)
            change = change + change.subs(4)
            next_matrix.append(pick(stay, matrix[r] - change, matrix[r]))
            next_pair.append(pick(stay, pick(lower4, to_right, to_left), pair[r]))
        matrix, pair = next_matrix, next_pair

    lower, pivots = factor(lambda r, c: matrix[r].row(c))
    reach = solve(lower, pivots, pair)
    reach_rows = [[reach[r].row(k) for k in range(8)] for r in range(4)]
    seed = seeds(lower, pivots)

    def level_of(group):
        return jnp.where(lower4, 2 * group - 1, 2 * group)

    own_level = jnp.ones((8, LANES), jnp.int32)
    for level in range(2, 9):
        own_level = own_level + (((lane + 1) & ((1 << (level - 1)) - 1)) == 0).astype(jnp.int32)

    odd = {}
    for group in range(1, GROUPS + 1):
        rows = [pick(own_level == level_of(group), seed[r], 0.0) for r in range(4)]
        for level in range(min(2 * group - 1, 7), 0, -1):
            step = 1 << (level - 1)
            here = own_level == level
            before = [row.lanes(step) for row in rows]
            after = [row.lanes(-step) for row in rows]
            fresh = []
            for r in range(4):
                terms = [reach_rows[r][k] * before[k] for k in range(4)]
                terms += [reach_rows[r][4 + k] * after[k] for k in range(4)]
                fresh.append(rows[r] + pick(here, total(terms), 0.0))
            rows = fresh
        odd[group] = rows

    reach_e_rows = [[reach_e[r].row(k) for k in range(8)] for r in range(4)]
    even = {0: [pick(first_lane & lower4, seeds_e[r], 0.0) for r in range(4)]}
    odd[0] = [nothing] * 4
    for group in range(1, GROUPS + 1):
        before = [row.lanes(1) for row in odd[group]]
        even[group] = []
        for r in range(4):
            terms = [reach_e_rows[r][k] * before[k] for k in range(4)]
            terms += [reach_e_rows[r][4 + k] * odd[group][k] for k in range(4)]
            even[group].append(total(terms))

    def corners(lefts, rights):
        return pick(
            lane == 0,
            lefts[0],
            pick(
                lane == 1,
                lefts[1].lanes(1),
                pick(lane == 2, rights[0].lanes(3), pick(lane == 3, rights[1].lanes(4), 0.0)),
            ),
        )

    gains_left = [west[0].row(r + 1) for r in range(4)]
    gains_right = [east[1].row(r + 1) for r in range(4)]
    gain_corner = [
        corners(gains_left[2 * t : 2 * t + 2], gains_right[2 * t : 2 * t + 2]) for t in range(2)
    ]
    inner, outer, corner = {}, {}, {}
    for group in range(GROUPS + 1):
        if group:
            low = natural(even[group][0], odd[group][0])
            high = natural(even[group][3], odd[group][3])
        else:
            low, high = [even[0][0], nothing], [even[0][3], nothing]
        inner[group] = [low[h] * gain_in[h] for h in range(2)]
        outer[group] = [high[h] * gain_out[h] for h in range(2)]
        corner[group] = [
            corners(even[group][2 * t : 2 * t + 2], odd[group][2 * t : 2 * t + 2]) * gain_corner[t]
            for t in range(2)
        ]

    left_parts, right_parts = [], []
    for group in range(GROUPS + 1):
        if group in (0, GROUPS):
            low, high = inner[group], outer[group]
        else:
            near = lane < (2 << level_of(group))
            low = [pick(near, inner[group][0], 0.0), nothing]
            high = [pick(near, outer[group][0], 0.0), nothing]
        side_a, side_b = corner[group]
        own = [pick(is_alpha, low[h], high[h]) for h in range(2)]
        own.append(pick(is_alpha, side_a, side_b))
        moved = [high[0].lanes(4), high[1].lanes(4)]
        every = [
            low[0],
            low[1],
            pick(lower_lanes(lane, 4), side_a, moved[0]),
            pick(lower_lanes(lane, 4), moved[0], moved[1]),
            pick(lower_lanes(lane, 4), moved[1], pick(lane < 8, side_b.lanes(4), 0.0)),
        ]
        left_parts.append([split(value) for value in own])
        right_parts.append([split(value) for value in every])

    def wide(parts, which, name, sign=1.0):
        rows = []
        for group in parts:
            pieces = [getattr(value[which], name) for value in group]
            rows.append(jnp.concatenate(pieces, axis=1) * sign)
        return rows

    fill = [jnp.zeros((8, 3 * LANES), jnp.float32)] * 2
    left = (
        wide(left_parts, 0, "re")
        + wide(left_parts, 0, "re")
        + wide(left_parts, 1, "re")
        + wide(left_parts, 0, "im")
        + wide(left_parts, 0, "im")
        + wide(left_parts, 1, "im")
        + fill
    )
    fill = [jnp.zeros((8, 5 * LANES), jnp.float32)] * 2
    right_re = (
        wide(right_parts, 0, "re")
        + wide(right_parts, 1, "re")
        + wide(right_parts, 0, "re")
        + wide(right_parts, 0, "im", -1.0)
        + wide(right_parts, 1, "im", -1.0)
        + wide(right_parts, 0, "im", -1.0)
        + fill
    )
    right_im = (
        wide(right_parts, 0, "im")
        + wide(right_parts, 1, "im")
        + wide(right_parts, 0, "im")
        + wide(right_parts, 0, "re")
        + wide(right_parts, 1, "re")
        + wide(right_parts, 0, "re")
        + fill
    )
    left = jnp.concatenate(left, axis=0)
    top = Cx(
        contract(left, jnp.concatenate(right_re, axis=0)),
        contract(left, jnp.concatenate(right_im, axis=0)),
    )

    masks = []
    for level in range(1, 7):
        for tile in range(max((1 << (6 - level)) // 2, 1)):
            masks.append((level, (lane >> (level + 1)) == 2 * tile + (sub >> 2)))

    def spread(value):
        out = []
        for level, mask in masks:
            out.append(jnp.where(mask, value[level], 0.0))
        return jnp.concatenate(out, axis=0)

    def both(values, half):
        levels = {}
        for group in range(1, GROUPS):
            value = values[group][half]
            if half == 0:
                value = pick(lane < (2 << level_of(group)), nothing, value)
            turned = value.subs(4)
            levels[2 * group - 1] = split(pick(lower4, value, turned))
            levels[2 * group] = split(pick(lower4, turned, value))
        return {
            (which, name): spread(
                {level: getattr(pair[which], name) for level, pair in levels.items()}
            )
            for which in range(2)
            for name in ("re", "im")
        }

    even_d = [inverse_e[0].row(0), inverse_e[0].row(3), inverse_e[3].row(3)]
    even_d = [natural(value, nothing) for value in even_d]

    def local(half):
        low, high = both(inner, half), both(outer, half)
        own = {key: jnp.where(is_alpha, low[key], high[key]) for key in low}
        every = {key: jnp.concatenate([low[key], high[key]], axis=1) for key in low}
        hr, hi, lr, li = (0, "re"), (0, "im"), (1, "re"), (1, "im")
        left = jnp.concatenate([own[key] for key in (hr, hi, hr, hi, lr, li)], axis=0)
        right_re = jnp.concatenate(
            [every[hr], -every[hi], every[lr], -every[li], every[hr], -every[hi]], axis=0
        )
        right_im = jnp.concatenate([every[key] for key in (hi, hr, li, lr, hi, hr)], axis=0)
        product = Cx(contract(left, right_re), contract(left, right_im))
        g_in, g_out = gain_in[half], gain_out[half]
        solo = (lane & 1) == 0
        if half == 0:
            solo = solo & (lane > 0)
        cross = even_d[1][half] * g_in * g_out
        on_in = pick(is_alpha, even_d[0][half] * g_in * g_in, cross)
        on_out = pick(is_alpha, cross, even_d[2][half] * g_out * g_out)
        on_in = pick(solo, on_in, 0.0) - pick(is_alpha, g_in, nothing)
        on_out = pick(solo, on_out, 0.0) - pick(is_alpha, nothing, g_out)
        return product, on_in, on_out

    edge = pick((lane == sub) & lower4, pick(is_alpha, gain_corner[0], gain_corner[1]), 0.0)
    return top, local, edge


def lower_lanes(lane, count):
    return lane < count


def finish(top, local, edge, is_alpha, store):
    lane, sub = iota(1), iota(0)
    full = [top.re, top.im]
    for half in range(2):
        terms = local(half)
        for row in range(0, LANES, 8):
            here = lane == sub + row
            at = half * LANES + row
            both = []
            for part, name in enumerate(("re", "im")):
                product, on_in, on_out = [getattr(value, name) for value in terms]
                low = product[row : row + 8, :LANES] + jnp.where(here, on_in, 0.0)
                high = product[row : row + 8, LANES:] + jnp.where(here, on_out, 0.0)
                high = lane_roll(high, 4)
                out = [full[part][at : at + 8, t * LANES : (t + 1) * LANES] for t in range(5)]
                out[half] = out[half] + low
                out[2 + half] = out[2 + half] + jnp.where(lane < 4, 0.0, high)
                out[3 + half] = out[3 + half] + jnp.where(lane < 4, high, 0.0)
                both.append([-value for value in out])
            store(at, 8, both)
    at = 2 * LANES
    both = []
    for part, name in enumerate(("re", "im")):
        edge_part = getattr(edge, name)
        out = [full[part][at : at + 8, t * LANES : (t + 1) * LANES] for t in range(5)]
        out[2] = out[2] - jnp.where(is_alpha, edge_part, 0.0)
        out[4] = out[4] - jnp.where(is_alpha, 0.0, lane_roll(edge_part, 4))
        both.append([-value for value in out])
    store(at, 4, both)


def interleaved(first, second, half):
    sub = iota(0)
    index = 4 * half + (sub >> 1)
    return jnp.where((sub & 1) == 0, sub_take(first, index), sub_take(second, index))


def cell_data(ref, angular):
    value = ref[...]
    levels = value[:2].astype(jnp.int32)
    lookups = []
    for row in (4, 5):
        table = jnp.broadcast_to(value[row : row + 1, :LANES], (8, LANES))
        halves = []
        for half in range(2):
            index = levels[:, half * LANES : (half + 1) * LANES]
            index = jnp.concatenate([index] * 4, axis=0)
            halves.append(lane_take(table, index)[:2])
        lookups.append(jnp.concatenate(halves, axis=1))
    sheet = value[2:4]
    return angular * lookups[0] * sheet * sheet, lookups[1]


def gather_rows(angular, own, other, is_alpha, is_first, is_last, main, side):
    lane = lax.broadcasted_iota(jnp.int32, (2, LANES), 1)
    own, other = [[cell_data(ref, angular) for ref in refs] for refs in (own, other)]
    for field in range(2):
        (mine, near, after, before), (theirs, far, after_x, before_x) = (
            [data[field] for data in part] for part in (own, other)
        )
        alpha, beta = jnp.where(is_alpha, mine, theirs), jnp.where(is_alpha, theirs, mine)
        main[field, 0:1, :] = jnp.where(is_first, alpha[0:1], jnp.where(is_alpha, near, far)[1:2])
        main[field, 1:3, :] = alpha
        main[field, 3:5, :] = beta
        main[field, 5:6, :] = jnp.where(is_last, beta[1:2], jnp.where(is_alpha, far, near)[0:1])
        main[field, 6:8, :] = beta
        ends = []
        for lefts, rights in ((before, after), (before_x, after_x)):
            left, right = lefts[:, LANES:], rights[:, :LANES]
            ends.append(jnp.where(lane == LANES - 1, left, jnp.where(lane == 0, right, 1.0)))
        ends_alpha = jnp.where(is_alpha, ends[0], ends[1])
        ends_beta = jnp.where(is_alpha, ends[1], ends[0])
        side[field, 0:1, :] = ends_alpha[0:1]
        side[field, 1:3, :] = ends_alpha
        side[field, 3:5, :] = ends_beta
        side[field, 5:7, :] = ends_beta
        side[field, 7:8, :] = ends_beta[0:1]


def merge_kernel(cycles, depth, angular, *refs):
    own, other, (out, main, side, held, sems) = refs[:4], refs[4:8], refs[8:]
    index = lax.axis_index("rad")
    is_alpha = index % 2 == 0
    is_first = index // 2 == 0
    is_last = index // 2 == cycles // 2 - 1
    gather_rows(angular[0], own, other, is_alpha, is_first, is_last, main, side)
    top, local, edge = strip(
        (main[0], main[1]),
        (side[0], side[1]),
        is_alpha,
        (index // 2) * (2 * depth),
        cycles * depth,
    )
    rows = out.shape[0]
    bounds = [0, 64, 128, 192, rows]
    copies = [
        pltpu.make_async_copy(
            held.at[first : last, :, :], out.at[first : last, :, :], sems.at[number]
        )
        for number, (first, last) in enumerate(zip(bounds, bounds[1:]))
    ]

    def store(row, count, both):
        for number, (real, imag) in enumerate(zip(*both)):
            at = number * LANES
            width = min(LANES, out.shape[2] - at)
            for half in range(count // 4):
                tile = interleaved(real, imag, half)
                first = row + 4 * half
                held[first : first + 4, :, at : at + width] = tile.reshape(4, 2, LANES)[
                    :, :, :width
                ]
        if row + count in bounds:
            copies[bounds.index(row + count) - 1].start()

    finish(top, local, edge, is_alpha, store)
    for copy in copies:
        copy.wait()


def pack_kernel(*refs):
    sources, (out_ref,), targets, sems = refs[:4], refs[4:5], refs[5:9], refs[9]
    copies = [
        pltpu.make_async_copy(source, target, sems.at[number])
        for number, (source, target) in enumerate(zip(sources, targets))
    ]
    for copy in copies:
        copy.start()
    for copy in copies:
        copy.wait()
    material_ref, sheet_ref, sigma_ref, nu_ref = targets
    out_ref[:2, :] = material_ref[...].astype(jnp.float32)
    out_ref[2:4, :] = sheet_ref[...]
    for row, ref in ((4, sigma_ref), (5, nu_ref)):
        out_ref[row : row + 1, : ref.shape[0]] = ref[...].reshape(1, ref.shape[0])


def packed(*arguments):
    held = [pltpu.with_memory_space_constraint(value, pltpu.HBM) for value in arguments]
    return pl.pallas_call(
        pack_kernel,
        out_shape=jax.ShapeDtypeStruct((8, arguments[1].shape[1]), jnp.float32),
        in_specs=[pl.BlockSpec(memory_space=pltpu.HBM)] * 4,
        out_specs=pl.BlockSpec(memory_space=pltpu.VMEM),
        scratch_shapes=[pltpu.VMEM(value.shape, value.dtype) for value in arguments]
        + [pltpu.SemaphoreType.DMA((4,))],
        compiler_params=pltpu.CompilerParams(vmem_limit_bytes=4 * 1024 * 1024),
        name="cells",
    )(*held)


def swapped(cells, axis, first):
    count = lax.axis_size(axis)
    route = []
    for low in range(first, count, 2):
        high = (low + 1) % count
        route += [(low, high), (high, low)]
    return lax.ppermute(cells, axis, route)


def per_device(material_id, thickness, sigma_table, nu_table, angular_frequency):
    depth, arc = thickness.shape
    cells = packed(material_id, thickness, sigma_table, nu_table)
    cycles = lax.axis_size("rad")
    blocks = lax.axis_size("az")
    before = lax.ppermute(cells, "az", [(i, (i + 1) % blocks) for i in range(blocks)])
    after = lax.ppermute(cells, "az", [((i + 1) % blocks, i) for i in range(blocks)])
    own = [cells, swapped(cells, "rad", 1), after, before]
    other = [swapped(part, "rad", 0) for part in own]
    outer_nodes = arc + 2 * depth
    out = pl.pallas_call(
        lambda *refs: merge_kernel(cycles, depth, *refs),
        out_shape=jax.ShapeDtypeStruct((outer_nodes, 2, 2 * outer_nodes), jnp.float32),
        in_specs=[pl.BlockSpec(memory_space=pltpu.SMEM)]
        + [pl.BlockSpec(memory_space=pltpu.VMEM)] * 8,
        out_specs=pl.BlockSpec(memory_space=pltpu.HBM),
        scratch_shapes=[
            pltpu.VMEM((2, 8, arc), jnp.float32),
            pltpu.VMEM((2, 8, LANES), jnp.float32),
            pltpu.VMEM((outer_nodes, 2, 2 * outer_nodes), jnp.float32),
            pltpu.SemaphoreType.DMA((4,)),
        ],
        compiler_params=pltpu.CompilerParams(vmem_limit_bytes=48 * 1024 * 1024),
        name="pair_map",
    )(angular_frequency, *own, *other)
    return jnp.transpose(out, (1, 0, 2))


def solution(mesh):
    placed = (P("rad", "az"), P("rad", "az"), P(), P(), P())
    return jax.shard_map(
        per_device, mesh=mesh, in_specs=placed, out_specs=P(None, "rad", "az"), check_vma=False
    )
```

```python
import jax
import jax.numpy as jnp
from jax import lax
from jax.experimental import pallas as pl
from jax.experimental.pallas import tpu as pltpu
from jax.sharding import PartitionSpec as P

SHEET_NODES = 16
LANES = 128
GROUPS = 4


def lane_roll(value, shift):
    return pltpu.roll(value, shift % value.shape[1], 1)


def sub_roll(value, shift):
    return pltpu.roll(value, shift % value.shape[0], 0)


def lane_take(value, index):
    return jnp.take_along_axis(value, index, axis=1, mode="promise_in_bounds")


def sub_take(value, index):
    return jnp.take_along_axis(value, index, axis=0, mode="promise_in_bounds")


def iota(dim):
    return lax.broadcasted_iota(jnp.int32, (8, LANES), dim)


class Cx:
    def __init__(self, re, im):
        self.re, self.im = re, im

    def __add__(self, other):
        return Cx(self.re + other.re, self.im + other.im)

    def __sub__(self, other):
        return Cx(self.re - other.re, self.im - other.im)

    def __neg__(self):
        return Cx(-self.re, -self.im)

    def __mul__(self, other):
        if not isinstance(other, Cx):
            return Cx(self.re * other, self.im * other)
        return Cx(
            self.re * other.re - self.im * other.im, self.re * other.im + self.im * other.re
        )

    def inverse(self):
        scale = 1.0 / (self.re * self.re + self.im * self.im)
        return Cx(self.re * scale, -self.im * scale)

    def root(self):
        size = jnp.sqrt(self.re * self.re + self.im * self.im)
        re = jnp.sqrt(0.5 * (size + self.re))
        return Cx(re, 0.5 * self.im / re)

    def map(self, function):
        return Cx(function(self.re), function(self.im))

    def row(self, index):
        return self.map(lambda part: jnp.broadcast_to(part[index : index + 1], (8, LANES)))

    def lanes(self, shift):
        return self.map(lambda part: lane_roll(part, shift))

    def subs(self, shift):
        return self.map(lambda part: sub_roll(part, shift))


def pick(mask, first, second):
    if not isinstance(second, Cx):
        return first.map(lambda part: jnp.where(mask, part, second))
    return Cx(jnp.where(mask, first.re, second.re), jnp.where(mask, first.im, second.im))


def total(terms):
    terms = list(terms)
    while len(terms) > 1:
        terms = [
            terms[i] + terms[i + 1] if i + 1 < len(terms) else terms[i]
            for i in range(0, len(terms), 2)
        ]
    return terms[0]


def harmonic(left, right):
    return (left * right) * (left + right).inverse() * 2.0


def lamination(skin, base):
    above = Cx(jnp.ones_like(skin), jnp.zeros_like(skin))
    field = Cx(jnp.ones_like(skin), 0.5 * skin)
    summed = above
    for _ in range(SHEET_NODES - 1):
        summed = summed + field
        below = Cx(
            2.0 * field.re - skin * field.im - above.re,
            2.0 * field.im + skin * field.re - above.im,
        )
        above, field = field, below
    return field * summed.inverse() * (base * SHEET_NODES)


def factor(entry):
    work = {(r, c): entry(r, c) for r in range(4) for c in range(r + 1)}
    lower, pivots = {}, []
    for k in range(4):
        inverse = work[k, k].inverse()
        pivots.append(inverse)
        for r in range(k + 1, 4):
            lower[r, k] = work[r, k] * inverse
        for r in range(k + 1, 4):
            for c in range(k + 1, r + 1):
                work[r, c] = work[r, c] - lower[r, k] * work[c, k]
    return lower, pivots


def solve(lower, pivots, right):
    half = []
    for r in range(4):
        value = right[r]
        for c in range(r):
            value = value - lower[r, c] * half[c]
        half.append(value)
    out = [None] * 4
    for r in range(3, -1, -1):
        value = half[r] * pivots[r]
        for c in range(r + 1, 4):
            value = value - lower[c, r] * out[c]
        out[r] = value
    return out


def seeds(lower, pivots):
    column = iota(0) & 3
    unit = {}
    for r in range(4):
        for c in range(r - 1, -1, -1):
            value = -lower[r, c]
            for k in range(c + 1, r):
                value = value - lower[r, k] * unit[k, c]
            unit[r, c] = value
    roots = [pivot.root() for pivot in pivots]
    out = []
    for r in range(4):
        value = pick(column == r, roots[r], 0.0)
        for k in range(r + 1, 4):
            value = pick(column == k, roots[k] * unit[k, r], value)
        out.append(value)
    return out


def evens(tiles):
    lane = iota(1)
    index = (2 * lane) & (LANES - 1)

    def one(offset):
        return Cx(
            *(
                jnp.where(
                    lane < LANES // 2,
                    lane_take(first, index + offset),
                    lane_take(second, index + offset),
                )
                for first, second in ((tiles[0].re, tiles[1].re), (tiles[0].im, tiles[1].im))
            )
        )

    return one(0), one(1)


def natural(even, odd):
    lane = iota(1)
    out = []
    for half in range(2):
        index = half * (LANES // 2) + (lane >> 1)
        out.append(
            Cx(
                *(
                    jnp.where((lane & 1) == 0, lane_take(first, index), lane_take(second, index))
                    for first, second in ((even.re, odd.re), (even.im, odd.im))
                )
            )
        )
    return out


def split(value):
    high = value.map(lambda part: part.astype(jnp.bfloat16).astype(jnp.float32))
    return high, value - high


def contract(left, right):
    return lax.dot_general(
        left.astype(jnp.bfloat16),
        right.astype(jnp.bfloat16),
        (((0,), (0,)), ((), ())),
        preferred_element_type=jnp.float32,
    )


def strip(main, side, is_alpha, first_cycle, radial_count):
    lane, sub = iota(1), iota(0)
    lower4 = sub < 4
    column = sub & 3

    cells = lamination(main[0], main[1])
    rims = lamination(side[0], side[1])
    tiles = [cells.map(lambda part: part[:, :LANES]), cells.map(lambda part: part[:, LANES:])]
    cycle = (first_cycle + sub - 1).astype(jnp.float32)
    center = 1.0 + (cycle + 0.5) / radial_count
    face = 1.0 + cycle / radial_count
    per_center = 1.0 / center
    first_lane, last_lane = lane == 0, lane == LANES - 1

    ahead = [tile.lanes(1) for tile in tiles]
    west = [
        harmonic(pick(first_lane, rims.lanes(1), ahead[0]), tiles[0]) * per_center,
        harmonic(pick(first_lane, ahead[0], ahead[1]), tiles[1]) * per_center,
    ]
    wall = harmonic(tiles[1], rims.lanes(-1)) * per_center * 2.0
    back = [tile.lanes(-1) for tile in west]
    east = [pick(last_lane, back[1], back[0]), pick(last_lane, wall, back[1])]
    west[0] = pick(first_lane, west[0] * 2.0, west[0])
    south, north = [], []
    for tile in tiles:
        radial = harmonic(tile.subs(1), tile) * face
        radial = pick((sub == 1) | (sub == 5), radial * 2.0, radial)
        south.append(radial)
        north.append(radial.subs(-1))
    diagonal = [west[h] + east[h] + south[h] + north[h] for h in range(2)]
    gain_in = [south[h].row(1) for h in range(2)]
    gain_out = [north[h].row(4) for h in range(2)]

    diag_e, diag_o = evens(diagonal)
    east_e, east_o = evens(east)
    up_e, up_o = evens(north)
    left_e = pick(last_lane, east_o, 0.0)
    left_e = (east_o - left_e).lanes(1)

    def entry_e(r, c):
        if r == c:
            return diag_e.row(r + 1)
        return -up_e.row(r)

    lower_e, pivots_e = {}, []
    work = diag_e.row(1)
    for r in range(4):
        pivots_e.append(work.inverse())
        if r < 3:
            coupling = up_e.row(r + 1)
            lower_e[r + 1, r] = -(coupling * pivots_e[r])
            work = diag_e.row(r + 2) + lower_e[r + 1, r] * coupling
    zero = jnp.zeros((8, LANES), jnp.float32)
    nothing = Cx(zero, zero)
    half = []
    for r in range(4):
        value = Cx(jnp.where(column == r, 1.0, zero), zero)
        if r:
            value = value - lower_e[r, r - 1] * half[r - 1]
        half.append(value)
    inverse_e = [None] * 4
    for r in range(3, -1, -1):
        value = half[r] * pivots_e[r]
        if r < 3:
            value = value - lower_e[r + 1, r] * inverse_e[r + 1]
        inverse_e[r] = value
    for r in range(4):
        for c in range(r - 1):
            lower_e[r, c] = nothing
    seeds_e = seeds(lower_e, pivots_e)
    sides_e = pick(lower4, left_e.subs(-1), east_e.subs(3))
    reach_e = [inverse_e[r] * sides_e for r in range(4)]
    matrix, pair = [], []
    for r in range(4):
        to_left = (left_e.row(r + 1) * reach_e[r]).lanes(-1)
        to_right = east_e.row(r + 1) * reach_e[r]
        pair.append(pick(lower4, to_right, to_left))
        change = pick(lower4, to_left, to_right)
        base = pick(column == r, diag_o.row(r + 1), 0.0)
        if r < 3:
            base = pick(column == r + 1, -up_o.row(r + 1), base)
        if r > 0:
            base = pick(column == r - 1, -up_o.row(r), base)
        matrix.append(base - change - change.subs(4))

    for level in range(1, 8):
        step = 1 << (level - 1)
        stay = ((lane + 1) & (2 * step - 1)) == 0
        reach = solve(*factor(lambda r, c: matrix[r].row(c)), pair)
        next_matrix, next_pair = [], []
        for r in range(4):
            to_left = total(pair[k].row(r) * reach[k] for k in range(4)).lanes(-step)
            to_right = total(pair[k].row(4 + r) * reach[k] for k in range(4)).lanes(step)
            change = pick(lower4, to_left, to_right)
            change = change + change.subs(4)
            next_matrix.append(pick(stay, matrix[r] - change, matrix[r]))
            next_pair.append(pick(stay, pick(lower4, to_right, to_left), pair[r]))
        matrix, pair = next_matrix, next_pair

    lower, pivots = factor(lambda r, c: matrix[r].row(c))
    reach = solve(lower, pivots, pair)
    reach_rows = [[reach[r].row(k) for k in range(8)] for r in range(4)]
    seed = seeds(lower, pivots)

    def level_of(group):
        return jnp.where(lower4, 2 * group - 1, 2 * group)

    own_level = jnp.ones((8, LANES), jnp.int32)
    for level in range(2, 9):
        own_level = own_level + (((lane + 1) & ((1 << (level - 1)) - 1)) == 0).astype(jnp.int32)

    odd = {}
    for group in range(1, GROUPS + 1):
        rows = [pick(own_level == level_of(group), seed[r], 0.0) for r in range(4)]
        for level in range(min(2 * group - 1, 7), 0, -1):
            step = 1 << (level - 1)
            here = own_level == level
            before = [row.lanes(step) for row in rows]
            after = [row.lanes(-step) for row in rows]
            fresh = []
            for r in range(4):
                terms = [reach_rows[r][k] * before[k] for k in range(4)]
                terms += [reach_rows[r][4 + k] * after[k] for k in range(4)]
                fresh.append(rows[r] + pick(here, total(terms), 0.0))
            rows = fresh
        odd[group] = rows

    reach_e_rows = [[reach_e[r].row(k) for k in range(8)] for r in range(4)]
    even = {0: [pick(first_lane & lower4, seeds_e[r], 0.0) for r in range(4)]}
    odd[0] = [nothing] * 4
    for group in range(1, GROUPS + 1):
        before = [row.lanes(1) for row in odd[group]]
        even[group] = []
        for r in range(4):
            terms = [reach_e_rows[r][k] * before[k] for k in range(4)]
            terms += [reach_e_rows[r][4 + k] * odd[group][k] for k in range(4)]
            even[group].append(total(terms))

    def corners(lefts, rights):
        return pick(
            lane == 0,
            lefts[0],
            pick(
                lane == 1,
                lefts[1].lanes(1),
                pick(lane == 2, rights[0].lanes(3), pick(lane == 3, rights[1].lanes(4), 0.0)),
            ),
        )

    gains_left = [west[0].row(r + 1) for r in range(4)]
    gains_right = [east[1].row(r + 1) for r in range(4)]
    gain_corner = [
        corners(gains_left[2 * t : 2 * t + 2], gains_right[2 * t : 2 * t + 2]) for t in range(2)
    ]
    inner, outer, corner = {}, {}, {}
    for group in range(GROUPS + 1):
        if group:
            low = natural(even[group][0], odd[group][0])
            high = natural(even[group][3], odd[group][3])
        else:
            low, high = [even[0][0], nothing], [even[0][3], nothing]
        inner[group] = [low[h] * gain_in[h] for h in range(2)]
        outer[group] = [high[h] * gain_out[h] for h in range(2)]
        corner[group] = [
            corners(even[group][2 * t : 2 * t + 2], odd[group][2 * t : 2 * t + 2]) * gain_corner[t]
            for t in range(2)
        ]

    left_parts, right_parts = [], []
    for group in range(GROUPS + 1):
        if group in (0, GROUPS):
            low, high = inner[group], outer[group]
        else:
            near = lane < (2 << level_of(group))
            low = [pick(near, inner[group][0], 0.0), nothing]
            high = [pick(near, outer[group][0], 0.0), nothing]
        side_a, side_b = corner[group]
        own = [pick(is_alpha, low[h], high[h]) for h in range(2)]
        own.append(pick(is_alpha, side_a, side_b))
        moved = [high[0].lanes(4), high[1].lanes(4)]
        every = [
            low[0],
            low[1],
            pick(lower_lanes(lane, 4), side_a, moved[0]),
            pick(lower_lanes(lane, 4), moved[0], moved[1]),
            pick(lower_lanes(lane, 4), moved[1], pick(lane < 8, side_b.lanes(4), 0.0)),
        ]
        left_parts.append([split(value) for value in own])
        right_parts.append([split(value) for value in every])

    def wide(parts, which, name, sign=1.0):
        rows = []
        for group in parts:
            pieces = [getattr(value[which], name) for value in group]
            rows.append(jnp.concatenate(pieces, axis=1) * sign)
        return rows

    fill = [jnp.zeros((8, 3 * LANES), jnp.float32)] * 2
    left = (
        wide(left_parts, 0, "re")
        + wide(left_parts, 0, "re")
        + wide(left_parts, 1, "re")
        + wide(left_parts, 0, "im")
        + wide(left_parts, 0, "im")
        + wide(left_parts, 1, "im")
        + fill
    )
    fill = [jnp.zeros((8, 5 * LANES), jnp.float32)] * 2
    right_re = (
        wide(right_parts, 0, "re")
        + wide(right_parts, 1, "re")
        + wide(right_parts, 0, "re")
        + wide(right_parts, 0, "im", -1.0)
        + wide(right_parts, 1, "im", -1.0)
        + wide(right_parts, 0, "im", -1.0)
        + fill
    )
    right_im = (
        wide(right_parts, 0, "im")
        + wide(right_parts, 1, "im")
        + wide(right_parts, 0, "im")
        + wide(right_parts, 0, "re")
        + wide(right_parts, 1, "re")
        + wide(right_parts, 0, "re")
        + fill
    )
    left = jnp.concatenate(left, axis=0)
    top = Cx(
        contract(left, jnp.concatenate(right_re, axis=0)),
        contract(left, jnp.concatenate(right_im, axis=0)),
    )

    masks = []
    for level in range(1, 7):
        for tile in range(max((1 << (6 - level)) // 2, 1)):
            masks.append((level, (lane >> (level + 1)) == 2 * tile + (sub >> 2)))

    def spread(value):
        out = []
        for level, mask in masks:
            out.append(jnp.where(mask, value[level], 0.0))
        return jnp.concatenate(out, axis=0)

    def both(values, half):
        levels = {}
        for group in range(1, GROUPS):
            value = values[group][half]
            if half == 0:
                value = pick(lane < (2 << level_of(group)), nothing, value)
            turned = value.subs(4)
            levels[2 * group - 1] = split(pick(lower4, value, turned))
            levels[2 * group] = split(pick(lower4, turned, value))
        return {
            (which, name): spread(
                {level: getattr(pair[which], name) for level, pair in levels.items()}
            )
            for which in range(2)
            for name in ("re", "im")
        }

    even_d = [inverse_e[0].row(0), inverse_e[0].row(3), inverse_e[3].row(3)]
    even_d = [natural(value, nothing) for value in even_d]

    def local(half):
        low, high = both(inner, half), both(outer, half)
        own = {key: jnp.where(is_alpha, low[key], high[key]) for key in low}
        every = {key: jnp.concatenate([low[key], high[key]], axis=1) for key in low}
        hr, hi, lr, li = (0, "re"), (0, "im"), (1, "re"), (1, "im")
        left = jnp.concatenate([own[key] for key in (hr, hi, hr, hi, lr, li)], axis=0)
        right_re = jnp.concatenate(
            [every[hr], -every[hi], every[lr], -every[li], every[hr], -every[hi]], axis=0
        )
        right_im = jnp.concatenate([every[key] for key in (hi, hr, li, lr, hi, hr)], axis=0)
        product = Cx(contract(left, right_re), contract(left, right_im))
        g_in, g_out = gain_in[half], gain_out[half]
        solo = (lane & 1) == 0
        if half == 0:
            solo = solo & (lane > 0)
        cross = even_d[1][half] * g_in * g_out
        on_in = pick(is_alpha, even_d[0][half] * g_in * g_in, cross)
        on_out = pick(is_alpha, cross, even_d[2][half] * g_out * g_out)
        on_in = pick(solo, on_in, 0.0) - pick(is_alpha, g_in, nothing)
        on_out = pick(solo, on_out, 0.0) - pick(is_alpha, nothing, g_out)
        return product, on_in, on_out

    edge = pick((lane == sub) & lower4, pick(is_alpha, gain_corner[0], gain_corner[1]), 0.0)
    return top, local, edge


def lower_lanes(lane, count):
    return lane < count


def finish(top, local, edge, is_alpha, store):
    lane, sub = iota(1), iota(0)
    full = [top.re, top.im]
    for half in range(2):
        terms = local(half)
        for row in range(0, LANES, 8):
            here = lane == sub + row
            at = half * LANES + row
            both = []
            for part, name in enumerate(("re", "im")):
                product, on_in, on_out = [getattr(value, name) for value in terms]
                low = product[row : row + 8, :LANES] + jnp.where(here, on_in, 0.0)
                high = product[row : row + 8, LANES:] + jnp.where(here, on_out, 0.0)
                high = lane_roll(high, 4)
                out = [full[part][at : at + 8, t * LANES : (t + 1) * LANES] for t in range(5)]
                out[half] = out[half] + low
                out[2 + half] = out[2 + half] + jnp.where(lane < 4, 0.0, high)
                out[3 + half] = out[3 + half] + jnp.where(lane < 4, high, 0.0)
                both.append([-value for value in out])
            store(at, 8, both)
    at = 2 * LANES
    both = []
    for part, name in enumerate(("re", "im")):
        edge_part = getattr(edge, name)
        out = [full[part][at : at + 8, t * LANES : (t + 1) * LANES] for t in range(5)]
        out[2] = out[2] - jnp.where(is_alpha, edge_part, 0.0)
        out[4] = out[4] - jnp.where(is_alpha, 0.0, lane_roll(edge_part, 4))
        both.append([-value for value in out])
    store(at, 4, both)


def interleaved(first, second, half):
    sub = iota(0)
    index = 4 * half + (sub >> 1)
    return jnp.where((sub & 1) == 0, sub_take(first, index), sub_take(second, index))


def cell_data(ref, angular):
    value = ref[...]
    levels = value[:2].astype(jnp.int32)
    lookups = []
    for row in (4, 5):
        table = jnp.broadcast_to(value[row : row + 1, :LANES], (8, LANES))
        halves = []
        for half in range(2):
            index = levels[:, half * LANES : (half + 1) * LANES]
            index = jnp.concatenate([index] * 4, axis=0)
            halves.append(lane_take(table, index)[:2])
        lookups.append(jnp.concatenate(halves, axis=1))
    sheet = value[2:4]
    return angular * lookups[0] * sheet * sheet, lookups[1]


def gather_rows(angular, own, other, is_alpha, is_first, is_last, main, side):
    lane = lax.broadcasted_iota(jnp.int32, (2, LANES), 1)
    own, other = [[cell_data(ref, angular) for ref in refs] for refs in (own, other)]
    for field in range(2):
        (mine, after, near, before), (theirs, after_x, far, before_x) = (
            [data[field] for data in part] for part in (own, other)
        )
        alpha, beta = jnp.where(is_alpha, mine, theirs), jnp.where(is_alpha, theirs, mine)
        main[field, 0:1, :] = jnp.where(is_first, alpha[0:1], jnp.where(is_alpha, near, far)[1:2])
        main[field, 1:3, :] = alpha
        main[field, 3:5, :] = beta
        main[field, 5:6, :] = jnp.where(is_last, beta[1:2], jnp.where(is_alpha, far, near)[0:1])
        main[field, 6:8, :] = beta
        ends = []
        for lefts, rights in ((before, after), (before_x, after_x)):
            left, right = lefts[:, LANES:], rights[:, :LANES]
            ends.append(jnp.where(lane == LANES - 1, left, jnp.where(lane == 0, right, 1.0)))
        ends_alpha = jnp.where(is_alpha, ends[0], ends[1])
        ends_beta = jnp.where(is_alpha, ends[1], ends[0])
        side[field, 0:1, :] = ends_alpha[0:1]
        side[field, 1:3, :] = ends_alpha
        side[field, 3:5, :] = ends_beta
        side[field, 5:7, :] = ends_beta
        side[field, 7:8, :] = ends_beta[0:1]


def merge_kernel(cycles, depth, angular, *refs):
    own, other, (out, main, side, held, sems) = refs[:4], refs[4:8], refs[8:]
    index = lax.axis_index("rad")
    is_alpha = index % 2 == 0
    is_first = index // 2 == 0
    is_last = index // 2 == cycles // 2 - 1
    gather_rows(angular[0], own, other, is_alpha, is_first, is_last, main, side)
    top, local, edge = strip(
        (main[0], main[1]),
        (side[0], side[1]),
        is_alpha,
        (index // 2) * (2 * depth),
        cycles * depth,
    )
    rows = out.shape[0]
    bounds = [0, 64, 128, 192, rows]
    copies = [
        pltpu.make_async_copy(
            held.at[first : last, :, :], out.at[first : last, :, :], sems.at[number]
        )
        for number, (first, last) in enumerate(zip(bounds, bounds[1:]))
    ]

    def store(row, count, both):
        for number, (real, imag) in enumerate(zip(*both)):
            at = number * LANES
            width = min(LANES, out.shape[2] - at)
            for half in range(count // 4):
                tile = interleaved(real, imag, half)
                first = row + 4 * half
                held[first : first + 4, :, at : at + width] = tile.reshape(4, 2, LANES)[
                    :, :, :width
                ]
        if row + count in bounds:
            copies[bounds.index(row + count) - 1].start()

    finish(top, local, edge, is_alpha, store)
    for copy in copies:
        copy.wait()


def pack_kernel(*refs):
    sources, (out_ref,), targets, sems = refs[:4], refs[4:5], refs[5:9], refs[9]
    copies = [
        pltpu.make_async_copy(source, target, sems.at[number])
        for number, (source, target) in enumerate(zip(sources, targets))
    ]
    for copy in copies:
        copy.start()
    for copy in copies:
        copy.wait()
    material_ref, sheet_ref, sigma_ref, nu_ref = targets
    out_ref[:2, :] = material_ref[...].astype(jnp.float32)
    out_ref[2:4, :] = sheet_ref[...]
    for row, ref in ((4, sigma_ref), (5, nu_ref)):
        out_ref[row : row + 1, : ref.shape[0]] = ref[...].reshape(1, ref.shape[0])


def packed(*arguments):
    held = [pltpu.with_memory_space_constraint(value, pltpu.HBM) for value in arguments]
    return pl.pallas_call(
        pack_kernel,
        out_shape=jax.ShapeDtypeStruct((8, arguments[1].shape[1]), jnp.float32),
        in_specs=[pl.BlockSpec(memory_space=pltpu.HBM)] * 4,
        out_specs=pl.BlockSpec(memory_space=pltpu.VMEM),
        scratch_shapes=[pltpu.VMEM(value.shape, value.dtype) for value in arguments]
        + [pltpu.SemaphoreType.DMA((4,))],
        compiler_params=pltpu.CompilerParams(vmem_limit_bytes=4 * 1024 * 1024),
        name="cells",
    )(*held)


def swapped(cells, axis, first):
    count = lax.axis_size(axis)
    route = []
    for low in range(first, count, 2):
        high = (low + 1) % count
        route += [(low, high), (high, low)]
    return lax.ppermute(cells, axis, route)


def per_device(material_id, thickness, sigma_table, nu_table, angular_frequency):
    depth, arc = thickness.shape
    cells = packed(material_id, thickness, sigma_table, nu_table)
    cycles = lax.axis_size("rad")
    blocks = lax.axis_size("az")
    before = lax.ppermute(cells, "az", [(i, (i + 1) % blocks) for i in range(blocks)])
    after = lax.ppermute(cells, "az", [((i + 1) % blocks, i) for i in range(blocks)])
    own = [cells, after, swapped(cells, "rad", 1), before]
    other = [swapped(part, "rad", 0) for part in own]
    outer_nodes = arc + 2 * depth
    out = pl.pallas_call(
        lambda *refs: merge_kernel(cycles, depth, *refs),
        out_shape=jax.ShapeDtypeStruct((outer_nodes, 2, 2 * outer_nodes), jnp.float32),
        in_specs=[pl.BlockSpec(memory_space=pltpu.SMEM)]
        + [pl.BlockSpec(memory_space=pltpu.VMEM)] * 8,
        out_specs=pl.BlockSpec(memory_space=pltpu.HBM),
        scratch_shapes=[
            pltpu.VMEM((2, 8, arc), jnp.float32),
            pltpu.VMEM((2, 8, LANES), jnp.float32),
            pltpu.VMEM((outer_nodes, 2, 2 * outer_nodes), jnp.float32),
            pltpu.SemaphoreType.DMA((4,)),
        ],
        compiler_params=pltpu.CompilerParams(vmem_limit_bytes=48 * 1024 * 1024),
        name="pair_map",
    )(angular_frequency, *own, *other)
    return jnp.transpose(out, (1, 0, 2))


def solution(mesh):
    placed = (P("rad", "az"), P("rad", "az"), P(), P(), P())
    return jax.shard_map(
        per_device, mesh=mesh, in_specs=placed, out_specs=P(None, "rad", "az"), check_vma=False
    )
```

```python
import jax
import jax.numpy as jnp
from jax import lax
from jax.experimental import pallas as pl
from jax.experimental.pallas import tpu as pltpu
from jax.sharding import PartitionSpec as P

SHEET_NODES = 16
LANES = 128
GROUPS = 4


def lane_roll(value, shift):
    return pltpu.roll(value, shift % value.shape[1], 1)


def sub_roll(value, shift):
    return pltpu.roll(value, shift % value.shape[0], 0)


def lane_take(value, index):
    return jnp.take_along_axis(value, index, axis=1, mode="promise_in_bounds")


def sub_take(value, index):
    return jnp.take_along_axis(value, index, axis=0, mode="promise_in_bounds")


def iota(dim):
    return lax.broadcasted_iota(jnp.int32, (8, LANES), dim)


class Cx:
    def __init__(self, re, im):
        self.re, self.im = re, im

    def __add__(self, other):
        return Cx(self.re + other.re, self.im + other.im)

    def __sub__(self, other):
        return Cx(self.re - other.re, self.im - other.im)

    def __neg__(self):
        return Cx(-self.re, -self.im)

    def __mul__(self, other):
        if not isinstance(other, Cx):
            return Cx(self.re * other, self.im * other)
        return Cx(
            self.re * other.re - self.im * other.im, self.re * other.im + self.im * other.re
        )

    def inverse(self):
        scale = 1.0 / (self.re * self.re + self.im * self.im)
        return Cx(self.re * scale, -self.im * scale)

    def root(self):
        size = jnp.sqrt(self.re * self.re + self.im * self.im)
        re = jnp.sqrt(0.5 * (size + self.re))
        return Cx(re, 0.5 * self.im / re)

    def map(self, function):
        return Cx(function(self.re), function(self.im))

    def row(self, index):
        return self.map(lambda part: jnp.broadcast_to(part[index : index + 1], (8, LANES)))

    def lanes(self, shift):
        return self.map(lambda part: lane_roll(part, shift))

    def subs(self, shift):
        return self.map(lambda part: sub_roll(part, shift))


def pick(mask, first, second):
    if not isinstance(second, Cx):
        return first.map(lambda part: jnp.where(mask, part, second))
    return Cx(jnp.where(mask, first.re, second.re), jnp.where(mask, first.im, second.im))


def total(terms):
    terms = list(terms)
    while len(terms) > 1:
        terms = [
            terms[i] + terms[i + 1] if i + 1 < len(terms) else terms[i]
            for i in range(0, len(terms), 2)
        ]
    return terms[0]


def harmonic(left, right):
    return (left * right) * (left + right).inverse() * 2.0


def lamination(skin, base):
    above = Cx(jnp.ones_like(skin), jnp.zeros_like(skin))
    field = Cx(jnp.ones_like(skin), 0.5 * skin)
    summed = above
    for _ in range(SHEET_NODES - 1):
        summed = summed + field
        below = Cx(
            2.0 * field.re - skin * field.im - above.re,
            2.0 * field.im + skin * field.re - above.im,
        )
        above, field = field, below
    return field * summed.inverse() * (base * SHEET_NODES)


def factor(entry):
    work = {(r, c): entry(r, c) for r in range(4) for c in range(r + 1)}
    lower, pivots = {}, []
    for k in range(4):
        inverse = work[k, k].inverse()
        pivots.append(inverse)
        for r in range(k + 1, 4):
            lower[r, k] = work[r, k] * inverse
        for r in range(k + 1, 4):
            for c in range(k + 1, r + 1):
                work[r, c] = work[r, c] - lower[r, k] * work[c, k]
    return lower, pivots


def solve(lower, pivots, right):
    half = []
    for r in range(4):
        value = right[r]
        for c in range(r):
            value = value - lower[r, c] * half[c]
        half.append(value)
    out = [None] * 4
    for r in range(3, -1, -1):
        value = half[r] * pivots[r]
        for c in range(r + 1, 4):
            value = value - lower[c, r] * out[c]
        out[r] = value
    return out


def inverse2(first, second, cross):
    scale = (first * second - cross * cross).inverse()
    return second * scale, first * scale, -(cross * scale)


def solve_blocks(entry, right):
    cross = [[entry(2 + c, r) for c in range(2)] for r in range(2)]
    i00, i11, i01 = inverse2(entry(0, 0), entry(1, 1), entry(1, 0))
    ratio = [
        [i00 * cross[0][c] + i01 * cross[1][c] for c in range(2)],
        [i01 * cross[0][c] + i11 * cross[1][c] for c in range(2)],
    ]

    def rest(r, c):
        return entry(2 + r, 2 + c) - (cross[0][r] * ratio[0][c] + cross[1][r] * ratio[1][c])

    j00, j11, j01 = inverse2(rest(0, 0), rest(1, 1), rest(1, 0))
    start = [i00 * right[0] + i01 * right[1], i01 * right[0] + i11 * right[1]]
    low = [right[2 + r] - (ratio[0][r] * right[0] + ratio[1][r] * right[1]) for r in range(2)]
    out = [j00 * low[0] + j01 * low[1], j01 * low[0] + j11 * low[1]]
    return [start[r] - (ratio[r][0] * out[0] + ratio[r][1] * out[1]) for r in range(2)] + out


def seeds(lower, pivots):
    column = iota(0) & 3
    unit = {}
    for r in range(4):
        for c in range(r - 1, -1, -1):
            value = -lower[r, c]
            for k in range(c + 1, r):
                value = value - lower[r, k] * unit[k, c]
            unit[r, c] = value
    roots = [pivot.root() for pivot in pivots]
    out = []
    for r in range(4):
        value = pick(column == r, roots[r], 0.0)
        for k in range(r + 1, 4):
            value = pick(column == k, roots[k] * unit[k, r], value)
        out.append(value)
    return out


def evens(tiles):
    lane = iota(1)
    index = (2 * lane) & (LANES - 1)

    def one(offset):
        return Cx(
            *(
                jnp.where(
                    lane < LANES // 2,
                    lane_take(first, index + offset),
                    lane_take(second, index + offset),
                )
                for first, second in ((tiles[0].re, tiles[1].re), (tiles[0].im, tiles[1].im))
            )
        )

    return one(0), one(1)


def natural(even, odd):
    lane = iota(1)
    out = []
    for half in range(2):
        index = half * (LANES // 2) + (lane >> 1)
        out.append(
            Cx(
                *(
                    jnp.where((lane & 1) == 0, lane_take(first, index), lane_take(second, index))
                    for first, second in ((even.re, odd.re), (even.im, odd.im))
                )
            )
        )
    return out


def split(value):
    high = value.map(lambda part: part.astype(jnp.bfloat16).astype(jnp.float32))
    return high, value - high


def contract(left, right):
    return lax.dot_general(
        left,
        right,
        (((0,), (0,)), ((), ())),
        preferred_element_type=jnp.float32,
    )


def strip(main, side, is_alpha, first_cycle, radial_count):
    lane, sub = iota(1), iota(0)
    lower4 = sub < 4
    column = sub & 3

    rims = lamination(*side)
    tiles = [lamination(*cells) for cells in main]
    cycle = (first_cycle + sub - 1).astype(jnp.float32)
    center = 1.0 + (cycle + 0.5) / radial_count
    face = 1.0 + cycle / radial_count
    per_center = 1.0 / center
    first_lane, last_lane = lane == 0, lane == LANES - 1

    ahead = [tile.lanes(1) for tile in tiles]
    west = [
        harmonic(pick(first_lane, rims.lanes(1), ahead[0]), tiles[0]) * per_center,
        harmonic(pick(first_lane, ahead[0], ahead[1]), tiles[1]) * per_center,
    ]
    wall = harmonic(tiles[1], rims.lanes(-1)) * per_center * 2.0
    back = [tile.lanes(-1) for tile in west]
    east = [pick(last_lane, back[1], back[0]), pick(last_lane, wall, back[1])]
    west[0] = pick(first_lane, west[0] * 2.0, west[0])
    south, north = [], []
    for tile in tiles:
        radial = harmonic(tile.subs(1), tile) * face
        radial = pick((sub == 1) | (sub == 5), radial * 2.0, radial)
        south.append(radial)
        north.append(radial.subs(-1))
    diagonal = [west[h] + east[h] + south[h] + north[h] for h in range(2)]
    gain_in = [south[h].row(1) for h in range(2)]
    gain_out = [north[h].row(4) for h in range(2)]

    diag_e, diag_o = evens(diagonal)
    east_e, east_o = evens(east)
    up_e, up_o = evens(north)
    left_e = pick(last_lane, east_o, 0.0)
    left_e = (east_o - left_e).lanes(1)

    def entry_e(r, c):
        if r == c:
            return diag_e.row(r + 1)
        return -up_e.row(r)

    lower_e, pivots_e = {}, []
    work = diag_e.row(1)
    for r in range(4):
        pivots_e.append(work.inverse())
        if r < 3:
            coupling = up_e.row(r + 1)
            lower_e[r + 1, r] = -(coupling * pivots_e[r])
            work = diag_e.row(r + 2) + lower_e[r + 1, r] * coupling
    zero = jnp.zeros((8, LANES), jnp.float32)
    nothing = Cx(zero, zero)
    half = []
    for r in range(4):
        value = Cx(jnp.where(column == r, 1.0, zero), zero)
        if r:
            value = value - lower_e[r, r - 1] * half[r - 1]
        half.append(value)
    inverse_e = [None] * 4
    for r in range(3, -1, -1):
        value = half[r] * pivots_e[r]
        if r < 3:
            value = value - lower_e[r + 1, r] * inverse_e[r + 1]
        inverse_e[r] = value
    for r in range(4):
        for c in range(r - 1):
            lower_e[r, c] = nothing
    seeds_e = seeds(lower_e, pivots_e)
    sides_e = pick(lower4, left_e.subs(-1), east_e.subs(3))
    reach_e = [inverse_e[r] * sides_e for r in range(4)]
    matrix, pair = [], []
    for r in range(4):
        to_left = (left_e.row(r + 1) * reach_e[r]).lanes(-1)
        to_right = east_e.row(r + 1) * reach_e[r]
        pair.append(pick(lower4, to_right, to_left))
        change = pick(lower4, to_left, to_right)
        base = pick(column == r, diag_o.row(r + 1), 0.0)
        if r < 3:
            base = pick(column == r + 1, -up_o.row(r + 1), base)
        if r > 0:
            base = pick(column == r - 1, -up_o.row(r), base)
        matrix.append(base - change - change.subs(4))

    for level in range(1, 8):
        step = 1 << (level - 1)
        stay = ((lane + 1) & (2 * step - 1)) == 0
        reach = solve_blocks(lambda r, c: matrix[r].row(c), pair)
        next_matrix, next_pair = [], []
        for r in range(4):
            to_left = total(pair[k].row(r) * reach[k] for k in range(4)).lanes(-step)
            to_right = total(pair[k].row(4 + r) * reach[k] for k in range(4)).lanes(step)
            change = pick(lower4, to_left, to_right)
            change = change + change.subs(4)
            next_matrix.append(pick(stay, matrix[r] - change, matrix[r]))
            next_pair.append(pick(stay, pick(lower4, to_right, to_left), pair[r]))
        matrix, pair = next_matrix, next_pair

    lower, pivots = factor(lambda r, c: matrix[r].row(c))
    reach = solve(lower, pivots, pair)
    reach_rows = [[reach[r].row(k) for k in range(8)] for r in range(4)]
    seed = seeds(lower, pivots)

    def level_of(group):
        return jnp.where(lower4, 2 * group - 1, 2 * group)

    own_level = jnp.ones((8, LANES), jnp.int32)
    for level in range(2, 9):
        own_level = own_level + (((lane + 1) & ((1 << (level - 1)) - 1)) == 0).astype(jnp.int32)

    odd = {}
    for group in range(1, GROUPS + 1):
        rows = [pick(own_level == level_of(group), seed[r], 0.0) for r in range(4)]
        for level in range(min(2 * group - 1, 7), 0, -1):
            step = 1 << (level - 1)
            here = own_level == level
            before = [row.lanes(step) for row in rows]
            after = [row.lanes(-step) for row in rows]
            fresh = []
            for r in range(4):
                terms = [reach_rows[r][k] * before[k] for k in range(4)]
                terms += [reach_rows[r][4 + k] * after[k] for k in range(4)]
                fresh.append(rows[r] + pick(here, total(terms), 0.0))
            rows = fresh
        odd[group] = rows

    reach_e_rows = [[reach_e[r].row(k) for k in range(8)] for r in range(4)]
    even = {0: [pick(first_lane & lower4, seeds_e[r], 0.0) for r in range(4)]}
    odd[0] = [nothing] * 4
    for group in range(1, GROUPS + 1):
        before = [row.lanes(1) for row in odd[group]]
        even[group] = []
        for r in range(4):
            terms = [reach_e_rows[r][4 + k] * odd[group][k] for k in range(4)]
            if r in (0, 3):
                terms += [reach_e_rows[r][k] * before[k] for k in range(4)]
            even[group].append(total(terms))

    def corners(lefts, rights):
        return pick(
            lane == 0,
            lefts[0],
            pick(
                lane == 1,
                lefts[1].lanes(1),
                pick(lane == 2, rights[0].lanes(3), pick(lane == 3, rights[1].lanes(4), 0.0)),
            ),
        )

    gains_left = [west[0].row(r + 1) for r in range(4)]
    gains_right = [east[1].row(r + 1) for r in range(4)]
    gain_corner = [
        corners(gains_left[2 * t : 2 * t + 2], gains_right[2 * t : 2 * t + 2]) for t in range(2)
    ]
    inner, outer, corner = {}, {}, {}
    for group in range(GROUPS + 1):
        if group:
            low = natural(even[group][0], odd[group][0])
            high = natural(even[group][3], odd[group][3])
        else:
            low, high = [even[0][0], nothing], [even[0][3], nothing]
        inner[group] = [low[h] * gain_in[h] for h in range(2)]
        outer[group] = [high[h] * gain_out[h] for h in range(2)]
        corner[group] = [
            corners(even[group][2 * t : 2 * t + 2], odd[group][2 * t : 2 * t + 2]) * gain_corner[t]
            for t in range(2)
        ]

    left_parts, right_parts = [], []
    for group in range(GROUPS + 1):
        if group in (0, GROUPS):
            low, high = inner[group], outer[group]
        else:
            near = lane < (2 << level_of(group))
            low = [pick(near, inner[group][0], 0.0), nothing]
            high = [pick(near, outer[group][0], 0.0), nothing]
        side_a, side_b = corner[group]
        own = [pick(is_alpha, low[h], high[h]) for h in range(2)]
        own.append(pick(is_alpha, side_a, side_b))
        moved = [high[0].lanes(4), high[1].lanes(4)]
        every = [
            low[0],
            low[1],
            pick(lower_lanes(lane, 4), side_a, moved[0]),
            pick(lower_lanes(lane, 4), moved[0], moved[1]),
            pick(lower_lanes(lane, 4), moved[1], pick(lane < 8, side_b.lanes(4), 0.0)),
        ]
        left_parts.append([split(value) for value in own])
        right_parts.append([split(value) for value in every])

    def wide(parts, which, name, sign=1.0):
        rows = []
        for group in parts:
            pieces = [getattr(value[which], name) for value in group]
            row = jnp.concatenate(pieces, axis=1)
            rows.append(row if sign > 0 else -row)
        return rows

    def stacked(parts, order):
        rows = [row for which, name, sign in order for row in wide(parts, which, name, sign)]
        rows += [jnp.zeros_like(rows[0])] * (32 - len(rows))
        return jnp.concatenate(rows, axis=0).astype(jnp.bfloat16)

    hr, hi, lr, li = (0, "re"), (0, "im"), (1, "re"), (1, "im")
    left = stacked(left_parts, [key + (-1.0,) for key in (hr, hr, lr, hi, hi, li)])
    signs = (1.0, 1.0, 1.0, -1.0, -1.0, -1.0)
    right_re = stacked(
        right_parts, [key + (sign,) for key, sign in zip((hr, lr, hr, hi, li, hi), signs)]
    )
    right_im = stacked(right_parts, [key + (1.0,) for key in (hi, li, hi, hr, lr, hr)])
    top = contract(left, jnp.concatenate([right_re, right_im], axis=1))
    top = Cx(top[:, : 5 * LANES], top[:, 5 * LANES :])

    wide_lane = lax.broadcasted_iota(jnp.int32, (16, LANES), 1)
    wide_sub = lax.broadcasted_iota(jnp.int32, (16, LANES), 0)
    masks = []
    for level in range(1, 5):
        for tile in range(1 << (4 - level)):
            mask = (wide_lane >> (level + 1)) == 4 * tile + (wide_sub >> 2)
            masks.append((level, mask))
    last = ((wide_lane >> 6) == (wide_sub >> 2)) | ((wide_sub >> 2) == 2)
    masks = [
        (level, jnp.where(mask, 1.0, 0.0).astype(jnp.bfloat16))
        for level, mask in masks + [(5, last)]
    ]

    def spread(values, half):
        levels = {}
        for group in range(1, GROUPS):
            value = values[group]
            if half == 0:
                value = pick(lane < (2 << level_of(group)), nothing, value)
            turned = value.subs(4)
            levels[2 * group - 1] = pick(lower4, value, turned)
            levels[2 * group] = pick(lower4, turned, value)
        out = {}
        for name in ("re", "im"):
            parts = {level: getattr(value, name) for level, value in levels.items()}
            tiles = {level: [parts[level]] * 2 for level in range(1, 5)}
            tiles[5] = [parts[5], parts[6]]
            tiles = {level: jnp.concatenate(tile, axis=0) for level, tile in tiles.items()}
            high = {level: tile.astype(jnp.bfloat16) for level, tile in tiles.items()}
            low = {
                level: (tile - high[level].astype(jnp.float32)).astype(jnp.bfloat16)
                for level, tile in tiles.items()
            }
            for which, part in enumerate((high, low)):
                rows = [part[level] * mask for level, mask in masks]
                out[which, name] = jnp.concatenate(rows, axis=0)
        return out

    even_d = [inverse_e[0].row(0), inverse_e[0].row(3), inverse_e[3].row(3)]
    even_d = [natural(value, nothing) for value in even_d]

    def local(half):
        low, high = {}, {}
        for group in range(1, GROUPS):
            low[group], high[group] = inner[group][half], outer[group][half]
        mine = {group: -pick(is_alpha, low[group], high[group]) for group in low}
        low, high, mine = [spread(values, half) for values in (low, high, mine)]
        every = {key: jnp.concatenate([low[key], high[key]], axis=1) for key in low}
        left = jnp.concatenate([mine[key] for key in (hr, hi, hr, hi, lr, li)], axis=0)
        right_re = jnp.concatenate(
            [every[hr], -every[hi], every[lr], -every[li], every[hr], -every[hi]], axis=0
        )
        right_im = jnp.concatenate([every[key] for key in (hi, hr, li, lr, hi, hr)], axis=0)
        product = contract(left, jnp.concatenate([right_re, right_im], axis=1))
        product = Cx(product[:, : 2 * LANES], product[:, 2 * LANES :])
        g_in, g_out = gain_in[half], gain_out[half]
        solo = (lane & 1) == 0
        if half == 0:
            solo = solo & (lane > 0)
        cross = even_d[1][half] * g_in * g_out
        on_in = pick(is_alpha, even_d[0][half] * g_in * g_in, cross)
        on_out = pick(is_alpha, cross, even_d[2][half] * g_out * g_out)
        on_in = pick(is_alpha, g_in, nothing) - pick(solo, on_in, 0.0)
        on_out = pick(is_alpha, nothing, g_out) - pick(solo, on_out, 0.0)
        return product, on_in, on_out

    edge = pick((lane == sub) & lower4, pick(is_alpha, gain_corner[0], gain_corner[1]), 0.0)
    return top, local, edge


def lower_lanes(lane, count):
    return lane < count


def finish(top, local, edge, is_alpha, store):
    lane, sub = iota(1), iota(0)
    full = [top.re, top.im]
    for half in range(2):
        terms = local(half)
        for row in range(0, LANES, 8):
            here = lane == sub + row
            at = half * LANES + row
            both = []
            for part, name in enumerate(("re", "im")):
                product, on_in, on_out = [getattr(value, name) for value in terms]
                low = product[row : row + 8, :LANES] + jnp.where(here, on_in, 0.0)
                high = product[row : row + 8, LANES:] + jnp.where(here, on_out, 0.0)
                high = lane_roll(high, 4)
                out = [full[part][at : at + 8, t * LANES : (t + 1) * LANES] for t in range(5)]
                out[half] = out[half] + low
                out[2 + half] = out[2 + half] + jnp.where(lane < 4, 0.0, high)
                out[3 + half] = out[3 + half] + jnp.where(lane < 4, high, 0.0)
                both.append(out)
            store(at, 8, both)
    at = 2 * LANES
    both = []
    for part, name in enumerate(("re", "im")):
        edge_part = getattr(edge, name)
        out = [full[part][at : at + 8, t * LANES : (t + 1) * LANES] for t in range(5)]
        out[2] = out[2] + jnp.where(is_alpha, edge_part, 0.0)
        out[4] = out[4] + jnp.where(is_alpha, 0.0, lane_roll(edge_part, 4))
        both.append(out)
    store(at, 4, both)


def interleaved(first, second, half):
    sub = iota(0)
    index = 4 * half + (sub >> 1)
    return jnp.where((sub & 1) == 0, sub_take(first, index), sub_take(second, index))


def gather_rows(own, other, is_alpha, is_first, is_last, main, side):
    lane = lax.broadcasted_iota(jnp.int32, (2, LANES), 1)
    for field in range(2):
        rows = slice(2 * field, 2 * field + 2)
        (mine, after, near, before), (theirs, after_x, far, before_x) = (
            [ref[rows, :] for ref in refs] for refs in (own, other)
        )
        alpha, beta = jnp.where(is_alpha, mine, theirs), jnp.where(is_alpha, theirs, mine)
        main[field, 0:1, :] = jnp.where(is_first, alpha[0:1], jnp.where(is_alpha, near, far)[1:2])
        main[field, 1:3, :] = alpha
        main[field, 3:5, :] = beta
        main[field, 5:6, :] = jnp.where(is_last, beta[1:2], jnp.where(is_alpha, far, near)[0:1])
        main[field, 6:8, :] = beta
        ends = []
        for lefts, rights in ((before, after), (before_x, after_x)):
            ends.append(jnp.where(lane == LANES - 1, lefts[:, LANES:], rights[:, :LANES]))
        ends_alpha = jnp.where(is_alpha, ends[0], ends[1])
        ends_beta = jnp.where(is_alpha, ends[1], ends[0])
        side[field, 0:1, :] = ends_alpha[0:1]
        side[field, 1:3, :] = ends_alpha
        side[field, 3:5, :] = ends_beta
        side[field, 5:7, :] = ends_beta
        side[field, 7:8, :] = ends_beta[0:1]


def looked_up(tables, angular, material, sheet):
    index = material.astype(jnp.int32)
    sigma, base = [lane_take(table, index) for table in tables]
    return angular * sigma * sheet * sheet, base


def merge_kernel(cycles, depth, angular, *refs):
    own, other, (out, main, side, held, sems) = refs[:4], refs[4:8], refs[8:]
    index = lax.axis_index("rad")
    is_alpha = index % 2 == 0
    is_first = index // 2 == 0
    is_last = index // 2 == cycles // 2 - 1
    gather_rows(own, other, is_alpha, is_first, is_last, main, side)
    tables = [
        jnp.broadcast_to(own[0][row : row + 1, :LANES], (8, LANES)) for row in (4, 5)
    ]
    parts = [(main, 0), (main, LANES), (side, 0)]
    parts = [
        looked_up(tables, angular[0], ref[0, :, at : at + LANES], ref[1, :, at : at + LANES])
        for ref, at in parts
    ]
    top, local, edge = strip(
        parts[:2],
        parts[2],
        is_alpha,
        (index // 2) * (2 * depth),
        cycles * depth,
    )
    rows = out.shape[0]
    bounds = [0, 64, 128, 192, rows]
    copies = [
        pltpu.make_async_copy(
            held.at[first : last, :, :], out.at[first : last, :, :], sems.at[number]
        )
        for number, (first, last) in enumerate(zip(bounds, bounds[1:]))
    ]

    def store(row, count, both):
        for number, (real, imag) in enumerate(zip(*both)):
            at = number * LANES
            width = min(LANES, out.shape[2] - at)
            for half in range(count // 4):
                tile = interleaved(real, imag, half)
                first = row + 4 * half
                held[first : first + 4, :, at : at + width] = tile.reshape(4, 2, LANES)[
                    :, :, :width
                ]
        if row + count in bounds:
            copies[bounds.index(row + count) - 1].start()

    finish(top, local, edge, is_alpha, store)
    for copy in copies:
        copy.wait()


def pack_kernel(*refs):
    sources, (out_ref,), targets, sems = refs[:4], refs[4:5], refs[5:9], refs[9]
    copies = [
        pltpu.make_async_copy(source, target, sems.at[number])
        for number, (source, target) in enumerate(zip(sources, targets))
    ]
    for copy in copies:
        copy.start()
    for copy in copies:
        copy.wait()
    material_ref, sheet_ref, sigma_ref, nu_ref = targets
    out_ref[:2, :] = material_ref[...].astype(jnp.float32)
    out_ref[2:4, :] = sheet_ref[...]
    for row, ref in ((4, sigma_ref), (5, nu_ref)):
        out_ref[row : row + 1, : ref.shape[0]] = ref[...].reshape(1, ref.shape[0])


def packed(*arguments):
    held = [pltpu.with_memory_space_constraint(value, pltpu.HBM) for value in arguments]
    return pl.pallas_call(
        pack_kernel,
        out_shape=jax.ShapeDtypeStruct((8, arguments[1].shape[1]), jnp.float32),
        in_specs=[pl.BlockSpec(memory_space=pltpu.HBM)] * 4,
        out_specs=pl.BlockSpec(memory_space=pltpu.VMEM),
        scratch_shapes=[pltpu.VMEM(value.shape, value.dtype) for value in arguments]
        + [pltpu.SemaphoreType.DMA((4,))],
        compiler_params=pltpu.CompilerParams(vmem_limit_bytes=4 * 1024 * 1024),
        name="cells",
    )(*held)


def swapped(cells, axis, first):
    count = lax.axis_size(axis)
    route = []
    for low in range(first, count, 2):
        high = (low + 1) % count
        route += [(low, high), (high, low)]
    return lax.ppermute(cells, axis, route)


def per_device(material_id, thickness, sigma_table, nu_table, angular_frequency):
    depth, arc = thickness.shape
    cells = packed(material_id, thickness, sigma_table, nu_table)
    cycles = lax.axis_size("rad")
    blocks = lax.axis_size("az")
    before = lax.ppermute(cells, "az", [(i, (i + 1) % blocks) for i in range(blocks)])
    after = lax.ppermute(cells, "az", [((i + 1) % blocks, i) for i in range(blocks)])
    own = [cells, after, swapped(cells, "rad", 1), before]
    other = [swapped(part, "rad", 0) for part in own]
    outer_nodes = arc + 2 * depth
    out = pl.pallas_call(
        lambda *refs: merge_kernel(cycles, depth, *refs),
        out_shape=jax.ShapeDtypeStruct((outer_nodes, 2, 2 * outer_nodes), jnp.float32),
        in_specs=[pl.BlockSpec(memory_space=pltpu.SMEM)]
        + [pl.BlockSpec(memory_space=pltpu.VMEM)] * 8,
        out_specs=pl.BlockSpec(memory_space=pltpu.HBM),
        scratch_shapes=[
            pltpu.VMEM((2, 8, arc), jnp.float32),
            pltpu.VMEM((2, 8, LANES), jnp.float32),
            pltpu.VMEM((outer_nodes, 2, 2 * outer_nodes), jnp.float32),
            pltpu.SemaphoreType.DMA((4,)),
        ],
        compiler_params=pltpu.CompilerParams(vmem_limit_bytes=48 * 1024 * 1024),
        name="pair_map",
    )(angular_frequency, *own, *other)
    return jnp.transpose(out, (1, 0, 2))


def solution(mesh):
    placed = (P("rad", "az"), P("rad", "az"), P(), P(), P())
    return jax.shard_map(
        per_device, mesh=mesh, in_specs=placed, out_specs=P(None, "rad", "az"), check_vma=False
    )
```

```python
import jax
import jax.numpy as jnp
from jax import lax
from jax.experimental import pallas as pl
from jax.experimental.pallas import tpu as pltpu
from jax.sharding import PartitionSpec as P

SHEET_NODES = 16
LANES = 128
GROUPS = 4


def lane_roll(value, shift):
    return pltpu.roll(value, shift % value.shape[1], 1)


def sub_roll(value, shift):
    return pltpu.roll(value, shift % value.shape[0], 0)


def lane_take(value, index):
    return jnp.take_along_axis(value, index, axis=1, mode="promise_in_bounds")


def sub_take(value, index):
    return jnp.take_along_axis(value, index, axis=0, mode="promise_in_bounds")


def iota(dim):
    return lax.broadcasted_iota(jnp.int32, (8, LANES), dim)


class Cx:
    def __init__(self, re, im):
        self.re, self.im = re, im

    def __add__(self, other):
        return Cx(self.re + other.re, self.im + other.im)

    def __sub__(self, other):
        return Cx(self.re - other.re, self.im - other.im)

    def __neg__(self):
        return Cx(-self.re, -self.im)

    def __mul__(self, other):
        if not isinstance(other, Cx):
            return Cx(self.re * other, self.im * other)
        return Cx(
            self.re * other.re - self.im * other.im, self.re * other.im + self.im * other.re
        )

    def inverse(self):
        scale = 1.0 / (self.re * self.re + self.im * self.im)
        return Cx(self.re * scale, -self.im * scale)

    def root(self):
        size = jnp.sqrt(self.re * self.re + self.im * self.im)
        re = jnp.sqrt(0.5 * (size + self.re))
        return Cx(re, 0.5 * self.im / re)

    def map(self, function):
        return Cx(function(self.re), function(self.im))

    def row(self, index):
        return self.map(lambda part: jnp.broadcast_to(part[index : index + 1], (8, LANES)))

    def lanes(self, shift):
        return self.map(lambda part: lane_roll(part, shift))

    def subs(self, shift):
        return self.map(lambda part: sub_roll(part, shift))


def pick(mask, first, second):
    if not isinstance(second, Cx):
        return first.map(lambda part: jnp.where(mask, part, second))
    return Cx(jnp.where(mask, first.re, second.re), jnp.where(mask, first.im, second.im))


def total(terms):
    terms = list(terms)
    while len(terms) > 1:
        terms = [
            terms[i] + terms[i + 1] if i + 1 < len(terms) else terms[i]
            for i in range(0, len(terms), 2)
        ]
    return terms[0]


def harmonic(left, right):
    return (left * right) * (left + right).inverse() * 2.0


def lamination(skin, base):
    above = Cx(jnp.ones_like(skin), jnp.zeros_like(skin))
    field = Cx(jnp.ones_like(skin), 0.5 * skin)
    summed = above
    for _ in range(SHEET_NODES - 1):
        summed = summed + field
        below = Cx(
            2.0 * field.re - skin * field.im - above.re,
            2.0 * field.im + skin * field.re - above.im,
        )
        above, field = field, below
    return field * summed.inverse() * (base * SHEET_NODES)


def factor(entry):
    work = {(r, c): entry(r, c) for r in range(4) for c in range(r + 1)}
    lower, pivots = {}, []
    for k in range(4):
        inverse = work[k, k].inverse()
        pivots.append(inverse)
        for r in range(k + 1, 4):
            lower[r, k] = work[r, k] * inverse
        for r in range(k + 1, 4):
            for c in range(k + 1, r + 1):
                work[r, c] = work[r, c] - lower[r, k] * work[c, k]
    return lower, pivots


def solve(lower, pivots, right):
    half = []
    for r in range(4):
        value = right[r]
        for c in range(r):
            value = value - lower[r, c] * half[c]
        half.append(value)
    out = [None] * 4
    for r in range(3, -1, -1):
        value = half[r] * pivots[r]
        for c in range(r + 1, 4):
            value = value - lower[c, r] * out[c]
        out[r] = value
    return out


def inverse2(first, second, cross):
    scale = (first * second - cross * cross).inverse()
    return second * scale, first * scale, -(cross * scale)


def solve_blocks(entry, right):
    cross = [[entry(2 + c, r) for c in range(2)] for r in range(2)]
    i00, i11, i01 = inverse2(entry(0, 0), entry(1, 1), entry(1, 0))
    ratio = [
        [i00 * cross[0][c] + i01 * cross[1][c] for c in range(2)],
        [i01 * cross[0][c] + i11 * cross[1][c] for c in range(2)],
    ]

    def rest(r, c):
        return entry(2 + r, 2 + c) - (cross[0][r] * ratio[0][c] + cross[1][r] * ratio[1][c])

    j00, j11, j01 = inverse2(rest(0, 0), rest(1, 1), rest(1, 0))
    start = [i00 * right[0] + i01 * right[1], i01 * right[0] + i11 * right[1]]
    low = [right[2 + r] - (ratio[0][r] * right[0] + ratio[1][r] * right[1]) for r in range(2)]
    out = [j00 * low[0] + j01 * low[1], j01 * low[0] + j11 * low[1]]
    return [start[r] - (ratio[r][0] * out[0] + ratio[r][1] * out[1]) for r in range(2)] + out


def seeds(lower, pivots):
    column = iota(0) & 3
    unit = {}
    for r in range(4):
        for c in range(r - 1, -1, -1):
            value = -lower[r, c]
            for k in range(c + 1, r):
                value = value - lower[r, k] * unit[k, c]
            unit[r, c] = value
    roots = [pivot.root() for pivot in pivots]
    out = []
    for r in range(4):
        value = pick(column == r, roots[r], 0.0)
        for k in range(r + 1, 4):
            value = pick(column == k, roots[k] * unit[k, r], value)
        out.append(value)
    return out


def evens(tiles):
    lane = iota(1)
    index = (2 * lane) & (LANES - 1)

    def one(offset):
        return Cx(
            *(
                jnp.where(
                    lane < LANES // 2,
                    lane_take(first, index + offset),
                    lane_take(second, index + offset),
                )
                for first, second in ((tiles[0].re, tiles[1].re), (tiles[0].im, tiles[1].im))
            )
        )

    return one(0), one(1)


def natural(even, odd):
    lane = iota(1)
    out = []
    for half in range(2):
        index = half * (LANES // 2) + (lane >> 1)
        out.append(
            Cx(
                *(
                    jnp.where((lane & 1) == 0, lane_take(first, index), lane_take(second, index))
                    for first, second in ((even.re, odd.re), (even.im, odd.im))
                )
            )
        )
    return out


def split(value):
    high = value.map(lambda part: part.astype(jnp.bfloat16).astype(jnp.float32))
    return high, value - high


def contract(left, right):
    return lax.dot_general(
        left,
        right,
        (((0,), (0,)), ((), ())),
        preferred_element_type=jnp.float32,
    )


def strip(main, side, is_alpha, first_cycle, radial_count):
    lane, sub = iota(1), iota(0)
    lower4 = sub < 4
    column = sub & 3

    rims = lamination(*side)
    tiles = [lamination(*cells) for cells in main]
    cycle = (first_cycle + sub - 1).astype(jnp.float32)
    center = 1.0 + (cycle + 0.5) / radial_count
    face = 1.0 + cycle / radial_count
    per_center = 1.0 / center
    first_lane, last_lane = lane == 0, lane == LANES - 1

    ahead = [tile.lanes(1) for tile in tiles]
    west = [
        harmonic(pick(first_lane, rims.lanes(1), ahead[0]), tiles[0]) * per_center,
        harmonic(pick(first_lane, ahead[0], ahead[1]), tiles[1]) * per_center,
    ]
    wall = harmonic(tiles[1], rims.lanes(-1)) * per_center * 2.0
    back = [tile.lanes(-1) for tile in west]
    east = [pick(last_lane, back[1], back[0]), pick(last_lane, wall, back[1])]
    west[0] = pick(first_lane, west[0] * 2.0, west[0])
    south, north = [], []
    for tile in tiles:
        radial = harmonic(tile.subs(1), tile) * face
        radial = pick((sub == 1) | (sub == 5), radial * 2.0, radial)
        south.append(radial)
        north.append(radial.subs(-1))
    diagonal = [west[h] + east[h] + south[h] + north[h] for h in range(2)]
    gain_in = [south[h].row(1) for h in range(2)]
    gain_out = [north[h].row(4) for h in range(2)]

    diag_e, diag_o = evens(diagonal)
    east_e, east_o = evens(east)
    up_e, up_o = evens(north)
    left_e = pick(last_lane, east_o, 0.0)
    left_e = (east_o - left_e).lanes(1)

    def entry_e(r, c):
        if r == c:
            return diag_e.row(r + 1)
        return -up_e.row(r)

    lower_e, pivots_e = {}, []
    work = diag_e.row(1)
    for r in range(4):
        pivots_e.append(work.inverse())
        if r < 3:
            coupling = up_e.row(r + 1)
            lower_e[r + 1, r] = -(coupling * pivots_e[r])
            work = diag_e.row(r + 2) + lower_e[r + 1, r] * coupling
    zero = jnp.zeros((8, LANES), jnp.float32)
    nothing = Cx(zero, zero)
    half = []
    for r in range(4):
        value = Cx(jnp.where(column == r, 1.0, zero), zero)
        if r:
            value = value - lower_e[r, r - 1] * half[r - 1]
        half.append(value)
    inverse_e = [None] * 4
    for r in range(3, -1, -1):
        value = half[r] * pivots_e[r]
        if r < 3:
            value = value - lower_e[r + 1, r] * inverse_e[r + 1]
        inverse_e[r] = value
    for r in range(4):
        for c in range(r - 1):
            lower_e[r, c] = nothing
    seeds_e = seeds(lower_e, pivots_e)
    sides_e = pick(lower4, left_e.subs(-1), east_e.subs(3))
    reach_e = [inverse_e[r] * sides_e for r in range(4)]
    matrix, pair = [], []
    for r in range(4):
        to_left = (left_e.row(r + 1) * reach_e[r]).lanes(-1)
        to_right = east_e.row(r + 1) * reach_e[r]
        pair.append(pick(lower4, to_right, to_left))
        change = pick(lower4, to_left, to_right)
        base = pick(column == r, diag_o.row(r + 1), 0.0)
        if r < 3:
            base = pick(column == r + 1, -up_o.row(r + 1), base)
        if r > 0:
            base = pick(column == r - 1, -up_o.row(r), base)
        matrix.append(base - change - change.subs(4))

    for level in range(1, 8):
        step = 1 << (level - 1)
        stay = ((lane + 1) & (2 * step - 1)) == 0
        reach = solve_blocks(lambda r, c: matrix[r].row(c), pair)
        next_matrix, next_pair = [], []
        for r in range(4):
            to_left = total(pair[k].row(r) * reach[k] for k in range(4)).lanes(-step)
            to_right = total(pair[k].row(4 + r) * reach[k] for k in range(4)).lanes(step)
            change = pick(lower4, to_left, to_right)
            change = change + change.subs(4)
            next_matrix.append(pick(stay, matrix[r] - change, matrix[r]))
            next_pair.append(pick(stay, pick(lower4, to_right, to_left), pair[r]))
        matrix, pair = next_matrix, next_pair

    lower, pivots = factor(lambda r, c: matrix[r].row(c))
    reach = solve(lower, pivots, pair)
    reach_rows = [[reach[r].row(k) for k in range(8)] for r in range(4)]
    seed = seeds(lower, pivots)

    def level_of(group):
        return jnp.where(lower4, 2 * group - 1, 2 * group)

    own_level = jnp.ones((8, LANES), jnp.int32)
    for level in range(2, 9):
        own_level = own_level + (((lane + 1) & ((1 << (level - 1)) - 1)) == 0).astype(jnp.int32)

    odd = {}
    for group in range(1, GROUPS + 1):
        rows = [pick(own_level == level_of(group), seed[r], 0.0) for r in range(4)]
        for level in range(min(2 * group - 1, 7), 0, -1):
            step = 1 << (level - 1)
            here = own_level == level
            before = [row.lanes(step) for row in rows]
            after = [row.lanes(-step) for row in rows]
            fresh = []
            for r in range(4):
                terms = [reach_rows[r][k] * before[k] for k in range(4)]
                terms += [reach_rows[r][4 + k] * after[k] for k in range(4)]
                fresh.append(rows[r] + pick(here, total(terms), 0.0))
            rows = fresh
        odd[group] = rows

    reach_e_rows = [[reach_e[r].row(k) for k in range(8)] for r in range(4)]
    even = {0: [pick(first_lane & lower4, seeds_e[r], 0.0) for r in range(4)]}
    odd[0] = [nothing] * 4
    for group in range(1, GROUPS + 1):
        before = [row.lanes(1) for row in odd[group]]
        even[group] = []
        for r in range(4):
            terms = [reach_e_rows[r][4 + k] * odd[group][k] for k in range(4)]
            if r in (0, 3):
                terms += [reach_e_rows[r][k] * before[k] for k in range(4)]
            even[group].append(total(terms))

    def corners(lefts, rights):
        return pick(
            lane == 0,
            lefts[0],
            pick(
                lane == 1,
                lefts[1].lanes(1),
                pick(lane == 2, rights[0].lanes(3), pick(lane == 3, rights[1].lanes(4), 0.0)),
            ),
        )

    gains_left = [west[0].row(r + 1) for r in range(4)]
    gains_right = [east[1].row(r + 1) for r in range(4)]
    gain_corner = [
        corners(gains_left[2 * t : 2 * t + 2], gains_right[2 * t : 2 * t + 2]) for t in range(2)
    ]
    inner, outer, corner = {}, {}, {}
    for group in range(GROUPS + 1):
        if group:
            low = natural(even[group][0], odd[group][0])
            high = natural(even[group][3], odd[group][3])
        else:
            low, high = [even[0][0], nothing], [even[0][3], nothing]
        inner[group] = [low[h] * gain_in[h] for h in range(2)]
        outer[group] = [high[h] * gain_out[h] for h in range(2)]
        corner[group] = [
            corners(even[group][2 * t : 2 * t + 2], odd[group][2 * t : 2 * t + 2]) * gain_corner[t]
            for t in range(2)
        ]

    left_parts, right_parts = [], []
    for group in range(GROUPS + 1):
        if group in (0, GROUPS):
            low, high = inner[group], outer[group]
        else:
            near = lane < (2 << level_of(group))
            low = [pick(near, inner[group][0], 0.0), nothing]
            high = [pick(near, outer[group][0], 0.0), nothing]
        side_a, side_b = corner[group]
        own = [pick(is_alpha, low[h], high[h]) for h in range(2)]
        own.append(pick(is_alpha, side_a, side_b))
        moved = [high[0].lanes(4), high[1].lanes(4)]
        every = [
            low[0],
            low[1],
            pick(lower_lanes(lane, 4), side_a, moved[0]),
            pick(lower_lanes(lane, 4), moved[0], moved[1]),
            pick(lower_lanes(lane, 4), moved[1], pick(lane < 8, side_b.lanes(4), 0.0)),
        ]
        left_parts.append([split(value) for value in own])
        right_parts.append([split(value) for value in every])

    def wide(parts, which, name, sign=1.0):
        rows = []
        for group in parts:
            pieces = [getattr(value[which], name) for value in group]
            row = jnp.concatenate(pieces, axis=1)
            rows.append(row if sign > 0 else -row)
        return rows

    def stacked(parts, order):
        rows = [row for which, name, sign in order for row in wide(parts, which, name, sign)]
        rows += [jnp.zeros_like(rows[0])] * (32 - len(rows))
        return jnp.concatenate(rows, axis=0).astype(jnp.bfloat16)

    hr, hi, lr, li = (0, "re"), (0, "im"), (1, "re"), (1, "im")
    left = stacked(left_parts, [key + (-1.0,) for key in (hr, hr, lr, hi, hi, li)])
    signs = (1.0, 1.0, 1.0, -1.0, -1.0, -1.0)
    right_re = stacked(
        right_parts, [key + (sign,) for key, sign in zip((hr, lr, hr, hi, li, hi), signs)]
    )
    right_im = stacked(right_parts, [key + (1.0,) for key in (hi, li, hi, hr, lr, hr)])
    top = contract(left, jnp.concatenate([right_re, right_im], axis=1))
    top = Cx(top[:, : 5 * LANES], top[:, 5 * LANES :])

    wide_lane = lax.broadcasted_iota(jnp.int32, (16, LANES), 1)
    wide_sub = lax.broadcasted_iota(jnp.int32, (16, LANES), 0)
    masks = []
    for level in range(1, 5):
        for tile in range(1 << (4 - level)):
            mask = (wide_lane >> (level + 1)) == 4 * tile + (wide_sub >> 2)
            masks.append((level, mask))
    last = ((wide_lane >> 6) == (wide_sub >> 2)) | ((wide_sub >> 2) == 2)
    masks = [
        (level, jnp.where(mask, 1.0, 0.0).astype(jnp.bfloat16))
        for level, mask in masks + [(5, last)]
    ]

    def spread(values, half):
        levels = {}
        for group in range(1, GROUPS):
            value = values[group]
            if half == 0:
                value = pick(lane < (2 << level_of(group)), nothing, value)
            turned = value.subs(4)
            levels[2 * group - 1] = pick(lower4, value, turned)
            levels[2 * group] = pick(lower4, turned, value)
        out = {}
        for name in ("re", "im"):
            parts = {level: getattr(value, name) for level, value in levels.items()}
            tiles = {level: [parts[level]] * 2 for level in range(1, 5)}
            tiles[5] = [parts[5], parts[6]]
            tiles = {level: jnp.concatenate(tile, axis=0) for level, tile in tiles.items()}
            high = {level: tile.astype(jnp.bfloat16) for level, tile in tiles.items()}
            low = {
                level: (tile - high[level].astype(jnp.float32)).astype(jnp.bfloat16)
                for level, tile in tiles.items()
            }
            for which, part in enumerate((high, low)):
                rows = [part[level] * mask for level, mask in masks]
                out[which, name] = jnp.concatenate(rows, axis=0)
        return out

    even_d = [inverse_e[0].row(0), inverse_e[0].row(3), inverse_e[3].row(3)]
    even_d = [natural(value, nothing) for value in even_d]

    def local(half):
        low, high = {}, {}
        for group in range(1, GROUPS):
            low[group], high[group] = inner[group][half], outer[group][half]
        mine = {group: -pick(is_alpha, low[group], high[group]) for group in low}
        low, high, mine = [spread(values, half) for values in (low, high, mine)]
        every = {key: jnp.concatenate([low[key], high[key]], axis=1) for key in low}
        left = jnp.concatenate([mine[key] for key in (hr, hi, hr, hi, lr, li)], axis=0)
        right_re = jnp.concatenate(
            [every[hr], -every[hi], every[lr], -every[li], every[hr], -every[hi]], axis=0
        )
        right_im = jnp.concatenate([every[key] for key in (hi, hr, li, lr, hi, hr)], axis=0)
        product = contract(left, jnp.concatenate([right_re, right_im], axis=1))
        product = Cx(product[:, : 2 * LANES], product[:, 2 * LANES :])
        g_in, g_out = gain_in[half], gain_out[half]
        solo = (lane & 1) == 0
        if half == 0:
            solo = solo & (lane > 0)
        cross = even_d[1][half] * g_in * g_out
        on_in = pick(is_alpha, even_d[0][half] * g_in * g_in, cross)
        on_out = pick(is_alpha, cross, even_d[2][half] * g_out * g_out)
        on_in = pick(is_alpha, g_in, nothing) - pick(solo, on_in, 0.0)
        on_out = pick(is_alpha, nothing, g_out) - pick(solo, on_out, 0.0)
        return product, on_in, on_out

    edge = pick((lane == sub) & lower4, pick(is_alpha, gain_corner[0], gain_corner[1]), 0.0)
    return top, local, edge


def lower_lanes(lane, count):
    return lane < count


def finish(top, local, edge, is_alpha, store):
    lane, sub = iota(1), iota(0)
    full = [top.re, top.im]
    for half in range(2):
        terms = local(half)
        for row in range(0, LANES, 8):
            here = lane == sub + row
            at = half * LANES + row
            both = []
            for part, name in enumerate(("re", "im")):
                product, on_in, on_out = [getattr(value, name) for value in terms]
                low = product[row : row + 8, :LANES] + jnp.where(here, on_in, 0.0)
                high = product[row : row + 8, LANES:] + jnp.where(here, on_out, 0.0)
                high = lane_roll(high, 4)
                out = [full[part][at : at + 8, t * LANES : (t + 1) * LANES] for t in range(5)]
                out[half] = out[half] + low
                out[2 + half] = out[2 + half] + jnp.where(lane < 4, 0.0, high)
                out[3 + half] = out[3 + half] + jnp.where(lane < 4, high, 0.0)
                both.append(out)
            store(at, 8, both)
    at = 2 * LANES
    both = []
    for part, name in enumerate(("re", "im")):
        edge_part = getattr(edge, name)
        out = [full[part][at : at + 8, t * LANES : (t + 1) * LANES] for t in range(5)]
        out[2] = out[2] + jnp.where(is_alpha, edge_part, 0.0)
        out[4] = out[4] + jnp.where(is_alpha, 0.0, lane_roll(edge_part, 4))
        both.append(out)
    store(at, 4, both)


def interleaved(first, second, half):
    sub = iota(0)
    index = 4 * half + (sub >> 1)
    return jnp.where((sub & 1) == 0, sub_take(first, index), sub_take(second, index))


def gather_rows(own, other, is_alpha, is_first, is_last, main, side):
    lane = lax.broadcasted_iota(jnp.int32, (2, LANES), 1)
    for field in range(2):
        rows = slice(2 * field, 2 * field + 2)
        (mine, after, near, before), (theirs, after_x, far, before_x) = (
            [ref[rows, :] for ref in refs] for refs in (own, other)
        )
        alpha, beta = jnp.where(is_alpha, mine, theirs), jnp.where(is_alpha, theirs, mine)
        main[field, 0:1, :] = jnp.where(is_first, alpha[0:1], jnp.where(is_alpha, near, far)[1:2])
        main[field, 1:3, :] = alpha
        main[field, 3:5, :] = beta
        main[field, 5:6, :] = jnp.where(is_last, beta[1:2], jnp.where(is_alpha, far, near)[0:1])
        main[field, 6:8, :] = beta
        ends = []
        for lefts, rights in ((before, after), (before_x, after_x)):
            ends.append(jnp.where(lane == LANES - 1, lefts[:, LANES:], rights[:, :LANES]))
        ends_alpha = jnp.where(is_alpha, ends[0], ends[1])
        ends_beta = jnp.where(is_alpha, ends[1], ends[0])
        side[field, 0:1, :] = ends_alpha[0:1]
        side[field, 1:3, :] = ends_alpha
        side[field, 3:5, :] = ends_beta
        side[field, 5:7, :] = ends_beta
        side[field, 7:8, :] = ends_beta[0:1]


def looked_up(tables, angular, material, sheet):
    index = material.astype(jnp.int32)
    sigma, base = [lane_take(table, index) for table in tables]
    return angular * sigma * sheet * sheet, base


def merge_kernel(cycles, depth, angular, *refs):
    own, other, (out, main, side, held, rest, sems) = refs[:4], refs[4:8], refs[8:]
    index = lax.axis_index("rad")
    is_alpha = index % 2 == 0
    is_first = index // 2 == 0
    is_last = index // 2 == cycles // 2 - 1
    gather_rows(own, other, is_alpha, is_first, is_last, main, side)
    tables = [
        jnp.broadcast_to(own[0][row : row + 1, :LANES], (8, LANES)) for row in (4, 5)
    ]
    parts = [(main, 0), (main, LANES), (side, 0)]
    parts = [
        looked_up(tables, angular[0], ref[0, :, at : at + LANES], ref[1, :, at : at + LANES])
        for ref, at in parts
    ]
    top, local, edge = strip(
        parts[:2],
        parts[2],
        is_alpha,
        (index // 2) * (2 * depth),
        cycles * depth,
    )
    rows, columns = out.shape[0], out.shape[2]
    bounds = [0, 64, 128, 192, rows]
    whole = held.shape[0]
    copies = []
    for number, (first, last) in enumerate(zip(bounds, bounds[1:])):
        part = []
        for tile in range(whole + 1):
            if tile < whole:
                source = held.at[tile].reshape(rows, 2, LANES)
            else:
                source = rest
            at = tile * LANES
            target = out.at[first:last, :, at : min(at + LANES, columns)]
            part.append(
                pltpu.make_async_copy(source.at[first:last, :, :], target, sems.at[number, tile])
            )
        copies.append(part)

    def store(row, count, both):
        for part, tiles in enumerate(both):
            for number, tile in enumerate(tiles[:whole]):
                held[number, pl.ds(2 * row + part, count, stride=2), :] = tile[:count]
        for half in range(count // 4):
            tile = interleaved(both[0][whole], both[1][whole], half).reshape(4, 2, LANES)
            first = row + 4 * half
            rest[first : first + 4, :, :] = tile[:, :, : rest.shape[2]]
        if row + count in bounds:
            for copy in copies[bounds.index(row + count) - 1]:
                copy.start()

    finish(top, local, edge, is_alpha, store)
    for part in copies:
        for copy in part:
            copy.wait()


def pack_kernel(*refs):
    sources, (out_ref,), targets, sems = refs[:4], refs[4:5], refs[5:9], refs[9]
    copies = [
        pltpu.make_async_copy(source, target, sems.at[number])
        for number, (source, target) in enumerate(zip(sources, targets))
    ]
    for copy in copies:
        copy.start()
    for copy in copies:
        copy.wait()
    material_ref, sheet_ref, sigma_ref, nu_ref = targets
    out_ref[:2, :] = material_ref[...].astype(jnp.float32)
    out_ref[2:4, :] = sheet_ref[...]
    for row, ref in ((4, sigma_ref), (5, nu_ref)):
        out_ref[row : row + 1, : ref.shape[0]] = ref[...].reshape(1, ref.shape[0])


def packed(*arguments):
    held = [pltpu.with_memory_space_constraint(value, pltpu.HBM) for value in arguments]
    return pl.pallas_call(
        pack_kernel,
        out_shape=jax.ShapeDtypeStruct((8, arguments[1].shape[1]), jnp.float32),
        in_specs=[pl.BlockSpec(memory_space=pltpu.HBM)] * 4,
        out_specs=pl.BlockSpec(memory_space=pltpu.VMEM),
        scratch_shapes=[pltpu.VMEM(value.shape, value.dtype) for value in arguments]
        + [pltpu.SemaphoreType.DMA((4,))],
        compiler_params=pltpu.CompilerParams(vmem_limit_bytes=4 * 1024 * 1024),
        name="cells",
    )(*held)


def swapped(cells, axis, first):
    count = lax.axis_size(axis)
    route = []
    for low in range(first, count, 2):
        high = (low + 1) % count
        route += [(low, high), (high, low)]
    return lax.ppermute(cells, axis, route)


def per_device(material_id, thickness, sigma_table, nu_table, angular_frequency):
    depth, arc = thickness.shape
    cells = packed(material_id, thickness, sigma_table, nu_table)
    cycles = lax.axis_size("rad")
    blocks = lax.axis_size("az")
    before = lax.ppermute(cells, "az", [(i, (i + 1) % blocks) for i in range(blocks)])
    after = lax.ppermute(cells, "az", [((i + 1) % blocks, i) for i in range(blocks)])
    own = [cells, after, swapped(cells, "rad", 1), before]
    other = [swapped(part, "rad", 0) for part in own]
    outer_nodes = arc + 2 * depth
    whole, rest = divmod(2 * outer_nodes, LANES)
    out = pl.pallas_call(
        lambda *refs: merge_kernel(cycles, depth, *refs),
        out_shape=jax.ShapeDtypeStruct((outer_nodes, 2, 2 * outer_nodes), jnp.float32),
        in_specs=[pl.BlockSpec(memory_space=pltpu.SMEM)]
        + [pl.BlockSpec(memory_space=pltpu.VMEM)] * 8,
        out_specs=pl.BlockSpec(memory_space=pltpu.HBM),
        scratch_shapes=[
            pltpu.VMEM((2, 8, arc), jnp.float32),
            pltpu.VMEM((2, 8, LANES), jnp.float32),
            pltpu.VMEM((whole, 2 * outer_nodes, LANES), jnp.float32),
            pltpu.VMEM((outer_nodes, 2, rest), jnp.float32),
            pltpu.SemaphoreType.DMA((4, whole + 1)),
        ],
        compiler_params=pltpu.CompilerParams(vmem_limit_bytes=48 * 1024 * 1024),
        name="pair_map",
    )(angular_frequency, *own, *other)
    return jnp.transpose(out, (1, 0, 2))


def solution(mesh):
    placed = (P("rad", "az"), P("rad", "az"), P(), P(), P())
    return jax.shard_map(
        per_device, mesh=mesh, in_specs=placed, out_specs=P(None, "rad", "az"), check_vma=False
    )
```

```python
import jax
import jax.numpy as jnp
from jax import lax
from jax.experimental import pallas as pl
from jax.experimental.pallas import tpu as pltpu
from jax.sharding import PartitionSpec as P

SHEET_NODES = 16
LANES = 128
GROUPS = 4


def lane_roll(value, shift):
    return pltpu.roll(value, shift % value.shape[1], 1)


def sub_roll(value, shift):
    return pltpu.roll(value, shift % value.shape[0], 0)


def lane_take(value, index):
    return jnp.take_along_axis(value, index, axis=1, mode="promise_in_bounds")


def sub_take(value, index):
    return jnp.take_along_axis(value, index, axis=0, mode="promise_in_bounds")


def iota(dim):
    return lax.broadcasted_iota(jnp.int32, (8, LANES), dim)


class Cx:
    def __init__(self, re, im):
        self.re, self.im = re, im

    def __add__(self, other):
        return Cx(self.re + other.re, self.im + other.im)

    def __sub__(self, other):
        return Cx(self.re - other.re, self.im - other.im)

    def __neg__(self):
        return Cx(-self.re, -self.im)

    def __mul__(self, other):
        if not isinstance(other, Cx):
            return Cx(self.re * other, self.im * other)
        return Cx(
            self.re * other.re - self.im * other.im, self.re * other.im + self.im * other.re
        )

    def inverse(self):
        scale = 1.0 / (self.re * self.re + self.im * self.im)
        return Cx(self.re * scale, -self.im * scale)

    def root(self):
        size = jnp.sqrt(self.re * self.re + self.im * self.im)
        re = jnp.sqrt(0.5 * (size + self.re))
        return Cx(re, 0.5 * self.im / re)

    def map(self, function):
        return Cx(function(self.re), function(self.im))

    def row(self, index):
        return self.map(lambda part: jnp.broadcast_to(part[index : index + 1], (8, LANES)))

    def lanes(self, shift):
        return self.map(lambda part: lane_roll(part, shift))

    def subs(self, shift):
        return self.map(lambda part: sub_roll(part, shift))


def roll_by(value, shift):
    return pltpu.roll(value, shift, 1)


def flat(values):
    return tuple(part for value in values for part in (value.re, value.im))


def packs(parts):
    return [Cx(*parts[i : i + 2]) for i in range(0, len(parts), 2)]


def pick(mask, first, second):
    if not isinstance(second, Cx):
        return first.map(lambda part: jnp.where(mask, part, second))
    return Cx(jnp.where(mask, first.re, second.re), jnp.where(mask, first.im, second.im))


def total(terms):
    terms = list(terms)
    while len(terms) > 1:
        terms = [
            terms[i] + terms[i + 1] if i + 1 < len(terms) else terms[i]
            for i in range(0, len(terms), 2)
        ]
    return terms[0]


def harmonic(left, right):
    return (left * right) * (left + right).inverse() * 2.0


def lamination(skin, base):
    above = Cx(jnp.ones_like(skin), jnp.zeros_like(skin))
    field = Cx(jnp.ones_like(skin), 0.5 * skin)
    summed = above
    for _ in range(SHEET_NODES - 1):
        summed = summed + field
        below = Cx(
            2.0 * field.re - skin * field.im - above.re,
            2.0 * field.im + skin * field.re - above.im,
        )
        above, field = field, below
    return field * summed.inverse() * (base * SHEET_NODES)


def factor(entry):
    work = {(r, c): entry(r, c) for r in range(4) for c in range(r + 1)}
    lower, pivots = {}, []
    for k in range(4):
        inverse = work[k, k].inverse()
        pivots.append(inverse)
        for r in range(k + 1, 4):
            lower[r, k] = work[r, k] * inverse
        for r in range(k + 1, 4):
            for c in range(k + 1, r + 1):
                work[r, c] = work[r, c] - lower[r, k] * work[c, k]
    return lower, pivots


def solve(lower, pivots, right):
    half = []
    for r in range(4):
        value = right[r]
        for c in range(r):
            value = value - lower[r, c] * half[c]
        half.append(value)
    out = [None] * 4
    for r in range(3, -1, -1):
        value = half[r] * pivots[r]
        for c in range(r + 1, 4):
            value = value - lower[c, r] * out[c]
        out[r] = value
    return out


def inverse2(first, second, cross):
    scale = (first * second - cross * cross).inverse()
    return second * scale, first * scale, -(cross * scale)


def solve_blocks(entry, right):
    cross = [[entry(2 + c, r) for c in range(2)] for r in range(2)]
    i00, i11, i01 = inverse2(entry(0, 0), entry(1, 1), entry(1, 0))
    ratio = [
        [i00 * cross[0][c] + i01 * cross[1][c] for c in range(2)],
        [i01 * cross[0][c] + i11 * cross[1][c] for c in range(2)],
    ]

    def rest(r, c):
        return entry(2 + r, 2 + c) - (cross[0][r] * ratio[0][c] + cross[1][r] * ratio[1][c])

    j00, j11, j01 = inverse2(rest(0, 0), rest(1, 1), rest(1, 0))
    start = [i00 * right[0] + i01 * right[1], i01 * right[0] + i11 * right[1]]
    low = [right[2 + r] - (ratio[0][r] * right[0] + ratio[1][r] * right[1]) for r in range(2)]
    out = [j00 * low[0] + j01 * low[1], j01 * low[0] + j11 * low[1]]
    return [start[r] - (ratio[r][0] * out[0] + ratio[r][1] * out[1]) for r in range(2)] + out


def seeds(lower, pivots):
    column = iota(0) & 3
    unit = {}
    for r in range(4):
        for c in range(r - 1, -1, -1):
            value = -lower[r, c]
            for k in range(c + 1, r):
                value = value - lower[r, k] * unit[k, c]
            unit[r, c] = value
    roots = [pivot.root() for pivot in pivots]
    out = []
    for r in range(4):
        value = pick(column == r, roots[r], 0.0)
        for k in range(r + 1, 4):
            value = pick(column == k, roots[k] * unit[k, r], value)
        out.append(value)
    return out


def evens(tiles):
    lane = iota(1)
    index = (2 * lane) & (LANES - 1)

    def one(offset):
        return Cx(
            *(
                jnp.where(
                    lane < LANES // 2,
                    lane_take(first, index + offset),
                    lane_take(second, index + offset),
                )
                for first, second in ((tiles[0].re, tiles[1].re), (tiles[0].im, tiles[1].im))
            )
        )

    return one(0), one(1)


def natural(even, odd):
    lane = iota(1)
    out = []
    for half in range(2):
        index = half * (LANES // 2) + (lane >> 1)
        out.append(
            Cx(
                *(
                    jnp.where((lane & 1) == 0, lane_take(first, index), lane_take(second, index))
                    for first, second in ((even.re, odd.re), (even.im, odd.im))
                )
            )
        )
    return out


def split(value):
    high = value.map(lambda part: part.astype(jnp.bfloat16).astype(jnp.float32))
    return high, value - high


def contract(left, right):
    return lax.dot_general(
        left,
        right,
        (((0,), (0,)), ((), ())),
        preferred_element_type=jnp.float32,
    )


def strip(main, side, is_alpha, first_cycle, radial_count):
    lane, sub = iota(1), iota(0)
    lower4 = sub < 4
    column = sub & 3

    rims = lamination(*side)
    tiles = [lamination(*cells) for cells in main]
    cycle = (first_cycle + sub - 1).astype(jnp.float32)
    center = 1.0 + (cycle + 0.5) / radial_count
    face = 1.0 + cycle / radial_count
    per_center = 1.0 / center
    first_lane, last_lane = lane == 0, lane == LANES - 1

    ahead = [tile.lanes(1) for tile in tiles]
    west = [
        harmonic(pick(first_lane, rims.lanes(1), ahead[0]), tiles[0]) * per_center,
        harmonic(pick(first_lane, ahead[0], ahead[1]), tiles[1]) * per_center,
    ]
    wall = harmonic(tiles[1], rims.lanes(-1)) * per_center * 2.0
    back = [tile.lanes(-1) for tile in west]
    east = [pick(last_lane, back[1], back[0]), pick(last_lane, wall, back[1])]
    west[0] = pick(first_lane, west[0] * 2.0, west[0])
    south, north = [], []
    for tile in tiles:
        radial = harmonic(tile.subs(1), tile) * face
        radial = pick((sub == 1) | (sub == 5), radial * 2.0, radial)
        south.append(radial)
        north.append(radial.subs(-1))
    diagonal = [west[h] + east[h] + south[h] + north[h] for h in range(2)]
    gain_in = [south[h].row(1) for h in range(2)]
    gain_out = [north[h].row(4) for h in range(2)]

    diag_e, diag_o = evens(diagonal)
    east_e, east_o = evens(east)
    up_e, up_o = evens(north)
    left_e = pick(last_lane, east_o, 0.0)
    left_e = (east_o - left_e).lanes(1)

    def entry_e(r, c):
        if r == c:
            return diag_e.row(r + 1)
        return -up_e.row(r)

    lower_e, pivots_e = {}, []
    work = diag_e.row(1)
    for r in range(4):
        pivots_e.append(work.inverse())
        if r < 3:
            coupling = up_e.row(r + 1)
            lower_e[r + 1, r] = -(coupling * pivots_e[r])
            work = diag_e.row(r + 2) + lower_e[r + 1, r] * coupling
    zero = jnp.zeros((8, LANES), jnp.float32)
    nothing = Cx(zero, zero)
    half = []
    for r in range(4):
        value = Cx(jnp.where(column == r, 1.0, zero), zero)
        if r:
            value = value - lower_e[r, r - 1] * half[r - 1]
        half.append(value)
    inverse_e = [None] * 4
    for r in range(3, -1, -1):
        value = half[r] * pivots_e[r]
        if r < 3:
            value = value - lower_e[r + 1, r] * inverse_e[r + 1]
        inverse_e[r] = value
    for r in range(4):
        for c in range(r - 1):
            lower_e[r, c] = nothing
    seeds_e = seeds(lower_e, pivots_e)
    sides_e = pick(lower4, left_e.subs(-1), east_e.subs(3))
    reach_e = [inverse_e[r] * sides_e for r in range(4)]
    matrix, pair = [], []
    for r in range(4):
        to_left = (left_e.row(r + 1) * reach_e[r]).lanes(-1)
        to_right = east_e.row(r + 1) * reach_e[r]
        pair.append(pick(lower4, to_right, to_left))
        change = pick(lower4, to_left, to_right)
        base = pick(column == r, diag_o.row(r + 1), 0.0)
        if r < 3:
            base = pick(column == r + 1, -up_o.row(r + 1), base)
        if r > 0:
            base = pick(column == r - 1, -up_o.row(r), base)
        matrix.append(base - change - change.subs(4))

    def halve(level, state):
        matrix, pair = packs(state[:8]), packs(state[8:])
        step = jnp.left_shift(1, level)
        stay = ((lane + 1) & (2 * step - 1)) == 0
        reach = solve_blocks(lambda r, c: matrix[r].row(c), pair)
        next_matrix, next_pair = [], []
        for r in range(4):
            to_left = total(pair[k].row(r) * reach[k] for k in range(4))
            to_left = to_left.map(lambda part: roll_by(part, LANES - step))
            to_right = total(pair[k].row(4 + r) * reach[k] for k in range(4))
            to_right = to_right.map(lambda part: roll_by(part, step))
            change = pick(lower4, to_left, to_right)
            change = change + change.subs(4)
            next_matrix.append(pick(stay, matrix[r] - change, matrix[r]))
            next_pair.append(pick(stay, pick(lower4, to_right, to_left), pair[r]))
        return flat(next_matrix) + flat(next_pair)

    state = lax.fori_loop(0, 7, halve, flat(matrix) + flat(pair))
    matrix, pair = packs(state[:8]), packs(state[8:])

    lower, pivots = factor(lambda r, c: matrix[r].row(c))
    reach = solve(lower, pivots, pair)
    reach_rows = [[reach[r].row(k) for k in range(8)] for r in range(4)]
    seed = seeds(lower, pivots)

    def level_of(group):
        return jnp.where(lower4, 2 * group - 1, 2 * group)

    own_level = jnp.ones((8, LANES), jnp.int32)
    for level in range(2, 9):
        own_level = own_level + (((lane + 1) & ((1 << (level - 1)) - 1)) == 0).astype(jnp.int32)

    odd = {}
    for group in range(1, GROUPS + 1):
        rows = [pick(own_level == level_of(group), seed[r], 0.0) for r in range(4)]
        for level in range(min(2 * group - 1, 7), 0, -1):
            step = 1 << (level - 1)
            here = own_level == level
            before = [row.lanes(step) for row in rows]
            after = [row.lanes(-step) for row in rows]
            fresh = []
            for r in range(4):
                terms = [reach_rows[r][k] * before[k] for k in range(4)]
                terms += [reach_rows[r][4 + k] * after[k] for k in range(4)]
                fresh.append(rows[r] + pick(here, total(terms), 0.0))
            rows = fresh
        odd[group] = rows

    reach_e_rows = [[reach_e[r].row(k) for k in range(8)] for r in range(4)]
    even = {0: [pick(first_lane & lower4, seeds_e[r], 0.0) for r in range(4)]}
    odd[0] = [nothing] * 4
    for group in range(1, GROUPS + 1):
        before = [row.lanes(1) for row in odd[group]]
        even[group] = []
        for r in range(4):
            terms = [reach_e_rows[r][4 + k] * odd[group][k] for k in range(4)]
            if r in (0, 3):
                terms += [reach_e_rows[r][k] * before[k] for k in range(4)]
            even[group].append(total(terms))

    def corners(lefts, rights):
        return pick(
            lane == 0,
            lefts[0],
            pick(
                lane == 1,
                lefts[1].lanes(1),
                pick(lane == 2, rights[0].lanes(3), pick(lane == 3, rights[1].lanes(4), 0.0)),
            ),
        )

    gains_left = [west[0].row(r + 1) for r in range(4)]
    gains_right = [east[1].row(r + 1) for r in range(4)]
    gain_corner = [
        corners(gains_left[2 * t : 2 * t + 2], gains_right[2 * t : 2 * t + 2]) for t in range(2)
    ]
    inner, outer, corner = {}, {}, {}
    for group in range(GROUPS + 1):
        if group:
            low = natural(even[group][0], odd[group][0])
            high = natural(even[group][3], odd[group][3])
        else:
            low, high = [even[0][0], nothing], [even[0][3], nothing]
        inner[group] = [low[h] * gain_in[h] for h in range(2)]
        outer[group] = [high[h] * gain_out[h] for h in range(2)]
        corner[group] = [
            corners(even[group][2 * t : 2 * t + 2], odd[group][2 * t : 2 * t + 2]) * gain_corner[t]
            for t in range(2)
        ]

    left_parts, right_parts = [], []
    for group in range(GROUPS + 1):
        if group in (0, GROUPS):
            low, high = inner[group], outer[group]
        else:
            near = lane < (2 << level_of(group))
            low = [pick(near, inner[group][0], 0.0), nothing]
            high = [pick(near, outer[group][0], 0.0), nothing]
        side_a, side_b = corner[group]
        own = [pick(is_alpha, low[h], high[h]) for h in range(2)]
        own.append(pick(is_alpha, side_a, side_b))
        moved = [high[0].lanes(4), high[1].lanes(4)]
        every = [
            low[0],
            low[1],
            pick(lower_lanes(lane, 4), side_a, moved[0]),
            pick(lower_lanes(lane, 4), moved[0], moved[1]),
            pick(lower_lanes(lane, 4), moved[1], pick(lane < 8, side_b.lanes(4), 0.0)),
        ]
        left_parts.append([split(value) for value in own])
        right_parts.append([split(value) for value in every])

    def wide(parts, which, name, sign=1.0):
        rows = []
        for group in parts:
            pieces = [getattr(value[which], name) for value in group]
            row = jnp.concatenate(pieces, axis=1)
            rows.append(row if sign > 0 else -row)
        return rows

    def stacked(parts, order):
        rows = [row for which, name, sign in order for row in wide(parts, which, name, sign)]
        rows += [jnp.zeros_like(rows[0])] * (32 - len(rows))
        return jnp.concatenate(rows, axis=0).astype(jnp.bfloat16)

    hr, hi, lr, li = (0, "re"), (0, "im"), (1, "re"), (1, "im")
    left = stacked(left_parts, [key + (-1.0,) for key in (hr, hr, lr, hi, hi, li)])
    signs = (1.0, 1.0, 1.0, -1.0, -1.0, -1.0)
    right_re = stacked(
        right_parts, [key + (sign,) for key, sign in zip((hr, lr, hr, hi, li, hi), signs)]
    )
    right_im = stacked(right_parts, [key + (1.0,) for key in (hi, li, hi, hr, lr, hr)])
    top = contract(left, jnp.concatenate([right_re, right_im], axis=1))
    top = Cx(top[:, : 5 * LANES], top[:, 5 * LANES :])

    wide_lane = lax.broadcasted_iota(jnp.int32, (16, LANES), 1)
    wide_sub = lax.broadcasted_iota(jnp.int32, (16, LANES), 0)
    masks = []
    for level in range(1, 5):
        for tile in range(1 << (4 - level)):
            mask = (wide_lane >> (level + 1)) == 4 * tile + (wide_sub >> 2)
            masks.append((level, mask))
    last = ((wide_lane >> 6) == (wide_sub >> 2)) | ((wide_sub >> 2) == 2)
    masks = [
        (level, jnp.where(mask, 1.0, 0.0).astype(jnp.bfloat16))
        for level, mask in masks + [(5, last)]
    ]

    def spread(values, half):
        levels = {}
        for group in range(1, GROUPS):
            value = values[group]
            if half == 0:
                value = pick(lane < (2 << level_of(group)), nothing, value)
            turned = value.subs(4)
            levels[2 * group - 1] = pick(lower4, value, turned)
            levels[2 * group] = pick(lower4, turned, value)
        out = {}
        for name in ("re", "im"):
            parts = {level: getattr(value, name) for level, value in levels.items()}
            tiles = {level: [parts[level]] * 2 for level in range(1, 5)}
            tiles[5] = [parts[5], parts[6]]
            tiles = {level: jnp.concatenate(tile, axis=0) for level, tile in tiles.items()}
            high = {level: tile.astype(jnp.bfloat16) for level, tile in tiles.items()}
            low = {
                level: (tile - high[level].astype(jnp.float32)).astype(jnp.bfloat16)
                for level, tile in tiles.items()
            }
            for which, part in enumerate((high, low)):
                rows = [part[level] * mask for level, mask in masks]
                out[which, name] = jnp.concatenate(rows, axis=0)
        return out

    even_d = [inverse_e[0].row(0), inverse_e[0].row(3), inverse_e[3].row(3)]
    even_d = [natural(value, nothing) for value in even_d]

    def local(half):
        low, high = {}, {}
        for group in range(1, GROUPS):
            low[group], high[group] = inner[group][half], outer[group][half]
        mine = {group: -pick(is_alpha, low[group], high[group]) for group in low}
        low, high, mine = [spread(values, half) for values in (low, high, mine)]
        every = {key: jnp.concatenate([low[key], high[key]], axis=1) for key in low}
        left = jnp.concatenate([mine[key] for key in (hr, hi, hr, hi, lr, li)], axis=0)
        right_re = jnp.concatenate(
            [every[hr], -every[hi], every[lr], -every[li], every[hr], -every[hi]], axis=0
        )
        right_im = jnp.concatenate([every[key] for key in (hi, hr, li, lr, hi, hr)], axis=0)
        product = contract(left, jnp.concatenate([right_re, right_im], axis=1))
        product = Cx(product[:, : 2 * LANES], product[:, 2 * LANES :])
        g_in, g_out = gain_in[half], gain_out[half]
        solo = (lane & 1) == 0
        if half == 0:
            solo = solo & (lane > 0)
        cross = even_d[1][half] * g_in * g_out
        on_in = pick(is_alpha, even_d[0][half] * g_in * g_in, cross)
        on_out = pick(is_alpha, cross, even_d[2][half] * g_out * g_out)
        on_in = pick(is_alpha, g_in, nothing) - pick(solo, on_in, 0.0)
        on_out = pick(is_alpha, nothing, g_out) - pick(solo, on_out, 0.0)
        return product, on_in, on_out

    edge = pick((lane == sub) & lower4, pick(is_alpha, gain_corner[0], gain_corner[1]), 0.0)
    return top, local, edge


def lower_lanes(lane, count):
    return lane < count


def finish(top, local, edge, is_alpha, store):
    lane, sub = iota(1), iota(0)
    full = [top.re, top.im]
    for half in range(2):
        terms = local(half)
        for row in range(0, LANES, 8):
            here = lane == sub + row
            at = half * LANES + row
            both = []
            for part, name in enumerate(("re", "im")):
                product, on_in, on_out = [getattr(value, name) for value in terms]
                low = product[row : row + 8, :LANES] + jnp.where(here, on_in, 0.0)
                high = product[row : row + 8, LANES:] + jnp.where(here, on_out, 0.0)
                high = lane_roll(high, 4)
                out = [full[part][at : at + 8, t * LANES : (t + 1) * LANES] for t in range(5)]
                out[half] = out[half] + low
                out[2 + half] = out[2 + half] + jnp.where(lane < 4, 0.0, high)
                out[3 + half] = out[3 + half] + jnp.where(lane < 4, high, 0.0)
                both.append(out)
            store(at, 8, both)
    at = 2 * LANES
    both = []
    for part, name in enumerate(("re", "im")):
        edge_part = getattr(edge, name)
        out = [full[part][at : at + 8, t * LANES : (t + 1) * LANES] for t in range(5)]
        out[2] = out[2] + jnp.where(is_alpha, edge_part, 0.0)
        out[4] = out[4] + jnp.where(is_alpha, 0.0, lane_roll(edge_part, 4))
        both.append(out)
    store(at, 4, both)


def interleaved(first, second, half):
    sub = iota(0)
    index = 4 * half + (sub >> 1)
    return jnp.where((sub & 1) == 0, sub_take(first, index), sub_take(second, index))


def gather_rows(own, other, is_alpha, is_first, is_last, main, side):
    lane = lax.broadcasted_iota(jnp.int32, (2, LANES), 1)
    for field in range(2):
        rows = slice(2 * field, 2 * field + 2)
        (mine, after, near, before), (theirs, after_x, far, before_x) = (
            [ref[rows, :] for ref in refs] for refs in (own, other)
        )
        alpha, beta = jnp.where(is_alpha, mine, theirs), jnp.where(is_alpha, theirs, mine)
        main[field, 0:1, :] = jnp.where(is_first, alpha[0:1], jnp.where(is_alpha, near, far)[1:2])
        main[field, 1:3, :] = alpha
        main[field, 3:5, :] = beta
        main[field, 5:6, :] = jnp.where(is_last, beta[1:2], jnp.where(is_alpha, far, near)[0:1])
        main[field, 6:8, :] = beta
        ends = []
        for lefts, rights in ((before, after), (before_x, after_x)):
            ends.append(jnp.where(lane == LANES - 1, lefts[:, LANES:], rights[:, :LANES]))
        ends_alpha = jnp.where(is_alpha, ends[0], ends[1])
        ends_beta = jnp.where(is_alpha, ends[1], ends[0])
        side[field, 0:1, :] = ends_alpha[0:1]
        side[field, 1:3, :] = ends_alpha
        side[field, 3:5, :] = ends_beta
        side[field, 5:7, :] = ends_beta
        side[field, 7:8, :] = ends_beta[0:1]


def looked_up(tables, angular, material, sheet):
    index = material.astype(jnp.int32)
    sigma, base = [lane_take(table, index) for table in tables]
    return angular * sigma * sheet * sheet, base


def merge_kernel(cycles, depth, angular, *refs):
    own, other, (out, main, side, held, rest, sems) = refs[:4], refs[4:8], refs[8:]
    index = lax.axis_index("rad")
    is_alpha = index % 2 == 0
    is_first = index // 2 == 0
    is_last = index // 2 == cycles // 2 - 1
    gather_rows(own, other, is_alpha, is_first, is_last, main, side)
    tables = [
        jnp.broadcast_to(own[0][row : row + 1, :LANES], (8, LANES)) for row in (4, 5)
    ]
    parts = [(main, 0), (main, LANES), (side, 0)]
    parts = [
        looked_up(tables, angular[0], ref[0, :, at : at + LANES], ref[1, :, at : at + LANES])
        for ref, at in parts
    ]
    top, local, edge = strip(
        parts[:2],
        parts[2],
        is_alpha,
        (index // 2) * (2 * depth),
        cycles * depth,
    )
    rows, columns = out.shape[0], out.shape[2]
    bounds = [0, 64, 128, 192, rows]
    whole = held.shape[0]
    copies = []
    for number, (first, last) in enumerate(zip(bounds, bounds[1:])):
        part = []
        for tile in range(whole + 1):
            if tile < whole:
                source = held.at[tile].reshape(rows, 2, LANES)
            else:
                source = rest
            at = tile * LANES
            target = out.at[first:last, :, at : min(at + LANES, columns)]
            part.append(
                pltpu.make_async_copy(source.at[first:last, :, :], target, sems.at[number, tile])
            )
        copies.append(part)

    def store(row, count, both):
        for part, tiles in enumerate(both):
            for number, tile in enumerate(tiles[:whole]):
                held[number, pl.ds(2 * row + part, count, stride=2), :] = tile[:count]
        for half in range(count // 4):
            tile = interleaved(both[0][whole], both[1][whole], half).reshape(4, 2, LANES)
            first = row + 4 * half
            rest[first : first + 4, :, :] = tile[:, :, : rest.shape[2]]
        if row + count in bounds:
            for copy in copies[bounds.index(row + count) - 1]:
                copy.start()

    finish(top, local, edge, is_alpha, store)
    for part in copies:
        for copy in part:
            copy.wait()


def pack_kernel(*refs):
    sources, (out_ref,), targets, sems = refs[:4], refs[4:5], refs[5:9], refs[9]
    copies = [
        pltpu.make_async_copy(source, target, sems.at[number])
        for number, (source, target) in enumerate(zip(sources, targets))
    ]
    for copy in copies:
        copy.start()
    for copy in copies:
        copy.wait()
    material_ref, sheet_ref, sigma_ref, nu_ref = targets
    out_ref[:2, :] = material_ref[...].astype(jnp.float32)
    out_ref[2:4, :] = sheet_ref[...]
    for row, ref in ((4, sigma_ref), (5, nu_ref)):
        out_ref[row : row + 1, : ref.shape[0]] = ref[...].reshape(1, ref.shape[0])


def packed(*arguments):
    held = [pltpu.with_memory_space_constraint(value, pltpu.HBM) for value in arguments]
    return pl.pallas_call(
        pack_kernel,
        out_shape=jax.ShapeDtypeStruct((8, arguments[1].shape[1]), jnp.float32),
        in_specs=[pl.BlockSpec(memory_space=pltpu.HBM)] * 4,
        out_specs=pl.BlockSpec(memory_space=pltpu.VMEM),
        scratch_shapes=[pltpu.VMEM(value.shape, value.dtype) for value in arguments]
        + [pltpu.SemaphoreType.DMA((4,))],
        compiler_params=pltpu.CompilerParams(vmem_limit_bytes=4 * 1024 * 1024),
        name="cells",
    )(*held)


def swapped(cells, axis, first):
    count = lax.axis_size(axis)
    route = []
    for low in range(first, count, 2):
        high = (low + 1) % count
        route += [(low, high), (high, low)]
    return lax.ppermute(cells, axis, route)


def per_device(material_id, thickness, sigma_table, nu_table, angular_frequency):
    depth, arc = thickness.shape
    cells = packed(material_id, thickness, sigma_table, nu_table)
    cycles = lax.axis_size("rad")
    blocks = lax.axis_size("az")
    before = lax.ppermute(cells, "az", [(i, (i + 1) % blocks) for i in range(blocks)])
    after = lax.ppermute(cells, "az", [((i + 1) % blocks, i) for i in range(blocks)])
    own = [cells, after, swapped(cells, "rad", 1), before]
    other = [swapped(part, "rad", 0) for part in own]
    outer_nodes = arc + 2 * depth
    whole, rest = divmod(2 * outer_nodes, LANES)
    out = pl.pallas_call(
        lambda *refs: merge_kernel(cycles, depth, *refs),
        out_shape=jax.ShapeDtypeStruct((outer_nodes, 2, 2 * outer_nodes), jnp.float32),
        in_specs=[pl.BlockSpec(memory_space=pltpu.SMEM)]
        + [pl.BlockSpec(memory_space=pltpu.VMEM)] * 8,
        out_specs=pl.BlockSpec(memory_space=pltpu.HBM),
        scratch_shapes=[
            pltpu.VMEM((2, 8, arc), jnp.float32),
            pltpu.VMEM((2, 8, LANES), jnp.float32),
            pltpu.VMEM((whole, 2 * outer_nodes, LANES), jnp.float32),
            pltpu.VMEM((outer_nodes, 2, rest), jnp.float32),
            pltpu.SemaphoreType.DMA((4, whole + 1)),
        ],
        compiler_params=pltpu.CompilerParams(vmem_limit_bytes=48 * 1024 * 1024),
        name="pair_map",
    )(angular_frequency, *own, *other)
    return jnp.transpose(out, (1, 0, 2))


def solution(mesh):
    placed = (P("rad", "az"), P("rad", "az"), P(), P(), P())
    return jax.shard_map(
        per_device, mesh=mesh, in_specs=placed, out_specs=P(None, "rad", "az"), check_vma=False
    )
```

```python
import jax
import jax.numpy as jnp
from jax import lax
from jax.experimental import pallas as pl
from jax.experimental.pallas import tpu as pltpu
from jax.sharding import PartitionSpec as P

SHEET_NODES = 16
LANES = 128
GROUPS = 4


def lane_roll(value, shift):
    return pltpu.roll(value, shift % value.shape[1], 1)


def sub_roll(value, shift):
    return pltpu.roll(value, shift % value.shape[0], 0)


def lane_take(value, index):
    return jnp.take_along_axis(value, index, axis=1, mode="promise_in_bounds")


def sub_take(value, index):
    return jnp.take_along_axis(value, index, axis=0, mode="promise_in_bounds")


def iota(dim):
    return lax.broadcasted_iota(jnp.int32, (8, LANES), dim)


class Cx:
    def __init__(self, re, im):
        self.re, self.im = re, im

    def __add__(self, other):
        return Cx(self.re + other.re, self.im + other.im)

    def __sub__(self, other):
        return Cx(self.re - other.re, self.im - other.im)

    def __neg__(self):
        return Cx(-self.re, -self.im)

    def __mul__(self, other):
        if not isinstance(other, Cx):
            return Cx(self.re * other, self.im * other)
        return Cx(
            self.re * other.re - self.im * other.im, self.re * other.im + self.im * other.re
        )

    def inverse(self):
        scale = 1.0 / (self.re * self.re + self.im * self.im)
        return Cx(self.re * scale, -self.im * scale)

    def root(self):
        size = jnp.sqrt(self.re * self.re + self.im * self.im)
        re = jnp.sqrt(0.5 * (size + self.re))
        return Cx(re, 0.5 * self.im / re)

    def map(self, function):
        return Cx(function(self.re), function(self.im))

    def row(self, index):
        return self.map(lambda part: jnp.broadcast_to(part[index : index + 1], (8, LANES)))

    def lanes(self, shift):
        return self.map(lambda part: lane_roll(part, shift))

    def subs(self, shift):
        return self.map(lambda part: sub_roll(part, shift))


def pick(mask, first, second):
    if not isinstance(second, Cx):
        return first.map(lambda part: jnp.where(mask, part, second))
    return Cx(jnp.where(mask, first.re, second.re), jnp.where(mask, first.im, second.im))


def total(terms):
    terms = list(terms)
    while len(terms) > 1:
        terms = [
            terms[i] + terms[i + 1] if i + 1 < len(terms) else terms[i]
            for i in range(0, len(terms), 2)
        ]
    return terms[0]


def harmonic(left, right):
    return (left * right) * (left + right).inverse() * 2.0


def lamination(skin, base):
    above = Cx(jnp.ones_like(skin), jnp.zeros_like(skin))
    field = Cx(jnp.ones_like(skin), 0.5 * skin)
    summed = above
    for _ in range(SHEET_NODES - 1):
        summed = summed + field
        below = Cx(
            2.0 * field.re - skin * field.im - above.re,
            2.0 * field.im + skin * field.re - above.im,
        )
        above, field = field, below
    return field * summed.inverse() * (base * SHEET_NODES)


def factor(entry):
    work = {(r, c): entry(r, c) for r in range(4) for c in range(r + 1)}
    lower, pivots = {}, []
    for k in range(4):
        inverse = work[k, k].inverse()
        pivots.append(inverse)
        for r in range(k + 1, 4):
            lower[r, k] = work[r, k] * inverse
        for r in range(k + 1, 4):
            for c in range(k + 1, r + 1):
                work[r, c] = work[r, c] - lower[r, k] * work[c, k]
    return lower, pivots


def solve(lower, pivots, right):
    half = []
    for r in range(4):
        value = right[r]
        for c in range(r):
            value = value - lower[r, c] * half[c]
        half.append(value)
    out = [None] * 4
    for r in range(3, -1, -1):
        value = half[r] * pivots[r]
        for c in range(r + 1, 4):
            value = value - lower[c, r] * out[c]
        out[r] = value
    return out


def inverse2(first, second, cross):
    scale = (first * second - cross * cross).inverse()
    return second * scale, first * scale, -(cross * scale)


def solve_blocks(entry, right):
    cross = [[entry(2 + c, r) for c in range(2)] for r in range(2)]
    i00, i11, i01 = inverse2(entry(0, 0), entry(1, 1), entry(1, 0))
    ratio = [
        [i00 * cross[0][c] + i01 * cross[1][c] for c in range(2)],
        [i01 * cross[0][c] + i11 * cross[1][c] for c in range(2)],
    ]

    def rest(r, c):
        return entry(2 + r, 2 + c) - (cross[0][r] * ratio[0][c] + cross[1][r] * ratio[1][c])

    j00, j11, j01 = inverse2(rest(0, 0), rest(1, 1), rest(1, 0))
    start = [i00 * right[0] + i01 * right[1], i01 * right[0] + i11 * right[1]]
    low = [right[2 + r] - (ratio[0][r] * right[0] + ratio[1][r] * right[1]) for r in range(2)]
    out = [j00 * low[0] + j01 * low[1], j01 * low[0] + j11 * low[1]]
    return [start[r] - (ratio[r][0] * out[0] + ratio[r][1] * out[1]) for r in range(2)] + out


def seeds(lower, pivots):
    column = iota(0) & 3
    unit = {}
    for r in range(4):
        for c in range(r - 1, -1, -1):
            value = -lower[r, c]
            for k in range(c + 1, r):
                value = value - lower[r, k] * unit[k, c]
            unit[r, c] = value
    roots = [pivot.root() for pivot in pivots]
    out = []
    for r in range(4):
        value = pick(column == r, roots[r], 0.0)
        for k in range(r + 1, 4):
            value = pick(column == k, roots[k] * unit[k, r], value)
        out.append(value)
    return out


def evens(tiles):
    lane = iota(1)
    index = (2 * lane) & (LANES - 1)

    def one(offset):
        return Cx(
            *(
                jnp.where(
                    lane < LANES // 2,
                    lane_take(first, index + offset),
                    lane_take(second, index + offset),
                )
                for first, second in ((tiles[0].re, tiles[1].re), (tiles[0].im, tiles[1].im))
            )
        )

    return one(0), one(1)


def natural(even, odd):
    lane = iota(1)
    out = []
    for half in range(2):
        index = half * (LANES // 2) + (lane >> 1)
        out.append(
            Cx(
                *(
                    jnp.where((lane & 1) == 0, lane_take(first, index), lane_take(second, index))
                    for first, second in ((even.re, odd.re), (even.im, odd.im))
                )
            )
        )
    return out


def split(value):
    high = value.map(lambda part: part.astype(jnp.bfloat16).astype(jnp.float32))
    return high, value - high


def contract(left, right):
    return lax.dot_general(
        left,
        right,
        (((0,), (0,)), ((), ())),
        preferred_element_type=jnp.float32,
    )


def strip(main, side, is_alpha, first_cycle, radial_count):
    lane, sub = iota(1), iota(0)
    lower4 = sub < 4
    column = sub & 3

    rims = lamination(*side)
    tiles = [lamination(*cells) for cells in main]
    cycle = (first_cycle + sub - 1).astype(jnp.float32)
    center = 1.0 + (cycle + 0.5) / radial_count
    face = 1.0 + cycle / radial_count
    per_center = 1.0 / center
    first_lane, last_lane = lane == 0, lane == LANES - 1

    ahead = [tile.lanes(1) for tile in tiles]
    west = [
        harmonic(pick(first_lane, rims.lanes(1), ahead[0]), tiles[0]) * per_center,
        harmonic(pick(first_lane, ahead[0], ahead[1]), tiles[1]) * per_center,
    ]
    wall = harmonic(tiles[1], rims.lanes(-1)) * per_center * 2.0
    back = [tile.lanes(-1) for tile in west]
    east = [pick(last_lane, back[1], back[0]), pick(last_lane, wall, back[1])]
    west[0] = pick(first_lane, west[0] * 2.0, west[0])
    south, north = [], []
    for tile in tiles:
        radial = harmonic(tile.subs(1), tile) * face
        radial = pick((sub == 1) | (sub == 5), radial * 2.0, radial)
        south.append(radial)
        north.append(radial.subs(-1))
    diagonal = [west[h] + east[h] + south[h] + north[h] for h in range(2)]
    gain_in = [south[h].row(1) for h in range(2)]
    gain_out = [north[h].row(4) for h in range(2)]

    diag_e, diag_o = evens(diagonal)
    east_e, east_o = evens(east)
    up_e, up_o = evens(north)
    left_e = pick(last_lane, east_o, 0.0)
    left_e = (east_o - left_e).lanes(1)

    def entry_e(r, c):
        if r == c:
            return diag_e.row(r + 1)
        return -up_e.row(r)

    lower_e, pivots_e = {}, []
    work = diag_e.row(1)
    for r in range(4):
        pivots_e.append(work.inverse())
        if r < 3:
            coupling = up_e.row(r + 1)
            lower_e[r + 1, r] = -(coupling * pivots_e[r])
            work = diag_e.row(r + 2) + lower_e[r + 1, r] * coupling
    zero = jnp.zeros((8, LANES), jnp.float32)
    nothing = Cx(zero, zero)
    half = []
    for r in range(4):
        value = Cx(jnp.where(column == r, 1.0, zero), zero)
        if r:
            value = value - lower_e[r, r - 1] * half[r - 1]
        half.append(value)
    inverse_e = [None] * 4
    for r in range(3, -1, -1):
        value = half[r] * pivots_e[r]
        if r < 3:
            value = value - lower_e[r + 1, r] * inverse_e[r + 1]
        inverse_e[r] = value
    for r in range(4):
        for c in range(r - 1):
            lower_e[r, c] = nothing
    seeds_e = seeds(lower_e, pivots_e)
    sides_e = pick(lower4, left_e.subs(-1), east_e.subs(3))
    reach_e = [inverse_e[r] * sides_e for r in range(4)]
    matrix, pair = [], []
    for r in range(4):
        to_left = (left_e.row(r + 1) * reach_e[r]).lanes(-1)
        to_right = east_e.row(r + 1) * reach_e[r]
        pair.append(pick(lower4, to_right, to_left))
        change = pick(lower4, to_left, to_right)
        base = pick(column == r, diag_o.row(r + 1), 0.0)
        if r < 3:
            base = pick(column == r + 1, -up_o.row(r + 1), base)
        if r > 0:
            base = pick(column == r - 1, -up_o.row(r), base)
        matrix.append(base - change - change.subs(4))

    for level in range(1, 8):
        step = 1 << (level - 1)
        stay = ((lane + 1) & (2 * step - 1)) == 0
        reach = solve_blocks(lambda r, c: matrix[r].row(c), pair)
        next_matrix, next_pair = [], []
        for r in range(4):
            to_left = total(pair[k].row(r) * reach[k] for k in range(4)).lanes(-step)
            to_right = total(pair[k].row(4 + r) * reach[k] for k in range(4)).lanes(step)
            change = pick(lower4, to_left, to_right)
            change = change + change.subs(4)
            next_matrix.append(pick(stay, matrix[r] - change, matrix[r]))
            next_pair.append(pick(stay, pick(lower4, to_right, to_left), pair[r]))
        matrix, pair = next_matrix, next_pair

    lower, pivots = factor(lambda r, c: matrix[r].row(c))
    reach = solve(lower, pivots, pair)
    reach_rows = [[reach[r].row(k) for k in range(8)] for r in range(4)]
    seed = seeds(lower, pivots)

    def level_of(group):
        return jnp.where(lower4, 2 * group - 1, 2 * group)

    own_level = jnp.ones((8, LANES), jnp.int32)
    for level in range(2, 9):
        own_level = own_level + (((lane + 1) & ((1 << (level - 1)) - 1)) == 0).astype(jnp.int32)

    odd = {}
    for group in range(1, GROUPS + 1):
        rows = [pick(own_level == level_of(group), seed[r], 0.0) for r in range(4)]
        for level in range(min(2 * group - 1, 7), 0, -1):
            step = 1 << (level - 1)
            here = own_level == level
            before = [row.lanes(step) for row in rows]
            after = [row.lanes(-step) for row in rows]
            fresh = []
            for r in range(4):
                terms = [reach_rows[r][k] * before[k] for k in range(4)]
                terms += [reach_rows[r][4 + k] * after[k] for k in range(4)]
                fresh.append(rows[r] + pick(here, total(terms), 0.0))
            rows = fresh
        odd[group] = rows

    reach_e_rows = [[reach_e[r].row(k) for k in range(8)] for r in range(4)]
    even = {0: [pick(first_lane & lower4, seeds_e[r], 0.0) for r in range(4)]}
    odd[0] = [nothing] * 4
    for group in range(1, GROUPS + 1):
        before = [row.lanes(1) for row in odd[group]]
        even[group] = []
        for r in range(4):
            terms = [reach_e_rows[r][4 + k] * odd[group][k] for k in range(4)]
            if r in (0, 3):
                terms += [reach_e_rows[r][k] * before[k] for k in range(4)]
            even[group].append(total(terms))

    def corners(lefts, rights):
        return pick(
            lane == 0,
            lefts[0],
            pick(
                lane == 1,
                lefts[1].lanes(1),
                pick(lane == 2, rights[0].lanes(3), pick(lane == 3, rights[1].lanes(4), 0.0)),
            ),
        )

    gains_left = [west[0].row(r + 1) for r in range(4)]
    gains_right = [east[1].row(r + 1) for r in range(4)]
    gain_corner = [
        corners(gains_left[2 * t : 2 * t + 2], gains_right[2 * t : 2 * t + 2]) for t in range(2)
    ]
    inner, outer, corner = {}, {}, {}
    for group in range(GROUPS + 1):
        if group:
            low = natural(even[group][0], odd[group][0])
            high = natural(even[group][3], odd[group][3])
        else:
            low, high = [even[0][0], nothing], [even[0][3], nothing]
        inner[group] = [low[h] * gain_in[h] for h in range(2)]
        outer[group] = [high[h] * gain_out[h] for h in range(2)]
        corner[group] = [
            corners(even[group][2 * t : 2 * t + 2], odd[group][2 * t : 2 * t + 2]) * gain_corner[t]
            for t in range(2)
        ]

    left_parts, right_parts = [], []
    for group in range(GROUPS + 1):
        if group in (0, GROUPS):
            low, high = inner[group], outer[group]
            if group == 0:
                low = [low[0], pick(lower4, nothing, inner[3][1])]
                high = [high[0], pick(lower4, nothing, outer[3][1])]
        else:
            near = lane < (2 << level_of(group))
            low = [pick(near, inner[group][0], 0.0), nothing]
            high = [pick(near, outer[group][0], 0.0), nothing]
        side_a, side_b = corner[group]
        own = [pick(is_alpha, low[h], high[h]) for h in range(2)]
        own.append(pick(is_alpha, side_a, side_b))
        moved = [high[0].lanes(4), high[1].lanes(4)]
        every = [
            low[0],
            low[1],
            pick(lower_lanes(lane, 4), side_a, moved[0]),
            pick(lower_lanes(lane, 4), moved[0], moved[1]),
            pick(lower_lanes(lane, 4), moved[1], pick(lane < 8, side_b.lanes(4), 0.0)),
        ]
        left_parts.append([split(value) for value in own])
        right_parts.append([split(value) for value in every])

    def wide(parts, which, name, sign=1.0):
        rows = []
        for group in parts:
            pieces = [getattr(value[which], name) for value in group]
            row = jnp.concatenate(pieces, axis=1)
            rows.append(row if sign > 0 else -row)
        return rows

    def stacked(parts, order):
        rows = [row for which, name, sign in order for row in wide(parts, which, name, sign)]
        rows += [jnp.zeros_like(rows[0])] * (32 - len(rows))
        return jnp.concatenate(rows, axis=0).astype(jnp.bfloat16)

    hr, hi, lr, li = (0, "re"), (0, "im"), (1, "re"), (1, "im")
    left = stacked(left_parts, [key + (-1.0,) for key in (hr, hr, lr, hi, hi, li)])
    signs = (1.0, 1.0, 1.0, -1.0, -1.0, -1.0)
    right_re = stacked(
        right_parts, [key + (sign,) for key, sign in zip((hr, lr, hr, hi, li, hi), signs)]
    )
    right_im = stacked(right_parts, [key + (1.0,) for key in (hi, li, hi, hr, lr, hr)])
    top = contract(left, jnp.concatenate([right_re, right_im], axis=1))
    top = Cx(top[:, : 5 * LANES], top[:, 5 * LANES :])

    wide_lane = lax.broadcasted_iota(jnp.int32, (16, LANES), 1)
    wide_sub = lax.broadcasted_iota(jnp.int32, (16, LANES), 0)
    masks = []
    within = wide_lane & 63
    for level in range(1, 4):
        for tile in range(1 << (3 - level)):
            masks.append((level, (within >> (level + 1)) == 4 * tile + (wide_sub >> 2)))
    last = ((within >> 5) == (wide_sub >> 2)) | ((wide_sub >> 2) == 2)
    masks = [
        (level, jnp.where(mask, 1.0, 0.0).astype(jnp.bfloat16))
        for level, mask in masks + [(4, last)]
    ]

    def spread(values):
        levels = {}
        for group in range(1, GROUPS):
            value = values[group]
            turned = value.subs(4)
            levels[2 * group - 1] = pick(lower4, value, turned)
            levels[2 * group] = pick(lower4, turned, value)
        out = {}
        for name in ("re", "im"):
            parts = {level: getattr(value, name) for level, value in levels.items()}
            tiles = {level: [parts[level]] * 2 for level in range(1, 4)}
            tiles[4] = [parts[4], parts[5]]
            tiles = {level: jnp.concatenate(tile, axis=0) for level, tile in tiles.items()}
            high = {level: tile.astype(jnp.bfloat16) for level, tile in tiles.items()}
            low = {
                level: (tile - high[level].astype(jnp.float32)).astype(jnp.bfloat16)
                for level, tile in tiles.items()
            }
            for which, part in enumerate((high, low)):
                rows = [part[level] * mask for level, mask in masks]
                out[which, name] = jnp.concatenate(rows, axis=0)
        return out

    even_d = [inverse_e[0].row(0), inverse_e[0].row(3), inverse_e[3].row(3)]
    even_d = [natural(value, nothing) for value in even_d]

    def local(half, quarter):
        packed, mine = {}, {}
        for group in range(1, GROUPS):
            low, high = inner[group][half], outer[group][half]
            if half == 0:
                near = lane < (2 << level_of(group))
                low, high = pick(near, nothing, low), pick(near, nothing, high)
            packed[group] = pick((lane >> 6) == quarter, low, high.lanes(64))
            turned = packed[group].lanes(64)
            pair = (packed[group], turned) if quarter == 0 else (turned, packed[group])
            mine[group] = -pick(is_alpha, *pair)
        every, mine = spread(packed), spread(mine)
        left = jnp.concatenate([mine[key] for key in (hr, hi, hr, hi, lr, li)], axis=0)
        right_re = jnp.concatenate(
            [every[hr], -every[hi], every[lr], -every[li], every[hr], -every[hi]], axis=0
        )
        right_im = jnp.concatenate([every[key] for key in (hi, hr, li, lr, hi, hr)], axis=0)
        product = contract(left[:, :64], jnp.concatenate([right_re, right_im], axis=1))
        return Cx(product[:, :LANES], product[:, LANES:])

    def diagonals(half):
        g_in, g_out = gain_in[half], gain_out[half]
        solo = (lane & 1) == 0
        if half == 0:
            solo = solo & (lane > 0)
        cross = even_d[1][half] * g_in * g_out
        on_in = pick(is_alpha, even_d[0][half] * g_in * g_in, cross)
        on_out = pick(is_alpha, cross, even_d[2][half] * g_out * g_out)
        on_in = pick(is_alpha, g_in, nothing) - pick(solo, on_in, 0.0)
        on_out = pick(is_alpha, nothing, g_out) - pick(solo, on_out, 0.0)
        return on_in, on_out.lanes(4)

    edge = pick((lane == sub) & lower4, pick(is_alpha, gain_corner[0], gain_corner[1]), 0.0)
    return top, (local, diagonals), edge


def lower_lanes(lane, count):
    return lane < count


def finish(top, local, edge, is_alpha, store):
    lane, sub = iota(1), iota(0)
    full = [top.re, top.im]
    local, diagonals = local
    for half, quarter in ((0, 0), (0, 1), (1, 0), (1, 1)):
        if quarter == 0:
            on_in, on_out = diagonals(half)
        product = local(half, quarter)
        inside = (lane >> 6) == quarter
        for row in range(0, 64, 8):
            here = lane == sub + (64 * quarter + row)
            moved = ((lane - 4) & (LANES - 1)) == sub + (64 * quarter + row)
            at = half * LANES + quarter * 64 + row
            both = []
            for part, name in enumerate(("re", "im")):
                value = getattr(product, name)[row : row + 8]
                low = jnp.where(inside, value, 0.0)
                low = low + jnp.where(here, getattr(on_in, name), 0.0)
                high = lane_roll(jnp.where(inside, 0.0, value), 68)
                high = high + jnp.where(moved, getattr(on_out, name), 0.0)
                out = [full[part][at : at + 8, t * LANES : (t + 1) * LANES] for t in range(5)]
                out[half] = out[half] + low
                if quarter == 0:
                    out[2 + half] = out[2 + half] + high
                else:
                    out[2 + half] = out[2 + half] + jnp.where(lane < 4, 0.0, high)
                    out[3 + half] = out[3 + half] + jnp.where(lane < 4, high, 0.0)
                both.append(out)
            store(at, 8, both)
    at = 2 * LANES
    both = []
    for part, name in enumerate(("re", "im")):
        edge_part = getattr(edge, name)
        out = [full[part][at : at + 8, t * LANES : (t + 1) * LANES] for t in range(5)]
        out[2] = out[2] + jnp.where(is_alpha, edge_part, 0.0)
        out[4] = out[4] + jnp.where(is_alpha, 0.0, lane_roll(edge_part, 4))
        both.append(out)
    store(at, 4, both)


def interleaved(first, second, half):
    sub = iota(0)
    index = 4 * half + (sub >> 1)
    return jnp.where((sub & 1) == 0, sub_take(first, index), sub_take(second, index))


def gather_rows(own, other, is_alpha, is_first, is_last, main, side):
    lane = lax.broadcasted_iota(jnp.int32, (2, LANES), 1)
    for field in range(2):
        rows = slice(2 * field, 2 * field + 2)
        (mine, after, near, before), (theirs, after_x, far, before_x) = (
            [ref[rows, :] for ref in refs] for refs in (own, other)
        )
        alpha, beta = jnp.where(is_alpha, mine, theirs), jnp.where(is_alpha, theirs, mine)
        main[field, 0:1, :] = jnp.where(is_first, alpha[0:1], jnp.where(is_alpha, near, far)[1:2])
        main[field, 1:3, :] = alpha
        main[field, 3:5, :] = beta
        main[field, 5:6, :] = jnp.where(is_last, beta[1:2], jnp.where(is_alpha, far, near)[0:1])
        main[field, 6:8, :] = beta
        ends = []
        for lefts, rights in ((before, after), (before_x, after_x)):
            ends.append(jnp.where(lane == LANES - 1, lefts[:, LANES:], rights[:, :LANES]))
        ends_alpha = jnp.where(is_alpha, ends[0], ends[1])
        ends_beta = jnp.where(is_alpha, ends[1], ends[0])
        side[field, 0:1, :] = ends_alpha[0:1]
        side[field, 1:3, :] = ends_alpha
        side[field, 3:5, :] = ends_beta
        side[field, 5:7, :] = ends_beta
        side[field, 7:8, :] = ends_beta[0:1]


def looked_up(tables, angular, material, sheet):
    index = material.astype(jnp.int32)
    sigma, base = [lane_take(table, index) for table in tables]
    return angular * sigma * sheet * sheet, base


def merge_kernel(cycles, depth, angular, *refs):
    own, other, (out, main, side, held, rest, sems) = refs[:4], refs[4:8], refs[8:]
    index = lax.axis_index("rad")
    is_alpha = index % 2 == 0
    is_first = index // 2 == 0
    is_last = index // 2 == cycles // 2 - 1
    gather_rows(own, other, is_alpha, is_first, is_last, main, side)
    tables = [
        jnp.broadcast_to(own[0][row : row + 1, :LANES], (8, LANES)) for row in (4, 5)
    ]
    parts = [(main, 0), (main, LANES), (side, 0)]
    parts = [
        looked_up(tables, angular[0], ref[0, :, at : at + LANES], ref[1, :, at : at + LANES])
        for ref, at in parts
    ]
    top, local, edge = strip(
        parts[:2],
        parts[2],
        is_alpha,
        (index // 2) * (2 * depth),
        cycles * depth,
    )
    rows, columns = out.shape[0], out.shape[2]
    bounds = [0, 64, 128, 192, rows]
    whole = held.shape[0]
    copies = []
    for number, (first, last) in enumerate(zip(bounds, bounds[1:])):
        part = []
        for tile in range(whole + 1):
            if tile < whole:
                source = held.at[tile].reshape(rows, 2, LANES)
            else:
                source = rest
            at = tile * LANES
            target = out.at[first:last, :, at : min(at + LANES, columns)]
            part.append(
                pltpu.make_async_copy(source.at[first:last, :, :], target, sems.at[number, tile])
            )
        copies.append(part)

    def store(row, count, both):
        for part, tiles in enumerate(both):
            for number, tile in enumerate(tiles[:whole]):
                held[number, pl.ds(2 * row + part, count, stride=2), :] = tile[:count]
        for half in range(count // 4):
            tile = interleaved(both[0][whole], both[1][whole], half).reshape(4, 2, LANES)
            first = row + 4 * half
            rest[first : first + 4, :, :] = tile[:, :, : rest.shape[2]]
        if row + count in bounds:
            for copy in copies[bounds.index(row + count) - 1]:
                copy.start()

    finish(top, local, edge, is_alpha, store)
    for part in copies:
        for copy in part:
            copy.wait()


def pack_kernel(*refs):
    sources, (out_ref,), targets, sems = refs[:4], refs[4:5], refs[5:9], refs[9]
    copies = [
        pltpu.make_async_copy(source, target, sems.at[number])
        for number, (source, target) in enumerate(zip(sources, targets))
    ]
    for copy in copies:
        copy.start()
    for copy in copies:
        copy.wait()
    material_ref, sheet_ref, sigma_ref, nu_ref = targets
    out_ref[:2, :] = material_ref[...].astype(jnp.float32)
    out_ref[2:4, :] = sheet_ref[...]
    for row, ref in ((4, sigma_ref), (5, nu_ref)):
        out_ref[row : row + 1, : ref.shape[0]] = ref[...].reshape(1, ref.shape[0])


def packed(*arguments):
    held = [pltpu.with_memory_space_constraint(value, pltpu.HBM) for value in arguments]
    return pl.pallas_call(
        pack_kernel,
        out_shape=jax.ShapeDtypeStruct((8, arguments[1].shape[1]), jnp.float32),
        in_specs=[pl.BlockSpec(memory_space=pltpu.HBM)] * 4,
        out_specs=pl.BlockSpec(memory_space=pltpu.VMEM),
        scratch_shapes=[pltpu.VMEM(value.shape, value.dtype) for value in arguments]
        + [pltpu.SemaphoreType.DMA((4,))],
        compiler_params=pltpu.CompilerParams(vmem_limit_bytes=4 * 1024 * 1024),
        name="cells",
    )(*held)


def swapped(cells, axis, first):
    count = lax.axis_size(axis)
    route = []
    for low in range(first, count, 2):
        high = (low + 1) % count
        route += [(low, high), (high, low)]
    return lax.ppermute(cells, axis, route)


def per_device(material_id, thickness, sigma_table, nu_table, angular_frequency):
    depth, arc = thickness.shape
    cells = packed(material_id, thickness, sigma_table, nu_table)
    cycles = lax.axis_size("rad")
    blocks = lax.axis_size("az")
    before = lax.ppermute(cells, "az", [(i, (i + 1) % blocks) for i in range(blocks)])
    after = lax.ppermute(cells, "az", [((i + 1) % blocks, i) for i in range(blocks)])
    own = [cells, after, swapped(cells, "rad", 1), before]
    other = [swapped(part, "rad", 0) for part in own]
    outer_nodes = arc + 2 * depth
    whole, rest = divmod(2 * outer_nodes, LANES)
    out = pl.pallas_call(
        lambda *refs: merge_kernel(cycles, depth, *refs),
        out_shape=jax.ShapeDtypeStruct((outer_nodes, 2, 2 * outer_nodes), jnp.float32),
        in_specs=[pl.BlockSpec(memory_space=pltpu.SMEM)]
        + [pl.BlockSpec(memory_space=pltpu.VMEM)] * 8,
        out_specs=pl.BlockSpec(memory_space=pltpu.HBM),
        scratch_shapes=[
            pltpu.VMEM((2, 8, arc), jnp.float32),
            pltpu.VMEM((2, 8, LANES), jnp.float32),
            pltpu.VMEM((whole, 2 * outer_nodes, LANES), jnp.float32),
            pltpu.VMEM((outer_nodes, 2, rest), jnp.float32),
            pltpu.SemaphoreType.DMA((4, whole + 1)),
        ],
        compiler_params=pltpu.CompilerParams(vmem_limit_bytes=48 * 1024 * 1024),
        name="pair_map",
    )(angular_frequency, *own, *other)
    return jnp.transpose(out, (1, 0, 2))


def solution(mesh):
    placed = (P("rad", "az"), P("rad", "az"), P(), P(), P())
    return jax.shard_map(
        per_device, mesh=mesh, in_specs=placed, out_specs=P(None, "rad", "az"), check_vma=False
    )
```

```python
import jax
import jax.numpy as jnp
from jax import lax
from jax.experimental import pallas as pl
from jax.experimental.pallas import tpu as pltpu
from jax.sharding import PartitionSpec as P

SHEET_NODES = 16
LANES = 128
GROUPS = 4


def lane_roll(value, shift):
    return pltpu.roll(value, shift % value.shape[1], 1)


def sub_roll(value, shift):
    return pltpu.roll(value, shift % value.shape[0], 0)


def lane_take(value, index):
    return jnp.take_along_axis(value, index, axis=1, mode="promise_in_bounds")


def sub_take(value, index):
    return jnp.take_along_axis(value, index, axis=0, mode="promise_in_bounds")


def iota(dim):
    return lax.broadcasted_iota(jnp.int32, (8, LANES), dim)


class Cx:
    def __init__(self, re, im):
        self.re, self.im = re, im

    def __add__(self, other):
        return Cx(self.re + other.re, self.im + other.im)

    def __sub__(self, other):
        return Cx(self.re - other.re, self.im - other.im)

    def __neg__(self):
        return Cx(-self.re, -self.im)

    def __mul__(self, other):
        if not isinstance(other, Cx):
            return Cx(self.re * other, self.im * other)
        return Cx(
            self.re * other.re - self.im * other.im, self.re * other.im + self.im * other.re
        )

    def inverse(self):
        scale = 1.0 / (self.re * self.re + self.im * self.im)
        return Cx(self.re * scale, -self.im * scale)

    def root(self):
        size = jnp.sqrt(self.re * self.re + self.im * self.im)
        re = jnp.sqrt(0.5 * (size + self.re))
        return Cx(re, 0.5 * self.im / re)

    def map(self, function):
        return Cx(function(self.re), function(self.im))

    def row(self, index):
        return self.map(lambda part: jnp.broadcast_to(part[index : index + 1], (8, LANES)))

    def lanes(self, shift):
        return self.map(lambda part: lane_roll(part, shift))

    def subs(self, shift):
        return self.map(lambda part: sub_roll(part, shift))


def pick(mask, first, second):
    if not isinstance(second, Cx):
        return first.map(lambda part: jnp.where(mask, part, second))
    return Cx(jnp.where(mask, first.re, second.re), jnp.where(mask, first.im, second.im))


def total(terms):
    terms = list(terms)
    while len(terms) > 1:
        terms = [
            terms[i] + terms[i + 1] if i + 1 < len(terms) else terms[i]
            for i in range(0, len(terms), 2)
        ]
    return terms[0]


def harmonic(left, right):
    return (left * right) * (left + right).inverse() * 2.0


def lamination(skin, base):
    above = Cx(jnp.ones_like(skin), jnp.zeros_like(skin))
    field = Cx(jnp.ones_like(skin), 0.5 * skin)
    summed = above
    for _ in range(SHEET_NODES - 1):
        summed = summed + field
        below = Cx(
            2.0 * field.re - skin * field.im - above.re,
            2.0 * field.im + skin * field.re - above.im,
        )
        above, field = field, below
    return field * summed.inverse() * (base * SHEET_NODES)


def factor(entry):
    work = {(r, c): entry(r, c) for r in range(4) for c in range(r + 1)}
    lower, pivots = {}, []
    for k in range(4):
        inverse = work[k, k].inverse()
        pivots.append(inverse)
        for r in range(k + 1, 4):
            lower[r, k] = work[r, k] * inverse
        for r in range(k + 1, 4):
            for c in range(k + 1, r + 1):
                work[r, c] = work[r, c] - lower[r, k] * work[c, k]
    return lower, pivots


def solve(lower, pivots, right):
    half = []
    for r in range(4):
        value = right[r]
        for c in range(r):
            value = value - lower[r, c] * half[c]
        half.append(value)
    out = [None] * 4
    for r in range(3, -1, -1):
        value = half[r] * pivots[r]
        for c in range(r + 1, 4):
            value = value - lower[c, r] * out[c]
        out[r] = value
    return out


def inverse2(first, second, cross):
    scale = (first * second - cross * cross).inverse()
    return second * scale, first * scale, -(cross * scale)


def solve_blocks(entry, right):
    cross = [[entry(2 + c, r) for c in range(2)] for r in range(2)]
    i00, i11, i01 = inverse2(entry(0, 0), entry(1, 1), entry(1, 0))
    ratio = [
        [i00 * cross[0][c] + i01 * cross[1][c] for c in range(2)],
        [i01 * cross[0][c] + i11 * cross[1][c] for c in range(2)],
    ]

    def rest(r, c):
        return entry(2 + r, 2 + c) - (cross[0][r] * ratio[0][c] + cross[1][r] * ratio[1][c])

    j00, j11, j01 = inverse2(rest(0, 0), rest(1, 1), rest(1, 0))
    start = [i00 * right[0] + i01 * right[1], i01 * right[0] + i11 * right[1]]
    low = [right[2 + r] - (ratio[0][r] * right[0] + ratio[1][r] * right[1]) for r in range(2)]
    out = [j00 * low[0] + j01 * low[1], j01 * low[0] + j11 * low[1]]
    return [start[r] - (ratio[r][0] * out[0] + ratio[r][1] * out[1]) for r in range(2)] + out


def seeds(lower, pivots):
    column = iota(0) & 3
    unit = {}
    for r in range(4):
        for c in range(r - 1, -1, -1):
            value = -lower[r, c]
            for k in range(c + 1, r):
                value = value - lower[r, k] * unit[k, c]
            unit[r, c] = value
    roots = [pivot.root() for pivot in pivots]
    out = []
    for r in range(4):
        value = pick(column == r, roots[r], 0.0)
        for k in range(r + 1, 4):
            value = pick(column == k, roots[k] * unit[k, r], value)
        out.append(value)
    return out


def evens(tiles):
    lane = iota(1)
    index = (2 * lane) & (LANES - 1)

    def one(offset):
        return Cx(
            *(
                jnp.where(
                    lane < LANES // 2,
                    lane_take(first, index + offset),
                    lane_take(second, index + offset),
                )
                for first, second in ((tiles[0].re, tiles[1].re), (tiles[0].im, tiles[1].im))
            )
        )

    return one(0), one(1)


def natural(even, odd):
    lane = iota(1)
    out = []
    for half in range(2):
        index = half * (LANES // 2) + (lane >> 1)
        out.append(
            Cx(
                *(
                    jnp.where((lane & 1) == 0, lane_take(first, index), lane_take(second, index))
                    for first, second in ((even.re, odd.re), (even.im, odd.im))
                )
            )
        )
    return out


def split(value):
    high = value.map(lambda part: part.astype(jnp.bfloat16).astype(jnp.float32))
    return high, value - high


def contract(left, right):
    return lax.dot_general(
        left,
        right,
        (((0,), (0,)), ((), ())),
        preferred_element_type=jnp.float32,
    )


def strip(main, side, is_alpha, first_cycle, radial_count):
    lane, sub = iota(1), iota(0)
    lower4 = sub < 4
    column = sub & 3

    rims = lamination(*side)
    tiles = [lamination(*cells) for cells in main]
    cycle = (first_cycle + sub - 1).astype(jnp.float32)
    center = 1.0 + (cycle + 0.5) / radial_count
    face = 1.0 + cycle / radial_count
    per_center = 1.0 / center
    first_lane, last_lane = lane == 0, lane == LANES - 1

    ahead = [tile.lanes(1) for tile in tiles]
    west = [
        harmonic(pick(first_lane, rims.lanes(1), ahead[0]), tiles[0]) * per_center,
        harmonic(pick(first_lane, ahead[0], ahead[1]), tiles[1]) * per_center,
    ]
    wall = harmonic(tiles[1], rims.lanes(-1)) * per_center * 2.0
    back = [tile.lanes(-1) for tile in west]
    east = [pick(last_lane, back[1], back[0]), pick(last_lane, wall, back[1])]
    west[0] = pick(first_lane, west[0] * 2.0, west[0])
    south, north = [], []
    for tile in tiles:
        radial = harmonic(tile.subs(1), tile) * face
        radial = pick((sub == 1) | (sub == 5), radial * 2.0, radial)
        south.append(radial)
        north.append(radial.subs(-1))
    diagonal = [west[h] + east[h] + south[h] + north[h] for h in range(2)]
    gain_in = [south[h].row(1) for h in range(2)]
    gain_out = [north[h].row(4) for h in range(2)]

    diag_e, diag_o = evens(diagonal)
    east_e, east_o = evens(east)
    up_e, up_o = evens(north)
    left_e = pick(last_lane, east_o, 0.0)
    left_e = (east_o - left_e).lanes(1)

    def entry_e(r, c):
        if r == c:
            return diag_e.row(r + 1)
        return -up_e.row(r)

    lower_e, pivots_e = {}, []
    work = diag_e.row(1)
    for r in range(4):
        pivots_e.append(work.inverse())
        if r < 3:
            coupling = up_e.row(r + 1)
            lower_e[r + 1, r] = -(coupling * pivots_e[r])
            work = diag_e.row(r + 2) + lower_e[r + 1, r] * coupling
    zero = jnp.zeros((8, LANES), jnp.float32)
    nothing = Cx(zero, zero)
    half = []
    for r in range(4):
        value = Cx(jnp.where(column == r, 1.0, zero), zero)
        if r:
            value = value - lower_e[r, r - 1] * half[r - 1]
        half.append(value)
    inverse_e = [None] * 4
    for r in range(3, -1, -1):
        value = half[r] * pivots_e[r]
        if r < 3:
            value = value - lower_e[r + 1, r] * inverse_e[r + 1]
        inverse_e[r] = value
    for r in range(4):
        for c in range(r - 1):
            lower_e[r, c] = nothing
    seeds_e = seeds(lower_e, pivots_e)
    sides_e = pick(lower4, left_e.subs(-1), east_e.subs(3))
    reach_e = [inverse_e[r] * sides_e for r in range(4)]
    matrix, pair = [], []
    for r in range(4):
        to_left = (left_e.row(r + 1) * reach_e[r]).lanes(-1)
        to_right = east_e.row(r + 1) * reach_e[r]
        pair.append(pick(lower4, to_right, to_left))
        change = pick(lower4, to_left, to_right)
        base = pick(column == r, diag_o.row(r + 1), 0.0)
        if r < 3:
            base = pick(column == r + 1, -up_o.row(r + 1), base)
        if r > 0:
            base = pick(column == r - 1, -up_o.row(r), base)
        matrix.append(base - change - change.subs(4))

    for level in range(1, 8):
        step = 1 << (level - 1)
        stay = ((lane + 1) & (2 * step - 1)) == 0
        reach = solve_blocks(lambda r, c: matrix[r].row(c), pair)
        next_matrix, next_pair = [], []
        for r in range(4):
            to_left = total(pair[k].row(r) * reach[k] for k in range(4)).lanes(-step)
            to_right = total(pair[k].row(4 + r) * reach[k] for k in range(4)).lanes(step)
            change = pick(lower4, to_left, to_right)
            change = change + change.subs(4)
            next_matrix.append(pick(stay, matrix[r] - change, matrix[r]))
            next_pair.append(pick(stay, pick(lower4, to_right, to_left), pair[r]))
        matrix, pair = next_matrix, next_pair

    lower, pivots = factor(lambda r, c: matrix[r].row(c))
    reach = solve(lower, pivots, pair)
    reach_rows = [[reach[r].row(k) for k in range(8)] for r in range(4)]
    seed = seeds(lower, pivots)

    def level_of(group):
        return jnp.where(lower4, 2 * group - 1, 2 * group)

    own_level = jnp.ones((8, LANES), jnp.int32)
    for level in range(2, 9):
        own_level = own_level + (((lane + 1) & ((1 << (level - 1)) - 1)) == 0).astype(jnp.int32)

    odd = {}
    for group in range(1, GROUPS + 1):
        rows = [pick(own_level == level_of(group), seed[r], 0.0) for r in range(4)]
        for level in range(min(2 * group - 1, 7), 0, -1):
            step = 1 << (level - 1)
            here = own_level == level
            before = [row.lanes(step) for row in rows]
            after = [row.lanes(-step) for row in rows]
            fresh = []
            for r in range(4):
                terms = [reach_rows[r][k] * before[k] for k in range(4)]
                terms += [reach_rows[r][4 + k] * after[k] for k in range(4)]
                fresh.append(rows[r] + pick(here, total(terms), 0.0))
            rows = fresh
        odd[group] = rows

    reach_e_rows = [[reach_e[r].row(k) for k in range(8)] for r in range(4)]
    even = {0: [pick(first_lane & lower4, seeds_e[r], 0.0) for r in range(4)]}
    odd[0] = [nothing] * 4
    for group in range(1, GROUPS + 1):
        before = [row.lanes(1) for row in odd[group]]
        even[group] = []
        for r in range(4):
            terms = [reach_e_rows[r][4 + k] * odd[group][k] for k in range(4)]
            if r in (0, 3):
                terms += [reach_e_rows[r][k] * before[k] for k in range(4)]
            even[group].append(total(terms))

    def corners(lefts, rights):
        return pick(
            lane == 0,
            lefts[0],
            pick(
                lane == 1,
                lefts[1].lanes(1),
                pick(lane == 2, rights[0].lanes(3), pick(lane == 3, rights[1].lanes(4), 0.0)),
            ),
        )

    gains_left = [west[0].row(r + 1) for r in range(4)]
    gains_right = [east[1].row(r + 1) for r in range(4)]
    gain_corner = [
        corners(gains_left[2 * t : 2 * t + 2], gains_right[2 * t : 2 * t + 2]) for t in range(2)
    ]
    inner, outer, corner = {}, {}, {}
    for group in range(GROUPS + 1):
        if group:
            low = natural(even[group][0], odd[group][0])
            high = natural(even[group][3], odd[group][3])
        else:
            low, high = [even[0][0], nothing], [even[0][3], nothing]
        inner[group] = [low[h] * gain_in[h] for h in range(2)]
        outer[group] = [high[h] * gain_out[h] for h in range(2)]
        corner[group] = [
            corners(even[group][2 * t : 2 * t + 2], odd[group][2 * t : 2 * t + 2]) * gain_corner[t]
            for t in range(2)
        ]

    left_parts, right_parts = [], []
    for group in range(GROUPS + 1):
        if group in (0, GROUPS):
            low, high = inner[group], outer[group]
            if group == 0:
                low = [low[0], pick(lower4, nothing, inner[3][1])]
                high = [high[0], pick(lower4, nothing, outer[3][1])]
        else:
            near = lane < (2 << level_of(group))
            low = [pick(near, inner[group][0], 0.0), nothing]
            high = [pick(near, outer[group][0], 0.0), nothing]
        side_a, side_b = corner[group]
        own = [pick(is_alpha, low[h], high[h]) for h in range(2)]
        own.append(pick(is_alpha, side_a, side_b))
        moved = [high[0].lanes(4), high[1].lanes(4)]
        every = [
            low[0],
            low[1],
            pick(lower_lanes(lane, 4), side_a, moved[0]),
            pick(lower_lanes(lane, 4), moved[0], moved[1]),
            pick(lower_lanes(lane, 4), moved[1], pick(lane < 8, side_b.lanes(4), 0.0)),
        ]
        left_parts.append([split(value) for value in own])
        right_parts.append([split(value) for value in every])

    def wide(parts, which, name, sign=1.0):
        rows = []
        for group in parts:
            pieces = [getattr(value[which], name) for value in group]
            row = jnp.concatenate(pieces, axis=1)
            rows.append(row if sign > 0 else -row)
        return rows

    def stacked(parts, order):
        rows = [row for which, name, sign in order for row in wide(parts, which, name, sign)]
        rows += [jnp.zeros_like(rows[0])] * (32 - len(rows))
        return jnp.concatenate(rows, axis=0).astype(jnp.bfloat16)

    hr, hi, lr, li = (0, "re"), (0, "im"), (1, "re"), (1, "im")
    left = stacked(left_parts, [key + (-1.0,) for key in (hr, hr, lr, hi, hi, li)])
    signs = (1.0, 1.0, 1.0, -1.0, -1.0, -1.0)
    right_re = stacked(
        right_parts, [key + (sign,) for key, sign in zip((hr, lr, hr, hi, li, hi), signs)]
    )
    right_im = stacked(right_parts, [key + (1.0,) for key in (hi, li, hi, hr, lr, hr)])
    top = contract(left, jnp.concatenate([right_re, right_im], axis=1))
    top = Cx(top[:, : 5 * LANES], top[:, 5 * LANES :])

    wide_lane = lax.broadcasted_iota(jnp.int32, (16, LANES), 1)
    wide_sub = lax.broadcasted_iota(jnp.int32, (16, LANES), 0)
    masks = []
    within = wide_lane & 63
    for level in range(1, 4):
        for tile in range(1 << (3 - level)):
            masks.append((level, (within >> (level + 1)) == 4 * tile + (wide_sub >> 2)))
    last = ((within >> 5) == (wide_sub >> 2)) | ((wide_sub >> 2) == 2)
    masks = [
        (level, jnp.where(mask, 1.0, 0.0).astype(jnp.bfloat16))
        for level, mask in masks + [(4, last)]
    ]

    def spread(values):
        levels = {}
        for group in range(1, GROUPS):
            value = values[group]
            turned = value.subs(4)
            levels[2 * group - 1] = pick(lower4, value, turned)
            levels[2 * group] = pick(lower4, turned, value)
        out = {}
        for name in ("re", "im"):
            parts = {level: getattr(value, name) for level, value in levels.items()}
            tiles = {level: [parts[level]] * 2 for level in range(1, 4)}
            tiles[4] = [parts[4], parts[5]]
            tiles = {level: jnp.concatenate(tile, axis=0) for level, tile in tiles.items()}
            high = {level: tile.astype(jnp.bfloat16) for level, tile in tiles.items()}
            low = {
                level: (tile - high[level].astype(jnp.float32)).astype(jnp.bfloat16)
                for level, tile in tiles.items()
            }
            for which, part in enumerate((high, low)):
                rows = [part[level] * mask for level, mask in masks]
                out[which, name] = jnp.concatenate(rows, axis=0)
        return out

    even_d = [inverse_e[0].row(0), inverse_e[0].row(3), inverse_e[3].row(3)]
    even_d = [natural(value, nothing) for value in even_d]

    def local(half, quarter):
        packed, mine = {}, {}
        for group in range(1, GROUPS):
            low, high = inner[group][half], outer[group][half]
            if half == 0:
                near = lane < (2 << level_of(group))
                low, high = pick(near, nothing, low), pick(near, nothing, high)
            packed[group] = pick((lane >> 6) == quarter, low, high.lanes(64))
            turned = packed[group].lanes(64)
            pair = (packed[group], turned) if quarter == 0 else (turned, packed[group])
            mine[group] = -pick(is_alpha, *pair)
        every, mine = spread(packed), spread(mine)
        left = jnp.concatenate([mine[key] for key in (hr, hi, hr, hi, lr, li)], axis=0)
        right_re = jnp.concatenate(
            [every[hr], -every[hi], every[lr], -every[li], every[hr], -every[hi]], axis=0
        )
        right_im = jnp.concatenate([every[key] for key in (hi, hr, li, lr, hi, hr)], axis=0)
        product = contract(left[:, :64], jnp.concatenate([right_re, right_im], axis=1))
        return Cx(product[:, :LANES], product[:, LANES:])

    def diagonals(half):
        g_in, g_out = gain_in[half], gain_out[half]
        solo = (lane & 1) == 0
        if half == 0:
            solo = solo & (lane > 0)
        cross = even_d[1][half] * g_in * g_out
        on_in = pick(is_alpha, even_d[0][half] * g_in * g_in, cross)
        on_out = pick(is_alpha, cross, even_d[2][half] * g_out * g_out)
        on_in = pick(is_alpha, g_in, nothing) - pick(solo, on_in, 0.0)
        on_out = pick(is_alpha, nothing, g_out) - pick(solo, on_out, 0.0)
        return on_in, on_out.lanes(4)

    edge = pick((lane == sub) & lower4, pick(is_alpha, gain_corner[0], gain_corner[1]), 0.0)
    return top, (local, diagonals), edge


def lower_lanes(lane, count):
    return lane < count


def finish(top, local, edge, is_alpha, store):
    lane, sub = iota(1), iota(0)
    full = [top.re, top.im]
    local, diagonals = local
    for half, quarter in ((0, 0), (0, 1), (1, 0), (1, 1)):
        if quarter == 0:
            on_in, on_out = diagonals(half)
        product = local(half, quarter)
        inside = (lane >> 6) == quarter
        for row in range(0, 64, 8):
            here = lane == sub + (64 * quarter + row)
            moved = ((lane - 4) & (LANES - 1)) == sub + (64 * quarter + row)
            at = half * LANES + quarter * 64 + row
            both = []
            for part, name in enumerate(("re", "im")):
                value = getattr(product, name)[row : row + 8]
                low = jnp.where(inside, value, 0.0)
                low = low + jnp.where(here, getattr(on_in, name), 0.0)
                high = lane_roll(jnp.where(inside, 0.0, value), 68)
                high = high + jnp.where(moved, getattr(on_out, name), 0.0)
                out = [full[part][at : at + 8, t * LANES : (t + 1) * LANES] for t in range(5)]
                out[half] = out[half] + low
                if quarter == 0:
                    out[2 + half] = out[2 + half] + high
                else:
                    out[2 + half] = out[2 + half] + jnp.where(lane < 4, 0.0, high)
                    out[3 + half] = out[3 + half] + jnp.where(lane < 4, high, 0.0)
                both.append(out)
            store(at, 8, both)
    at = 2 * LANES
    both = []
    for part, name in enumerate(("re", "im")):
        edge_part = getattr(edge, name)
        out = [full[part][at : at + 8, t * LANES : (t + 1) * LANES] for t in range(5)]
        out[2] = out[2] + jnp.where(is_alpha, edge_part, 0.0)
        out[4] = out[4] + jnp.where(is_alpha, 0.0, lane_roll(edge_part, 4))
        both.append(out)
    store(at, 4, both)


def interleaved(first, second, half):
    sub = iota(0)
    index = 4 * half + (sub >> 1)
    return jnp.where((sub & 1) == 0, sub_take(first, index), sub_take(second, index))


def gather_rows(own, other, is_alpha, is_first, is_last, main, side):
    lane = lax.broadcasted_iota(jnp.int32, (2, LANES), 1)
    for field in range(2):
        rows = slice(2 * field, 2 * field + 2)
        (mine, after, near, before), (theirs, after_x, far, before_x) = (
            [ref[rows, :] for ref in refs] for refs in (own, other)
        )
        alpha, beta = jnp.where(is_alpha, mine, theirs), jnp.where(is_alpha, theirs, mine)
        main[field, 0:1, :] = jnp.where(is_first, alpha[0:1], jnp.where(is_alpha, near, far)[1:2])
        main[field, 1:3, :] = alpha
        main[field, 3:5, :] = beta
        main[field, 5:6, :] = jnp.where(is_last, beta[1:2], jnp.where(is_alpha, far, near)[0:1])
        main[field, 6:8, :] = beta
        ends = []
        for lefts, rights in ((before, after), (before_x, after_x)):
            ends.append(jnp.where(lane == LANES - 1, lefts[:, LANES:], rights[:, :LANES]))
        ends_alpha = jnp.where(is_alpha, ends[0], ends[1])
        ends_beta = jnp.where(is_alpha, ends[1], ends[0])
        side[field, 0:1, :] = ends_alpha[0:1]
        side[field, 1:3, :] = ends_alpha
        side[field, 3:5, :] = ends_beta
        side[field, 5:7, :] = ends_beta
        side[field, 7:8, :] = ends_beta[0:1]


def looked_up(tables, angular, material, sheet):
    index = material.astype(jnp.int32)
    sigma, base = [lane_take(table, index) for table in tables]
    return angular * sigma * sheet * sheet, base


def merge_kernel(cycles, depth, angular, *refs):
    own, other, (out, main, side, held, rest, sems) = refs[:4], refs[4:8], refs[8:]
    index = lax.axis_index("rad")
    is_alpha = index % 2 == 0
    is_first = index // 2 == 0
    is_last = index // 2 == cycles // 2 - 1
    gather_rows(own, other, is_alpha, is_first, is_last, main, side)
    tables = [
        jnp.broadcast_to(own[0][row : row + 1, :LANES], (8, LANES)) for row in (4, 5)
    ]
    parts = [(main, 0), (main, LANES), (side, 0)]
    parts = [
        looked_up(tables, angular[0], ref[0, :, at : at + LANES], ref[1, :, at : at + LANES])
        for ref, at in parts
    ]
    top, local, edge = strip(
        parts[:2],
        parts[2],
        is_alpha,
        (index // 2) * (2 * depth),
        cycles * depth,
    )
    rows, columns = out.shape[0], out.shape[2]
    bounds = [0, 64, 128, 192, rows]
    whole = held.shape[0]
    copies = []
    for number, (first, last) in enumerate(zip(bounds, bounds[1:])):
        part = []
        for tile in range(whole + 1):
            if tile < whole:
                source = held.at[tile].reshape(rows, 2, LANES)
            else:
                source = rest
            at = tile * LANES
            target = out.at[first:last, :, at : min(at + LANES, columns)]
            part.append(
                pltpu.make_async_copy(source.at[first:last, :, :], target, sems.at[number, tile])
            )
        copies.append(part)

    def store(row, count, both):
        for part, tiles in enumerate(both):
            for number, tile in enumerate(tiles[:whole]):
                held[number, pl.ds(2 * row + part, count, stride=2), :] = tile[:count]
        for half in range(count // 4):
            tile = interleaved(both[0][whole], both[1][whole], half).reshape(4, 2, LANES)
            first = row + 4 * half
            rest[first : first + 4, :, :] = tile[:, :, : rest.shape[2]]
        if row + count in bounds:
            for number, copy in enumerate(copies[bounds.index(row + count) - 1]):
                copy.start(priority=number % 2)

    finish(top, local, edge, is_alpha, store)
    for part in copies:
        for copy in part:
            copy.wait()


def pack_kernel(*refs):
    sources, (out_ref,), targets, sems = refs[:4], refs[4:5], refs[5:9], refs[9]
    copies = [
        pltpu.make_async_copy(source, target, sems.at[number])
        for number, (source, target) in enumerate(zip(sources, targets))
    ]
    for copy in copies:
        copy.start()
    for copy in copies:
        copy.wait()
    material_ref, sheet_ref, sigma_ref, nu_ref = targets
    out_ref[:2, :] = material_ref[...].astype(jnp.float32)
    out_ref[2:4, :] = sheet_ref[...]
    for row, ref in ((4, sigma_ref), (5, nu_ref)):
        out_ref[row : row + 1, : ref.shape[0]] = ref[...].reshape(1, ref.shape[0])


def packed(*arguments):
    held = [pltpu.with_memory_space_constraint(value, pltpu.HBM) for value in arguments]
    return pl.pallas_call(
        pack_kernel,
        out_shape=jax.ShapeDtypeStruct((8, arguments[1].shape[1]), jnp.float32),
        in_specs=[pl.BlockSpec(memory_space=pltpu.HBM)] * 4,
        out_specs=pl.BlockSpec(memory_space=pltpu.VMEM),
        scratch_shapes=[pltpu.VMEM(value.shape, value.dtype) for value in arguments]
        + [pltpu.SemaphoreType.DMA((4,))],
        compiler_params=pltpu.CompilerParams(vmem_limit_bytes=4 * 1024 * 1024),
        name="cells",
    )(*held)


def swapped(cells, axis, first):
    count = lax.axis_size(axis)
    route = []
    for low in range(first, count, 2):
        high = (low + 1) % count
        route += [(low, high), (high, low)]
    return lax.ppermute(cells, axis, route)


def per_device(material_id, thickness, sigma_table, nu_table, angular_frequency):
    depth, arc = thickness.shape
    cells = packed(material_id, thickness, sigma_table, nu_table)
    cycles = lax.axis_size("rad")
    blocks = lax.axis_size("az")
    before = lax.ppermute(cells, "az", [(i, (i + 1) % blocks) for i in range(blocks)])
    after = lax.ppermute(cells, "az", [((i + 1) % blocks, i) for i in range(blocks)])
    own = [cells, after, swapped(cells, "rad", 1), before]
    other = [swapped(part, "rad", 0) for part in own]
    outer_nodes = arc + 2 * depth
    whole, rest = divmod(2 * outer_nodes, LANES)
    out = pl.pallas_call(
        lambda *refs: merge_kernel(cycles, depth, *refs),
        out_shape=jax.ShapeDtypeStruct((outer_nodes, 2, 2 * outer_nodes), jnp.float32),
        in_specs=[pl.BlockSpec(memory_space=pltpu.SMEM)]
        + [pl.BlockSpec(memory_space=pltpu.VMEM)] * 8,
        out_specs=pl.BlockSpec(memory_space=pltpu.HBM),
        scratch_shapes=[
            pltpu.VMEM((2, 8, arc), jnp.float32),
            pltpu.VMEM((2, 8, LANES), jnp.float32),
            pltpu.VMEM((whole, 2 * outer_nodes, LANES), jnp.float32),
            pltpu.VMEM((outer_nodes, 2, rest), jnp.float32),
            pltpu.SemaphoreType.DMA((4, whole + 1)),
        ],
        compiler_params=pltpu.CompilerParams(vmem_limit_bytes=48 * 1024 * 1024),
        name="pair_map",
    )(angular_frequency, *own, *other)
    return jnp.transpose(out, (1, 0, 2))


def solution(mesh):
    placed = (P("rad", "az"), P("rad", "az"), P(), P(), P())
    return jax.shard_map(
        per_device, mesh=mesh, in_specs=placed, out_specs=P(None, "rad", "az"), check_vma=False
    )
```

```python
import jax
import jax.numpy as jnp
from jax import lax
from jax.experimental import pallas as pl
from jax.experimental.pallas import tpu as pltpu
from jax.sharding import PartitionSpec as P

SHEET_NODES = 16
LANES = 128
GROUPS = 4


def lane_roll(value, shift):
    return pltpu.roll(value, shift % value.shape[1], 1)


def sub_roll(value, shift):
    return pltpu.roll(value, shift % value.shape[0], 0)


def lane_take(value, index):
    return jnp.take_along_axis(value, index, axis=1, mode="promise_in_bounds")


def sub_take(value, index):
    return jnp.take_along_axis(value, index, axis=0, mode="promise_in_bounds")


def iota(dim):
    return lax.broadcasted_iota(jnp.int32, (8, LANES), dim)


class Cx:
    def __init__(self, re, im):
        self.re, self.im = re, im

    def __add__(self, other):
        return Cx(self.re + other.re, self.im + other.im)

    def __sub__(self, other):
        return Cx(self.re - other.re, self.im - other.im)

    def __neg__(self):
        return Cx(-self.re, -self.im)

    def __mul__(self, other):
        if not isinstance(other, Cx):
            return Cx(self.re * other, self.im * other)
        return Cx(
            self.re * other.re - self.im * other.im, self.re * other.im + self.im * other.re
        )

    def inverse(self):
        scale = 1.0 / (self.re * self.re + self.im * self.im)
        return Cx(self.re * scale, -self.im * scale)

    def root(self):
        size = jnp.sqrt(self.re * self.re + self.im * self.im)
        re = jnp.sqrt(0.5 * (size + self.re))
        return Cx(re, 0.5 * self.im / re)

    def map(self, function):
        return Cx(function(self.re), function(self.im))

    def row(self, index):
        return self.map(lambda part: jnp.broadcast_to(part[index : index + 1], (8, LANES)))

    def lanes(self, shift):
        return self.map(lambda part: lane_roll(part, shift))

    def subs(self, shift):
        return self.map(lambda part: sub_roll(part, shift))


def pick(mask, first, second):
    if not isinstance(second, Cx):
        return first.map(lambda part: jnp.where(mask, part, second))
    return Cx(jnp.where(mask, first.re, second.re), jnp.where(mask, first.im, second.im))


def total(terms):
    terms = list(terms)
    while len(terms) > 1:
        terms = [
            terms[i] + terms[i + 1] if i + 1 < len(terms) else terms[i]
            for i in range(0, len(terms), 2)
        ]
    return terms[0]


def harmonic(left, right):
    return (left * right) * (left + right).inverse() * 2.0


def lamination(skin, base):
    above = Cx(jnp.ones_like(skin), jnp.zeros_like(skin))
    field = Cx(jnp.ones_like(skin), 0.5 * skin)
    summed = above
    for _ in range(SHEET_NODES - 1):
        summed = summed + field
        below = Cx(
            2.0 * field.re - skin * field.im - above.re,
            2.0 * field.im + skin * field.re - above.im,
        )
        above, field = field, below
    return field * summed.inverse() * (base * SHEET_NODES)


def factor(entry):
    work = {(r, c): entry(r, c) for r in range(4) for c in range(r + 1)}
    lower, pivots = {}, []
    for k in range(4):
        inverse = work[k, k].inverse()
        pivots.append(inverse)
        for r in range(k + 1, 4):
            lower[r, k] = work[r, k] * inverse
        for r in range(k + 1, 4):
            for c in range(k + 1, r + 1):
                work[r, c] = work[r, c] - lower[r, k] * work[c, k]
    return lower, pivots


def solve(lower, pivots, right):
    half = []
    for r in range(4):
        value = right[r]
        for c in range(r):
            value = value - lower[r, c] * half[c]
        half.append(value)
    out = [None] * 4
    for r in range(3, -1, -1):
        value = half[r] * pivots[r]
        for c in range(r + 1, 4):
            value = value - lower[c, r] * out[c]
        out[r] = value
    return out


def seeds(lower, pivots):
    column = iota(0) & 3
    unit = {}
    for r in range(4):
        for c in range(r - 1, -1, -1):
            value = -lower[r, c]
            for k in range(c + 1, r):
                value = value - lower[r, k] * unit[k, c]
            unit[r, c] = value
    roots = [pivot.root() for pivot in pivots]
    out = []
    for r in range(4):
        value = pick(column == r, roots[r], 0.0)
        for k in range(r + 1, 4):
            value = pick(column == k, roots[k] * unit[k, r], value)
        out.append(value)
    return out


def evens(tiles):
    lane = iota(1)
    index = (2 * lane) & (LANES - 1)

    def one(offset):
        return Cx(
            *(
                jnp.where(
                    lane < LANES // 2,
                    lane_take(first, index + offset),
                    lane_take(second, index + offset),
                )
                for first, second in ((tiles[0].re, tiles[1].re), (tiles[0].im, tiles[1].im))
            )
        )

    return one(0), one(1)


def natural(even, odd):
    lane = iota(1)
    out = []
    for half in range(2):
        index = half * (LANES // 2) + (lane >> 1)
        out.append(
            Cx(
                *(
                    jnp.where((lane & 1) == 0, lane_take(first, index), lane_take(second, index))
                    for first, second in ((even.re, odd.re), (even.im, odd.im))
                )
            )
        )
    return out


def split(value):
    high = value.map(lambda part: part.astype(jnp.bfloat16).astype(jnp.float32))
    return high, value - high


def contract(left, right):
    return lax.dot_general(
        left.astype(jnp.bfloat16),
        right.astype(jnp.bfloat16),
        (((0,), (0,)), ((), ())),
        preferred_element_type=jnp.float32,
    )


def strip(main, side, is_alpha, first_cycle, radial_count):
    lane, sub = iota(1), iota(0)
    lower4 = sub < 4
    column = sub & 3

    cells = lamination(main[0], main[1])
    rims = lamination(side[0], side[1])
    tiles = [cells.map(lambda part: part[:, :LANES]), cells.map(lambda part: part[:, LANES:])]
    cycle = (first_cycle + sub - 1).astype(jnp.float32)
    center = 1.0 + (cycle + 0.5) / radial_count
    face = 1.0 + cycle / radial_count
    per_center = 1.0 / center
    first_lane, last_lane = lane == 0, lane == LANES - 1

    ahead = [tile.lanes(1) for tile in tiles]
    west = [
        harmonic(pick(first_lane, rims.lanes(1), ahead[0]), tiles[0]) * per_center,
        harmonic(pick(first_lane, ahead[0], ahead[1]), tiles[1]) * per_center,
    ]
    wall = harmonic(tiles[1], rims.lanes(-1)) * per_center * 2.0
    back = [tile.lanes(-1) for tile in west]
    east = [pick(last_lane, back[1], back[0]), pick(last_lane, wall, back[1])]
    west[0] = pick(first_lane, west[0] * 2.0, west[0])
    south, north = [], []
    for tile in tiles:
        radial = harmonic(tile.subs(1), tile) * face
        radial = pick((sub == 1) | (sub == 5), radial * 2.0, radial)
        south.append(radial)
        north.append(radial.subs(-1))
    diagonal = [west[h] + east[h] + south[h] + north[h] for h in range(2)]
    gain_in = [south[h].row(1) for h in range(2)]
    gain_out = [north[h].row(4) for h in range(2)]

    diag_e, diag_o = evens(diagonal)
    east_e, east_o = evens(east)
    up_e, up_o = evens(north)
    left_e = pick(last_lane, east_o, 0.0)
    left_e = (east_o - left_e).lanes(1)

    def entry_e(r, c):
        if r == c:
            return diag_e.row(r + 1)
        return -up_e.row(r)

    lower_e, pivots_e = {}, []
    work = diag_e.row(1)
    for r in range(4):
        pivots_e.append(work.inverse())
        if r < 3:
            coupling = up_e.row(r + 1)
            lower_e[r + 1, r] = -(coupling * pivots_e[r])
            work = diag_e.row(r + 2) + lower_e[r + 1, r] * coupling
    zero = jnp.zeros((8, LANES), jnp.float32)
    nothing = Cx(zero, zero)
    half = []
    for r in range(4):
        value = Cx(jnp.where(column == r, 1.0, zero), zero)
        if r:
            value = value - lower_e[r, r - 1] * half[r - 1]
        half.append(value)
    inverse_e = [None] * 4
    for r in range(3, -1, -1):
        value = half[r] * pivots_e[r]
        if r < 3:
            value = value - lower_e[r + 1, r] * inverse_e[r + 1]
        inverse_e[r] = value
    for r in range(4):
        for c in range(r - 1):
            lower_e[r, c] = nothing
    seeds_e = seeds(lower_e, pivots_e)
    sides_e = pick(lower4, left_e.subs(-1), east_e.subs(3))
    reach_e = [inverse_e[r] * sides_e for r in range(4)]
    matrix, pair = [], []
    for r in range(4):
        to_left = (left_e.row(r + 1) * reach_e[r]).lanes(-1)
        to_right = east_e.row(r + 1) * reach_e[r]
        pair.append(pick(lower4, to_right, to_left))
        change = pick(lower4, to_left, to_right)
        base = pick(column == r, diag_o.row(r + 1), 0.0)
        if r < 3:
            base = pick(column == r + 1, -up_o.row(r + 1), base)
        if r > 0:
            base = pick(column == r - 1, -up_o.row(r), base)
        matrix.append(base - change - change.subs(4))

    for level in range(1, 8):
        step = 1 << (level - 1)
        stay = ((lane + 1) & (2 * step - 1)) == 0
        reach = solve(*factor(lambda r, c: matrix[r].row(c)), pair)
        next_matrix, next_pair = [], []
        for r in range(4):
            to_left = total(pair[k].row(r) * reach[k] for k in range(4)).lanes(-step)
            to_right = total(pair[k].row(4 + r) * reach[k] for k in range(4)).lanes(step)
            change = pick(lower4, to_left, to_right)
            change = change + change.subs(4)
            next_matrix.append(pick(stay, matrix[r] - change, matrix[r]))
            next_pair.append(pick(stay, pick(lower4, to_right, to_left), pair[r]))
        matrix, pair = next_matrix, next_pair

    lower, pivots = factor(lambda r, c: matrix[r].row(c))
    reach = solve(lower, pivots, pair)
    reach_rows = [[reach[r].row(k) for k in range(8)] for r in range(4)]
    seed = seeds(lower, pivots)

    def level_of(group):
        return jnp.where(lower4, 2 * group - 1, 2 * group)

    own_level = jnp.ones((8, LANES), jnp.int32)
    for level in range(2, 9):
        own_level = own_level + (((lane + 1) & ((1 << (level - 1)) - 1)) == 0).astype(jnp.int32)

    odd = {}
    for group in range(1, GROUPS + 1):
        rows = [pick(own_level == level_of(group), seed[r], 0.0) for r in range(4)]
        for level in range(min(2 * group - 1, 7), 0, -1):
            step = 1 << (level - 1)
            here = own_level == level
            before = [row.lanes(step) for row in rows]
            after = [row.lanes(-step) for row in rows]
            fresh = []
            for r in range(4):
                terms = [reach_rows[r][k] * before[k] for k in range(4)]
                terms += [reach_rows[r][4 + k] * after[k] for k in range(4)]
                fresh.append(rows[r] + pick(here, total(terms), 0.0))
            rows = fresh
        odd[group] = rows

    reach_e_rows = [[reach_e[r].row(k) for k in range(8)] for r in range(4)]
    even = {0: [pick(first_lane & lower4, seeds_e[r], 0.0) for r in range(4)]}
    odd[0] = [nothing] * 4
    for group in range(1, GROUPS + 1):
        before = [row.lanes(1) for row in odd[group]]
        even[group] = []
        for r in range(4):
            terms = [reach_e_rows[r][k] * before[k] for k in range(4)]
            terms += [reach_e_rows[r][4 + k] * odd[group][k] for k in range(4)]
            even[group].append(total(terms))

    def corners(lefts, rights):
        return pick(
            lane == 0,
            lefts[0],
            pick(
                lane == 1,
                lefts[1].lanes(1),
                pick(lane == 2, rights[0].lanes(3), pick(lane == 3, rights[1].lanes(4), 0.0)),
            ),
        )

    gains_left = [west[0].row(r + 1) for r in range(4)]
    gains_right = [east[1].row(r + 1) for r in range(4)]
    gain_corner = [
        corners(gains_left[2 * t : 2 * t + 2], gains_right[2 * t : 2 * t + 2]) for t in range(2)
    ]
    inner, outer, corner = {}, {}, {}
    for group in range(GROUPS + 1):
        if group:
            low = natural(even[group][0], odd[group][0])
            high = natural(even[group][3], odd[group][3])
        else:
            low, high = [even[0][0], nothing], [even[0][3], nothing]
        inner[group] = [low[h] * gain_in[h] for h in range(2)]
        outer[group] = [high[h] * gain_out[h] for h in range(2)]
        corner[group] = [
            corners(even[group][2 * t : 2 * t + 2], odd[group][2 * t : 2 * t + 2]) * gain_corner[t]
            for t in range(2)
        ]

    left_parts, right_parts = [], []
    for group in range(GROUPS + 1):
        if group in (0, GROUPS):
            low, high = inner[group], outer[group]
        else:
            near = lane < (2 << level_of(group))
            low = [pick(near, inner[group][0], 0.0), nothing]
            high = [pick(near, outer[group][0], 0.0), nothing]
        side_a, side_b = corner[group]
        own = [pick(is_alpha, low[h], high[h]) for h in range(2)]
        own.append(pick(is_alpha, side_a, side_b))
        moved = [high[0].lanes(4), high[1].lanes(4)]
        every = [
            low[0],
            low[1],
            pick(lower_lanes(lane, 4), side_a, moved[0]),
            pick(lower_lanes(lane, 4), moved[0], moved[1]),
            pick(lower_lanes(lane, 4), moved[1], pick(lane < 8, side_b.lanes(4), 0.0)),
        ]
        left_parts.append([split(value) for value in own])
        right_parts.append([split(value) for value in every])

    def wide(parts, which, name, sign=1.0):
        rows = []
        for group in parts:
            pieces = [getattr(value[which], name) for value in group]
            rows.append(jnp.concatenate(pieces, axis=1) * sign)
        return rows

    fill = [jnp.zeros((8, 3 * LANES), jnp.float32)] * 2
    left = (
        wide(left_parts, 0, "re")
        + wide(left_parts, 0, "re")
        + wide(left_parts, 1, "re")
        + wide(left_parts, 0, "im")
        + wide(left_parts, 0, "im")
        + wide(left_parts, 1, "im")
        + fill
    )
    fill = [jnp.zeros((8, 5 * LANES), jnp.float32)] * 2
    right_re = (
        wide(right_parts, 0, "re")
        + wide(right_parts, 1, "re")
        + wide(right_parts, 0, "re")
        + wide(right_parts, 0, "im", -1.0)
        + wide(right_parts, 1, "im", -1.0)
        + wide(right_parts, 0, "im", -1.0)
        + fill
    )
    right_im = (
        wide(right_parts, 0, "im")
        + wide(right_parts, 1, "im")
        + wide(right_parts, 0, "im")
        + wide(right_parts, 0, "re")
        + wide(right_parts, 1, "re")
        + wide(right_parts, 0, "re")
        + fill
    )
    left = jnp.concatenate(left, axis=0)
    top = Cx(
        contract(left, jnp.concatenate(right_re, axis=0)),
        contract(left, jnp.concatenate(right_im, axis=0)),
    )

    masks = []
    for level in range(1, 7):
        for tile in range(max((1 << (6 - level)) // 2, 1)):
            masks.append((level, (lane >> (level + 1)) == 2 * tile + (sub >> 2)))

    def spread(value):
        out = []
        for level, mask in masks:
            out.append(jnp.where(mask, value[level], 0.0))
        return jnp.concatenate(out, axis=0)

    def both(values, half):
        levels = {}
        for group in range(1, GROUPS):
            value = values[group][half]
            if half == 0:
                value = pick(lane < (2 << level_of(group)), nothing, value)
            turned = value.subs(4)
            levels[2 * group - 1] = split(pick(lower4, value, turned))
            levels[2 * group] = split(pick(lower4, turned, value))
        return {
            (which, name): spread(
                {level: getattr(pair[which], name) for level, pair in levels.items()}
            )
            for which in range(2)
            for name in ("re", "im")
        }

    even_d = [inverse_e[0].row(0), inverse_e[0].row(3), inverse_e[3].row(3)]
    even_d = [natural(value, nothing) for value in even_d]

    def local(half):
        low, high = both(inner, half), both(outer, half)
        own = {key: jnp.where(is_alpha, low[key], high[key]) for key in low}
        every = {key: jnp.concatenate([low[key], high[key]], axis=1) for key in low}
        hr, hi, lr, li = (0, "re"), (0, "im"), (1, "re"), (1, "im")
        left = jnp.concatenate([own[key] for key in (hr, hi, hr, hi, lr, li)], axis=0)
        right_re = jnp.concatenate(
            [every[hr], -every[hi], every[lr], -every[li], every[hr], -every[hi]], axis=0
        )
        right_im = jnp.concatenate([every[key] for key in (hi, hr, li, lr, hi, hr)], axis=0)
        product = Cx(contract(left, right_re), contract(left, right_im))
        g_in, g_out = gain_in[half], gain_out[half]
        solo = (lane & 1) == 0
        if half == 0:
            solo = solo & (lane > 0)
        cross = even_d[1][half] * g_in * g_out
        on_in = pick(is_alpha, even_d[0][half] * g_in * g_in, cross)
        on_out = pick(is_alpha, cross, even_d[2][half] * g_out * g_out)
        on_in = pick(solo, on_in, 0.0) - pick(is_alpha, g_in, nothing)
        on_out = pick(solo, on_out, 0.0) - pick(is_alpha, nothing, g_out)
        return product, on_in, on_out

    edge = pick((lane == sub) & lower4, pick(is_alpha, gain_corner[0], gain_corner[1]), 0.0)
    return top, local, edge


def lower_lanes(lane, count):
    return lane < count


def finish(top, local, edge, is_alpha, store):
    lane, sub = iota(1), iota(0)
    full = [top.re, top.im]
    at = 2 * LANES
    both = []
    for part, name in enumerate(("re", "im")):
        edge_part = getattr(edge, name)
        out = [full[part][at : at + 8, t * LANES : (t + 1) * LANES] for t in range(5)]
        out[2] = out[2] - jnp.where(is_alpha, edge_part, 0.0)
        out[4] = out[4] - jnp.where(is_alpha, 0.0, lane_roll(edge_part, 4))
        both.append([-value for value in out])
    store(at, 4, both)
    for half in range(2):
        terms = local(half)
        for row in range(0, LANES, 8):
            here = lane == sub + row
            at = half * LANES + row
            both = []
            for part, name in enumerate(("re", "im")):
                product, on_in, on_out = [getattr(value, name) for value in terms]
                low = product[row : row + 8, :LANES] + jnp.where(here, on_in, 0.0)
                high = product[row : row + 8, LANES:] + jnp.where(here, on_out, 0.0)
                high = lane_roll(high, 4)
                out = [full[part][at : at + 8, t * LANES : (t + 1) * LANES] for t in range(5)]
                out[half] = out[half] + low
                out[2 + half] = out[2 + half] + jnp.where(lane < 4, 0.0, high)
                out[3 + half] = out[3 + half] + jnp.where(lane < 4, high, 0.0)
                both.append([-value for value in out])
            store(at, 8, both)


def interleaved(first, second, half):
    sub = iota(0)
    index = 4 * half + (sub >> 1)
    return jnp.where((sub & 1) == 0, sub_take(first, index), sub_take(second, index))


def cell_data(ref, angular):
    value = ref[...]
    levels = value[:2].astype(jnp.int32)
    lookups = []
    for row in (4, 5):
        table = jnp.broadcast_to(value[row : row + 1, :LANES], (8, LANES))
        halves = []
        for half in range(2):
            index = levels[:, half * LANES : (half + 1) * LANES]
            index = jnp.concatenate([index] * 4, axis=0)
            halves.append(lane_take(table, index)[:2])
        lookups.append(jnp.concatenate(halves, axis=1))
    sheet = value[2:4]
    return angular * lookups[0] * sheet * sheet, lookups[1]


def gather_rows(angular, own, other, is_alpha, is_first, is_last, main, side):
    lane = lax.broadcasted_iota(jnp.int32, (2, LANES), 1)
    own, other = [[cell_data(ref, angular) for ref in refs] for refs in (own, other)]
    for field in range(2):
        (mine, after, near, before), (theirs, after_x, far, before_x) = (
            [data[field] for data in part] for part in (own, other)
        )
        alpha, beta = jnp.where(is_alpha, mine, theirs), jnp.where(is_alpha, theirs, mine)
        main[field, 0:1, :] = jnp.where(is_first, alpha[0:1], jnp.where(is_alpha, near, far)[1:2])
        main[field, 1:3, :] = alpha
        main[field, 3:5, :] = beta
        main[field, 5:6, :] = jnp.where(is_last, beta[1:2], jnp.where(is_alpha, far, near)[0:1])
        main[field, 6:8, :] = beta
        ends = []
        for lefts, rights in ((before, after), (before_x, after_x)):
            left, right = lefts[:, LANES:], rights[:, :LANES]
            ends.append(jnp.where(lane == LANES - 1, left, jnp.where(lane == 0, right, 1.0)))
        ends_alpha = jnp.where(is_alpha, ends[0], ends[1])
        ends_beta = jnp.where(is_alpha, ends[1], ends[0])
        side[field, 0:1, :] = ends_alpha[0:1]
        side[field, 1:3, :] = ends_alpha
        side[field, 3:5, :] = ends_beta
        side[field, 5:7, :] = ends_beta
        side[field, 7:8, :] = ends_beta[0:1]


def merge_kernel(cycles, depth, angular, *refs):
    own, other, (out, main, side, held, sems) = refs[:4], refs[4:8], refs[8:]
    index = lax.axis_index("rad")
    is_alpha = index % 2 == 0
    is_first = index // 2 == 0
    is_last = index // 2 == cycles // 2 - 1
    gather_rows(angular[0], own, other, is_alpha, is_first, is_last, main, side)
    top, local, edge = strip(
        (main[0], main[1]),
        (side[0], side[1]),
        is_alpha,
        (index // 2) * (2 * depth),
        cycles * depth,
    )
    rows = out.shape[0]
    bounds = [*range(0, rows - 2 * depth + 1, 32), rows]
    copies = [
        pltpu.make_async_copy(
            held.at[first : last, :, :], out.at[first : last, :, :], sems.at[number]
        )
        for number, (first, last) in enumerate(zip(bounds, bounds[1:]))
    ]

    def store(row, count, both):
        for number, (real, imag) in enumerate(zip(*both)):
            at = number * LANES
            width = min(LANES, out.shape[2] - at)
            for half in range(count // 4):
                tile = interleaved(real, imag, half)
                first = row + 4 * half
                held[first : first + 4, :, at : at + width] = tile.reshape(4, 2, LANES)[
                    :, :, :width
                ]
        if row + count in bounds:
            copies[bounds.index(row + count) - 1].start()

    finish(top, local, edge, is_alpha, store)
    for copy in copies:
        copy.wait()


def pack_kernel(*refs):
    sources, (out_ref,), targets, sems = refs[:4], refs[4:5], refs[5:9], refs[9]
    copies = [
        pltpu.make_async_copy(source, target, sems.at[number])
        for number, (source, target) in enumerate(zip(sources, targets))
    ]
    for copy in copies:
        copy.start()
    for copy in copies:
        copy.wait()
    material_ref, sheet_ref, sigma_ref, nu_ref = targets
    out_ref[:2, :] = material_ref[...].astype(jnp.float32)
    out_ref[2:4, :] = sheet_ref[...]
    for row, ref in ((4, sigma_ref), (5, nu_ref)):
        out_ref[row : row + 1, : ref.shape[0]] = ref[...].reshape(1, ref.shape[0])


def packed(*arguments):
    held = [pltpu.with_memory_space_constraint(value, pltpu.HBM) for value in arguments]
    return pl.pallas_call(
        pack_kernel,
        out_shape=jax.ShapeDtypeStruct((8, arguments[1].shape[1]), jnp.float32),
        in_specs=[pl.BlockSpec(memory_space=pltpu.HBM)] * 4,
        out_specs=pl.BlockSpec(memory_space=pltpu.VMEM),
        scratch_shapes=[pltpu.VMEM(value.shape, value.dtype) for value in arguments]
        + [pltpu.SemaphoreType.DMA((4,))],
        compiler_params=pltpu.CompilerParams(vmem_limit_bytes=4 * 1024 * 1024),
        name="cells",
    )(*held)


def swapped(cells, axis, first):
    count = lax.axis_size(axis)
    route = []
    for low in range(first, count, 2):
        high = (low + 1) % count
        route += [(low, high), (high, low)]
    return lax.ppermute(cells, axis, route)


def per_device(material_id, thickness, sigma_table, nu_table, angular_frequency):
    depth, arc = thickness.shape
    cells = packed(material_id, thickness, sigma_table, nu_table)
    cycles = lax.axis_size("rad")
    blocks = lax.axis_size("az")
    before = lax.ppermute(cells, "az", [(i, (i + 1) % blocks) for i in range(blocks)])
    after = lax.ppermute(cells, "az", [((i + 1) % blocks, i) for i in range(blocks)])
    own = [cells, after, swapped(cells, "rad", 1), before]
    other = [swapped(part, "rad", 0) for part in own]
    outer_nodes = arc + 2 * depth
    out = pl.pallas_call(
        lambda *refs: merge_kernel(cycles, depth, *refs),
        out_shape=jax.ShapeDtypeStruct((outer_nodes, 2, 2 * outer_nodes), jnp.float32),
        in_specs=[pl.BlockSpec(memory_space=pltpu.SMEM)]
        + [pl.BlockSpec(memory_space=pltpu.VMEM)] * 8,
        out_specs=pl.BlockSpec(memory_space=pltpu.HBM),
        scratch_shapes=[
            pltpu.VMEM((2, 8, arc), jnp.float32),
            pltpu.VMEM((2, 8, LANES), jnp.float32),
            pltpu.VMEM((outer_nodes, 2, 2 * outer_nodes), jnp.float32),
            pltpu.SemaphoreType.DMA((arc // 32 + 1,)),
        ],
        compiler_params=pltpu.CompilerParams(vmem_limit_bytes=48 * 1024 * 1024),
        name="pair_map",
    )(angular_frequency, *own, *other)
    return jnp.transpose(out, (1, 0, 2))


def solution(mesh):
    placed = (P("rad", "az"), P("rad", "az"), P(), P(), P())
    return jax.shard_map(
        per_device, mesh=mesh, in_specs=placed, out_specs=P(None, "rad", "az"), check_vma=False
    )
```

```python
import jax
import jax.numpy as jnp
from jax import lax
from jax.experimental import pallas as pl
from jax.experimental.pallas import tpu as pltpu
from jax.sharding import PartitionSpec as P

SHEET_NODES = 16
LANES = 128
GROUPS = 4


def lane_roll(value, shift):
    return pltpu.roll(value, shift % value.shape[1], 1)


def sub_roll(value, shift):
    return pltpu.roll(value, shift % value.shape[0], 0)


def lane_take(value, index):
    return jnp.take_along_axis(value, index, axis=1, mode="promise_in_bounds")


def sub_take(value, index):
    return jnp.take_along_axis(value, index, axis=0, mode="promise_in_bounds")


def iota(dim):
    return lax.broadcasted_iota(jnp.int32, (8, LANES), dim)


class Cx:
    def __init__(self, re, im):
        self.re, self.im = re, im

    def __add__(self, other):
        return Cx(self.re + other.re, self.im + other.im)

    def __sub__(self, other):
        return Cx(self.re - other.re, self.im - other.im)

    def __neg__(self):
        return Cx(-self.re, -self.im)

    def __mul__(self, other):
        if not isinstance(other, Cx):
            return Cx(self.re * other, self.im * other)
        return Cx(
            self.re * other.re - self.im * other.im, self.re * other.im + self.im * other.re
        )

    def inverse(self):
        size = self.re * self.re + self.im * self.im
        scale = pl.reciprocal(size, approx=True)
        for _ in range(2):
            scale = scale * (2.0 - size * scale)
        return Cx(self.re * scale, -self.im * scale)

    def root(self):
        size = jnp.sqrt(self.re * self.re + self.im * self.im)
        re = jnp.sqrt(0.5 * (size + self.re))
        return Cx(re, 0.5 * self.im / re)

    def map(self, function):
        return Cx(function(self.re), function(self.im))

    def row(self, index):
        return self.map(lambda part: jnp.broadcast_to(part[index : index + 1], (8, LANES)))

    def lanes(self, shift):
        return self.map(lambda part: lane_roll(part, shift))

    def subs(self, shift):
        return self.map(lambda part: sub_roll(part, shift))


def pick(mask, first, second):
    if not isinstance(second, Cx):
        return first.map(lambda part: jnp.where(mask, part, second))
    return Cx(jnp.where(mask, first.re, second.re), jnp.where(mask, first.im, second.im))


def total(terms):
    terms = list(terms)
    while len(terms) > 1:
        terms = [
            terms[i] + terms[i + 1] if i + 1 < len(terms) else terms[i]
            for i in range(0, len(terms), 2)
        ]
    return terms[0]


def harmonic(left, right):
    return (left * right) * (left + right).inverse() * 2.0


def lamination(skin, base):
    above = Cx(jnp.ones_like(skin), jnp.zeros_like(skin))
    field = Cx(jnp.ones_like(skin), 0.5 * skin)
    summed = above
    for _ in range(SHEET_NODES - 1):
        summed = summed + field
        below = Cx(
            2.0 * field.re - skin * field.im - above.re,
            2.0 * field.im + skin * field.re - above.im,
        )
        above, field = field, below
    return field * summed.inverse() * (base * SHEET_NODES)


def factor(entry):
    work = {(r, c): entry(r, c) for r in range(4) for c in range(r + 1)}
    lower, pivots = {}, []
    for k in range(4):
        inverse = work[k, k].inverse()
        pivots.append(inverse)
        for r in range(k + 1, 4):
            lower[r, k] = work[r, k] * inverse
        for r in range(k + 1, 4):
            for c in range(k + 1, r + 1):
                work[r, c] = work[r, c] - lower[r, k] * work[c, k]
    return lower, pivots


def solve(lower, pivots, right):
    half = []
    for r in range(4):
        value = right[r]
        for c in range(r):
            value = value - lower[r, c] * half[c]
        half.append(value)
    out = [None] * 4
    for r in range(3, -1, -1):
        value = half[r] * pivots[r]
        for c in range(r + 1, 4):
            value = value - lower[c, r] * out[c]
        out[r] = value
    return out


def inverse2(first, second, cross):
    scale = (first * second - cross * cross).inverse()
    return second * scale, first * scale, -(cross * scale)


def solve_blocks(entry, right):
    cross = [[entry(2 + c, r) for c in range(2)] for r in range(2)]
    i00, i11, i01 = inverse2(entry(0, 0), entry(1, 1), entry(1, 0))
    ratio = [
        [i00 * cross[0][c] + i01 * cross[1][c] for c in range(2)],
        [i01 * cross[0][c] + i11 * cross[1][c] for c in range(2)],
    ]

    def rest(r, c):
        return entry(2 + r, 2 + c) - (cross[0][r] * ratio[0][c] + cross[1][r] * ratio[1][c])

    j00, j11, j01 = inverse2(rest(0, 0), rest(1, 1), rest(1, 0))
    start = [i00 * right[0] + i01 * right[1], i01 * right[0] + i11 * right[1]]
    low = [right[2 + r] - (ratio[0][r] * right[0] + ratio[1][r] * right[1]) for r in range(2)]
    out = [j00 * low[0] + j01 * low[1], j01 * low[0] + j11 * low[1]]
    return [start[r] - (ratio[r][0] * out[0] + ratio[r][1] * out[1]) for r in range(2)] + out


def seeds(lower, pivots):
    column = iota(0) & 3
    unit = {}
    for r in range(4):
        for c in range(r - 1, -1, -1):
            value = -lower[r, c]
            for k in range(c + 1, r):
                value = value - lower[r, k] * unit[k, c]
            unit[r, c] = value
    roots = [pivot.root() for pivot in pivots]
    out = []
    for r in range(4):
        value = pick(column == r, roots[r], 0.0)
        for k in range(r + 1, 4):
            value = pick(column == k, roots[k] * unit[k, r], value)
        out.append(value)
    return out


def evens(tiles):
    lane = iota(1)
    index = (2 * lane) & (LANES - 1)

    def one(offset):
        return Cx(
            *(
                jnp.where(
                    lane < LANES // 2,
                    lane_take(first, index + offset),
                    lane_take(second, index + offset),
                )
                for first, second in ((tiles[0].re, tiles[1].re), (tiles[0].im, tiles[1].im))
            )
        )

    return one(0), one(1)


def natural(even, odd):
    lane = iota(1)
    out = []
    for half in range(2):
        index = half * (LANES // 2) + (lane >> 1)
        out.append(
            Cx(
                *(
                    jnp.where((lane & 1) == 0, lane_take(first, index), lane_take(second, index))
                    for first, second in ((even.re, odd.re), (even.im, odd.im))
                )
            )
        )
    return out


def split(value):
    high = value.map(lambda part: part.astype(jnp.bfloat16).astype(jnp.float32))
    return high, value - high


def contract(left, right):
    return lax.dot_general(
        left,
        right,
        (((0,), (0,)), ((), ())),
        preferred_element_type=jnp.float32,
    )


def strip(main, side, is_alpha, first_cycle, radial_count):
    lane, sub = iota(1), iota(0)
    lower4 = sub < 4
    column = sub & 3

    rims = lamination(*side)
    tiles = [lamination(*cells) for cells in main]
    cycle = (first_cycle + sub - 1).astype(jnp.float32)
    center = 1.0 + (cycle + 0.5) / radial_count
    face = 1.0 + cycle / radial_count
    per_center = 1.0 / center
    first_lane, last_lane = lane == 0, lane == LANES - 1

    ahead = [tile.lanes(1) for tile in tiles]
    west = [
        harmonic(pick(first_lane, rims.lanes(1), ahead[0]), tiles[0]) * per_center,
        harmonic(pick(first_lane, ahead[0], ahead[1]), tiles[1]) * per_center,
    ]
    wall = harmonic(tiles[1], rims.lanes(-1)) * per_center * 2.0
    back = [tile.lanes(-1) for tile in west]
    east = [pick(last_lane, back[1], back[0]), pick(last_lane, wall, back[1])]
    west[0] = pick(first_lane, west[0] * 2.0, west[0])
    south, north = [], []
    for tile in tiles:
        radial = harmonic(tile.subs(1), tile) * face
        radial = pick((sub == 1) | (sub == 5), radial * 2.0, radial)
        south.append(radial)
        north.append(radial.subs(-1))
    diagonal = [west[h] + east[h] + south[h] + north[h] for h in range(2)]
    gain_in = [south[h].row(1) for h in range(2)]
    gain_out = [north[h].row(4) for h in range(2)]

    diag_e, diag_o = evens(diagonal)
    east_e, east_o = evens(east)
    up_e, up_o = evens(north)
    left_e = pick(last_lane, east_o, 0.0)
    left_e = (east_o - left_e).lanes(1)

    def entry_e(r, c):
        if r == c:
            return diag_e.row(r + 1)
        return -up_e.row(r)

    lower_e, pivots_e = {}, []
    work = diag_e.row(1)
    for r in range(4):
        pivots_e.append(work.inverse())
        if r < 3:
            coupling = up_e.row(r + 1)
            lower_e[r + 1, r] = -(coupling * pivots_e[r])
            work = diag_e.row(r + 2) + lower_e[r + 1, r] * coupling
    zero = jnp.zeros((8, LANES), jnp.float32)
    nothing = Cx(zero, zero)
    half = []
    for r in range(4):
        value = Cx(jnp.where(column == r, 1.0, zero), zero)
        if r:
            value = value - lower_e[r, r - 1] * half[r - 1]
        half.append(value)
    inverse_e = [None] * 4
    for r in range(3, -1, -1):
        value = half[r] * pivots_e[r]
        if r < 3:
            value = value - lower_e[r + 1, r] * inverse_e[r + 1]
        inverse_e[r] = value
    for r in range(4):
        for c in range(r - 1):
            lower_e[r, c] = nothing
    seeds_e = seeds(lower_e, pivots_e)
    sides_e = pick(lower4, left_e.subs(-1), east_e.subs(3))
    reach_e = [inverse_e[r] * sides_e for r in range(4)]
    matrix, pair = [], []
    for r in range(4):
        to_left = (left_e.row(r + 1) * reach_e[r]).lanes(-1)
        to_right = east_e.row(r + 1) * reach_e[r]
        pair.append(pick(lower4, to_right, to_left))
        change = pick(lower4, to_left, to_right)
        base = pick(column == r, diag_o.row(r + 1), 0.0)
        if r < 3:
            base = pick(column == r + 1, -up_o.row(r + 1), base)
        if r > 0:
            base = pick(column == r - 1, -up_o.row(r), base)
        matrix.append(base - change - change.subs(4))

    for level in range(1, 8):
        step = 1 << (level - 1)
        stay = ((lane + 1) & (2 * step - 1)) == 0
        reach = solve_blocks(lambda r, c: matrix[r].row(c), pair)
        next_matrix, next_pair = [], []
        for r in range(4):
            to_left = total(pair[k].row(r) * reach[k] for k in range(4)).lanes(-step)
            to_right = total(pair[k].row(4 + r) * reach[k] for k in range(4)).lanes(step)
            change = pick(lower4, to_left, to_right)
            change = change + change.subs(4)
            next_matrix.append(pick(stay, matrix[r] - change, matrix[r]))
            next_pair.append(pick(stay, pick(lower4, to_right, to_left), pair[r]))
        matrix, pair = next_matrix, next_pair

    lower, pivots = factor(lambda r, c: matrix[r].row(c))
    reach = solve(lower, pivots, pair)
    reach_rows = [[reach[r].row(k) for k in range(8)] for r in range(4)]
    seed = seeds(lower, pivots)

    def level_of(group):
        return jnp.where(lower4, 2 * group - 1, 2 * group)

    own_level = jnp.ones((8, LANES), jnp.int32)
    for level in range(2, 9):
        own_level = own_level + (((lane + 1) & ((1 << (level - 1)) - 1)) == 0).astype(jnp.int32)

    odd = {}
    for group in range(1, GROUPS + 1):
        rows = [pick(own_level == level_of(group), seed[r], 0.0) for r in range(4)]
        for level in range(min(2 * group - 1, 7), 0, -1):
            step = 1 << (level - 1)
            here = own_level == level
            before = [row.lanes(step) for row in rows]
            after = [row.lanes(-step) for row in rows]
            fresh = []
            for r in range(4):
                terms = [reach_rows[r][k] * before[k] for k in range(4)]
                terms += [reach_rows[r][4 + k] * after[k] for k in range(4)]
                fresh.append(rows[r] + pick(here, total(terms), 0.0))
            rows = fresh
        odd[group] = rows

    reach_e_rows = [[reach_e[r].row(k) for k in range(8)] for r in range(4)]
    even = {0: [pick(first_lane & lower4, seeds_e[r], 0.0) for r in range(4)]}
    odd[0] = [nothing] * 4
    for group in range(1, GROUPS + 1):
        before = [row.lanes(1) for row in odd[group]]
        even[group] = []
        for r in range(4):
            terms = [reach_e_rows[r][4 + k] * odd[group][k] for k in range(4)]
            if r in (0, 3):
                terms += [reach_e_rows[r][k] * before[k] for k in range(4)]
            even[group].append(total(terms))

    def corners(lefts, rights):
        return pick(
            lane == 0,
            lefts[0],
            pick(
                lane == 1,
                lefts[1].lanes(1),
                pick(lane == 2, rights[0].lanes(3), pick(lane == 3, rights[1].lanes(4), 0.0)),
            ),
        )

    gains_left = [west[0].row(r + 1) for r in range(4)]
    gains_right = [east[1].row(r + 1) for r in range(4)]
    gain_corner = [
        corners(gains_left[2 * t : 2 * t + 2], gains_right[2 * t : 2 * t + 2]) for t in range(2)
    ]
    inner, outer, corner = {}, {}, {}
    for group in range(GROUPS + 1):
        if group:
            low = natural(even[group][0], odd[group][0])
            high = natural(even[group][3], odd[group][3])
        else:
            low, high = [even[0][0], nothing], [even[0][3], nothing]
        inner[group] = [low[h] * gain_in[h] for h in range(2)]
        outer[group] = [high[h] * gain_out[h] for h in range(2)]
        corner[group] = [
            corners(even[group][2 * t : 2 * t + 2], odd[group][2 * t : 2 * t + 2]) * gain_corner[t]
            for t in range(2)
        ]

    left_parts, right_parts = [], []
    for group in range(GROUPS + 1):
        if group in (0, GROUPS):
            low, high = inner[group], outer[group]
            if group == 0:
                low = [low[0], pick(lower4, nothing, inner[3][1])]
                high = [high[0], pick(lower4, nothing, outer[3][1])]
        else:
            near = lane < (2 << level_of(group))
            low = [pick(near, inner[group][0], 0.0), nothing]
            high = [pick(near, outer[group][0], 0.0), nothing]
        side_a, side_b = corner[group]
        own = [pick(is_alpha, low[h], high[h]) for h in range(2)]
        own.append(pick(is_alpha, side_a, side_b))
        moved = [high[0].lanes(4), high[1].lanes(4)]
        every = [
            low[0],
            low[1],
            pick(lower_lanes(lane, 4), side_a, moved[0]),
            pick(lower_lanes(lane, 4), moved[0], moved[1]),
            pick(lower_lanes(lane, 4), moved[1], pick(lane < 8, side_b.lanes(4), 0.0)),
        ]
        left_parts.append([split(value) for value in own])
        right_parts.append([split(value) for value in every])

    def wide(parts, which, name, sign=1.0):
        rows = []
        for group in parts:
            pieces = [getattr(value[which], name) for value in group]
            row = jnp.concatenate(pieces, axis=1)
            rows.append(row if sign > 0 else -row)
        return rows

    def stacked(parts, order):
        rows = [row for which, name, sign in order for row in wide(parts, which, name, sign)]
        rows += [jnp.zeros_like(rows[0])] * (32 - len(rows))
        return jnp.concatenate(rows, axis=0).astype(jnp.bfloat16)

    hr, hi, lr, li = (0, "re"), (0, "im"), (1, "re"), (1, "im")
    left = stacked(left_parts, [key + (-1.0,) for key in (hr, hr, lr, hi, hi, li)])
    signs = (1.0, 1.0, 1.0, -1.0, -1.0, -1.0)
    right_re = stacked(
        right_parts, [key + (sign,) for key, sign in zip((hr, lr, hr, hi, li, hi), signs)]
    )
    right_im = stacked(right_parts, [key + (1.0,) for key in (hi, li, hi, hr, lr, hr)])
    top = contract(left, jnp.concatenate([right_re, right_im], axis=1))
    top = Cx(top[:, : 5 * LANES], top[:, 5 * LANES :])

    wide_lane = lax.broadcasted_iota(jnp.int32, (16, LANES), 1)
    wide_sub = lax.broadcasted_iota(jnp.int32, (16, LANES), 0)
    masks = []
    within = wide_lane & 63
    for level in range(1, 4):
        for tile in range(1 << (3 - level)):
            masks.append((level, (within >> (level + 1)) == 4 * tile + (wide_sub >> 2)))
    last = ((within >> 5) == (wide_sub >> 2)) | ((wide_sub >> 2) == 2)
    masks = [
        (level, jnp.where(mask, 1.0, 0.0).astype(jnp.bfloat16))
        for level, mask in masks + [(4, last)]
    ]

    def spread(values):
        levels = {}
        for group in range(1, GROUPS):
            value = values[group]
            turned = value.subs(4)
            levels[2 * group - 1] = pick(lower4, value, turned)
            levels[2 * group] = pick(lower4, turned, value)
        out = {}
        for name in ("re", "im"):
            parts = {level: getattr(value, name) for level, value in levels.items()}
            tiles = {level: [parts[level]] * 2 for level in range(1, 4)}
            tiles[4] = [parts[4], parts[5]]
            tiles = {level: jnp.concatenate(tile, axis=0) for level, tile in tiles.items()}
            high = {level: tile.astype(jnp.bfloat16) for level, tile in tiles.items()}
            low = {
                level: (tile - high[level].astype(jnp.float32)).astype(jnp.bfloat16)
                for level, tile in tiles.items()
            }
            for which, part in enumerate((high, low)):
                rows = [part[level] * mask for level, mask in masks]
                out[which, name] = jnp.concatenate(rows, axis=0)
        return out

    even_d = [inverse_e[0].row(0), inverse_e[0].row(3), inverse_e[3].row(3)]
    even_d = [natural(value, nothing) for value in even_d]

    def local(half, quarter):
        packed, mine = {}, {}
        for group in range(1, GROUPS):
            low, high = inner[group][half], outer[group][half]
            if half == 0:
                near = lane < (2 << level_of(group))
                low, high = pick(near, nothing, low), pick(near, nothing, high)
            packed[group] = pick((lane >> 6) == quarter, low, high.lanes(64))
            turned = packed[group].lanes(64)
            pair = (packed[group], turned) if quarter == 0 else (turned, packed[group])
            mine[group] = -pick(is_alpha, *pair)
        every, mine = spread(packed), spread(mine)
        left = jnp.concatenate([mine[key] for key in (hr, hi, hr, hi, lr, li)], axis=0)
        right_re = jnp.concatenate(
            [every[hr], -every[hi], every[lr], -every[li], every[hr], -every[hi]], axis=0
        )
        right_im = jnp.concatenate([every[key] for key in (hi, hr, li, lr, hi, hr)], axis=0)
        product = contract(left[:, :64], jnp.concatenate([right_re, right_im], axis=1))
        return Cx(product[:, :LANES], product[:, LANES:])

    def diagonals(half):
        g_in, g_out = gain_in[half], gain_out[half]
        solo = (lane & 1) == 0
        if half == 0:
            solo = solo & (lane > 0)
        cross = even_d[1][half] * g_in * g_out
        on_in = pick(is_alpha, even_d[0][half] * g_in * g_in, cross)
        on_out = pick(is_alpha, cross, even_d[2][half] * g_out * g_out)
        on_in = pick(is_alpha, g_in, nothing) - pick(solo, on_in, 0.0)
        on_out = pick(is_alpha, nothing, g_out) - pick(solo, on_out, 0.0)
        return on_in, on_out.lanes(4)

    edge = pick((lane == sub) & lower4, pick(is_alpha, gain_corner[0], gain_corner[1]), 0.0)
    return top, (local, diagonals), edge


def lower_lanes(lane, count):
    return lane < count


def finish(top, local, edge, is_alpha, store):
    lane, sub = iota(1), iota(0)
    full = [top.re, top.im]
    local, diagonals = local
    for half, quarter in ((0, 0), (0, 1), (1, 0), (1, 1)):
        if quarter == 0:
            on_in, on_out = diagonals(half)
        product = local(half, quarter)
        inside = (lane >> 6) == quarter
        for row in range(0, 64, 8):
            here = lane == sub + (64 * quarter + row)
            moved = ((lane - 4) & (LANES - 1)) == sub + (64 * quarter + row)
            at = half * LANES + quarter * 64 + row
            both = []
            for part, name in enumerate(("re", "im")):
                value = getattr(product, name)[row : row + 8]
                low = jnp.where(inside, value, 0.0)
                low = low + jnp.where(here, getattr(on_in, name), 0.0)
                high = lane_roll(jnp.where(inside, 0.0, value), 68)
                high = high + jnp.where(moved, getattr(on_out, name), 0.0)
                out = [full[part][at : at + 8, t * LANES : (t + 1) * LANES] for t in range(5)]
                out[half] = out[half] + low
                if quarter == 0:
                    out[2 + half] = out[2 + half] + high
                else:
                    out[2 + half] = out[2 + half] + jnp.where(lane < 4, 0.0, high)
                    out[3 + half] = out[3 + half] + jnp.where(lane < 4, high, 0.0)
                both.append(out)
            store(at, 8, both)
    at = 2 * LANES
    both = []
    for part, name in enumerate(("re", "im")):
        edge_part = getattr(edge, name)
        out = [full[part][at : at + 8, t * LANES : (t + 1) * LANES] for t in range(5)]
        out[2] = out[2] + jnp.where(is_alpha, edge_part, 0.0)
        out[4] = out[4] + jnp.where(is_alpha, 0.0, lane_roll(edge_part, 4))
        both.append(out)
    store(at, 4, both)


def interleaved(first, second, half):
    sub = iota(0)
    index = 4 * half + (sub >> 1)
    return jnp.where((sub & 1) == 0, sub_take(first, index), sub_take(second, index))


def gather_rows(own, other, is_alpha, is_first, is_last, main, side):
    lane = lax.broadcasted_iota(jnp.int32, (2, LANES), 1)
    for field in range(2):
        rows = slice(2 * field, 2 * field + 2)
        (mine, after, near, before), (theirs, after_x, far, before_x) = (
            [ref[rows, :] for ref in refs] for refs in (own, other)
        )
        alpha, beta = jnp.where(is_alpha, mine, theirs), jnp.where(is_alpha, theirs, mine)
        main[field, 0:1, :] = jnp.where(is_first, alpha[0:1], jnp.where(is_alpha, near, far)[1:2])
        main[field, 1:3, :] = alpha
        main[field, 3:5, :] = beta
        main[field, 5:6, :] = jnp.where(is_last, beta[1:2], jnp.where(is_alpha, far, near)[0:1])
        main[field, 6:8, :] = beta
        ends = []
        for lefts, rights in ((before, after), (before_x, after_x)):
            ends.append(jnp.where(lane == LANES - 1, lefts[:, LANES:], rights[:, :LANES]))
        ends_alpha = jnp.where(is_alpha, ends[0], ends[1])
        ends_beta = jnp.where(is_alpha, ends[1], ends[0])
        side[field, 0:1, :] = ends_alpha[0:1]
        side[field, 1:3, :] = ends_alpha
        side[field, 3:5, :] = ends_beta
        side[field, 5:7, :] = ends_beta
        side[field, 7:8, :] = ends_beta[0:1]


def looked_up(tables, angular, material, sheet):
    index = material.astype(jnp.int32)
    sigma, base = [lane_take(table, index) for table in tables]
    return angular * sigma * sheet * sheet, base


def merge_kernel(cycles, depth, angular, *refs):
    own, other, (out, main, side, held, rest, sems) = refs[:4], refs[4:8], refs[8:]
    index = lax.axis_index("rad")
    is_alpha = index % 2 == 0
    is_first = index // 2 == 0
    is_last = index // 2 == cycles // 2 - 1
    gather_rows(own, other, is_alpha, is_first, is_last, main, side)
    tables = [
        jnp.broadcast_to(own[0][row : row + 1, :LANES], (8, LANES)) for row in (4, 5)
    ]
    parts = [(main, 0), (main, LANES), (side, 0)]
    parts = [
        looked_up(tables, angular[0], ref[0, :, at : at + LANES], ref[1, :, at : at + LANES])
        for ref, at in parts
    ]
    top, local, edge = strip(
        parts[:2],
        parts[2],
        is_alpha,
        (index // 2) * (2 * depth),
        cycles * depth,
    )
    rows, columns = out.shape[0], out.shape[2]
    bounds = [0, 64, 128, 192, rows]
    whole = held.shape[0]
    copies = []
    for number, (first, last) in enumerate(zip(bounds, bounds[1:])):
        part = []
        for tile in range(whole + 1):
            if tile < whole:
                source = held.at[tile].reshape(rows, 2, LANES)
            else:
                source = rest
            at = tile * LANES
            target = out.at[first:last, :, at : min(at + LANES, columns)]
            part.append(
                pltpu.make_async_copy(source.at[first:last, :, :], target, sems.at[number, tile])
            )
        copies.append(part)

    def store(row, count, both):
        for part, tiles in enumerate(both):
            for number, tile in enumerate(tiles[:whole]):
                held[number, pl.ds(2 * row + part, count, stride=2), :] = tile[:count]
        for half in range(count // 4):
            tile = interleaved(both[0][whole], both[1][whole], half).reshape(4, 2, LANES)
            first = row + 4 * half
            rest[first : first + 4, :, :] = tile[:, :, : rest.shape[2]]
        if row + count in bounds:
            for copy in copies[bounds.index(row + count) - 1]:
                copy.start()

    finish(top, local, edge, is_alpha, store)
    for part in copies:
        for copy in part:
            copy.wait()


def pack_kernel(*refs):
    sources, (out_ref,), targets, sems = refs[:4], refs[4:5], refs[5:9], refs[9]
    copies = [
        pltpu.make_async_copy(source, target, sems.at[number])
        for number, (source, target) in enumerate(zip(sources, targets))
    ]
    for copy in copies:
        copy.start()
    for copy in copies:
        copy.wait()
    material_ref, sheet_ref, sigma_ref, nu_ref = targets
    out_ref[:2, :] = material_ref[...].astype(jnp.float32)
    out_ref[2:4, :] = sheet_ref[...]
    for row, ref in ((4, sigma_ref), (5, nu_ref)):
        out_ref[row : row + 1, : ref.shape[0]] = ref[...].reshape(1, ref.shape[0])


def packed(*arguments):
    held = [pltpu.with_memory_space_constraint(value, pltpu.HBM) for value in arguments]
    return pl.pallas_call(
        pack_kernel,
        out_shape=jax.ShapeDtypeStruct((8, arguments[1].shape[1]), jnp.float32),
        in_specs=[pl.BlockSpec(memory_space=pltpu.HBM)] * 4,
        out_specs=pl.BlockSpec(memory_space=pltpu.VMEM),
        scratch_shapes=[pltpu.VMEM(value.shape, value.dtype) for value in arguments]
        + [pltpu.SemaphoreType.DMA((4,))],
        compiler_params=pltpu.CompilerParams(vmem_limit_bytes=4 * 1024 * 1024),
        name="cells",
    )(*held)


def swapped(cells, axis, first):
    count = lax.axis_size(axis)
    route = []
    for low in range(first, count, 2):
        high = (low + 1) % count
        route += [(low, high), (high, low)]
    return lax.ppermute(cells, axis, route)


def per_device(material_id, thickness, sigma_table, nu_table, angular_frequency):
    depth, arc = thickness.shape
    cells = packed(material_id, thickness, sigma_table, nu_table)
    cycles = lax.axis_size("rad")
    blocks = lax.axis_size("az")
    before = lax.ppermute(cells, "az", [(i, (i + 1) % blocks) for i in range(blocks)])
    after = lax.ppermute(cells, "az", [((i + 1) % blocks, i) for i in range(blocks)])
    own = [cells, after, swapped(cells, "rad", 1), before]
    other = [swapped(part, "rad", 0) for part in own]
    outer_nodes = arc + 2 * depth
    whole, rest = divmod(2 * outer_nodes, LANES)
    out = pl.pallas_call(
        lambda *refs: merge_kernel(cycles, depth, *refs),
        out_shape=jax.ShapeDtypeStruct((outer_nodes, 2, 2 * outer_nodes), jnp.float32),
        in_specs=[pl.BlockSpec(memory_space=pltpu.SMEM)]
        + [pl.BlockSpec(memory_space=pltpu.VMEM)] * 8,
        out_specs=pl.BlockSpec(memory_space=pltpu.HBM),
        scratch_shapes=[
            pltpu.VMEM((2, 8, arc), jnp.float32),
            pltpu.VMEM((2, 8, LANES), jnp.float32),
            pltpu.VMEM((whole, 2 * outer_nodes, LANES), jnp.float32),
            pltpu.VMEM((outer_nodes, 2, rest), jnp.float32),
            pltpu.SemaphoreType.DMA((4, whole + 1)),
        ],
        compiler_params=pltpu.CompilerParams(vmem_limit_bytes=48 * 1024 * 1024),
        name="pair_map",
    )(angular_frequency, *own, *other)
    return jnp.transpose(out, (1, 0, 2))


def solution(mesh):
    placed = (P("rad", "az"), P("rad", "az"), P(), P(), P())
    return jax.shard_map(
        per_device, mesh=mesh, in_specs=placed, out_specs=P(None, "rad", "az"), check_vma=False
    )
```
